32 devices in a mesh: grp: 2 (over x), dex: 16 (over z, y, core).
Axes of the slice: x: 2, y: 2, z: 4, core: 2. Of those that a mesh axis runs over, the one named last changes fastest.
Arguments:
- resident_state: float32 [512, 16, 16384], P('grp', None, 'dex'), parts along dimension 0, may hold values from -6 to 6
- resident_conv: float32 [512, 3, 16384], P('grp', None, 'dex'), parts along dimension 0, may hold values from -6 to 6
- prefilled_state: float32 [128, 16, 16384], P(('grp', 'dex')), parts along dimension 0, may hold values from -6 to 6
- prefilled_conv: float32 [128, 3, 16384], P(('grp', 'dex')), parts along dimension 0, may hold values from -6 to 6
- live_counts: int32 [32], P('grp'), parts along dimension 0, may hold values from 1 to 4, 32 in all
- batch_rows: int32 [128], P('grp'), parts along dimension 0, may hold values from 0 to 255, as said below
- step_x: bfloat16 [4, 512, 16384], P(None, 'grp', 'dex'), parts along dimension 1, may hold values from -6 to 6
- step_z: bfloat16 [4, 512, 16384], P(None, 'grp', 'dex'), parts along dimension 1, may hold values from -6 to 6
- conv_weight: float32 [4, 16384], P(None, 'dex'), may hold values from -3 to 3
- conv_bias: float32 [16384], P('dex'), may hold values from -0.5 to 0.5
- x_proj: bfloat16 [16384, 544], P('dex'), may hold values from -0.046875 to 0.046875
- norm_gain: float32 [544], replicated, may hold values from 0.1 to 1.9
- dt_proj: bfloat16 [512, 16384], P(None, 'dex'), may hold values from -0.25 to 0.25
- dt_bias: float32 [16384], P('dex'), may hold values from -4 to 0
- a_log: float32 [16, 16384], P(None, 'dex'), may hold values from 0 to 2.8
- d_skip: float32 [16384], P('dex'), may hold values from 0.5 to 1.5
- out_weight: bfloat16 [16384, 8192], P('dex'), may hold values from -0.046875 to 0.046875
Outputs:
- mixed: bfloat16 [512, 4, 8192], P(('grp', 'dex')), parts along dimension 0
The draws below stay inside these ranges and needn't reach their ends.
There are 2 independent parts, one for each index of `grp`. The reference program is written for one: setup_inputs(seed, part) draws one part's arguments, and reference() takes and returns one part's arrays. A program takes and returns all parts, laid end to end along the dimension named above; an argument that names none is the same for every part. Nothing has to cross between parts.
Inputs may be any that keep to these rules, and one draw needn't show every extreme that they name: `live_counts`: each device's live prefilled requests fill its first slots; the counts add up to 4 * 16 / 2. `batch_rows`: all entries are distinct.
All inputs are finite; a program needn't handle non-finite values.
Results may differ from the reference program's by a relative error of at most 0.025.
Values may be sent and summed in bfloat16 or wider, within the bound.
No kernel may reach another device: no remote copies, remote signals or barrier semaphores. Data moves between devices by JAX's collectives and lax.ppermute only.
A program may use at most 256 MiB of HBM per device.

```python
import math
import jax
import jax.numpy as jnp
import numpy as np
from jax import lax

D = 8192
INNER = 16384
STATE = 16
CONV = 4
DT_RANK = 512
BATCH = 256
CAP = 4
STEPS = 4
MIG = 64
N_DEX = 16


def draw_batch_rows(key, part):
    key = jax.random.fold_in(key, 7)
    first_key, second_key = jax.random.split(key)
    middle = jax.random.permutation(first_key, BATCH - 2)[:MIG - 2] + 1
    values = jnp.concatenate([middle.astype(jnp.int32), jnp.array([0, BATCH - 1], dtype=jnp.int32)])
    order = jax.random.permutation(second_key, MIG)
    return values[order].astype(jnp.int32)


def levels(key, dims, pieces, low, top_value):
    factor_of, own = 1.0, jax.random.fold_in(key, 6)
    for dim, blocks in pieces:
        steps = jnp.exp(jax.random.uniform(jax.random.fold_in(own, dim), (blocks,), jnp.float32, low / len(pieces), top_value / len(pieces)))
        factor_of = factor_of * jnp.repeat(steps, dims[dim] // blocks).reshape([-1 if axis == dim else 1 for axis in range(len(dims))])
    return factor_of


def split_up(number_of, total, limit, slope):
    loads = [(1 << 20) // math.isqrt(standing ** slope) + 1 for standing in range(2, number_of + 1)]
    spare, holding = total - limit - (number_of - 1), [1] * (number_of - 1)
    while spare > 0:
        movable = [i for i in range(number_of - 1) if holding[i] < limit]
        pool, remaining = sum([loads[i] for i in movable]), spare
        for i in movable:
            extra = min(limit - holding[i], max(1, remaining * loads[i] // pool), spare)
            holding[i] = holding[i] + extra
            spare = spare - extra
    return np.array([limit] + holding)


def uneven(rng, number_of, total, reach, lean):
    if number_of == 2:
        one = jax.random.randint(rng, (), max(1, total - reach), min(reach, total - 1) + 1)
        return jnp.stack([one, total - one])
    lengths = jnp.asarray(split_up(number_of, total, reach, lean), jnp.int32)
    twos = (number_of - 1) // 2
    giver, taker = lengths[1:1 + 2 * twos:2], lengths[2:2 + 2 * twos:2]
    room = jnp.minimum(giver - 1, reach - taker)
    moved = jax.random.randint(jax.random.fold_in(rng, 1), (twos,), 0, 1 << 20) % (room + 1)
    lengths = lengths.at[1:1 + 2 * twos:2].set(giver - moved).at[2:2 + 2 * twos:2].set(taker + moved)
    return lengths[jax.random.permutation(jax.random.fold_in(rng, 2), number_of)]


def bell_draw(rng, dims, spread, most, cuts=(), kind=jnp.bfloat16):
    drawn = spread * jax.random.normal(rng, dims, jnp.float32)
    if cuts:
        drawn = drawn * levels(rng, dims, cuts, -0.22, 0.18)
    return jnp.clip(drawn, -most, most).astype(kind)


def setup_inputs(seed: int = 0, part: int = 0) -> dict:
    streams_of = jax.random.split(jax.random.key(seed), 18)
    part_splits = jax.random.split(jax.random.fold_in(streams_of[17], part), 18)
    resident_state = bell_draw(part_splits[0], (BATCH, STATE, INNER), 1.0, 6.0, ((2, 16),), jnp.float32)
    resident_conv = bell_draw(part_splits[1], (BATCH, CONV - 1, INNER), 1.0, 6.0, ((2, 16),), jnp.float32)
    prefilled_state = bell_draw(part_splits[2], (MIG, STATE, INNER), 1.0, 6.0, ((0, 16),), jnp.float32)
    prefilled_conv = bell_draw(part_splits[3], (MIG, CONV - 1, INNER), 1.0, 6.0, ((0, 16),), jnp.float32)
    live_counts = uneven(part_splits[4], N_DEX, CAP * N_DEX // 2, CAP, 2).astype(jnp.int32)
    batch_rows = draw_batch_rows(jax.random.fold_in(jax.random.fold_in(streams_of[17], part), 71), part)
    step_x = bell_draw(part_splits[6], (STEPS, BATCH, INNER), 1.0, 6.0, ((2, 16),))
    step_z = bell_draw(part_splits[7], (STEPS, BATCH, INNER), 1.0, 6.0, ((2, 16),))
    conv_weight = bell_draw(streams_of[8], (CONV, INNER), 0.5, 3.0, ((1, 16),), jnp.float32)
    conv_bias = jnp.clip(jax.random.uniform(streams_of[9], (INNER,), jnp.float32, -0.5, 0.5) * levels(streams_of[9], (INNER,), ((0, 16),), -0.4, 0.0), -0.5, 0.5)
    x_proj = bell_draw(streams_of[10], (INNER, DT_RANK + 2 * STATE), INNER ** -0.5, 0.046875, ((0, 16),))
    norm_gain = jnp.clip(1.0 + 0.18 * jax.random.normal(streams_of[11], (DT_RANK + 2 * STATE,), jnp.float32), 0.1, 1.9)
    dt_proj = bell_draw(streams_of[12], (DT_RANK, INNER), DT_RANK ** -0.5, 0.25, ((1, 16),))
    dt_bias = jnp.clip(-4.0 + 4.0 * jax.random.uniform(streams_of[13], (INNER,), jnp.float32) ** levels(streams_of[13], (INNER,), ((0, 16),), -0.2, 0.2), -4.0, 0.0)
    a_log = jnp.clip(2.8 * jax.random.uniform(streams_of[14], (STATE, INNER), jnp.float32) ** levels(streams_of[14], (STATE, INNER), ((1, 16),), -0.2, 0.2), 0.0, 2.8)
    d_skip = jnp.clip(0.5 + 1.0 * jax.random.uniform(streams_of[15], (INNER,), jnp.float32) ** levels(streams_of[15], (INNER,), ((0, 16),), -0.2, 0.2), 0.5, 1.5)
    out_weight = bell_draw(streams_of[16], (INNER, D), INNER ** -0.5, 0.046875, ((0, 16),))
    return {"resident_state": resident_state, "resident_conv": resident_conv, "prefilled_state": prefilled_state, "prefilled_conv": prefilled_conv, "live_counts": live_counts, "batch_rows": batch_rows, "step_x": step_x, "step_z": step_z, "conv_weight": conv_weight, "conv_bias": conv_bias, "x_proj": x_proj, "norm_gain": norm_gain, "dt_proj": dt_proj, "dt_bias": dt_bias, "a_log": a_log, "d_skip": d_skip, "out_weight": out_weight}


RMS_EPS = 1e-06
BC_FLOOR = 0.2

def normalize(projected, norm_gain):
    dt_part = projected[:, :DT_RANK]
    dt_low = dt_part * lax.rsqrt(lax.optimization_barrier(jnp.mean(dt_part * dt_part, axis=1, keepdims=True)) + RMS_EPS) * norm_gain[:DT_RANK]
    b_part = projected[:, DT_RANK:DT_RANK + STATE]
    c_part = projected[:, DT_RANK + STATE:]
    b_coef = b_part * lax.rsqrt(jnp.maximum(lax.optimization_barrier(jnp.mean(b_part * b_part, axis=1, keepdims=True)), BC_FLOOR)) * norm_gain[DT_RANK:DT_RANK + STATE]
    c_coef = c_part * lax.rsqrt(jnp.maximum(lax.optimization_barrier(jnp.mean(c_part * c_part, axis=1, keepdims=True)), BC_FLOOR)) * norm_gain[DT_RANK + STATE:]
    return (dt_low, b_coef, c_coef)

def output_blocks(gated, out_weight):
    width = INNER // N_DEX

    def add_block(total, block_index):
        g_block = lax.dynamic_slice_in_dim(gated, block_index * width, width, 1)
        w_block = lax.dynamic_slice_in_dim(out_weight, block_index * width, width, 0)
        partial_value = jnp.dot(g_block, w_block, preferred_element_type=jnp.float32).astype(jnp.bfloat16)
        partial_value = lax.optimization_barrier(partial_value)
        return (total + partial_value.astype(jnp.float32), None)
    start_total = jnp.zeros((gated.shape[0], out_weight.shape[1]), jnp.float32)
    total, unused = lax.scan(add_block, start_total, jnp.arange(N_DEX, dtype=jnp.int32))
    return total.astype(jnp.bfloat16)

def reference(resident_state, resident_conv, prefilled_state, prefilled_conv, live_counts, batch_rows, step_x, step_z, conv_weight, conv_bias, x_proj, norm_gain, dt_proj, dt_bias, a_log, d_skip, out_weight):
    is_live = (jnp.arange(CAP, dtype=jnp.int32)[None, :] < live_counts[:, None]).reshape(-1)
    target = jnp.where(is_live, batch_rows, BATCH).astype(jnp.int32)
    ssm_state = resident_state.at[target].set(prefilled_state, mode='drop')
    window = resident_conv.at[target].set(prefilled_conv, mode='drop')
    decay_rate = -jnp.exp(a_log)
    outputs = []
    for step_index in range(STEPS):
        stacked = jnp.concatenate([window, step_x[step_index].astype(jnp.float32)[:, None, :]], axis=1)
        conv_out = jax.nn.silu(lax.optimization_barrier(jnp.sum(stacked * conv_weight[None], axis=1)) + conv_bias)
        window = stacked[:, 1:, :]
        conv_low = conv_out.astype(jnp.bfloat16)
        projected = jnp.dot(conv_low, x_proj, preferred_element_type=jnp.float32)
        dt_low, b_coef, c_coef = normalize(projected, norm_gain)
        step_size = jax.nn.softplus(jnp.dot(dt_low.astype(jnp.bfloat16), dt_proj, preferred_element_type=jnp.float32) + dt_bias)
        ssm_state = jnp.exp(step_size[:, None, :] * decay_rate[None]) * ssm_state + (step_size * conv_out)[:, None, :] * b_coef[:, :, None]
        gated = ((lax.optimization_barrier(jnp.sum(ssm_state * c_coef[:, :, None], axis=1)) + d_skip * conv_out) * jax.nn.silu(step_z[step_index].astype(jnp.float32))).astype(jnp.bfloat16)
        outputs.append(output_blocks(gated, out_weight))
    return jnp.stack(outputs, axis=1)
```

```python
import functools

import jax
import jax.numpy as jnp
from jax import lax
from jax.experimental import pallas as pl
from jax.experimental.pallas import tpu as pltpu
from jax.sharding import PartitionSpec as P

STATE = 16
DT_RANK = 512
STEPS = 4
TAPS = 3
WIDE = DT_RANK + 128

RMS_EPS = 1e-06
BC_FLOOR = 0.2
LOG2E = 1.4426950408889634

BF16 = jnp.bfloat16
F32 = jnp.float32
VMEM_LIMIT = 56 * 1024 * 1024


def params(**kw):
    return pltpu.CompilerParams(vmem_limit_bytes=VMEM_LIMIT, **kw)


def swap(x, mask, n):
    return lax.ppermute(x, "dex", [(i, i ^ mask) for i in range(n)])


def sigmoid(x):
    return 1.0 / (1.0 + jnp.exp(-x))


def whole(shape):
    zeros = (0,) * len(shape)
    return pl.BlockSpec(shape, lambda *_: zeros)


def pack_conv_kernel(x_ref, o_ref):
    slots = x_ref.shape[1]
    for p in range(TAPS):
        o_ref[0, slots * p : slots * (p + 1), :] = x_ref[p].astype(BF16)
    o_ref[0, slots * TAPS :, :] = jnp.zeros_like(o_ref[0, slots * TAPS :, :])


def pack_conv(prefilled_conv, n):
    slots, _, inner = prefilled_conv.shape
    c = inner // n
    return pl.pallas_call(
        pack_conv_kernel,
        grid=(n,),
        in_specs=[pl.BlockSpec((TAPS, slots, c), lambda d: (0, 0, d))],
        out_specs=pl.BlockSpec((1, 4 * slots, c), lambda d: (d, 0, 0)),
        out_shape=jax.ShapeDtypeStruct((n, 4 * slots, c), BF16),
        compiler_params=params(),
        cost_estimate=pl.CostEstimate(flops=0, bytes_accessed=slots * 3 * inner * 6, transcendentals=0),
        name="pack_conv",
    )(jnp.transpose(prefilled_conv, (1, 0, 2)))


def pack_state_kernel(x_ref, o_ref):
    slots = x_ref.shape[0]
    for k in range(slots):
        o_ref[0, STATE * k : STATE * (k + 1), :] = x_ref[k].astype(BF16)


def pack_state(prefilled_state, n):
    slots, _, inner = prefilled_state.shape
    c = inner // n
    return pl.pallas_call(
        pack_state_kernel,
        grid=(n,),
        in_specs=[pl.BlockSpec((slots, STATE, c), lambda d: (0, 0, d))],
        out_specs=pl.BlockSpec((1, slots * STATE, c), lambda d: (d, 0, 0)),
        out_shape=jax.ShapeDtypeStruct((n, slots * STATE, c), BF16),
        compiler_params=params(),
        cost_estimate=pl.CostEstimate(
            flops=0, bytes_accessed=slots * STATE * inner * 6, transcendentals=0
        ),
        name="pack_state",
    )(prefilled_state)


def conv_kernel(steps, n, target_ref, old_ref, moved_ref, x_ref, w_ref, bias_ref, proj_ref, conv_ref, part_ref, win):
    rows, c = win.shape[1:]
    columns = target_ref.shape[1]
    row_id = lax.broadcasted_iota(jnp.int32, (rows, columns), 0)
    for p in range(TAPS):
        hot = row_id == target_ref[p : p + 1, :]
        taken = jnp.max(hot.astype(F32), axis=1, keepdims=True) > 0.0
        fresh = jnp.dot(hot.astype(BF16), moved_ref[...], preferred_element_type=F32)
        win[p] = jnp.where(taken, fresh, old_ref[p])
    for i, t in enumerate(steps):
        total = None
        for q in range(TAPS + 1):
            place = t + q
            value = win[place] if place < TAPS else x_ref[place - TAPS].astype(F32)
            term = value * w_ref[q : q + 1, :]
            total = term if total is None else total + term
        total = total + bias_ref[...]
        conv_out = total * sigmoid(total)
        conv_ref[i] = conv_out
        part = lax.dot_general(
            conv_out.astype(BF16), proj_ref[...], (((1,), (1,)), ((), ())), preferred_element_type=F32
        )
        for d in range(n):
            own = rows // n
            part_ref[d, i, :, : part.shape[1]] = part[d * own : (d + 1) * own, :].astype(BF16)
            part_ref[d, i, :, part.shape[1] :] = jnp.zeros((own, WIDE - part.shape[1]), BF16)


def conv_steps(steps, n, target, old, moved, step_x, conv_weight, conv_bias, proj):
    _, rows, c = old.shape
    s = len(steps)
    last = max(steps) + 1
    return pl.pallas_call(
        functools.partial(conv_kernel, steps, n),
        grid=(1,),
        in_specs=[
            whole(target.shape),
            whole(old.shape),
            whole(moved.shape),
            whole((last, rows, c)),
            whole(conv_weight.shape),
            whole((1, c)),
            whole(proj.shape),
        ],
        out_specs=[whole((s, rows, c)), whole((n, s, rows // n, WIDE))],
        out_shape=[
            jax.ShapeDtypeStruct((s, rows, c), F32),
            jax.ShapeDtypeStruct((n, s, rows // n, WIDE), BF16),
        ],
        scratch_shapes=[pltpu.VMEM((TAPS, rows, c), F32)],
        compiler_params=params(),
        cost_estimate=pl.CostEstimate(
            flops=2 * s * rows * c * 544,
            bytes_accessed=rows * c * (12 + 6 * s) + c * 1088,
            transcendentals=s * rows * c,
        ),
        name="conv_project",
    )(target, old, moved, step_x, conv_weight, conv_bias, proj)


def norm_kernel(n, part_ref, gain_ref, o_ref):
    total = part_ref[0].astype(F32)
    for d in range(1, n):
        total = total + part_ref[d].astype(F32)
    dt = total[:, :, :DT_RANK]
    dt = dt * lax.rsqrt(jnp.mean(dt * dt, axis=2, keepdims=True) + RMS_EPS) * gain_ref[:, :DT_RANK][None]
    tail = total[:, :, DT_RANK:]
    lane = lax.broadcasted_iota(jnp.int32, tail.shape, 2)
    square = tail * tail
    is_b = lane < STATE
    is_c = jnp.logical_and(lane >= STATE, lane < 2 * STATE)
    mean_b = jnp.sum(jnp.where(is_b, square, 0.0), axis=2, keepdims=True) / STATE
    mean_c = jnp.sum(jnp.where(is_c, square, 0.0), axis=2, keepdims=True) / STATE
    scale_b = lax.rsqrt(jnp.maximum(mean_b, BC_FLOOR))
    scale_c = lax.rsqrt(jnp.maximum(mean_c, BC_FLOOR))
    tail = tail * jnp.where(is_b, scale_b, scale_c) * gain_ref[:, DT_RANK:][None]
    tail = jnp.where(lane < 2 * STATE, tail, 0.0)
    dt = dt.astype(BF16)
    tail = tail.astype(BF16)
    for d in range(n):
        o_ref[d, :, :, :DT_RANK] = dt
        o_ref[d, :, :, DT_RANK:] = tail


def norm(part, gain, n):
    return pl.pallas_call(
        functools.partial(norm_kernel, n),
        grid=(1,),
        in_specs=[whole(part.shape), whole(gain.shape)],
        out_specs=whole(part.shape),
        out_shape=jax.ShapeDtypeStruct(part.shape, BF16),
        compiler_params=params(),
        cost_estimate=pl.CostEstimate(flops=part.size, bytes_accessed=part.size * 4, transcendentals=0),
        name="norm",
    )(part, gain)


def state_kernel(first, last, n, me_ref, slot_ref, *refs):
    if first:
        moved_ref, refs = refs[0], refs[1:]
    low_ref, conv_ref, z_ref, dtp_ref, dtb_ref, alog_ref, skip_ref, state_ref, *refs = refs
    if last:
        gated_ref, step_scr, bc_scr, decay_scr, y_scr = refs
        new_ref = None
    else:
        new_ref, gated_ref, step_scr, bc_scr, decay_scr, y_scr = refs
    block = pl.program_id(0)
    rows, c = step_scr.shape
    take = state_ref.shape[0]
    blocks = rows // take

    @pl.when(block == 0)
    def _():
        low = low_ref[...].reshape(rows, WIDE)
        pre = jnp.dot(low[:, :DT_RANK], dtp_ref[...], preferred_element_type=F32) + dtb_ref[...]
        step_scr[...] = jnp.maximum(pre, 0.0) + jnp.log(1.0 + jnp.exp(-jnp.abs(pre)))
        decay_scr[...] = jnp.exp(alog_ref[...]) * (-LOG2E)
        tail = low[:, DT_RANK:].astype(F32)
        per = 128 // take
        for h in range(rows // 128):
            turned = tail[128 * h : 128 * (h + 1), :].T
            for i in range(per):
                bc_scr[h * per + i, :, :take] = turned[: 2 * STATE, take * i : take * (i + 1)]

    base = block * take
    bc = bc_scr[block]
    from_ref = new_ref if first else state_ref
    lanes = 256
    for r in range(take):
        if first:
            slot = slot_ref[base + r]

            @pl.when(slot >= 0)
            def _(r=r, slot=slot):
                new_ref[r] = moved_ref[slot].astype(F32)

            @pl.when(slot < 0)
            def _(r=r):
                new_ref[r] = state_ref[r]

        b = bc[:STATE, r : r + 1]
        g = bc[STATE : 2 * STATE, r : r + 1]
        for l in range(0, c, lanes):
            cols = slice(l, l + lanes)
            step = step_scr[pl.ds(base + r, 1), cols]
            drive = step * conv_ref[pl.ds(r, 1), cols]
            state = jnp.exp2(step * decay_scr[:, cols]) * from_ref[r, :, cols] + drive * b
            if new_ref is not None:
                new_ref[r, :, cols] = state
            y_scr[pl.ds(r, 1), cols] = jnp.sum(state * g, axis=0, keepdims=True)
    z = z_ref[0].astype(F32)
    gated = (y_scr[...] + skip_ref[...] * conv_ref[...]) * (z * sigmoid(z))
    gated_ref[...] = gated.astype(BF16)


def state_step(t, index, me, slot_of_row, moved, low, conv, step_z, dt_proj, dt_bias, a_log, d_skip, state, n):
    rows, _, c = state.shape
    take = 2 * rows // n
    blocks = rows // take
    first, last = t == 0, t == STEPS - 1
    own = rows // n

    def placed(i, me_ref, slot_ref):
        z, y = i // 2, i % 2
        mine = (y == (me_ref[0] // 2) % 2).astype(jnp.int32)
        return (mine * (blocks // 2) + z, 0)

    in_specs = [
        pl.BlockSpec((n, None, own, WIDE), lambda i, *_: (0, index, 0, 0)),
        pl.BlockSpec((None, take, c), lambda i, *_: (index, i, 0)),
        pl.BlockSpec((1, take, c), lambda i, *_: (t, i, 0)),
        whole(dt_proj.shape),
        whole((1, c)),
        whole(a_log.shape),
        whole((1, c)),
        pl.BlockSpec((take, STATE, c), lambda i, *_: (i, 0, 0)),
    ]
    args = [low, conv, step_z, dt_proj, dt_bias, a_log, d_skip, state]
    if first:
        in_specs = [whole(moved.shape)] + in_specs
        args = [moved] + args
    out_specs = [pl.BlockSpec((take, c), placed)]
    out_shape = [jax.ShapeDtypeStruct((rows, c), BF16)]
    if not last:
        out_specs = [pl.BlockSpec((take, STATE, c), lambda i, *_: (i, 0, 0))] + out_specs
        out_shape = [jax.ShapeDtypeStruct(state.shape, F32)] + out_shape
    out = pl.pallas_call(
        functools.partial(state_kernel, first, last, n),
        grid_spec=pltpu.PrefetchScalarGridSpec(
            num_scalar_prefetch=2,
            grid=(blocks,),
            in_specs=in_specs,
            out_specs=out_specs,
            scratch_shapes=[
                pltpu.VMEM((rows, c), F32),
                pltpu.VMEM((blocks, 2 * STATE, 128), F32),
                pltpu.VMEM((STATE, c), F32),
                pltpu.VMEM((take, c), F32),
            ],
        ),
        out_shape=out_shape,
        compiler_params=params(),
        cost_estimate=pl.CostEstimate(
            flops=8 * state.size, bytes_accessed=8 * state.size, transcendentals=state.size
        ),
        name="state_step",
    )(me, slot_of_row, *args)
    return (None, out[0]) if last else (out[0], out[1])


def out_kernel(me_ref, own_ref, other_ref, wown_ref, wother_ref, send_ref, keep_ref):
    total = jnp.dot(own_ref[...], wown_ref[...], preferred_element_type=F32)
    total = total + jnp.dot(other_ref[...], wother_ref[...], preferred_element_type=F32)
    half = send_ref.shape[0]
    send_ref[...] = total[:half].astype(BF16)
    keep_ref[...] = total[half:].astype(BF16)


def out_project(me, own, other, out_weight, other_weight):
    rows, c = own.shape
    cols = other_weight.shape[1]
    tile = 512
    tiles = cols // tile
    half = jax.ShapeDtypeStruct((rows // 2, cols), BF16)
    return pl.pallas_call(
        out_kernel,
        grid_spec=pltpu.PrefetchScalarGridSpec(
            num_scalar_prefetch=1,
            grid=(tiles,),
            in_specs=[
                whole(own.shape),
                whole(other.shape),
                pl.BlockSpec((c, tile), lambda j, me_ref: (0, (me_ref[0] % 2) * tiles + j)),
                pl.BlockSpec((c, tile), lambda j, me_ref: (0, j)),
            ],
            out_specs=[pl.BlockSpec((rows // 2, tile), lambda j, me_ref: (0, j))] * 2,
        ),
        out_shape=[half, half],
        compiler_params=params(),
        cost_estimate=pl.CostEstimate(
            flops=4 * rows * c * cols, bytes_accessed=4 * c * cols + 2 * rows * cols, transcendentals=0
        ),
        name="out_project",
    )(me, own, other, out_weight, other_weight)


def pieces_kernel(zs, me_ref, keep_ref, got_ref, *o_refs):
    core = me_ref[0] % 2
    z = me_ref[0] // 4
    for m in range(zs):
        at = jnp.bitwise_xor(z, m)
        total = keep_ref[at].astype(F32) + got_ref[at].astype(F32)
        own = total.shape[0] // 2
        low, high = total[:own], total[own:]
        o_refs[2 * m][...] = jnp.where(core == 0, low, high).astype(BF16)
        o_refs[2 * m + 1][...] = jnp.where(core == 0, high, low).astype(BF16)


def sum_pieces(me, keep, got, n):
    half, cols = keep.shape
    zs = n // 4
    take = half // zs
    own = take // 2
    tile = 1024
    shape = jax.ShapeDtypeStruct((own, cols), BF16)
    return pl.pallas_call(
        functools.partial(pieces_kernel, zs),
        grid_spec=pltpu.PrefetchScalarGridSpec(
            num_scalar_prefetch=1,
            grid=(cols // tile,),
            in_specs=[pl.BlockSpec((zs, take, tile), lambda j, me_ref: (0, 0, j))] * 2,
            out_specs=[pl.BlockSpec((own, tile), lambda j, me_ref: (0, j))] * (2 * zs),
        ),
        out_shape=[shape] * (2 * zs),
        compiler_params=params(),
        cost_estimate=pl.CostEstimate(flops=half * cols, bytes_accessed=6 * half * cols, transcendentals=0),
        name="sum_pieces",
    )(me, keep.reshape(zs, take, cols), got.reshape(zs, take, cols))


def final_kernel(zs, me_ref, *refs):
    o_ref = refs[-1]
    pieces = refs[:-1]
    side = pl.program_id(0)
    own_half = side == me_ref[0] % 2
    for t in range(STEPS):
        at = 2 * zs * t
        mine = pieces[at][...].astype(F32)
        theirs = pieces[at + 1][...].astype(F32)
        for m in range(1, zs):
            mine = mine + pieces[at + 2 * m][...].astype(F32)
            theirs = theirs + pieces[at + 2 * m + 1][...].astype(F32)
        o_ref[:, t, :] = jnp.where(own_half, mine, theirs).astype(BF16)


def final_sum(me, pieces, n):
    own, cols = pieces[0].shape
    zs = n // 4
    tile = 1024
    tiles = cols // tile
    return pl.pallas_call(
        functools.partial(final_kernel, zs),
        grid_spec=pltpu.PrefetchScalarGridSpec(
            num_scalar_prefetch=1,
            grid=(2, tiles),
            in_specs=[pl.BlockSpec((own, tile), lambda s, j, me_ref: (0, j))] * len(pieces),
            out_specs=pl.BlockSpec((own, STEPS, tile), lambda s, j, me_ref: (0, 0, s * tiles + j)),
        ),
        out_shape=jax.ShapeDtypeStruct((own, STEPS, 2 * cols), BF16),
        compiler_params=params(),
        cost_estimate=pl.CostEstimate(
            flops=own * cols * len(pieces), bytes_accessed=own * cols * 2 * len(pieces), transcendentals=0
        ),
        name="final_sum",
    )(me, *pieces)


def shards(
    resident_state,
    resident_conv,
    prefilled_state,
    prefilled_conv,
    live_counts,
    batch_rows,
    step_x,
    step_z,
    conv_weight,
    conv_bias,
    x_proj,
    norm_gain,
    dt_proj,
    dt_bias,
    a_log,
    d_skip,
    out_weight,
):
    n = lax.axis_size("dex")
    rows = resident_state.shape[0]
    slots = prefilled_state.shape[0]
    c = resident_state.shape[2]
    me_scalar = lax.axis_index("dex").astype(jnp.int32)
    me = me_scalar.reshape(1)

    moved_conv = lax.all_to_all(pack_conv(prefilled_conv, n), "dex", 0, 0, tiled=True)
    moved_state = lax.all_to_all(pack_state(prefilled_state, n), "dex", 0, 0, tiled=True)

    cols = out_weight.shape[1] // 2
    core = me_scalar % 2
    other_weight = swap(lax.dynamic_slice_in_dim(out_weight, (1 - core) * cols, cols, 1), 1, n)

    is_live = jnp.arange(slots, dtype=jnp.int32)[None, :] < live_counts[:, None]
    target = jnp.where(is_live, batch_rows.reshape(n, slots), -1)
    spread = jnp.full((TAPS, n, 4, slots), -1, jnp.int32)
    place = jnp.arange(4, dtype=jnp.int32)[None, None, :, None]
    tap = jnp.arange(TAPS, dtype=jnp.int32)[:, None, None, None]
    spread = jnp.where(place == tap, target[None, :, None, :], spread).reshape(TAPS, n * 4 * slots)
    hit = target.reshape(1, n * slots) == jnp.arange(rows, dtype=jnp.int32)[:, None]
    slot_of_row = jnp.max(
        jnp.where(hit, jnp.arange(n * slots, dtype=jnp.int32)[None, :], -1), axis=1
    )
    gain = jnp.concatenate([norm_gain, jnp.zeros((WIDE - norm_gain.shape[0],), F32)]).reshape(1, WIDE)
    old = jnp.transpose(resident_conv, (1, 0, 2))
    proj = x_proj.T
    bias = conv_bias.reshape(1, c)
    moved_conv = moved_conv.reshape(n * 4 * slots, c)
    moved_state = moved_state.reshape(n * slots, STATE, c)

    lows = {}
    convs = {}
    for steps in ((0,), tuple(range(1, STEPS))):
        conv, part = conv_steps(steps, n, spread, old, moved_conv, step_x, conv_weight, bias, proj)
        part = lax.all_to_all(part, "dex", 0, 0, tiled=True)
        low = lax.all_to_all(norm(part, gain, n), "dex", 0, 0, tiled=True)
        for i, t in enumerate(steps):
            lows[t] = (low, i)
            convs[t] = conv

    state = resident_state
    pieces = []
    for t in range(STEPS):
        low, i = lows[t]
        state, gated = state_step(
            t, i, me, slot_of_row, moved_state, low, convs[t], step_z, dt_proj,
            dt_bias.reshape(1, c), a_log, d_skip.reshape(1, c), state, n,
        )
        send, keep = out_project(me, gated, swap(gated, 1, n), out_weight, other_weight)
        cut = sum_pieces(me, keep, swap(send, 2, n), n)
        for m in range(n // 4):
            for k in range(2):
                mask = 4 * m + k
                pieces.append(cut[2 * m + k] if mask == 0 else swap(cut[2 * m + k], mask, n))
    return final_sum(me, pieces, n)


def solution(mesh):
    placed = (
        P("grp", None, "dex"),
        P("grp", None, "dex"),
        P(("grp", "dex"), None, None),
        P(("grp", "dex"), None, None),
        P("grp"),
        P("grp"),
        P(None, "grp", "dex"),
        P(None, "grp", "dex"),
        P(None, "dex"),
        P("dex"),
        P("dex", None),
        P(),
        P(None, "dex"),
        P("dex"),
        P(None, "dex"),
        P("dex"),
        P("dex", None),
    )
    return jax.shard_map(
        shards, mesh=mesh, in_specs=placed, out_specs=P(("grp", "dex"), None, None), check_vma=False
    )
```

```python
import functools

import jax
import jax.numpy as jnp
from jax import lax
from jax.experimental import pallas as pl
from jax.experimental.pallas import tpu as pltpu
from jax.sharding import PartitionSpec as P

STATE = 16
DT_RANK = 512
STEPS = 4
TAPS = 3
WIDE = DT_RANK + 128

RMS_EPS = 1e-06
BC_FLOOR = 0.2
LOG2E = 1.4426950408889634

BF16 = jnp.bfloat16
F32 = jnp.float32
VMEM_LIMIT = 56 * 1024 * 1024


def params(**kw):
    return pltpu.CompilerParams(vmem_limit_bytes=VMEM_LIMIT, **kw)


def swap(x, mask, n):
    return lax.ppermute(x, "dex", [(i, i ^ mask) for i in range(n)])


def cost(flops, bytes_accessed, transcendentals=0):
    return pl.CostEstimate(flops=1024, bytes_accessed=1024, transcendentals=0)


def sigmoid(x):
    return 1.0 / (1.0 + jnp.exp(-x))


def whole(shape):
    zeros = (0,) * len(shape)
    return pl.BlockSpec(shape, lambda *_: zeros)


def pack_conv_kernel(x_ref, o_ref):
    slots = x_ref.shape[1]
    n, tall, c = o_ref.shape
    for d in range(n):
        parts = [x_ref[p, :, d * c : (d + 1) * c] for p in range(TAPS)]
        parts.append(jnp.zeros((tall - slots * TAPS, c), F32))
        o_ref[d] = jnp.concatenate(parts, axis=0).astype(BF16)


def pack_conv(prefilled_conv, n):
    slots, _, inner = prefilled_conv.shape
    c = inner // n
    return pl.pallas_call(
        pack_conv_kernel,
        grid=(1,),
        in_specs=[whole((TAPS, slots, inner))],
        out_specs=whole((n, 4 * slots, c)),
        out_shape=jax.ShapeDtypeStruct((n, 4 * slots, c), BF16),
        compiler_params=params(),
        cost_estimate=cost(0, slots * 3 * inner * 6),
        name="pack_conv",
    )(jnp.transpose(prefilled_conv, (1, 0, 2)))


def pack_state_kernel(after_ref, x_ref, o_ref):
    slots = x_ref.shape[0]
    some, _, c = o_ref.shape
    for d in range(some):
        for k in range(slots):
            o_ref[d, STATE * k : STATE * (k + 1), :] = x_ref[k, :, d * c : (d + 1) * c].astype(BF16)


def pack_state(after, prefilled_state, n):
    slots, _, inner = prefilled_state.shape
    c = inner // n
    some = 4
    return pl.pallas_call(
        pack_state_kernel,
        grid=(n // some,),
        in_specs=[
            pl.BlockSpec(memory_space=pl.ANY),
            pl.BlockSpec((slots, STATE, some * c), lambda d: (0, 0, d)),
        ],
        out_specs=pl.BlockSpec((some, slots * STATE, c), lambda d: (d, 0, 0)),
        out_shape=jax.ShapeDtypeStruct((n, slots * STATE, c), BF16),
        compiler_params=params(),
        cost_estimate=cost(0, slots * STATE * inner * 6),
        name="pack_state",
    )(after, prefilled_state)


def half_kernel(me_ref, after_ref, w_ref, o_ref):
    o_ref[...] = w_ref[...]


def weight_half(me, after, out_weight):
    c, cols = out_weight.shape
    tile = 1024
    tiles = cols // 2 // tile
    return pl.pallas_call(
        half_kernel,
        grid_spec=pltpu.PrefetchScalarGridSpec(
            num_scalar_prefetch=1,
            grid=(tiles,),
            in_specs=[
                pl.BlockSpec(memory_space=pl.ANY),
                pl.BlockSpec((c, tile), lambda j, me_ref: (0, (1 - me_ref[0] % 2) * tiles + j)),
            ],
            out_specs=pl.BlockSpec((c, tile), lambda j, me_ref: (0, j)),
        ),
        out_shape=jax.ShapeDtypeStruct((c, cols // 2), BF16),
        compiler_params=params(),
        cost_estimate=cost(0, 2 * c * cols),
        name="weight_half",
    )(me, after, out_weight)


def conv_kernel(
    steps, n, me_ref, after_ref, target_ref, old_ref, moved_ref, x_ref, w_ref, bias_ref, proj_ref, conv_ref, send_ref, keep_ref, win
):
    rows, c = win.shape[1:]
    columns = target_ref.shape[1]
    own = rows // n
    core = me_ref[0] % 2
    row_id = lax.broadcasted_iota(jnp.int32, (rows, columns), 0)
    for p in range(TAPS):
        hot = row_id == target_ref[p : p + 1, :]
        taken = jnp.max(hot.astype(F32), axis=1, keepdims=True) > 0.0
        fresh = jnp.dot(hot.astype(BF16), moved_ref[...], preferred_element_type=F32)
        win[p] = jnp.where(taken, fresh, old_ref[p])
    for i, t in enumerate(steps):
        total = None
        for q in range(TAPS + 1):
            place = t + q
            value = win[place] if place < TAPS else x_ref[place - TAPS].astype(F32)
            term = value * w_ref[q : q + 1, :]
            total = term if total is None else total + term
        total = total + bias_ref[...]
        conv_out = total * sigmoid(total)
        conv_ref[i] = conv_out
        part = lax.dot_general(
            conv_out.astype(BF16), proj_ref[...], (((1,), (1,)), ((), ())), preferred_element_type=F32
        )
        pad = jnp.zeros((own, WIDE - part.shape[1]), BF16)
        for q in range(n // 2):
            low = part[2 * q * own : (2 * q + 1) * own, :]
            high = part[(2 * q + 1) * own : (2 * q + 2) * own, :]
            send_ref[q, i, :, : part.shape[1]] = jnp.where(core == 0, high, low).astype(BF16)
            keep_ref[q, i, :, : part.shape[1]] = jnp.where(core == 0, low, high).astype(BF16)
            send_ref[q, i, :, part.shape[1] :] = pad
            keep_ref[q, i, :, part.shape[1] :] = pad


def conv_steps(steps, n, me, after, target, old, moved, step_x, conv_weight, conv_bias, proj):
    _, rows, c = old.shape
    s = len(steps)
    last = max(steps) + 1
    parts = (n // 2, s, rows // n, WIDE)
    return pl.pallas_call(
        functools.partial(conv_kernel, steps, n),
        grid_spec=pltpu.PrefetchScalarGridSpec(
            num_scalar_prefetch=1,
            grid=(1,),
            in_specs=[
                pl.BlockSpec(memory_space=pl.ANY),
                whole(target.shape),
                whole(old.shape),
                whole(moved.shape),
                whole((last, rows, c)),
                whole(conv_weight.shape),
                whole((1, c)),
                whole(proj.shape),
            ],
            out_specs=[whole((s, rows, c)), whole(parts), whole(parts)],
            scratch_shapes=[pltpu.VMEM((TAPS, rows, c), F32)],
        ),
        out_shape=[jax.ShapeDtypeStruct((s, rows, c), F32)] + [jax.ShapeDtypeStruct(parts, BF16)] * 2,
        compiler_params=params(),
        cost_estimate=cost(2 * s * rows * c * 544, rows * c * (12 + 6 * s) + c * 1088, s * rows * c),
        name="conv_project",
    )(me, after, target, old, moved, step_x, conv_weight, conv_bias, proj)


def add_y_kernel(me_ref, keep_ref, got_ref, send_ref, left_ref):
    y = (me_ref[0] // 2) % 2
    for z in range(send_ref.shape[0]):
        for o_ref, at in ((send_ref, 2 * z + 1 - y), (left_ref, 2 * z + y)):
            o_ref[z] = (keep_ref[at].astype(F32) + got_ref[at].astype(F32)).astype(BF16)


def add_z_kernel(me_ref, keep_ref, got_ref, *o_refs):
    z = me_ref[0] // 4
    for m, o_ref in enumerate(o_refs):
        at = jnp.bitwise_xor(z, m)
        o_ref[...] = (keep_ref[at].astype(F32) + got_ref[at].astype(F32)).astype(BF16)


def norm_kernel(gain_ref, *refs):
    o_ref = refs[-1]
    total = refs[0][...].astype(F32)
    for ref in refs[1:-1]:
        total = total + ref[...].astype(F32)
    dt = total[:, :, :DT_RANK]
    dt = dt * lax.rsqrt(jnp.mean(dt * dt, axis=2, keepdims=True) + RMS_EPS) * gain_ref[:, :DT_RANK][None]
    tail = total[:, :, DT_RANK:]
    lane = lax.broadcasted_iota(jnp.int32, tail.shape, 2)
    square = tail * tail
    is_b = lane < STATE
    is_c = jnp.logical_and(lane >= STATE, lane < 2 * STATE)
    mean_b = jnp.sum(jnp.where(is_b, square, 0.0), axis=2, keepdims=True) / STATE
    mean_c = jnp.sum(jnp.where(is_c, square, 0.0), axis=2, keepdims=True) / STATE
    scale_b = lax.rsqrt(jnp.maximum(mean_b, BC_FLOOR))
    scale_c = lax.rsqrt(jnp.maximum(mean_c, BC_FLOOR))
    tail = tail * jnp.where(is_b, scale_b, scale_c) * gain_ref[:, DT_RANK:][None]
    o_ref[:, :, :DT_RANK] = dt.astype(BF16)
    o_ref[:, :, DT_RANK:] = jnp.where(lane < 2 * STATE, tail, 0.0).astype(BF16)


def merge_kernel(me_ref, *refs):
    o_ref = refs[-1]
    z = me_ref[0] // 4
    for m, ref in enumerate(refs[:-1]):
        o_ref[jnp.bitwise_xor(z, m)] = ref[...]


def small(kernel, me, args, shapes, name, after=()):
    size = sum(a.size for a in args)
    return pl.pallas_call(
        kernel,
        grid_spec=pltpu.PrefetchScalarGridSpec(
            num_scalar_prefetch=1,
            grid=(1,),
            in_specs=[pl.BlockSpec(memory_space=pl.ANY)] * len(after) + [whole(a.shape) for a in args],
            out_specs=[whole(s) for s in shapes],
        ),
        out_shape=[jax.ShapeDtypeStruct(s, BF16) for s in shapes],
        compiler_params=params(),
        cost_estimate=cost(size, 4 * size),
        name=name,
    )(me, *after, *args)


def reduce_projection(send, keep, gain, me, n):
    zs = n // 4
    piece = keep.shape[1:]
    got = swap(send, 1, n)
    send, keep = small(add_y_kernel, me, [keep, got], [(zs,) + piece] * 2, "add_y")
    got = swap(send, 2, n)
    cut = small(add_z_kernel, me, [keep, got], [piece] * zs, "add_z")
    cut = [cut[0]] + [swap(cut[m], 4 * m, n) for m in range(1, zs)]
    low = pl.pallas_call(
        norm_kernel,
        grid=(1,),
        in_specs=[whole(gain.shape)] + [whole(piece)] * zs,
        out_specs=whole(piece),
        out_shape=jax.ShapeDtypeStruct(piece, BF16),
        compiler_params=params(),
        cost_estimate=cost(cut[0].size * zs, cut[0].size * 2 * zs),
        name="norm",
    )(gain, *cut)
    lows = [low] + [swap(low, 4 * m, n) for m in range(1, zs)]
    (mine,) = small(merge_kernel, me, lows, [(zs,) + piece], "merge_z")
    beside = swap(mine, 2, n)
    return low, (mine, beside, swap(mine, 1, n), swap(beside, 1, n))


def state_kernel(first, last, me_ref, slot_ref, *refs):
    if first:
        moved_ref, fresh_ref, *refs = refs
    else:
        _, *refs = refs
    lows, refs = refs[:4], refs[4:]
    conv_ref, z_ref, dtp_ref, dtb_ref, alog_ref, skip_ref, *refs = refs
    states = conv_ref.shape[1] // 128 if first else 1
    states, refs = refs[:states], refs[states:]
    new_ref = None
    if not last:
        new_ref, *refs = refs
    gated_ref, low_scr, step_scr, tail_scr, decay_scr, *refs = refs
    block = pl.program_id(0)
    rows, c = step_scr.shape
    take = conv_ref.shape[0]
    y, core = (me_ref[0] // 2) % 2, me_ref[0] % 2

    @pl.when(block == 0)
    def _():
        for i, low_ref in enumerate(lows):
            for z in range(low_ref.shape[0]):
                low_scr[z, jnp.bitwise_xor(y, i % 2), jnp.bitwise_xor(core, i // 2)] = low_ref[z]
        low = low_scr[...].reshape(rows, WIDE)
        pre = jnp.dot(low[:, :DT_RANK], dtp_ref[...], preferred_element_type=F32) + dtb_ref[...]
        step_scr[...] = jnp.maximum(pre, 0.0) + jnp.log(1.0 + jnp.exp(-jnp.abs(pre)))
        decay_scr[...] = jnp.exp(alog_ref[...]) * (-LOG2E)
        tail_scr[...] = low[:, DT_RANK:].astype(F32)

    base = block * take
    if first:
        fresh_scr = refs[0]
        for r in range(take):
            slot = slot_ref[base + r]

            @pl.when(slot >= 0)
            def _(r=r, slot=slot):
                value = moved_ref[slot].astype(F32)
                for l in range(c // 128):
                    fresh_scr[l, STATE * r : STATE * (r + 1), :] = value[:, 128 * l : 128 * (l + 1)]

    tall, lanes = 16, min(512, c)
    for r in range(0, take, tall):
        tail = tail_scr[pl.ds(base + r, tall), :]
        for l in range(0, c, lanes):
            cols = slice(l, l + lanes)
            step = step_scr[pl.ds(base + r, tall), cols]
            conv = conv_ref[r : r + tall, cols]
            drive = step * conv
            total = skip_ref[:, cols] * conv
            for s in range(STATE):
                if first:
                    at = pl.ds(STATE * r + s, tall, stride=STATE)
                    taken = fresh_ref[r : r + tall, :] > 0.0
                    old = jnp.concatenate(
                        [
                            jnp.where(taken, fresh_scr[k, at, :], states[k][at, :])
                            for k in range(l // 128, (l + lanes) // 128)
                        ],
                        axis=1,
                    )
                else:
                    old = states[0][s, r : r + tall, cols].astype(F32)
                state = jnp.exp2(step * decay_scr[s : s + 1, cols]) * old + drive * tail[:, s : s + 1]
                if not last:
                    new_ref[s, r : r + tall, cols] = state.astype(BF16)
                total = total + state * tail[:, STATE + s : STATE + s + 1]
            z = z_ref[0, r : r + tall, cols].astype(F32)
            gated_ref[r : r + tall, cols] = (total * (z * sigmoid(z))).astype(BF16)


def state_step(t, index, me, slot_of_row, extra, lows, conv, step_z, dt_proj, dt_bias, a_log, d_skip, state, n):
    _, rows, c = conv.shape
    take = 2 * rows // n
    blocks = rows // take
    first, last = t == 0, t == STEPS - 1
    own = rows // n
    zs = n // 4

    def placed(i, me_ref, slot_ref):
        z, y = i // 2, i % 2
        mine = (y == (me_ref[0] // 2) % 2).astype(jnp.int32)
        return (mine * (blocks // 2) + z, 0)

    in_specs = [pl.BlockSpec((zs, None, own, WIDE), lambda i, *_: (0, index, 0, 0))] * 4 + [
        pl.BlockSpec((None, take, c), lambda i, *_: (index, i, 0)),
        pl.BlockSpec((1, take, c), lambda i, *_: (t, i, 0)),
        whole(dt_proj.shape),
        whole((1, c)),
        whole(a_log.shape),
        whole((1, c)),
    ]
    scratch = [
        pltpu.VMEM((zs, 2, 2, own, WIDE), BF16),
        pltpu.VMEM((rows, c), F32),
        pltpu.VMEM((rows, 128), F32),
        pltpu.VMEM((STATE, c), F32),
    ]
    flat = pl.BlockSpec((STATE, take, c), lambda i, *_: (0, i, 0))
    if first:
        moved, fresh = extra
        in_specs = [whole(moved.shape), pl.BlockSpec((take, 128), lambda i, *_: (i, 0))] + in_specs
        tiles = c // 128
        in_specs += [pl.BlockSpec((take * STATE, 128), lambda i, *_, l=l: (i, l)) for l in range(tiles)]
        scratch.append(pltpu.VMEM((tiles, take * STATE, 128), F32))
        states = [state] * tiles
    else:
        in_specs = [pl.BlockSpec(memory_space=pl.ANY)] + in_specs + [flat]
        states = [state]
    out_specs = [pl.BlockSpec((take, c), placed)]
    out_shape = [jax.ShapeDtypeStruct((rows, c), BF16)]
    if not last:
        out_specs = [flat] + out_specs
        out_shape = [jax.ShapeDtypeStruct((STATE, rows, c), BF16)] + out_shape
    size = rows * STATE * c
    out = pl.pallas_call(
        functools.partial(state_kernel, first, last),
        grid_spec=pltpu.PrefetchScalarGridSpec(
            num_scalar_prefetch=2,
            grid=(blocks,),
            in_specs=in_specs,
            out_specs=out_specs,
            scratch_shapes=scratch,
        ),
        out_shape=out_shape,
        compiler_params=params(),
        cost_estimate=cost(8 * size, 4 * size, size),
        name="state_step",
    )(me, slot_of_row, *extra, *lows, conv, step_z, dt_proj, dt_bias, a_log, d_skip, *states)
    return (None, out[0]) if last else (out[0], out[1])


def out_kernel(me_ref, own_ref, other_ref, wown_ref, wother_ref, send_ref, keep_ref):
    total = jnp.dot(own_ref[...], wown_ref[...], preferred_element_type=F32)
    total = total + jnp.dot(other_ref[...], wother_ref[...], preferred_element_type=F32)
    half = send_ref.shape[0]
    send_ref[...] = total[:half].astype(BF16)
    keep_ref[...] = total[half:].astype(BF16)


def out_project(me, own, other, out_weight, other_weight):
    rows, c = own.shape
    cols = other_weight.shape[1]
    tile = 1024
    tiles = cols // tile
    half = jax.ShapeDtypeStruct((rows // 2, cols), BF16)
    return pl.pallas_call(
        out_kernel,
        grid_spec=pltpu.PrefetchScalarGridSpec(
            num_scalar_prefetch=1,
            grid=(tiles,),
            in_specs=[
                whole(own.shape),
                whole(other.shape),
                pl.BlockSpec((c, tile), lambda j, me_ref: (0, (me_ref[0] % 2) * tiles + j)),
                pl.BlockSpec((c, tile), lambda j, me_ref: (0, j)),
            ],
            out_specs=[pl.BlockSpec((rows // 2, tile), lambda j, me_ref: (0, j))] * 2,
        ),
        out_shape=[half, half],
        compiler_params=params(),
        cost_estimate=cost(4 * rows * c * cols, 4 * c * cols + 2 * rows * cols),
        name="out_project",
    )(me, own, other, out_weight, other_weight)


def pieces_kernel(behind, me_ref, keep_ref, got_ref, *refs):
    z = me_ref[0] // 4
    for m, o_ref in enumerate(refs[behind:]):
        at = jnp.bitwise_xor(z, m)
        o_ref[...] = (keep_ref[at].astype(F32) + got_ref[at].astype(F32)).astype(BF16)


def sum_pieces(me, keep, got, after, n):
    half, cols = keep.shape
    zs = n // 4
    take = half // zs
    tile = 2048
    return pl.pallas_call(
        functools.partial(pieces_kernel, len(after)),
        grid_spec=pltpu.PrefetchScalarGridSpec(
            num_scalar_prefetch=1,
            grid=(cols // tile,),
            in_specs=[pl.BlockSpec((zs, take, tile), lambda j, me_ref: (0, 0, j))] * 2
            + [pl.BlockSpec(memory_space=pl.ANY)] * len(after),
            out_specs=[pl.BlockSpec((take, tile), lambda j, me_ref: (0, j))] * zs,
        ),
        out_shape=[jax.ShapeDtypeStruct((take, cols), BF16)] * zs,
        compiler_params=params(),
        cost_estimate=cost(half * cols, 6 * half * cols),
        name="sum_pieces",
    )(me, keep.reshape(zs, take, cols), got.reshape(zs, take, cols), *after)


def sum_z_kernel(me_ref, after_ref, *refs):
    send_ref, keep_ref = refs[-2:]
    total = refs[0][...].astype(F32)
    for ref in refs[1:-2]:
        total = total + ref[...].astype(F32)
    own = total.shape[0] // 2
    low, high = total[:own], total[own:]
    core = me_ref[0] % 2
    send_ref[...] = jnp.where(core == 0, high, low).astype(BF16)
    keep_ref[...] = jnp.where(core == 0, low, high).astype(BF16)


def final_kernel(tiles, me_ref, *refs):
    o_ref = refs[-1]
    own_half = pl.program_id(0) // tiles == me_ref[0] % 2
    parts = []
    for t in range(STEPS):
        value = jnp.where(own_half, refs[t][...].astype(F32), refs[STEPS + t][...].astype(F32))
        o_ref[:, t, :] = value.astype(BF16)


def final_join(me, keeps, gots):
    own, cols = keeps[0].shape
    tile = 2048
    tiles = cols // tile
    return pl.pallas_call(
        functools.partial(final_kernel, tiles),
        grid_spec=pltpu.PrefetchScalarGridSpec(
            num_scalar_prefetch=1,
            grid=(2 * tiles,),
            in_specs=[pl.BlockSpec((own, tile), lambda j, me_ref: (0, j % tiles))] * (2 * STEPS),
            out_specs=pl.BlockSpec((own, STEPS, tile), lambda j, me_ref: (0, 0, j)),
        ),
        out_shape=jax.ShapeDtypeStruct((own, STEPS, 2 * cols), BF16),
        compiler_params=params(),
        cost_estimate=cost(0, own * cols * 32),
        name="final_join",
    )(me, *keeps, *gots)


def shards(
    resident_state,
    resident_conv,
    prefilled_state,
    prefilled_conv,
    live_counts,
    batch_rows,
    step_x,
    step_z,
    conv_weight,
    conv_bias,
    x_proj,
    norm_gain,
    dt_proj,
    dt_bias,
    a_log,
    d_skip,
    out_weight,
):
    n = lax.axis_size("dex")
    zs = n // 4
    rows = resident_state.shape[0]
    slots = prefilled_state.shape[0]
    c = resident_state.shape[2]
    me_scalar = lax.axis_index("dex").astype(jnp.int32)
    me = me_scalar.reshape(1)

    packed_conv = pack_conv(prefilled_conv, n)
    moved_conv = lax.all_to_all(packed_conv, "dex", 0, 0, tiled=True)
    packed_state = pack_state(packed_conv, prefilled_state, n)
    moved_state = lax.all_to_all(packed_state, "dex", 0, 0, tiled=True)

    cols = out_weight.shape[1] // 2
    half_weight = weight_half(me, packed_state, out_weight)
    other_weight = swap(half_weight, 1, n)

    is_live = jnp.arange(slots, dtype=jnp.int32)[None, :] < live_counts[:, None]
    target = jnp.where(is_live, batch_rows.reshape(n, slots), -1)
    spread = jnp.full((TAPS, n, 4, slots), -1, jnp.int32)
    place = jnp.arange(4, dtype=jnp.int32)[None, None, :, None]
    tap = jnp.arange(TAPS, dtype=jnp.int32)[:, None, None, None]
    spread = jnp.where(place == tap, target[None, :, None, :], spread).reshape(TAPS, n * 4 * slots)
    hit = target.reshape(1, n * slots) == jnp.arange(rows, dtype=jnp.int32)[:, None]
    slot_of_row = jnp.max(
        jnp.where(hit, jnp.arange(n * slots, dtype=jnp.int32)[None, :], -1), axis=1
    )
    fresh = jnp.broadcast_to(jnp.any(hit, axis=1, keepdims=True).astype(F32), (rows, 128))
    gain = jnp.concatenate([norm_gain, jnp.zeros((WIDE - norm_gain.shape[0],), F32)]).reshape(1, WIDE)
    old = jnp.transpose(resident_conv, (1, 0, 2))
    proj = x_proj.T
    bias = conv_bias.reshape(1, c)
    moved_conv = moved_conv.reshape(n * 4 * slots, c)
    moved_state = moved_state.reshape(n * slots, STATE, c)

    lows = {}
    convs = {}
    after = half_weight
    for steps in ((0,), tuple(range(1, STEPS))):
        conv, send, keep = conv_steps(
            steps, n, me, after, spread, old, moved_conv, step_x, conv_weight, bias, proj
        )
        after, low = reduce_projection(send, keep, gain, me, n)
        for i, t in enumerate(steps):
            lows[t] = (low, i)
            convs[t] = conv

    state = resident_state.reshape(rows * STATE, c)
    extra = (moved_state, fresh)
    sends, keeps, cuts, mine, theirs = [], [], [], [], []

    def reduce_z(t, after):
        cut = [cuts[t][0]] + [swap(cuts[t][m], 4 * m, n) for m in range(1, zs)]
        half = (rows // n, cols)
        send, keep = small(sum_z_kernel, me, cut, [half, half], "sum_z", (after,))
        mine.append(keep)
        theirs.append(swap(send, 1, n))

    def reduce_y(t, after):
        if t > 0:
            reduce_z(t - 1, after)
            after = mine[-1]
        cuts.append(sum_pieces(me, keeps[t], swap(sends[t], 2, n), (after,), n))
        return (cuts[-1][0],)

    for t in range(STEPS):
        low, i = lows[t]
        state, gated = state_step(
            t, i, me, slot_of_row, extra, low, convs[t], step_z, dt_proj,
            dt_bias.reshape(1, c), a_log, d_skip.reshape(1, c), state, n,
        )
        send, keep = out_project(me, gated, swap(gated, 1, n), out_weight, other_weight)
        sends.append(send)
        keeps.append(keep)
        extra = (send,)
        if t > 0:
            extra = reduce_y(t - 1, keep)
    reduce_y(STEPS - 1, keeps[-1])
    reduce_z(STEPS - 1, keeps[-1])
    return final_join(me, mine, theirs)


def solution(mesh):
    placed = (
        P("grp", None, "dex"),
        P("grp", None, "dex"),
        P(("grp", "dex"), None, None),
        P(("grp", "dex"), None, None),
        P("grp"),
        P("grp"),
        P(None, "grp", "dex"),
        P(None, "grp", "dex"),
        P(None, "dex"),
        P("dex"),
        P("dex", None),
        P(),
        P(None, "dex"),
        P("dex"),
        P(None, "dex"),
        P("dex"),
        P("dex", None),
    )
    return jax.shard_map(
        shards, mesh=mesh, in_specs=placed, out_specs=P(("grp", "dex"), None, None), check_vma=False
    )
```

```python
import functools

import jax
import jax.numpy as jnp
from jax import lax
from jax.experimental import pallas as pl
from jax.experimental.pallas import tpu as pltpu
from jax.sharding import PartitionSpec as P

STATE = 16
DT_RANK = 512
STEPS = 4
TAPS = 3
WIDE = DT_RANK + 128

RMS_EPS = 1e-06
BC_FLOOR = 0.2

BF16 = jnp.bfloat16
F32 = jnp.float32


def params(mib):
    return pltpu.CompilerParams(vmem_limit_bytes=mib * 1024 * 1024)


def swap(x, mask, n):
    return lax.ppermute(x, "dex", [(i, i ^ mask) for i in range(n)])


def cost(flops, bytes_accessed, transcendentals=0):
    return pl.CostEstimate(flops=1024, bytes_accessed=1024, transcendentals=0)


def sigmoid(x):
    return 1.0 / (1.0 + jnp.exp(-x))


def whole(shape):
    zeros = (0,) * len(shape)
    return pl.BlockSpec(shape, lambda *_: zeros)


def small(kernel, me, args, shapes, name, after=()):
    size = sum(a.size for a in args)
    return pl.pallas_call(
        kernel,
        grid_spec=pltpu.PrefetchScalarGridSpec(
            num_scalar_prefetch=1,
            grid=(1,),
            in_specs=[pl.BlockSpec(memory_space=pl.ANY)] * len(after) + [whole(a.shape) for a in args],
            out_specs=[whole(s) for s in shapes],
        ),
        out_shape=[jax.ShapeDtypeStruct(s, BF16) for s in shapes],
        compiler_params=params(8),
        cost_estimate=cost(size, 4 * size),
        name=name,
    )(me, *after, *args)


def pack_conv_kernel(me_ref, x_ref, *o_refs):
    zs, _, wide = o_refs[0].shape
    y, core = (me_ref[0] // 2) % 2, me_ref[0] % 2
    c = wide * (TAPS + 1) // TAPS
    for i, o_ref in enumerate(o_refs):
        for z in range(zs):
            dest = 4 * z + 2 * jnp.bitwise_xor(y, i % 2) + jnp.bitwise_xor(core, i // 2)
            x = x_ref[:, :, pl.ds(pl.multiple_of(dest * c, 128), c)]
            parts = [x[p, :, :wide] for p in range(TAPS)]
            parts.append(jnp.concatenate([x[p, :, wide:] for p in range(TAPS)], axis=1))
            o_ref[z] = jnp.concatenate(parts, axis=0).astype(BF16)


def cut_conv_kernel(me_ref, after_ref, *refs):
    zs = refs[0].shape[0]
    z, y, core = me_ref[0] // 4, (me_ref[0] // 2) % 2, me_ref[0] % 2
    for m in range(zs):
        for i in range(4):
            at = 2 * jnp.bitwise_xor(y, i % 2) + jnp.bitwise_xor(core, i // 2)
            refs[4 + m][at] = refs[i][jnp.bitwise_xor(z, m)]


def exchange_conv(prefilled_conv, prefilled_state, me, n):
    slots, _, inner = prefilled_conv.shape
    zs = n // 4
    piece = ((TAPS + 1) * slots, inner // n * TAPS // (TAPS + 1))
    packed = small(pack_conv_kernel, me, [jnp.transpose(prefilled_conv, (1, 0, 2))], [(zs,) + piece] * 4, "pack_conv")
    packed_state = pack_state(packed[0], prefilled_state, n)
    near, far = swap(packed[2], 1, n), swap(packed[3], 1, n)
    got = [packed[0], swap(packed[1], 2, n), near, swap(far, 2, n)]
    cut = small(cut_conv_kernel, me, got, [(4,) + piece] * zs, "cut_conv", (packed_state,))
    return packed_state, [cut[0]] + [swap(cut[m], 4 * m, n) for m in range(1, zs)]


def pack_state_kernel(after_ref, x_ref, o_ref):
    slots = x_ref.shape[0]
    some, _, c = o_ref.shape
    for d in range(some):
        for k in range(slots):
            o_ref[d, STATE * k : STATE * (k + 1), :] = x_ref[k, :, d * c : (d + 1) * c].astype(BF16)


def pack_state(after, prefilled_state, n):
    slots, _, inner = prefilled_state.shape
    c = inner // n
    some = 4
    return pl.pallas_call(
        pack_state_kernel,
        grid=(n // some,),
        in_specs=[
            pl.BlockSpec(memory_space=pl.ANY),
            pl.BlockSpec((slots, STATE, some * c), lambda d: (0, 0, d)),
        ],
        out_specs=pl.BlockSpec((some, slots * STATE, c), lambda d: (d, 0, 0)),
        out_shape=jax.ShapeDtypeStruct((n, slots * STATE, c), BF16),
        compiler_params=params(24),
        cost_estimate=cost(0, slots * STATE * inner * 6),
        name="pack_state",
    )(after, prefilled_state)


def conv_kernel(steps, n, me_ref, target_ref, old_ref, x_ref, w_ref, bias_ref, proj_ref, *refs):
    zs = n // 4
    moved, (conv_ref, send_ref, keep_ref, moved_scr, win) = refs[:zs], refs[-5:]
    rows, c = win.shape[1:]
    columns = target_ref.shape[1]
    own = rows // n
    core, my_z = me_ref[0] % 2, me_ref[0] // 4
    for m in range(zs):
        moved_scr[jnp.bitwise_xor(my_z, m)] = moved[m][...]
    fresh = moved_scr[...].reshape(columns, moved_scr.shape[3])
    wide = fresh.shape[1]
    row_id = lax.broadcasted_iota(jnp.int32, (rows, columns), 0)
    hots = [row_id == target_ref[p : p + 1, :] for p in range(TAPS + 1)]
    taken = jnp.max(hots[0].astype(F32), axis=1, keepdims=True) > 0.0
    fresh = [jnp.dot(hot.astype(BF16), fresh, preferred_element_type=F32) for hot in hots]
    for p in range(TAPS):
        part = (c - wide) * p
        win[p, :, :wide] = jnp.where(taken, fresh[p], old_ref[p, :, :wide])
        win[p, :, wide:] = jnp.where(taken, fresh[TAPS][:, part : part + c - wide], old_ref[p, :, wide:])
    for i, t in enumerate(steps):
        total = None
        for q in range(TAPS + 1):
            place = t + q
            value = win[place] if place < TAPS else x_ref[place - TAPS].astype(F32)
            term = value * w_ref[q : q + 1, :]
            total = term if total is None else total + term
        total = total + bias_ref[...]
        conv_out = total * sigmoid(total)
        conv_ref[i] = conv_out
        part = lax.dot_general(
            conv_out.astype(BF16), proj_ref[...], (((1,), (1,)), ((), ())), preferred_element_type=F32
        )
        pad = jnp.zeros((own, WIDE - part.shape[1]), BF16)
        for q in range(n // 2):
            low = part[2 * q * own : (2 * q + 1) * own, :]
            high = part[(2 * q + 1) * own : (2 * q + 2) * own, :]
            send_ref[q, i, :, : part.shape[1]] = jnp.where(core == 0, high, low).astype(BF16)
            keep_ref[q, i, :, : part.shape[1]] = jnp.where(core == 0, low, high).astype(BF16)
            send_ref[q, i, :, part.shape[1] :] = pad
            keep_ref[q, i, :, part.shape[1] :] = pad


def conv_steps(steps, n, me, after, target, old, moved, step_x, conv_weight, conv_bias, proj):
    _, rows, c = old.shape
    s = len(steps)
    last = max(steps) + 1
    parts = (n // 2, s, rows // n, WIDE)
    return pl.pallas_call(
        functools.partial(conv_kernel, steps, n),
        grid_spec=pltpu.PrefetchScalarGridSpec(
            num_scalar_prefetch=1,
            grid=(1,),
            in_specs=[
                whole(target.shape),
                whole(old.shape),
                whole((last, rows, c)),
                whole(conv_weight.shape),
                whole((1, c)),
                whole(proj.shape),
            ]
            + [whole(moved[0].shape)] * len(moved)
            + [pl.BlockSpec(memory_space=pl.ANY)] * len(after),
            out_specs=[whole((s, rows, c)), whole(parts), whole(parts)],
            scratch_shapes=[
                pltpu.VMEM((len(moved),) + moved[0].shape, BF16),
                pltpu.VMEM((TAPS, rows, c), F32),
            ],
        ),
        out_shape=[jax.ShapeDtypeStruct((s, rows, c), F32)] + [jax.ShapeDtypeStruct(parts, BF16)] * 2,
        compiler_params=params(40),
        cost_estimate=cost(2 * s * rows * c * 544, rows * c * (12 + 6 * s) + c * 1088, s * rows * c),
        name="conv_project",
    )(me, target, old, step_x, conv_weight, conv_bias, proj, *moved, *after)


def add_y_kernel(me_ref, keep_ref, got_ref, send_ref, left_ref):
    y = (me_ref[0] // 2) % 2
    for z in range(send_ref.shape[0]):
        for o_ref, at in ((send_ref, 2 * z + 1 - y), (left_ref, 2 * z + y)):
            o_ref[z] = (keep_ref[at].astype(F32) + got_ref[at].astype(F32)).astype(BF16)


def add_z_kernel(me_ref, keep_ref, got_ref, *o_refs):
    z = me_ref[0] // 4
    for m, o_ref in enumerate(o_refs):
        at = jnp.bitwise_xor(z, m)
        o_ref[...] = (keep_ref[at].astype(F32) + got_ref[at].astype(F32)).astype(BF16)


def norm_kernel(gain_ref, *refs):
    o_ref = refs[-1]
    total = refs[0][...].astype(F32)
    for ref in refs[1:-1]:
        total = total + ref[...].astype(F32)
    dt = total[:, :, :DT_RANK]
    dt = dt * lax.rsqrt(jnp.mean(dt * dt, axis=2, keepdims=True) + RMS_EPS) * gain_ref[:, :DT_RANK][None]
    tail = total[:, :, DT_RANK:]
    lane = lax.broadcasted_iota(jnp.int32, tail.shape, 2)
    square = tail * tail
    is_b = lane < STATE
    is_c = jnp.logical_and(lane >= STATE, lane < 2 * STATE)
    mean_b = jnp.sum(jnp.where(is_b, square, 0.0), axis=2, keepdims=True) / STATE
    mean_c = jnp.sum(jnp.where(is_c, square, 0.0), axis=2, keepdims=True) / STATE
    scale_b = lax.rsqrt(jnp.maximum(mean_b, BC_FLOOR))
    scale_c = lax.rsqrt(jnp.maximum(mean_c, BC_FLOOR))
    tail = tail * jnp.where(is_b, scale_b, scale_c) * gain_ref[:, DT_RANK:][None]
    o_ref[:, :, :DT_RANK] = dt.astype(BF16)
    o_ref[:, :, DT_RANK:] = jnp.where(lane < 2 * STATE, tail, 0.0).astype(BF16)


def merge_kernel(me_ref, *refs):
    o_ref = refs[-1]
    z = me_ref[0] // 4
    for m, ref in enumerate(refs[:-1]):
        o_ref[jnp.bitwise_xor(z, m)] = ref[...]


def reduce_projection(send, keep, gain, me, n):
    zs = n // 4
    piece = keep.shape[1:]
    got = swap(send, 1, n)
    send, keep = small(add_y_kernel, me, [keep, got], [(zs,) + piece] * 2, "add_y")
    got = swap(send, 2, n)
    cut = small(add_z_kernel, me, [keep, got], [piece] * zs, "add_z")
    cut = [cut[0]] + [swap(cut[m], 4 * m, n) for m in range(1, zs)]
    low = pl.pallas_call(
        norm_kernel,
        grid=(1,),
        in_specs=[whole(gain.shape)] + [whole(piece)] * zs,
        out_specs=whole(piece),
        out_shape=jax.ShapeDtypeStruct(piece, BF16),
        compiler_params=params(8),
        cost_estimate=cost(cut[0].size * zs, cut[0].size * 2 * zs),
        name="norm",
    )(gain, *cut)
    lows = [low] + [swap(low, 4 * m, n) for m in range(1, zs)]
    (mine,) = small(merge_kernel, me, lows, [(zs,) + piece], "merge_z")
    beside = swap(mine, 2, n)
    return low, (mine, beside, swap(mine, 1, n), swap(beside, 1, n))


def state_kernel(first, last, me_ref, live_ref, *refs):
    if first:
        moved_ref, *refs = refs
    else:
        _, *refs = refs
    lows, refs = refs[:4], refs[4:]
    conv_ref, z_ref, dtp_ref, dtb_ref, alog_ref, skip_ref, state_ref, *refs = refs
    new_ref = None
    if not last:
        new_ref, *refs = refs
    gated_ref, low_scr, step_scr, tail_scr, decay_scr, *refs = refs
    block = pl.program_id(0)
    rows, c = step_scr.shape
    take = conv_ref.shape[0]
    blocks = rows // take
    y, core = (me_ref[0] // 2) % 2, me_ref[0] % 2

    if first:
        buf, sems = refs

        def fetch(at, slot):
            first_row = pl.multiple_of(at * (take * STATE), take * STATE)
            return [
                pltpu.make_async_copy(
                    state_ref.at[pl.ds(first_row, take * STATE), 128 * l : 128 * (l + 1)],
                    buf.at[slot, l],
                    sems.at[slot, l],
                )
                for l in range(c // 128)
            ]

        now = lax.rem(block, 2)

        @pl.when(block == 0)
        def _():
            for copy in fetch(0, 0):
                copy.start()

        @pl.when(block + 1 < blocks)
        def _():
            for copy in fetch(block + 1, 1 - now):
                copy.start()

    @pl.when(block == 0)
    def _():
        for i, low_ref in enumerate(lows):
            for z in range(low_ref.shape[0]):
                low_scr[z, jnp.bitwise_xor(y, i % 2), jnp.bitwise_xor(core, i // 2)] = low_ref[z]
        low = low_scr[...].reshape(rows, WIDE)
        pre = jnp.dot(low[:, :DT_RANK], dtp_ref[...], preferred_element_type=F32) + dtb_ref[...]
        step_scr[...] = jnp.maximum(pre, 0.0) + jnp.log(1.0 + jnp.exp(-jnp.abs(pre)))
        decay_scr[...] = -jnp.exp(alog_ref[...])
        tail_scr[...] = low[:, DT_RANK:].astype(F32)

    base = block * take
    if first:
        for copy in fetch(block, now):
            copy.wait()

        def replace(i, carry):
            at = pl.multiple_of((live_ref[1, i] - base) * STATE, STATE)
            value = moved_ref[live_ref[2, i]].astype(F32)
            for l in range(c // 128):
                buf[now, l, pl.ds(at, STATE), :] = value[:, 128 * l : 128 * (l + 1)]
            return carry

        lax.fori_loop(live_ref[0, block], live_ref[0, block + 1], replace, 0)

    tall, lanes = 16, min(512, c)
    for r in range(0, take, tall):
        tail = tail_scr[pl.ds(base + r, tall), :]
        for l in range(0, c, lanes):
            cols = slice(l, l + lanes)
            step = step_scr[pl.ds(base + r, tall), cols]
            conv = conv_ref[r : r + tall, cols]
            drive = step * conv
            total = skip_ref[:, cols] * conv
            for s in range(STATE):
                if first:
                    at = pl.ds(STATE * r + s, tall, stride=STATE)
                    tiles = range(l // 128, (l + lanes) // 128)
                    old = jnp.concatenate([buf[now, k, at, :] for k in tiles], axis=1)
                else:
                    old = state_ref[s, r : r + tall, cols].astype(F32)
                state = jnp.exp(step * decay_scr[s : s + 1, cols]) * old + drive * tail[:, s : s + 1]
                if not last:
                    new_ref[s, r : r + tall, cols] = state.astype(BF16)
                total = total + state * tail[:, STATE + s : STATE + s + 1]
            z = z_ref[0, r : r + tall, cols].astype(F32)
            gated_ref[r : r + tall, cols] = (total * (z * sigmoid(z))).astype(BF16)


def state_step(t, index, me, live, extra, lows, conv, step_z, dt_proj, dt_bias, a_log, d_skip, state, n):
    _, rows, c = conv.shape
    take = 2 * rows // n
    blocks = rows // take
    first, last = t == 0, t == STEPS - 1
    own = rows // n
    zs = n // 4

    def placed(i, me_ref, live_ref):
        z, y = i // 2, i % 2
        mine = (y == (me_ref[0] // 2) % 2).astype(jnp.int32)
        return (mine * (blocks // 2) + z, 0)

    in_specs = [pl.BlockSpec((zs, None, own, WIDE), lambda i, *_: (0, index, 0, 0))] * 4 + [
        pl.BlockSpec((None, take, c), lambda i, *_: (index, i, 0)),
        pl.BlockSpec((1, take, c), lambda i, *_: (t, i, 0)),
        whole(dt_proj.shape),
        whole((1, c)),
        whole(a_log.shape),
        whole((1, c)),
    ]
    scratch = [
        pltpu.VMEM((zs, 2, 2, own, WIDE), BF16),
        pltpu.VMEM((rows, c), F32),
        pltpu.VMEM((rows, 128), F32),
        pltpu.VMEM((STATE, c), F32),
    ]
    flat = pl.BlockSpec((STATE, take, c), lambda i, *_: (0, i, 0))
    if first:
        in_specs = [whole(extra[0].shape)] + in_specs + [pl.BlockSpec(memory_space=pl.ANY)]
        scratch += [
            pltpu.VMEM((2, c // 128, take * STATE, 128), F32),
            pltpu.SemaphoreType.DMA((2, c // 128)),
        ]
    else:
        in_specs = [pl.BlockSpec(memory_space=pl.ANY)] + in_specs + [flat]
    out_specs = [pl.BlockSpec((take, c), placed)]
    out_shape = [jax.ShapeDtypeStruct((rows, c), BF16)]
    if not last:
        out_specs = [flat] + out_specs
        out_shape = [jax.ShapeDtypeStruct((STATE, rows, c), BF16)] + out_shape
    size = rows * STATE * c
    out = pl.pallas_call(
        functools.partial(state_kernel, first, last),
        grid_spec=pltpu.PrefetchScalarGridSpec(
            num_scalar_prefetch=2,
            grid=(blocks,),
            in_specs=in_specs,
            out_specs=out_specs,
            scratch_shapes=scratch,
        ),
        out_shape=out_shape,
        compiler_params=params(32),
        cost_estimate=cost(8 * size, 4 * size, size),
        name="state_step",
    )(me, live, *extra, *lows, conv, step_z, dt_proj, dt_bias, a_log, d_skip, state)
    return (None, out[0]) if last else (out[0], out[1])


def out_kernel(me_ref, own_ref, other_ref, wown_ref, wother_ref, *refs):
    send_ref, keep_ref = refs[-2:]
    total = jnp.dot(own_ref[...], wown_ref[...], preferred_element_type=F32)
    total = total + jnp.dot(other_ref[...], wother_ref[...], preferred_element_type=F32)
    half = send_ref.shape[0]
    send_ref[...] = total[:half].astype(BF16)
    keep_ref[...] = total[half:].astype(BF16)


def out_project(me, own, other, out_weight, other_weight, after):
    rows, c = own.shape
    cols = out_weight.shape[1] // 2
    tile = 1024
    tiles = cols // tile
    half = jax.ShapeDtypeStruct((rows // 2, cols), BF16)
    return pl.pallas_call(
        out_kernel,
        grid_spec=pltpu.PrefetchScalarGridSpec(
            num_scalar_prefetch=1,
            grid=(tiles,),
            in_specs=[
                whole(own.shape),
                whole(other.shape),
                pl.BlockSpec((c, tile), lambda j, me_ref: (0, (me_ref[0] % 2) * tiles + j)),
                pl.BlockSpec((c, tile), lambda j, me_ref: (0, (me_ref[0] % 2) * tiles + j)),
            ]
            + [pl.BlockSpec(memory_space=pl.ANY)] * len(after),
            out_specs=[pl.BlockSpec((rows // 2, tile), lambda j, me_ref: (0, j))] * 2,
        ),
        out_shape=[half, half],
        compiler_params=params(24),
        cost_estimate=cost(4 * rows * c * cols, 4 * c * cols + 2 * rows * cols),
        name="out_project",
    )(me, own, other, out_weight, other_weight, *after)


def pieces_kernel(behind, me_ref, keep_ref, got_ref, *refs):
    z = me_ref[0] // 4
    for m, o_ref in enumerate(refs[behind:]):
        at = jnp.bitwise_xor(z, m)
        o_ref[...] = (keep_ref[at].astype(F32) + got_ref[at].astype(F32)).astype(BF16)


def sum_pieces(me, keep, got, after, n):
    half, cols = keep.shape
    zs = n // 4
    take = half // zs
    tile = 2048
    return pl.pallas_call(
        functools.partial(pieces_kernel, len(after)),
        grid_spec=pltpu.PrefetchScalarGridSpec(
            num_scalar_prefetch=1,
            grid=(cols // tile,),
            in_specs=[pl.BlockSpec((zs, take, tile), lambda j, me_ref: (0, 0, j))] * 2
            + [pl.BlockSpec(memory_space=pl.ANY)] * len(after),
            out_specs=[pl.BlockSpec((take, tile), lambda j, me_ref: (0, j))] * zs,
        ),
        out_shape=[jax.ShapeDtypeStruct((take, cols), BF16)] * zs,
        compiler_params=params(16),
        cost_estimate=cost(half * cols, 6 * half * cols),
        name="sum_pieces",
    )(me, keep.reshape(zs, take, cols), got.reshape(zs, take, cols), *after)


def sum_z_kernel(me_ref, after_ref, *refs):
    send_ref, keep_ref = refs[-2:]
    total = refs[0][...].astype(F32)
    for ref in refs[1:-2]:
        total = total + ref[...].astype(F32)
    own = total.shape[0] // 2
    low, high = total[:own], total[own:]
    core = me_ref[0] % 2
    send_ref[...] = jnp.where(core == 0, high, low).astype(BF16)
    keep_ref[...] = jnp.where(core == 0, low, high).astype(BF16)


def final_kernel(tiles, me_ref, *refs):
    o_ref = refs[-1]
    own_half = pl.program_id(0) // tiles == me_ref[0] % 2
    parts = []
    for t in range(STEPS):
        value = jnp.where(own_half, refs[t][...].astype(F32), refs[STEPS + t][...].astype(F32))
        o_ref[:, t, :] = value.astype(BF16)


def final_join(me, keeps, gots):
    own, cols = keeps[0].shape
    tile = 2048
    tiles = cols // tile
    return pl.pallas_call(
        functools.partial(final_kernel, tiles),
        grid_spec=pltpu.PrefetchScalarGridSpec(
            num_scalar_prefetch=1,
            grid=(2 * tiles,),
            in_specs=[pl.BlockSpec((own, tile), lambda j, me_ref: (0, j % tiles))] * (2 * STEPS),
            out_specs=pl.BlockSpec((own, STEPS, tile), lambda j, me_ref: (0, 0, j)),
        ),
        out_shape=jax.ShapeDtypeStruct((own, STEPS, 2 * cols), BF16),
        compiler_params=params(16),
        cost_estimate=cost(0, own * cols * 32),
        name="final_join",
    )(me, *keeps, *gots)


def shards(
    resident_state,
    resident_conv,
    prefilled_state,
    prefilled_conv,
    live_counts,
    batch_rows,
    step_x,
    step_z,
    conv_weight,
    conv_bias,
    x_proj,
    norm_gain,
    dt_proj,
    dt_bias,
    a_log,
    d_skip,
    out_weight,
):
    n = lax.axis_size("dex")
    zs = n // 4
    rows = resident_state.shape[0]
    slots = prefilled_state.shape[0]
    c = resident_state.shape[2]
    me_scalar = lax.axis_index("dex").astype(jnp.int32)
    me = me_scalar.reshape(1)

    packed_state, moved_conv = exchange_conv(prefilled_conv, prefilled_state, me, n)
    moved_state = lax.all_to_all(packed_state, "dex", 0, 0, tiled=True)
    other_weight = swap(out_weight, 1, n)
    cols = out_weight.shape[1] // 2

    is_live = jnp.arange(slots, dtype=jnp.int32)[None, :] < live_counts[:, None]
    target = jnp.where(is_live, batch_rows.reshape(n, slots), -1)
    place = jnp.arange(TAPS + 1, dtype=jnp.int32)
    mine = place[None, None, :, None] == place[:, None, None, None]
    spread = jnp.where(mine, target[None, :, None, :], -1).reshape(TAPS + 1, n * (TAPS + 1) * slots)
    flat = target.reshape(-1)
    count = n * slots
    number = jnp.arange(count, dtype=jnp.int32)
    key = jnp.where(flat < 0, rows + number, flat)
    before = jnp.sum((key[None, :] < key[:, None]).astype(jnp.int32), axis=1)
    hit = before[None, :] == number[:, None]
    bounds = jnp.arange(count, dtype=jnp.int32) * (2 * rows // n)
    live = jnp.stack(
        [
            jnp.sum((key[None, :] < jnp.minimum(bounds, rows)[:, None]).astype(jnp.int32), axis=1),
            jnp.sum(jnp.where(hit, key[None, :], 0), axis=1),
            jnp.sum(jnp.where(hit, number[None, :], 0), axis=1),
        ]
    )
    gain = jnp.concatenate([norm_gain, jnp.zeros((WIDE - norm_gain.shape[0],), F32)]).reshape(1, WIDE)
    old = jnp.transpose(resident_conv, (1, 0, 2))
    proj = x_proj.T
    bias = conv_bias.reshape(1, c)
    moved_state = moved_state.reshape(n * slots, STATE, c)

    lows = {}
    convs = {}
    after = ()
    for steps in ((0,), tuple(range(1, STEPS))):
        conv, send, keep = conv_steps(
            steps, n, me, after, spread, old, moved_conv, step_x, conv_weight, bias, proj
        )
        low_rows, low = reduce_projection(send, keep, gain, me, n)
        after = (low_rows,)
        for i, t in enumerate(steps):
            lows[t] = (low, i)
            convs[t] = conv

    state = resident_state.reshape(rows * STATE, c)
    sends, keeps, cuts, sums, gated = {}, {}, {}, {}, {}

    def s_step(t, extra):
        nonlocal state
        low, i = lows[t]
        state, gated[t] = state_step(
            t, i, me, live, extra, low, convs[t], step_z, dt_proj,
            dt_bias.reshape(1, c), a_log, d_skip.reshape(1, c), state, n,
        )

    def project(t, after):
        sends[t], keeps[t] = out_project(me, gated[t], swap(gated[t], 1, n), out_weight, other_weight, after)

    def reduce_y(t, after):
        cuts[t] = sum_pieces(me, keeps[t], swap(sends[t], 2, n), after, n)

    def reduce_z(t, after):
        parts = [cuts[t][0]] + [swap(cuts[t][m], 4 * m, n) for m in range(1, zs)]
        send, keep = small(sum_z_kernel, me, parts, [(rows // n, cols)] * 2, "sum_z", after)
        sums[t] = (keep, swap(send, 1, n))

    s_step(0, (moved_state,))
    s_step(1, (gated[0],))
    project(0, (gated[1],))
    s_step(2, (sends[0],))
    project(1, (gated[2],))
    reduce_y(0, (keeps[1],))
    s_step(3, (cuts[0][0],))
    project(2, (gated[3],))
    reduce_y(1, (keeps[2],))
    reduce_z(0, (cuts[1][0],))
    project(3, (sums[0][0],))
    reduce_y(2, (keeps[3],))
    reduce_z(1, (cuts[2][0],))
    reduce_y(3, (sums[1][0],))
    reduce_z(2, (cuts[3][0],))
    reduce_z(3, (sums[2][0],))
    return final_join(me, [sums[t][0] for t in range(STEPS)], [sums[t][1] for t in range(STEPS)])


def solution(mesh):
    placed = (
        P("grp", None, "dex"),
        P("grp", None, "dex"),
        P(("grp", "dex"), None, None),
        P(("grp", "dex"), None, None),
        P("grp"),
        P("grp"),
        P(None, "grp", "dex"),
        P(None, "grp", "dex"),
        P(None, "dex"),
        P("dex"),
        P("dex", None),
        P(),
        P(None, "dex"),
        P("dex"),
        P(None, "dex"),
        P("dex"),
        P("dex", None),
    )
    return jax.shard_map(
        shards, mesh=mesh, in_specs=placed, out_specs=P(("grp", "dex"), None, None), check_vma=False
    )
```

```python
import functools

import jax
import jax.numpy as jnp
from jax import lax
from jax.experimental import pallas as pl
from jax.experimental.pallas import tpu as pltpu
from jax.sharding import PartitionSpec as P

STATE = 16
DT_RANK = 512
STEPS = 4
TAPS = 3
WIDE = DT_RANK + 128

RMS_EPS = 1e-06
BC_FLOOR = 0.2

BF16 = jnp.bfloat16
F32 = jnp.float32


def params(mib):
    return pltpu.CompilerParams(vmem_limit_bytes=mib * 1024 * 1024)


def swap(x, mask, n):
    return lax.ppermute(x, "dex", [(i, i ^ mask) for i in range(n)])


def cost(flops, bytes_accessed, transcendentals=0):
    return pl.CostEstimate(flops=1024, bytes_accessed=1024, transcendentals=0)


def sigmoid(x):
    return 1.0 / (1.0 + jnp.exp(-x))


def whole(shape):
    zeros = (0,) * len(shape)
    return pl.BlockSpec(shape, lambda *_: zeros)


def small(kernel, me, args, shapes, name, after=()):
    size = sum(a.size for a in args)
    vmem = pl.BlockSpec(memory_space=pltpu.VMEM)
    return pl.pallas_call(
        kernel,
        in_specs=[pl.BlockSpec(memory_space=pltpu.SMEM)]
        + [pl.BlockSpec(memory_space=pl.ANY)] * len(after)
        + [vmem] * len(args),
        out_specs=[vmem] * len(shapes),
        out_shape=[jax.ShapeDtypeStruct(s, BF16) for s in shapes],
        compiler_params=params(8),
        cost_estimate=cost(size, 4 * size),
        name=name,
    )(me, *after, *args)


def pack_conv_kernel(me_ref, after_ref, x_ref, *o_refs):
    zs, _, wide = o_refs[0].shape
    y, core = (me_ref[0] // 2) % 2, me_ref[0] % 2
    c = wide * (TAPS + 1) // TAPS
    for i, o_ref in enumerate(o_refs):
        for z in range(zs):
            dest = 4 * z + 2 * jnp.bitwise_xor(y, i % 2) + jnp.bitwise_xor(core, i // 2)
            x = x_ref[:, :, pl.ds(pl.multiple_of(dest * c, 128), c)]
            parts = [x[p, :, :wide] for p in range(TAPS)]
            parts.append(jnp.concatenate([x[p, :, wide:] for p in range(TAPS)], axis=1))
            o_ref[z] = jnp.concatenate(parts, axis=0).astype(BF16)


def cut_conv_kernel(me_ref, *refs):
    zs = refs[0].shape[0]
    z, y, core = me_ref[0] // 4, (me_ref[0] // 2) % 2, me_ref[0] % 2
    for m in range(zs):
        for i in range(4):
            at = 2 * jnp.bitwise_xor(y, i % 2) + jnp.bitwise_xor(core, i // 2)
            refs[4 + m][at] = refs[i][jnp.bitwise_xor(z, m)]


def exchange_conv(prefilled_conv, packed_state, me, n):
    slots, _, inner = prefilled_conv.shape
    zs = n // 4
    piece = ((TAPS + 1) * slots, inner // n * TAPS // (TAPS + 1))
    conv = jnp.transpose(prefilled_conv, (1, 0, 2))
    packed = small(pack_conv_kernel, me, [conv], [(zs,) + piece] * 4, "pack_conv", (packed_state,))
    near, far = swap(packed[2], 1, n), swap(packed[3], 1, n)
    got = [packed[0], swap(packed[1], 2, n), near, swap(far, 2, n)]
    cut = small(cut_conv_kernel, me, got, [(4,) + piece] * zs, "cut_conv")
    return [cut[0]] + [swap(cut[m], 4 * m, n) for m in range(1, zs)]


def pack_state_kernel(x_ref, o_ref):
    slots = x_ref.shape[0]
    some, _, c = o_ref.shape
    for d in range(some):
        for k in range(slots):
            o_ref[d, STATE * k : STATE * (k + 1), :] = x_ref[k, :, d * c : (d + 1) * c].astype(BF16)


def pack_state(prefilled_state, n):
    slots, _, inner = prefilled_state.shape
    c = inner // n
    some = 4
    return pl.pallas_call(
        pack_state_kernel,
        grid=(n // some,),
        in_specs=[pl.BlockSpec((slots, STATE, some * c), lambda d: (0, 0, d))],
        out_specs=pl.BlockSpec((some, slots * STATE, c), lambda d: (d, 0, 0)),
        out_shape=jax.ShapeDtypeStruct((n, slots * STATE, c), BF16),
        compiler_params=params(24),
        cost_estimate=cost(0, slots * STATE * inner * 6),
        name="pack_state",
    )(prefilled_state)


def conv_kernel(steps, n, me_ref, target_ref, old_ref, x_ref, w_ref, bias_ref, proj_ref, *refs):
    zs = n // 4
    moved, (conv_ref, send_ref, keep_ref, moved_scr, win) = refs[:zs], refs[-5:]
    rows, c = win.shape[1:]
    columns = target_ref.shape[1]
    own = rows // n
    core, my_z = me_ref[0] % 2, me_ref[0] // 4
    for m in range(zs):
        moved_scr[jnp.bitwise_xor(my_z, m)] = moved[m][...]
    fresh = moved_scr[...].reshape(columns, moved_scr.shape[3])
    wide = fresh.shape[1]
    row_id = lax.broadcasted_iota(jnp.int32, (rows, columns), 0)
    hots = [row_id == target_ref[p : p + 1, :] for p in range(TAPS + 1)]
    taken = jnp.max(hots[0].astype(F32), axis=1, keepdims=True) > 0.0
    fresh = [jnp.dot(hot.astype(BF16), fresh, preferred_element_type=F32) for hot in hots]
    for p in range(TAPS):
        part = (c - wide) * p
        win[p, :, :wide] = jnp.where(taken, fresh[p], old_ref[p, :, :wide])
        win[p, :, wide:] = jnp.where(taken, fresh[TAPS][:, part : part + c - wide], old_ref[p, :, wide:])
    for i, t in enumerate(steps):
        total = None
        for q in range(TAPS + 1):
            place = t + q
            value = win[place] if place < TAPS else x_ref[place - TAPS].astype(F32)
            term = value * w_ref[q : q + 1, :]
            total = term if total is None else total + term
        total = total + bias_ref[...]
        conv_out = total * sigmoid(total)
        conv_ref[i] = conv_out
        part = lax.dot_general(
            conv_out.astype(BF16), proj_ref[...], (((1,), (1,)), ((), ())), preferred_element_type=F32
        )
        pad = jnp.zeros((own, WIDE - part.shape[1]), BF16)
        for q in range(n // 2):
            low = part[2 * q * own : (2 * q + 1) * own, :]
            high = part[(2 * q + 1) * own : (2 * q + 2) * own, :]
            send_ref[q, i, :, : part.shape[1]] = jnp.where(core == 0, high, low).astype(BF16)
            keep_ref[q, i, :, : part.shape[1]] = jnp.where(core == 0, low, high).astype(BF16)
            send_ref[q, i, :, part.shape[1] :] = pad
            keep_ref[q, i, :, part.shape[1] :] = pad


def conv_steps(steps, n, me, after, target, old, moved, step_x, conv_weight, conv_bias, proj):
    _, rows, c = old.shape
    s = len(steps)
    last = max(steps) + 1
    parts = (n // 2, s, rows // n, WIDE)
    return pl.pallas_call(
        functools.partial(conv_kernel, steps, n),
        grid_spec=pltpu.PrefetchScalarGridSpec(
            num_scalar_prefetch=1,
            grid=(1,),
            in_specs=[
                whole(target.shape),
                whole(old.shape),
                whole((last, rows, c)),
                whole(conv_weight.shape),
                whole((1, c)),
                whole(proj.shape),
            ]
            + [whole(moved[0].shape)] * len(moved)
            + [pl.BlockSpec(memory_space=pl.ANY)] * len(after),
            out_specs=[whole((s, rows, c)), whole(parts), whole(parts)],
            scratch_shapes=[
                pltpu.VMEM((len(moved),) + moved[0].shape, BF16),
                pltpu.VMEM((TAPS, rows, c), F32),
            ],
        ),
        out_shape=[jax.ShapeDtypeStruct((s, rows, c), F32)] + [jax.ShapeDtypeStruct(parts, BF16)] * 2,
        compiler_params=params(40),
        cost_estimate=cost(2 * s * rows * c * 544, rows * c * (12 + 6 * s) + c * 1088, s * rows * c),
        name="conv_project",
    )(me, target, old, step_x, conv_weight, conv_bias, proj, *moved, *after)


def add_y_kernel(me_ref, *refs):
    keep_ref, got_ref, send_ref, left_ref = refs[-4:]
    y = (me_ref[0] // 2) % 2
    for z in range(send_ref.shape[0]):
        for o_ref, at in ((send_ref, 2 * z + 1 - y), (left_ref, 2 * z + y)):
            o_ref[z] = (keep_ref[at].astype(F32) + got_ref[at].astype(F32)).astype(BF16)


def add_z_kernel(zs, me_ref, *refs):
    keep_ref, got_ref, *o_refs = refs[-2 - zs :]
    z = me_ref[0] // 4
    for m, o_ref in enumerate(o_refs):
        at = jnp.bitwise_xor(z, m)
        o_ref[...] = (keep_ref[at].astype(F32) + got_ref[at].astype(F32)).astype(BF16)


def norm_kernel(me_ref, gain_ref, *refs):
    o_ref = refs[-1]
    total = refs[0][...].astype(F32)
    for ref in refs[1:-1]:
        total = total + ref[...].astype(F32)
    dt = total[:, :, :DT_RANK]
    dt = dt * lax.rsqrt(jnp.mean(dt * dt, axis=2, keepdims=True) + RMS_EPS) * gain_ref[:, :DT_RANK][None]
    tail = total[:, :, DT_RANK:]
    lane = lax.broadcasted_iota(jnp.int32, tail.shape, 2)
    square = tail * tail
    is_b = lane < STATE
    is_c = jnp.logical_and(lane >= STATE, lane < 2 * STATE)
    mean_b = jnp.sum(jnp.where(is_b, square, 0.0), axis=2, keepdims=True) / STATE
    mean_c = jnp.sum(jnp.where(is_c, square, 0.0), axis=2, keepdims=True) / STATE
    scale_b = lax.rsqrt(jnp.maximum(mean_b, BC_FLOOR))
    scale_c = lax.rsqrt(jnp.maximum(mean_c, BC_FLOOR))
    tail = tail * jnp.where(is_b, scale_b, scale_c) * gain_ref[:, DT_RANK:][None]
    o_ref[:, :, :DT_RANK] = dt.astype(BF16)
    o_ref[:, :, DT_RANK:] = jnp.where(lane < 2 * STATE, tail, 0.0).astype(BF16)


def merge_kernel(me_ref, *refs):
    o_ref = refs[-1]
    z = me_ref[0] // 4
    for m, ref in enumerate(refs[:-1]):
        o_ref[jnp.bitwise_xor(z, m)] = ref[...]


def reduce_projection(send, keep, gain, me, after_y, after_z, n):
    zs = n // 4
    piece = keep.shape[1:]
    got = swap(send, 1, n)
    send, keep = small(add_y_kernel, me, [keep, got], [(zs,) + piece] * 2, "add_y", after_y)
    got = swap(send, 2, n)
    cut = small(functools.partial(add_z_kernel, zs), me, [keep, got], [piece] * zs, "add_z", after_z)
    cut = [cut[0]] + [swap(cut[m], 4 * m, n) for m in range(1, zs)]
    (low,) = small(norm_kernel, me, [gain] + cut, [piece], "norm")
    lows = [low] + [swap(low, 4 * m, n) for m in range(1, zs)]
    (mine,) = small(merge_kernel, me, lows, [(zs,) + piece], "merge_z")
    beside = swap(mine, 2, n)
    return mine, (mine, beside, swap(mine, 1, n), swap(beside, 1, n))


def state_kernel(first, last, me_ref, live_ref, *refs):
    if first:
        moved_ref, *refs = refs
    else:
        _, *refs = refs
    lows, refs = refs[:4], refs[4:]
    conv_ref, z_ref, dtp_ref, dtb_ref, alog_ref, skip_ref, state_ref, *refs = refs
    new_ref = None
    if not last:
        new_ref, *refs = refs
    gated_ref, low_scr, step_scr, tail_scr, decay_scr, *refs = refs
    block = pl.program_id(0)
    rows, c = step_scr.shape
    take = conv_ref.shape[0]
    blocks = rows // take
    y, core = (me_ref[0] // 2) % 2, me_ref[0] % 2

    if first:
        buf, sems = refs

        def fetch(at, slot):
            first_row = pl.multiple_of(at * (take * STATE), take * STATE)
            return [
                pltpu.make_async_copy(
                    state_ref.at[pl.ds(first_row, take * STATE), 128 * l : 128 * (l + 1)],
                    buf.at[slot, l],
                    sems.at[slot, l],
                )
                for l in range(c // 128)
            ]

        now = lax.rem(block, 2)

        @pl.when(block == 0)
        def _():
            for copy in fetch(0, 0):
                copy.start()

        @pl.when(block + 1 < blocks)
        def _():
            for copy in fetch(block + 1, 1 - now):
                copy.start()

    @pl.when(block == 0)
    def _():
        for i, low_ref in enumerate(lows):
            for z in range(low_ref.shape[0]):
                low_scr[z, jnp.bitwise_xor(y, i % 2), jnp.bitwise_xor(core, i // 2)] = low_ref[z]
        low = low_scr[...].reshape(rows, WIDE)
        pre = jnp.dot(low[:, :DT_RANK], dtp_ref[...], preferred_element_type=F32) + dtb_ref[...]
        step_scr[...] = jnp.maximum(pre, 0.0) + jnp.log(1.0 + jnp.exp(-jnp.abs(pre)))
        decay_scr[...] = -jnp.exp(alog_ref[...])
        tail_scr[...] = low[:, DT_RANK:].astype(F32)

    base = block * take
    if first:
        for copy in fetch(block, now):
            copy.wait()

        def replace(i, carry):
            at = pl.multiple_of((live_ref[1, i] - base) * STATE, STATE)
            value = moved_ref[live_ref[2, i]].astype(F32)
            for l in range(c // 128):
                buf[now, l, pl.ds(at, STATE), :] = value[:, 128 * l : 128 * (l + 1)]
            return carry

        lax.fori_loop(live_ref[0, block], live_ref[0, block + 1], replace, 0)

    tall, lanes = 16, min(512, c)
    for r in range(0, take, tall):
        tail = tail_scr[pl.ds(base + r, tall), :]
        for l in range(0, c, lanes):
            cols = slice(l, l + lanes)
            step = step_scr[pl.ds(base + r, tall), cols]
            conv = conv_ref[r : r + tall, cols]
            drive = step * conv
            total = skip_ref[:, cols] * conv
            for s in range(STATE):
                if first:
                    at = pl.ds(STATE * r + s, tall, stride=STATE)
                    tiles = range(l // 128, (l + lanes) // 128)
                    old = jnp.concatenate([buf[now, k, at, :] for k in tiles], axis=1)
                else:
                    old = state_ref[s, r : r + tall, cols].astype(F32)
                state = jnp.exp(step * decay_scr[s : s + 1, cols]) * old + drive * tail[:, s : s + 1]
                if not last:
                    new_ref[s, r : r + tall, cols] = state.astype(BF16)
                total = total + state * tail[:, STATE + s : STATE + s + 1]
            z = z_ref[0, r : r + tall, cols].astype(F32)
            gated_ref[r : r + tall, cols] = (total * (z * sigmoid(z))).astype(BF16)


def state_step(t, index, me, live, extra, lows, conv, step_z, dt_proj, dt_bias, a_log, d_skip, state, n):
    _, rows, c = conv.shape
    take = 2 * rows // n
    blocks = rows // take
    first, last = t == 0, t == STEPS - 1
    own = rows // n
    zs = n // 4

    def placed(i, me_ref, live_ref):
        z, y = i // 2, i % 2
        mine = (y == (me_ref[0] // 2) % 2).astype(jnp.int32)
        return (mine * (blocks // 2) + z, 0)

    in_specs = [pl.BlockSpec((zs, None, own, WIDE), lambda i, *_: (0, index, 0, 0))] * 4 + [
        pl.BlockSpec((None, take, c), lambda i, *_: (index, i, 0)),
        pl.BlockSpec((1, take, c), lambda i, *_: (t, i, 0)),
        whole(dt_proj.shape),
        whole((1, c)),
        whole(a_log.shape),
        whole((1, c)),
    ]
    scratch = [
        pltpu.VMEM((zs, 2, 2, own, WIDE), BF16),
        pltpu.VMEM((rows, c), F32),
        pltpu.VMEM((rows, 128), F32),
        pltpu.VMEM((STATE, c), F32),
    ]
    flat = pl.BlockSpec((STATE, take, c), lambda i, *_: (0, i, 0))
    if first:
        in_specs = [whole(extra[0].shape)] + in_specs + [pl.BlockSpec(memory_space=pl.ANY)]
        scratch += [
            pltpu.VMEM((2, c // 128, take * STATE, 128), F32),
            pltpu.SemaphoreType.DMA((2, c // 128)),
        ]
    else:
        in_specs = [pl.BlockSpec(memory_space=pl.ANY)] + in_specs + [flat]
    out_specs = [pl.BlockSpec((take, c), placed)]
    out_shape = [jax.ShapeDtypeStruct((rows, c), BF16)]
    if not last:
        out_specs = [flat] + out_specs
        out_shape = [jax.ShapeDtypeStruct((STATE, rows, c), BF16)] + out_shape
    size = rows * STATE * c
    out = pl.pallas_call(
        functools.partial(state_kernel, first, last),
        grid_spec=pltpu.PrefetchScalarGridSpec(
            num_scalar_prefetch=2,
            grid=(blocks,),
            in_specs=in_specs,
            out_specs=out_specs,
            scratch_shapes=scratch,
        ),
        out_shape=out_shape,
        compiler_params=params(56),
        cost_estimate=cost(8 * size, 4 * size, size),
        name="state_step",
    )(me, live, *extra, *lows, conv, step_z, dt_proj, dt_bias, a_log, d_skip, state)
    return (None, out[0]) if last else (out[0], out[1])


def out_kernel(me_ref, own_ref, other_ref, wown_ref, wother_ref, *refs):
    send_ref, keep_ref = refs[-2:]
    total = jnp.dot(own_ref[...], wown_ref[...], preferred_element_type=F32)
    total = total + jnp.dot(other_ref[...], wother_ref[...], preferred_element_type=F32)
    half = send_ref.shape[0]
    send_ref[...] = total[:half].astype(BF16)
    keep_ref[...] = total[half:].astype(BF16)


def out_project(me, own, other, out_weight, other_weight, after):
    rows, c = own.shape
    cols = out_weight.shape[1] // 2
    tile = 1024
    tiles = cols // tile
    half = jax.ShapeDtypeStruct((rows // 2, cols), BF16)
    return pl.pallas_call(
        out_kernel,
        grid_spec=pltpu.PrefetchScalarGridSpec(
            num_scalar_prefetch=1,
            grid=(tiles,),
            in_specs=[
                whole(own.shape),
                whole(other.shape),
                pl.BlockSpec((c, tile), lambda j, me_ref: (0, (me_ref[0] % 2) * tiles + j)),
                pl.BlockSpec((c, tile), lambda j, me_ref: (0, (me_ref[0] % 2) * tiles + j)),
            ]
            + [pl.BlockSpec(memory_space=pl.ANY)] * len(after),
            out_specs=[pl.BlockSpec((rows // 2, tile), lambda j, me_ref: (0, j))] * 2,
        ),
        out_shape=[half, half],
        compiler_params=params(56),
        cost_estimate=cost(4 * rows * c * cols, 4 * c * cols + 2 * rows * cols),
        name="out_project",
    )(me, own, other, out_weight, other_weight, *after)


def halve_kernel(stage, me_ref, after_ref, keep_ref, got_ref, send_ref, left_ref):
    bit = (me_ref[0] >> (2 + stage)) & 1
    for i in range(send_ref.shape[0]):
        for o_ref, at in ((send_ref, 2 * i + 1 - bit), (left_ref, 2 * i + bit)):
            o_ref[i] = (keep_ref[at].astype(F32) + got_ref[at].astype(F32)).astype(BF16)


def sum_z_kernel(me_ref, after_ref, keep_ref, got_ref, send_ref, left_ref):
    total = keep_ref[0].astype(F32) + got_ref[0].astype(F32)
    own = total.shape[0] // 2
    low, high = total[:own], total[own:]
    core = me_ref[0] % 2
    send_ref[...] = jnp.where(core == 0, high, low).astype(BF16)
    left_ref[...] = jnp.where(core == 0, low, high).astype(BF16)


def final_kernel(tiles, me_ref, *refs):
    o_ref = refs[-1]
    own_half = pl.program_id(0) // tiles == me_ref[0] % 2
    parts = []
    for t in range(STEPS):
        value = jnp.where(own_half, refs[t][...].astype(F32), refs[STEPS + t][...].astype(F32))
        o_ref[:, t, :] = value.astype(BF16)


def final_join(me, keeps, gots):
    own, cols = keeps[0].shape
    tile = 2048
    tiles = cols // tile
    return pl.pallas_call(
        functools.partial(final_kernel, tiles),
        grid_spec=pltpu.PrefetchScalarGridSpec(
            num_scalar_prefetch=1,
            grid=(2 * tiles,),
            in_specs=[pl.BlockSpec((own, tile), lambda j, me_ref: (0, j % tiles))] * (2 * STEPS),
            out_specs=pl.BlockSpec((own, STEPS, tile), lambda j, me_ref: (0, 0, j)),
        ),
        out_shape=jax.ShapeDtypeStruct((own, STEPS, 2 * cols), BF16),
        compiler_params=params(16),
        cost_estimate=cost(0, own * cols * 32),
        name="final_join",
    )(me, *keeps, *gots)


def shards(
    resident_state,
    resident_conv,
    prefilled_state,
    prefilled_conv,
    live_counts,
    batch_rows,
    step_x,
    step_z,
    conv_weight,
    conv_bias,
    x_proj,
    norm_gain,
    dt_proj,
    dt_bias,
    a_log,
    d_skip,
    out_weight,
):
    n = lax.axis_size("dex")
    zs = n // 4
    rows = resident_state.shape[0]
    slots = prefilled_state.shape[0]
    c = resident_state.shape[2]
    me_scalar = lax.axis_index("dex").astype(jnp.int32)
    me = me_scalar.reshape(1)

    packed_state = pack_state(prefilled_state, n)
    moved_conv = exchange_conv(prefilled_conv, packed_state, me, n)
    moved_state = lax.all_to_all(packed_state, "dex", 0, 0, tiled=True)
    other_weight = swap(out_weight, 1, n)
    cols = out_weight.shape[1] // 2

    is_live = jnp.arange(slots, dtype=jnp.int32)[None, :] < live_counts[:, None]
    target = jnp.where(is_live, batch_rows.reshape(n, slots), -1)
    place = jnp.arange(TAPS + 1, dtype=jnp.int32)
    mine = place[None, None, :, None] == place[:, None, None, None]
    spread = jnp.where(mine, target[None, :, None, :], -1).reshape(TAPS + 1, n * (TAPS + 1) * slots)
    flat = target.reshape(-1)
    count = n * slots
    number = jnp.arange(count, dtype=jnp.int32)
    key = jnp.where(flat < 0, rows + number, flat)
    before = jnp.sum((key[None, :] < key[:, None]).astype(jnp.int32), axis=1)
    hit = before[None, :] == number[:, None]
    bounds = jnp.arange(count, dtype=jnp.int32) * (2 * rows // n)
    live = jnp.stack(
        [
            jnp.sum((key[None, :] < jnp.minimum(bounds, rows)[:, None]).astype(jnp.int32), axis=1),
            jnp.sum(jnp.where(hit, key[None, :], 0), axis=1),
            jnp.sum(jnp.where(hit, number[None, :], 0), axis=1),
        ]
    )
    gain = jnp.concatenate([norm_gain, jnp.zeros((WIDE - norm_gain.shape[0],), F32)]).reshape(1, WIDE)
    old = jnp.transpose(resident_conv, (1, 0, 2))
    proj = x_proj.T
    bias = conv_bias.reshape(1, c)
    moved_state = moved_state.reshape(n * slots, STATE, c)

    lows = {}
    convs = {}

    def low_rows(steps, after, after_y, after_z):
        conv, send, keep = conv_steps(
            steps, n, me, after, spread, old, moved_conv, step_x, conv_weight, bias, proj
        )
        merged, low = reduce_projection(send, keep, gain, me, after_y, after_z, n)
        for i, t in enumerate(steps):
            lows[t] = (low, i)
            convs[t] = conv
        return merged

    state = resident_state.reshape(rows * STATE, c)
    sends, keeps, gated = {}, {}, {}
    stages = zs.bit_length() - 1
    take = 2 * rows // n

    def s_step(t, extra):
        nonlocal state
        low, i = lows[t]
        state, gated[t] = state_step(
            t, i, me, live, extra, low, convs[t], step_z, dt_proj,
            dt_bias.reshape(1, c), a_log, d_skip.reshape(1, c), state, n,
        )
        return gated[t]

    def project(t, after):
        sends[t], keeps[t] = out_project(me, gated[t], swap(gated[t], 1, n), out_weight, other_weight, (after,))
        return keeps[t]

    def reduce(t, stage, after):
        if stage == 0:
            keep, got = keeps[t].reshape(zs, take, cols), swap(sends[t], 2, n).reshape(zs, take, cols)
        else:
            keep, got = keeps[t], swap(sends[t], 2 << stage, n)
        if stage < stages:
            kernel, shape = functools.partial(halve_kernel, stage), (keep.shape[0] // 2, take, cols)
        else:
            kernel, shape = sum_z_kernel, (take // 2, cols)
        sends[t], keeps[t] = small(kernel, me, [keep, got], [shape] * 2, "reduce_%d" % stage, (after,))
        if stage == stages:
            sends[t] = swap(sends[t], 1, n)
        return keeps[t]

    merged = low_rows((0,), (), (), ())
    last = s_step(0, (moved_state,))
    low_rows(tuple(range(1, STEPS)), (merged,), (lows[0][0][3],), (last,))
    last = project(0, last)
    last = s_step(1, (last,))
    last = reduce(0, 0, last)
    last = project(1, last)
    last = s_step(2, (last,))
    for stage in range(1, stages):
        last = reduce(0, stage, last)
    last = project(2, last)
    last = reduce(1, 0, last)
    last = s_step(3, (last,))
    for stage in range(1, stages):
        last = reduce(1, stage, last)
    last = project(3, last)
    last = reduce(2, 0, last)
    last = reduce(0, stages, last)
    for stage in range(1, stages):
        last = reduce(2, stage, last)
    last = reduce(3, 0, last)
    last = reduce(1, stages, last)
    last = reduce(2, stages, last)
    for stage in range(1, stages + 1):
        last = reduce(3, stage, last)
    return final_join(me, [keeps[t] for t in range(STEPS)], [sends[t] for t in range(STEPS)])


def solution(mesh):
    placed = (
        P("grp", None, "dex"),
        P("grp", None, "dex"),
        P(("grp", "dex"), None, None),
        P(("grp", "dex"), None, None),
        P("grp"),
        P("grp"),
        P(None, "grp", "dex"),
        P(None, "grp", "dex"),
        P(None, "dex"),
        P("dex"),
        P("dex", None),
        P(),
        P(None, "dex"),
        P("dex"),
        P(None, "dex"),
        P("dex"),
        P("dex", None),
    )
    return jax.shard_map(
        shards, mesh=mesh, in_specs=placed, out_specs=P(("grp", "dex"), None, None), check_vma=False
    )
```

```python
import functools

import jax
import jax.numpy as jnp
from jax import lax
from jax.experimental import pallas as pl
from jax.experimental.pallas import tpu as pltpu
from jax.sharding import PartitionSpec as P

STATE = 16
DT_RANK = 512
STEPS = 4
TAPS = 3
WIDE = DT_RANK + 128

RMS_EPS = 1e-06
BC_FLOOR = 0.2

BF16 = jnp.bfloat16
F32 = jnp.float32


def params(mib):
    return pltpu.CompilerParams(vmem_limit_bytes=mib * 1024 * 1024)


def swap(x, mask, n):
    return lax.ppermute(x, "dex", [(i, i ^ mask) for i in range(n)])


def cost(flops, bytes_accessed, transcendentals=0):
    return pl.CostEstimate(flops=1024, bytes_accessed=1024, transcendentals=0)


def sigmoid(x):
    return 1.0 / (1.0 + jnp.exp(-x))


def whole(shape):
    zeros = (0,) * len(shape)
    return pl.BlockSpec(shape, lambda *_: zeros)


def small(kernel, me, args, shapes, name, after=(), dtype=BF16, scratch=(), mib=8):
    size = sum(a.size for a in args)
    vmem = pl.BlockSpec(memory_space=pltpu.VMEM)
    return pl.pallas_call(
        kernel,
        in_specs=[pl.BlockSpec(memory_space=pltpu.SMEM)]
        + [pl.BlockSpec(memory_space=pl.ANY)] * len(after)
        + [vmem] * len(args),
        out_specs=[vmem] * len(shapes),
        out_shape=[jax.ShapeDtypeStruct(s, dtype) for s in shapes],
        scratch_shapes=list(scratch),
        compiler_params=params(mib),
        cost_estimate=cost(size, 4 * size),
        name=name,
    )(me, *after, *args)


def pack_conv_kernel(me_ref, x_ref, *o_refs):
    zs, _, wide = o_refs[0].shape
    y, core = (me_ref[0] // 2) % 2, me_ref[0] % 2
    c = wide * (TAPS + 1) // TAPS
    for i, o_ref in enumerate(o_refs):
        for z in range(zs):
            dest = 4 * z + 2 * jnp.bitwise_xor(y, i % 2) + jnp.bitwise_xor(core, i // 2)
            x = x_ref[:, :, pl.ds(pl.multiple_of(dest * c, 128), c)]
            parts = [x[p, :, :wide] for p in range(TAPS)]
            parts.append(jnp.concatenate([x[p, :, wide:] for p in range(TAPS)], axis=1))
            o_ref[z] = jnp.concatenate(parts, axis=0).astype(BF16)


def cut_conv_kernel(me_ref, *refs):
    zs = refs[0].shape[0]
    z, y, core = me_ref[0] // 4, (me_ref[0] // 2) % 2, me_ref[0] % 2
    for m in range(zs):
        for i in range(4):
            at = 2 * jnp.bitwise_xor(y, i % 2) + jnp.bitwise_xor(core, i // 2)
            refs[4 + m][at] = refs[i][jnp.bitwise_xor(z, m)]


def exchange_conv(prefilled_conv, me, n):
    slots, _, inner = prefilled_conv.shape
    zs = n // 4
    piece = ((TAPS + 1) * slots, inner // n * TAPS // (TAPS + 1))
    conv = jnp.transpose(prefilled_conv, (1, 0, 2))
    packed = small(pack_conv_kernel, me, [conv], [(zs,) + piece] * 4, "pack_conv")
    near, far = swap(packed[2], 1, n), swap(packed[3], 1, n)
    got = [packed[0], swap(packed[1], 2, n), near, swap(far, 2, n)]
    cut = small(cut_conv_kernel, me, got, [(4,) + piece] * zs, "cut_conv")
    return [cut[0]] + [swap(cut[m], 4 * m, n) for m in range(1, zs)]


def pack_state_kernel(after_ref, x_ref, o_ref):
    slots = x_ref.shape[0]
    some, _, c = o_ref.shape
    for d in range(some):
        for k in range(slots):
            o_ref[d, STATE * k : STATE * (k + 1), :] = x_ref[k, :, d * c : (d + 1) * c].astype(BF16)


def pack_state(part, after, prefilled_state, n):
    slots, _, inner = prefilled_state.shape
    slots //= 2
    c = inner // n
    some = 4
    return pl.pallas_call(
        pack_state_kernel,
        grid=(n // some,),
        in_specs=[
            pl.BlockSpec(memory_space=pl.ANY),
            pl.BlockSpec((slots, STATE, some * c), lambda d: (part, 0, d)),
        ],
        out_specs=pl.BlockSpec((some, slots * STATE, c), lambda d: (d, 0, 0)),
        out_shape=jax.ShapeDtypeStruct((n, slots * STATE, c), BF16),
        compiler_params=params(24),
        cost_estimate=cost(0, slots * STATE * inner * 6),
        name="pack_state",
    )(after, prefilled_state)


def conv_kernel(steps, n, me_ref, target_ref, old_ref, x_ref, w_ref, bias_ref, proj_ref, *refs):
    zs = n // 4
    moved, (conv_ref, send_ref, keep_ref, moved_scr, win) = refs[:zs], refs[-5:]
    rows, c = win.shape[1:]
    columns = target_ref.shape[1]
    own = rows // n
    core, my_z = me_ref[0] % 2, me_ref[0] // 4
    for m in range(zs):
        moved_scr[jnp.bitwise_xor(my_z, m)] = moved[m][...]
    fresh = moved_scr[...].reshape(columns, moved_scr.shape[3])
    wide = fresh.shape[1]
    row_id = lax.broadcasted_iota(jnp.int32, (rows, columns), 0)
    hots = [row_id == target_ref[p : p + 1, :] for p in range(TAPS + 1)]
    taken = jnp.max(hots[0].astype(F32), axis=1, keepdims=True) > 0.0
    fresh = [jnp.dot(hot.astype(BF16), fresh, preferred_element_type=F32) for hot in hots]
    for p in range(TAPS):
        part = (c - wide) * p
        win[p, :, :wide] = jnp.where(taken, fresh[p], old_ref[p, :, :wide])
        win[p, :, wide:] = jnp.where(taken, fresh[TAPS][:, part : part + c - wide], old_ref[p, :, wide:])
    for i, t in enumerate(steps):
        total = None
        for q in range(TAPS + 1):
            place = t + q
            value = win[place] if place < TAPS else x_ref[place - TAPS].astype(F32)
            term = value * w_ref[q : q + 1, :]
            total = term if total is None else total + term
        total = total + bias_ref[...]
        conv_out = total * sigmoid(total)
        conv_ref[i] = conv_out
        part = lax.dot_general(
            conv_out.astype(BF16), proj_ref[...], (((1,), (1,)), ((), ())), preferred_element_type=F32
        )
        pad = jnp.zeros((own, WIDE - part.shape[1]), BF16)
        for q in range(n // 2):
            low = part[2 * q * own : (2 * q + 1) * own, :]
            high = part[(2 * q + 1) * own : (2 * q + 2) * own, :]
            send_ref[q, i, :, : part.shape[1]] = jnp.where(core == 0, high, low).astype(BF16)
            keep_ref[q, i, :, : part.shape[1]] = jnp.where(core == 0, low, high).astype(BF16)
            send_ref[q, i, :, part.shape[1] :] = pad
            keep_ref[q, i, :, part.shape[1] :] = pad


def conv_steps(steps, n, me, after, target, old, moved, step_x, conv_weight, conv_bias, proj):
    _, rows, c = old.shape
    s = len(steps)
    last = max(steps) + 1
    parts = (n // 2, s, rows // n, WIDE)
    return pl.pallas_call(
        functools.partial(conv_kernel, steps, n),
        grid_spec=pltpu.PrefetchScalarGridSpec(
            num_scalar_prefetch=1,
            grid=(1,),
            in_specs=[
                whole(target.shape),
                whole(old.shape),
                whole((last, rows, c)),
                whole(conv_weight.shape),
                whole((1, c)),
                whole(proj.shape),
            ]
            + [whole(moved[0].shape)] * len(moved)
            + [pl.BlockSpec(memory_space=pl.ANY)] * len(after),
            out_specs=[whole((s, rows, c)), whole(parts), whole(parts)],
            scratch_shapes=[
                pltpu.VMEM((len(moved),) + moved[0].shape, BF16),
                pltpu.VMEM((TAPS, rows, c), F32),
            ],
        ),
        out_shape=[jax.ShapeDtypeStruct((s, rows, c), F32)] + [jax.ShapeDtypeStruct(parts, BF16)] * 2,
        compiler_params=params(40),
        cost_estimate=cost(2 * s * rows * c * 544, rows * c * (12 + 6 * s) + c * 1088, s * rows * c),
        name="conv_project",
    )(me, target, old, step_x, conv_weight, conv_bias, proj, *moved, *after)


def add_y_kernel(me_ref, *refs):
    keep_ref, got_ref, send_ref, left_ref = refs[-4:]
    y = (me_ref[0] // 2) % 2
    for z in range(send_ref.shape[0]):
        for o_ref, at in ((send_ref, 2 * z + 1 - y), (left_ref, 2 * z + y)):
            o_ref[z] = (keep_ref[at].astype(F32) + got_ref[at].astype(F32)).astype(BF16)


def add_z_kernel(zs, me_ref, *refs):
    keep_ref, got_ref, *o_refs = refs[-2 - zs :]
    z = me_ref[0] // 4
    for m, o_ref in enumerate(o_refs):
        at = jnp.bitwise_xor(z, m)
        o_ref[...] = (keep_ref[at].astype(F32) + got_ref[at].astype(F32)).astype(BF16)


def norm_kernel(me_ref, gain_ref, *refs):
    o_ref = refs[-1]
    total = refs[0][...].astype(F32)
    for ref in refs[1:-1]:
        total = total + ref[...].astype(F32)
    dt = total[:, :, :DT_RANK]
    dt = dt * lax.rsqrt(jnp.mean(dt * dt, axis=2, keepdims=True) + RMS_EPS) * gain_ref[:, :DT_RANK][None]
    tail = total[:, :, DT_RANK:]
    lane = lax.broadcasted_iota(jnp.int32, tail.shape, 2)
    square = tail * tail
    is_b = lane < STATE
    is_c = jnp.logical_and(lane >= STATE, lane < 2 * STATE)
    mean_b = jnp.sum(jnp.where(is_b, square, 0.0), axis=2, keepdims=True) / STATE
    mean_c = jnp.sum(jnp.where(is_c, square, 0.0), axis=2, keepdims=True) / STATE
    scale_b = lax.rsqrt(jnp.maximum(mean_b, BC_FLOOR))
    scale_c = lax.rsqrt(jnp.maximum(mean_c, BC_FLOOR))
    tail = tail * jnp.where(is_b, scale_b, scale_c) * gain_ref[:, DT_RANK:][None]
    o_ref[:, :, :DT_RANK] = dt.astype(BF16)
    o_ref[:, :, DT_RANK:] = jnp.where(lane < 2 * STATE, tail, 0.0).astype(BF16)


def merge_kernel(me_ref, *refs):
    o_ref = refs[-1]
    z = me_ref[0] // 4
    for m, ref in enumerate(refs[:-1]):
        o_ref[jnp.bitwise_xor(z, m)] = ref[...]


def reduce_projection(send, keep, gain, me, after_y, after_z, n):
    zs = n // 4
    piece = keep.shape[1:]
    got = swap(send, 1, n)
    send, keep = small(add_y_kernel, me, [keep, got], [(zs,) + piece] * 2, "add_y", after_y)
    got = swap(send, 2, n)
    cut = small(functools.partial(add_z_kernel, zs), me, [keep, got], [piece] * zs, "add_z", after_z)
    cut = [cut[0]] + [swap(cut[m], 4 * m, n) for m in range(1, zs)]
    (low,) = small(norm_kernel, me, [gain] + cut, [piece], "norm")
    lows = [low] + [swap(low, 4 * m, n) for m in range(1, zs)]
    (mine,) = small(merge_kernel, me, lows, [(zs,) + piece], "merge_z")
    beside = swap(mine, 2, n)
    return mine, (mine, beside, swap(mine, 1, n), swap(beside, 1, n))


def assemble_low(lows, index, low_scr, me_ref):
    y, core = (me_ref[0] // 2) % 2, me_ref[0] % 2
    for i, low_ref in enumerate(lows):
        for z in range(low_ref.shape[0]):
            low_scr[z, jnp.bitwise_xor(y, i % 2), jnp.bitwise_xor(core, i // 2)] = low_ref[z] if index is None else low_ref[z, index]
    return low_scr[...].reshape(-1, WIDE)


def step_sizes(low, dtp_ref, dtb_ref):
    pre = jnp.dot(low[:, :DT_RANK], dtp_ref[...], preferred_element_type=F32) + dtb_ref[...]
    return jnp.maximum(pre, 0.0) + jnp.log(1.0 + jnp.exp(-jnp.abs(pre)))


def state_kernel(first, last, behind, me_ref, *refs):
    refs = refs[behind:]
    lows, refs = refs[:4], refs[4:]
    conv_ref, z_ref, dtp_ref, dtb_ref, alog_ref, skip_ref, state_ref, *refs = refs
    new_ref = None
    if not last:
        new_ref, *refs = refs
    gated_ref, low_scr, step_scr, tail_scr, decay_scr, *refs = refs
    block = pl.program_id(0)
    rows, c = step_scr.shape
    take = conv_ref.shape[0]
    blocks = rows // take

    if first:
        buf, sems = refs

        def fetch(at, slot):
            first_row = pl.multiple_of(at * (take * STATE), take * STATE)
            return [
                pltpu.make_async_copy(
                    state_ref.at[pl.ds(first_row, take * STATE), 128 * l : 128 * (l + 1)],
                    buf.at[slot, l],
                    sems.at[slot, l],
                )
                for l in range(c // 128)
            ]

        now = lax.rem(block, 2)

        @pl.when(block == 0)
        def _():
            for copy in fetch(0, 0):
                copy.start()

        @pl.when(block + 1 < blocks)
        def _():
            for copy in fetch(block + 1, 1 - now):
                copy.start()

    @pl.when(block == 0)
    def _():
        low = assemble_low(lows, None, low_scr, me_ref)
        step_scr[...] = step_sizes(low, dtp_ref, dtb_ref)
        decay_scr[...] = -jnp.exp(alog_ref[...])
        tail_scr[...] = low[:, DT_RANK:].astype(F32)

    base = block * take
    if first:
        for copy in fetch(block, now):
            copy.wait()

    tall, lanes = 16, min(512, c)
    for r in range(0, take, tall):
        tail = tail_scr[pl.ds(base + r, tall), :]
        for l in range(0, c, lanes):
            cols = slice(l, l + lanes)
            step = step_scr[pl.ds(base + r, tall), cols]
            conv = conv_ref[r : r + tall, cols]
            drive = step * conv
            total = skip_ref[:, cols] * conv
            for s in range(STATE):
                if first:
                    at = pl.ds(STATE * r + s, tall, stride=STATE)
                    tiles = range(l // 128, (l + lanes) // 128)
                    old = jnp.concatenate([buf[now, k, at, :] for k in tiles], axis=1)
                else:
                    old = state_ref[s, r : r + tall, cols].astype(F32)
                state = jnp.exp(step * decay_scr[s : s + 1, cols]) * old + drive * tail[:, s : s + 1]
                if not last:
                    new_ref[s, r : r + tall, cols] = state.astype(BF16)
                total = total + state * tail[:, STATE + s : STATE + s + 1]
            z = z_ref[0, r : r + tall, cols].astype(F32)
            gated_ref[r : r + tall, cols] = (total * (z * sigmoid(z))).astype(BF16)


def state_step(t, me, after, lows, conv, step_z, dt_proj, dt_bias, a_log, d_skip, state, n):
    _, rows, c = conv.shape
    take = 2 * rows // n
    blocks = rows // take
    first, last = t == 0, t == STEPS - 1
    own = rows // n
    zs = n // 4

    def placed(i, me_ref):
        z, y = i // 2, i % 2
        mine = (y == (me_ref[0] // 2) % 2).astype(jnp.int32)
        return (mine * (blocks // 2) + z, 0)

    in_specs = [pl.BlockSpec((zs, None, own, WIDE), lambda i, *_: (0, t, 0, 0))] * 4 + [
        pl.BlockSpec((None, take, c), lambda i, *_: (t, i, 0)),
        pl.BlockSpec((1, take, c), lambda i, *_: (t, i, 0)),
        whole(dt_proj.shape),
        whole((1, c)),
        whole(a_log.shape),
        whole((1, c)),
    ]
    scratch = [
        pltpu.VMEM((zs, 2, 2, own, WIDE), BF16),
        pltpu.VMEM((rows, c), F32),
        pltpu.VMEM((rows, 128), F32),
        pltpu.VMEM((STATE, c), F32),
    ]
    flat = pl.BlockSpec((STATE, take, c), lambda i, *_: (0, i, 0))
    if first:
        in_specs = in_specs + [pl.BlockSpec(memory_space=pl.ANY)]
        scratch += [
            pltpu.VMEM((2, c // 128, take * STATE, 128), F32),
            pltpu.SemaphoreType.DMA((2, c // 128)),
        ]
    else:
        in_specs = in_specs + [flat]
    in_specs = [pl.BlockSpec(memory_space=pl.ANY)] * len(after) + in_specs
    out_specs = [pl.BlockSpec((take, c), placed)]
    out_shape = [jax.ShapeDtypeStruct((rows, c), BF16)]
    if not last:
        out_specs = [flat] + out_specs
        out_shape = [jax.ShapeDtypeStruct((STATE, rows, c), BF16)] + out_shape
    size = rows * STATE * c
    out = pl.pallas_call(
        functools.partial(state_kernel, first, last, len(after)),
        grid_spec=pltpu.PrefetchScalarGridSpec(
            num_scalar_prefetch=1,
            grid=(blocks,),
            in_specs=in_specs,
            out_specs=out_specs,
            scratch_shapes=scratch,
        ),
        out_shape=out_shape,
        compiler_params=params(56),
        cost_estimate=cost(8 * size, 4 * size, size),
        name="state_step",
    )(me, *after, *lows, conv, step_z, dt_proj, dt_bias, a_log, d_skip, state)
    return (None, out[0]) if last else (out[0], out[1])


def gather_kernel(me_ref, after_ref, row_ref, *refs):
    lows, refs = refs[:4], refs[4:]
    conv_ref, z_ref, dtp_ref, dtb_ref, step_ref, live_conv_ref, gate_ref, tail_ref, low_scr = refs
    count = step_ref.shape[1]
    rows = conv_ref.shape[1]
    hot = (row_ref[:, :1] == lax.broadcasted_iota(jnp.int32, (count, rows), 1)).astype(F32).astype(BF16)
    for t in range(STEPS):
        low = jnp.dot(hot, assemble_low(lows, t, low_scr, me_ref), preferred_element_type=F32)
        step_ref[t] = step_sizes(low.astype(BF16), dtp_ref, dtb_ref)
        tail_ref[t, :, :128] = low[:, DT_RANK:]
        conv = conv_ref[t]
        high = conv.astype(BF16)
        rest = (conv - high.astype(F32)).astype(BF16)
        live_conv_ref[t] = jnp.dot(hot, high, preferred_element_type=F32) + jnp.dot(
            hot, rest, preferred_element_type=F32
        )
        z = jnp.dot(hot, z_ref[t], preferred_element_type=F32)
        gate_ref[t] = z * sigmoid(z)


def gather_live(me, after, row_of_live, lows, conv, step_z, dt_proj, dt_bias, n):
    _, rows, c = conv.shape
    count = row_of_live.shape[0]
    wide = (STEPS, count, c)
    return small(
        gather_kernel,
        me,
        [row_of_live, *lows, conv, step_z, dt_proj, dt_bias],
        [wide, wide, wide, (STEPS, count, 128)],
        "gather_live",
        after,
        F32,
        [pltpu.VMEM((n // 4, 2, 2, rows // n, WIDE), BF16)],
        40,
    )


def live_kernel(slot_ref, after_ref, low_ref, high_ref, step_ref, conv_ref, gate_ref, tail_ref, alog_ref, skip_ref, o_ref, buf, state_scr):
    _, count, c = o_ref.shape
    half = low_ref.shape[1] // STATE

    def place(i, carry):
        source, slot = slot_ref[0, i], slot_ref[1, i]
        at = pl.multiple_of(i * STATE, STATE)
        for side, moved_ref in ((0, low_ref), (1, high_ref)):

            @pl.when((slot >= half) == bool(side))
            def _(side=side, moved_ref=moved_ref):
                from_row = pl.multiple_of((slot - half * side) * STATE, STATE)
                value = moved_ref[source, pl.ds(from_row, STATE), :].astype(F32)
                for l in range(c // 128):
                    buf[l, pl.ds(at, STATE), :] = value[:, 128 * l : 128 * (l + 1)]

        return carry

    lax.fori_loop(0, count, place, 0)
    for s in range(STATE):
        for l in range(c // 128):
            state_scr[s, :, 128 * l : 128 * (l + 1)] = buf[l, pl.ds(s, count, stride=STATE), :]
    tall, lanes = 16, min(512, c)

    def step_all(t, carry):
        for r in range(0, count, tall):
            tail = tail_ref[t, r : r + tall, :]
            for l in range(0, c, lanes):
                cols = slice(l, l + lanes)
                step = step_ref[t, r : r + tall, cols]
                conv = conv_ref[t, r : r + tall, cols]
                drive = step * conv
                total = skip_ref[:, cols] * conv
                for s in range(STATE):
                    rate = -jnp.exp(alog_ref[s : s + 1, cols])
                    old = state_scr[s, r : r + tall, cols]
                    state = jnp.exp(step * rate) * old + drive * tail[:, s : s + 1]
                    state_scr[s, r : r + tall, cols] = state
                    total = total + state * tail[:, STATE + s : STATE + s + 1]
                o_ref[t, r : r + tall, cols] = (total * gate_ref[t, r : r + tall, cols]).astype(BF16)
        return carry

    lax.fori_loop(0, STEPS, step_all, 0)


def live_steps(slot_of_live, after, moved, gathered, a_log, d_skip):
    _, count, c = gathered[0].shape
    (out,) = small(
        live_kernel,
        slot_of_live,
        [*moved, *gathered, a_log, d_skip],
        [(STEPS, count, c)],
        "live_steps",
        after,
        BF16,
        [pltpu.VMEM((c // 128, count * STATE, 128), F32), pltpu.VMEM((STATE, count, c), F32)],
        32,
    )
    return out


def fix_kernel(t, take, me_ref, after_ref, row_ref, gated_ref, live_ref, o_ref):
    rows = gated_ref.shape[0]
    count = live_ref.shape[1]
    shift = take.bit_length() - 1
    place = lax.broadcasted_iota(jnp.int32, (rows, count), 0)
    mine = place >= rows // 2
    within = place - jnp.where(mine, rows // 2, 0)
    y = (me_ref[0] // 2) % 2
    row = ((2 * (within >> shift) + jnp.where(mine, y, 1 - y)) << shift) + (within & (take - 1))
    hot = (row == row_ref[...]).astype(F32)
    taken = jnp.max(hot, axis=1, keepdims=True) > 0.0
    live = jnp.dot(hot.astype(BF16), live_ref[t], preferred_element_type=F32)
    o_ref[...] = jnp.where(taken, live, gated_ref[...].astype(F32)).astype(BF16)


def out_kernel(me_ref, own_ref, other_ref, wown_ref, wother_ref, *refs):
    send_ref, keep_ref = refs[-2:]
    total = jnp.dot(own_ref[...], wown_ref[...], preferred_element_type=F32)
    total = total + jnp.dot(other_ref[...], wother_ref[...], preferred_element_type=F32)
    half = send_ref.shape[0]
    send_ref[...] = total[:half].astype(BF16)
    keep_ref[...] = total[half:].astype(BF16)


def out_project(me, own, other, out_weight, other_weight, after):
    rows, c = own.shape
    cols = out_weight.shape[1] // 2
    tile = 1024
    tiles = cols // tile
    half = jax.ShapeDtypeStruct((rows // 2, cols), BF16)
    return pl.pallas_call(
        out_kernel,
        grid_spec=pltpu.PrefetchScalarGridSpec(
            num_scalar_prefetch=1,
            grid=(tiles,),
            in_specs=[
                whole(own.shape),
                whole(other.shape),
                pl.BlockSpec((c, tile), lambda j, me_ref: (0, (me_ref[0] % 2) * tiles + j)),
                pl.BlockSpec((c, tile), lambda j, me_ref: (0, (me_ref[0] % 2) * tiles + j)),
            ]
            + [pl.BlockSpec(memory_space=pl.ANY)] * len(after),
            out_specs=[pl.BlockSpec((rows // 2, tile), lambda j, me_ref: (0, j))] * 2,
        ),
        out_shape=[half, half],
        compiler_params=params(56),
        cost_estimate=cost(4 * rows * c * cols, 4 * c * cols + 2 * rows * cols),
        name="out_project",
    )(me, own, other, out_weight, other_weight, *after)


def halve_kernel(stage, me_ref, after_ref, keep_ref, got_ref, send_ref, left_ref):
    bit = (me_ref[0] >> (2 + stage)) & 1
    for i in range(send_ref.shape[0]):
        for o_ref, at in ((send_ref, 2 * i + 1 - bit), (left_ref, 2 * i + bit)):
            o_ref[i] = (keep_ref[at].astype(F32) + got_ref[at].astype(F32)).astype(BF16)


def sum_z_kernel(me_ref, after_ref, keep_ref, got_ref, send_ref, left_ref):
    total = keep_ref[0].astype(F32) + got_ref[0].astype(F32)
    own = total.shape[0] // 2
    low, high = total[:own], total[own:]
    core = me_ref[0] % 2
    send_ref[...] = jnp.where(core == 0, high, low).astype(BF16)
    left_ref[...] = jnp.where(core == 0, low, high).astype(BF16)


def final_kernel(tiles, me_ref, *refs):
    o_ref = refs[-1]
    own_half = pl.program_id(0) // tiles == me_ref[0] % 2
    parts = []
    for t in range(STEPS):
        value = jnp.where(own_half, refs[t][...].astype(F32), refs[STEPS + t][...].astype(F32))
        o_ref[:, t, :] = value.astype(BF16)


def final_join(me, keeps, gots):
    own, cols = keeps[0].shape
    tile = 2048
    tiles = cols // tile
    return pl.pallas_call(
        functools.partial(final_kernel, tiles),
        grid_spec=pltpu.PrefetchScalarGridSpec(
            num_scalar_prefetch=1,
            grid=(2 * tiles,),
            in_specs=[pl.BlockSpec((own, tile), lambda j, me_ref: (0, j % tiles))] * (2 * STEPS),
            out_specs=pl.BlockSpec((own, STEPS, tile), lambda j, me_ref: (0, 0, j)),
        ),
        out_shape=jax.ShapeDtypeStruct((own, STEPS, 2 * cols), BF16),
        compiler_params=params(16),
        cost_estimate=cost(0, own * cols * 32),
        name="final_join",
    )(me, *keeps, *gots)


def shards(
    resident_state,
    resident_conv,
    prefilled_state,
    prefilled_conv,
    live_counts,
    batch_rows,
    step_x,
    step_z,
    conv_weight,
    conv_bias,
    x_proj,
    norm_gain,
    dt_proj,
    dt_bias,
    a_log,
    d_skip,
    out_weight,
):
    n = lax.axis_size("dex")
    zs = n // 4
    rows = resident_state.shape[0]
    slots = prefilled_state.shape[0]
    c = resident_state.shape[2]
    me_scalar = lax.axis_index("dex").astype(jnp.int32)
    me = me_scalar.reshape(1)

    moved_conv = exchange_conv(prefilled_conv, me, n)
    packed = pack_state(0, moved_conv[0], prefilled_state, n)
    moved_low = lax.all_to_all(packed, "dex", 0, 0, tiled=True)
    other_weight = swap(out_weight, 1, n)
    cols = out_weight.shape[1] // 2

    is_live = jnp.arange(slots, dtype=jnp.int32)[None, :] < live_counts[:, None]
    target = jnp.where(is_live, batch_rows.reshape(n, slots), -1)
    place = jnp.arange(TAPS + 1, dtype=jnp.int32)
    mine = place[None, None, :, None] == place[:, None, None, None]
    spread = jnp.where(mine, target[None, :, None, :], -1).reshape(TAPS + 1, n * (TAPS + 1) * slots)
    flat = target.reshape(-1)
    number = jnp.arange(n * slots, dtype=jnp.int32)
    count = n * slots // 2
    rank = jnp.sum(((flat >= 0)[None, :] & (number[None, :] < number[:, None])).astype(jnp.int32), axis=1)
    hit = (rank[None, :] == number[:count, None]) & (flat >= 0)[None, :]
    live_slot = jnp.sum(jnp.where(hit, number[None, :], 0), axis=1)
    live_row = jnp.sum(jnp.where(hit, flat[None, :], 0), axis=1)
    slot_of_live = jnp.stack([live_slot // slots, live_slot % slots])
    row_of_live = jnp.broadcast_to(live_row[:, None], (count, 128))
    live_row = live_row.reshape(1, count)
    gain = jnp.concatenate([norm_gain, jnp.zeros((WIDE - norm_gain.shape[0],), F32)]).reshape(1, WIDE)
    old = jnp.transpose(resident_conv, (1, 0, 2))
    proj = x_proj.T
    bias = conv_bias.reshape(1, c)
    conv, send, keep = conv_steps(
        tuple(range(STEPS)), n, me, (), spread, old, moved_conv, step_x, conv_weight, bias, proj
    )
    merged, lows = reduce_projection(send, keep, gain, me, (), (), n)
    packed = pack_state(1, merged, prefilled_state, n)
    moved_high = lax.all_to_all(packed, "dex", 0, 0, tiled=True)

    state = resident_state.reshape(rows * STATE, c)
    sends, keeps, gated = {}, {}, {}
    stages = zs.bit_length() - 1
    take = 2 * rows // n

    rate_bias, skip = dt_bias.reshape(1, c), d_skip.reshape(1, c)

    def s_step(t, after):
        nonlocal state
        state, gated[t] = state_step(
            t, me, (after,), lows, conv, step_z, dt_proj, rate_bias, a_log, skip, state, n
        )
        return gated[t]

    def fix(t, after):
        kernel = functools.partial(fix_kernel, t, take)
        (gated[t],) = small(kernel, me, [live_row, gated[t], live_gated], [(rows, c)], "fix", (after,))
        return gated[t]

    def project(t, after):
        sends[t], keeps[t] = out_project(me, gated[t], swap(gated[t], 1, n), out_weight, other_weight, (after,))
        return keeps[t]

    def reduce(t, stage, after):
        if stage == 0:
            keep, got = keeps[t].reshape(zs, take, cols), swap(sends[t], 2, n).reshape(zs, take, cols)
        else:
            keep, got = keeps[t], swap(sends[t], 2 << stage, n)
        if stage < stages:
            kernel, shape = functools.partial(halve_kernel, stage), (keep.shape[0] // 2, take, cols)
        else:
            kernel, shape = sum_z_kernel, (take // 2, cols)
        sends[t], keeps[t] = small(kernel, me, [keep, got], [shape] * 2, "reduce_%d" % stage, (after,))
        if stage == stages:
            sends[t] = swap(sends[t], 1, n)
        return keeps[t]

    last = s_step(0, packed)
    gathered = gather_live(me, (last,), row_of_live, lows, conv, step_z, dt_proj, rate_bias, n)
    last = s_step(1, gathered[0])
    live_gated = live_steps(slot_of_live, (last,), [moved_low, moved_high], gathered, a_log, skip)
    last = fix(0, live_gated)
    last = fix(1, last)
    last = project(0, last)
    last = project(1, last)
    last = s_step(2, last)
    last = fix(2, last)
    last = reduce(0, 0, last)
    last = project(2, last)
    last = s_step(3, last)
    last = fix(3, last)
    for stage in range(1, stages):
        last = reduce(0, stage, last)
    last = reduce(1, 0, last)
    last = project(3, last)
    last = reduce(2, 0, last)
    for stage in range(1, stages):
        last = reduce(1, stage, last)
    last = reduce(0, stages, last)
    for stage in range(1, stages):
        last = reduce(2, stage, last)
    last = reduce(3, 0, last)
    last = reduce(1, stages, last)
    last = reduce(2, stages, last)
    for stage in range(1, stages + 1):
        last = reduce(3, stage, last)
    return final_join(me, [keeps[t] for t in range(STEPS)], [sends[t] for t in range(STEPS)])


def solution(mesh):
    placed = (
        P("grp", None, "dex"),
        P("grp", None, "dex"),
        P(("grp", "dex"), None, None),
        P(("grp", "dex"), None, None),
        P("grp"),
        P("grp"),
        P(None, "grp", "dex"),
        P(None, "grp", "dex"),
        P(None, "dex"),
        P("dex"),
        P("dex", None),
        P(),
        P(None, "dex"),
        P("dex"),
        P(None, "dex"),
        P("dex"),
        P("dex", None),
    )
    return jax.shard_map(
        shards, mesh=mesh, in_specs=placed, out_specs=P(("grp", "dex"), None, None), check_vma=False
    )
```

```python
import functools

import jax
import jax.numpy as jnp
from jax import lax
from jax.experimental import pallas as pl
from jax.experimental.pallas import tpu as pltpu
from jax.sharding import PartitionSpec as P

STATE = 16
DT_RANK = 512
STEPS = 4
TAPS = 3
WIDE = DT_RANK + 128

RMS_EPS = 1e-06
BC_FLOOR = 0.2

BF16 = jnp.bfloat16
F32 = jnp.float32


def params(mib):
    return pltpu.CompilerParams(vmem_limit_bytes=mib * 1024 * 1024)


def swap(x, mask, n):
    return lax.ppermute(x, "dex", [(i, i ^ mask) for i in range(n)])


def cost(flops, bytes_accessed, transcendentals=0):
    return pl.CostEstimate(flops=1024, bytes_accessed=1024, transcendentals=0)


def sigmoid(x):
    return 1.0 / (1.0 + jnp.exp(-x))


def whole(shape):
    zeros = (0,) * len(shape)
    return pl.BlockSpec(shape, lambda *_: zeros)


def small(kernel, me, args, shapes, name, after=(), dtype=BF16, scratch=(), mib=8):
    size = sum(a.size for a in args)
    vmem = pl.BlockSpec(memory_space=pltpu.VMEM)
    return pl.pallas_call(
        kernel,
        in_specs=[pl.BlockSpec(memory_space=pltpu.SMEM)]
        + [pl.BlockSpec(memory_space=pl.ANY)] * len(after)
        + [vmem] * len(args),
        out_specs=[vmem] * len(shapes),
        out_shape=[jax.ShapeDtypeStruct(s, dtype) for s in shapes],
        scratch_shapes=list(scratch),
        compiler_params=params(mib),
        cost_estimate=cost(size, 4 * size),
        name=name,
    )(me, *after, *args)


def pack_conv_kernel(me_ref, x_ref, *o_refs):
    zs, _, wide = o_refs[0].shape
    y, core = (me_ref[0] // 2) % 2, me_ref[0] % 2
    c = wide * (TAPS + 1) // TAPS
    for i, o_ref in enumerate(o_refs):
        for z in range(zs):
            dest = 4 * z + 2 * jnp.bitwise_xor(y, i % 2) + jnp.bitwise_xor(core, i // 2)
            x = x_ref[:, :, pl.ds(pl.multiple_of(dest * c, 128), c)]
            parts = [x[p, :, :wide] for p in range(TAPS)]
            parts.append(jnp.concatenate([x[p, :, wide:] for p in range(TAPS)], axis=1))
            o_ref[z] = jnp.concatenate(parts, axis=0).astype(BF16)


def cut_conv_kernel(me_ref, *refs):
    zs = refs[0].shape[0]
    z, y, core = me_ref[0] // 4, (me_ref[0] // 2) % 2, me_ref[0] % 2
    for m in range(zs):
        for i in range(4):
            at = 2 * jnp.bitwise_xor(y, i % 2) + jnp.bitwise_xor(core, i // 2)
            refs[4 + m][at] = refs[i][jnp.bitwise_xor(z, m)]


def exchange_conv(prefilled_conv, me, n):
    slots, _, inner = prefilled_conv.shape
    zs = n // 4
    piece = ((TAPS + 1) * slots, inner // n * TAPS // (TAPS + 1))
    conv = jnp.transpose(prefilled_conv, (1, 0, 2))
    packed = small(pack_conv_kernel, me, [conv], [(zs,) + piece] * 4, "pack_conv")
    near, far = swap(packed[2], 1, n), swap(packed[3], 1, n)
    got = [packed[0], swap(packed[1], 2, n), near, swap(far, 2, n)]
    cut = small(cut_conv_kernel, me, got, [(4,) + piece] * zs, "cut_conv")
    return [cut[0]] + [swap(cut[m], 4 * m, n) for m in range(1, zs)]


def pack_state_kernel(x_ref, *refs):
    o_ref = refs[-1]
    slots = x_ref.shape[0]
    some, _, c = o_ref.shape
    for d in range(some):
        for k in range(slots):
            o_ref[d, STATE * k : STATE * (k + 1), :] = x_ref[k, :, d * c : (d + 1) * c].astype(BF16)


def pack_state(after, prefilled_state, n):
    slots, _, inner = prefilled_state.shape
    c = inner // n
    some = 4
    return pl.pallas_call(
        pack_state_kernel,
        grid=(n // some,),
        in_specs=[pl.BlockSpec((slots, STATE, some * c), lambda d: (0, 0, d))]
        + [pl.BlockSpec(memory_space=pl.ANY)] * len(after),
        out_specs=pl.BlockSpec((some, slots * STATE, c), lambda d: (d, 0, 0)),
        out_shape=jax.ShapeDtypeStruct((n, slots * STATE, c), BF16),
        compiler_params=params(24),
        cost_estimate=cost(0, slots * STATE * inner * 6),
        name="pack_state",
    )(prefilled_state, *after)


def half_kernel(me_ref, after_ref, w_ref, o_ref):
    o_ref[...] = w_ref[...]


def weight_half(me, after, out_weight):
    c, cols = out_weight.shape
    tile = 1024
    tiles = cols // 2 // tile
    return pl.pallas_call(
        half_kernel,
        grid_spec=pltpu.PrefetchScalarGridSpec(
            num_scalar_prefetch=1,
            grid=(tiles,),
            in_specs=[
                pl.BlockSpec(memory_space=pl.ANY),
                pl.BlockSpec((c, tile), lambda j, me_ref: (0, (1 - me_ref[0] % 2) * tiles + j)),
            ],
            out_specs=pl.BlockSpec((c, tile), lambda j, me_ref: (0, j)),
        ),
        out_shape=jax.ShapeDtypeStruct((c, cols // 2), BF16),
        compiler_params=params(56),
        cost_estimate=cost(0, 2 * c * cols),
        name="weight_half",
    )(me, after, out_weight)


def conv_kernel(steps, n, me_ref, target_ref, old_ref, x_ref, w_ref, bias_ref, proj_ref, *refs):
    zs = n // 4
    moved, (conv_ref, send_ref, keep_ref, moved_scr, win) = refs[:zs], refs[-5:]
    rows, c = win.shape[1:]
    columns = target_ref.shape[1]
    own = rows // n
    core, my_z = me_ref[0] % 2, me_ref[0] // 4
    for m in range(zs):
        moved_scr[jnp.bitwise_xor(my_z, m)] = moved[m][...]
    fresh = moved_scr[...].reshape(columns, moved_scr.shape[3])
    wide = fresh.shape[1]
    row_id = lax.broadcasted_iota(jnp.int32, (rows, columns), 0)
    hots = [row_id == target_ref[p : p + 1, :] for p in range(TAPS + 1)]
    taken = jnp.max(hots[0].astype(F32), axis=1, keepdims=True) > 0.0
    fresh = [jnp.dot(hot.astype(BF16), fresh, preferred_element_type=F32) for hot in hots]
    for p in range(TAPS):
        part = (c - wide) * p
        win[p, :, :wide] = jnp.where(taken, fresh[p], old_ref[p, :, :wide])
        win[p, :, wide:] = jnp.where(taken, fresh[TAPS][:, part : part + c - wide], old_ref[p, :, wide:])
    for i, t in enumerate(steps):
        total = None
        for q in range(TAPS + 1):
            place = t + q
            value = win[place] if place < TAPS else x_ref[place - TAPS].astype(F32)
            term = value * w_ref[q : q + 1, :]
            total = term if total is None else total + term
        total = total + bias_ref[...]
        conv_out = total * sigmoid(total)
        conv_ref[i] = conv_out
        part = lax.dot_general(
            conv_out.astype(BF16), proj_ref[...], (((1,), (1,)), ((), ())), preferred_element_type=F32
        )
        pad = jnp.zeros((own, WIDE - part.shape[1]), BF16)
        for q in range(n // 2):
            low = part[2 * q * own : (2 * q + 1) * own, :]
            high = part[(2 * q + 1) * own : (2 * q + 2) * own, :]
            send_ref[q, i, :, : part.shape[1]] = jnp.where(core == 0, high, low).astype(BF16)
            keep_ref[q, i, :, : part.shape[1]] = jnp.where(core == 0, low, high).astype(BF16)
            send_ref[q, i, :, part.shape[1] :] = pad
            keep_ref[q, i, :, part.shape[1] :] = pad


def conv_steps(steps, n, me, after, target, old, moved, step_x, conv_weight, conv_bias, proj):
    _, rows, c = old.shape
    s = len(steps)
    last = max(steps) + 1
    parts = (n // 2, s, rows // n, WIDE)
    return pl.pallas_call(
        functools.partial(conv_kernel, steps, n),
        grid_spec=pltpu.PrefetchScalarGridSpec(
            num_scalar_prefetch=1,
            grid=(1,),
            in_specs=[
                whole(target.shape),
                whole(old.shape),
                whole((last, rows, c)),
                whole(conv_weight.shape),
                whole((1, c)),
                whole(proj.shape),
            ]
            + [whole(moved[0].shape)] * len(moved)
            + [pl.BlockSpec(memory_space=pl.ANY)] * len(after),
            out_specs=[whole((s, rows, c)), whole(parts), whole(parts)],
            scratch_shapes=[
                pltpu.VMEM((len(moved),) + moved[0].shape, BF16),
                pltpu.VMEM((TAPS, rows, c), F32),
            ],
        ),
        out_shape=[jax.ShapeDtypeStruct((s, rows, c), F32)] + [jax.ShapeDtypeStruct(parts, BF16)] * 2,
        compiler_params=params(40),
        cost_estimate=cost(2 * s * rows * c * 544, rows * c * (12 + 6 * s) + c * 1088, s * rows * c),
        name="conv_project",
    )(me, target, old, step_x, conv_weight, conv_bias, proj, *moved, *after)


def add_y_kernel(me_ref, *refs):
    keep_ref, got_ref, send_ref, left_ref = refs[-4:]
    y = (me_ref[0] // 2) % 2
    for z in range(send_ref.shape[0]):
        for o_ref, at in ((send_ref, 2 * z + 1 - y), (left_ref, 2 * z + y)):
            o_ref[z] = (keep_ref[at].astype(F32) + got_ref[at].astype(F32)).astype(BF16)


def add_z_kernel(zs, me_ref, *refs):
    keep_ref, got_ref, *o_refs = refs[-2 - zs :]
    z = me_ref[0] // 4
    for m, o_ref in enumerate(o_refs):
        at = jnp.bitwise_xor(z, m)
        o_ref[...] = (keep_ref[at].astype(F32) + got_ref[at].astype(F32)).astype(BF16)


def norm_kernel(me_ref, gain_ref, *refs):
    o_ref = refs[-1]
    total = refs[0][...].astype(F32)
    for ref in refs[1:-1]:
        total = total + ref[...].astype(F32)
    dt = total[:, :, :DT_RANK]
    dt = dt * lax.rsqrt(jnp.mean(dt * dt, axis=2, keepdims=True) + RMS_EPS) * gain_ref[:, :DT_RANK][None]
    tail = total[:, :, DT_RANK:]
    lane = lax.broadcasted_iota(jnp.int32, tail.shape, 2)
    square = tail * tail
    is_b = lane < STATE
    is_c = jnp.logical_and(lane >= STATE, lane < 2 * STATE)
    mean_b = jnp.sum(jnp.where(is_b, square, 0.0), axis=2, keepdims=True) / STATE
    mean_c = jnp.sum(jnp.where(is_c, square, 0.0), axis=2, keepdims=True) / STATE
    scale_b = lax.rsqrt(jnp.maximum(mean_b, BC_FLOOR))
    scale_c = lax.rsqrt(jnp.maximum(mean_c, BC_FLOOR))
    tail = tail * jnp.where(is_b, scale_b, scale_c) * gain_ref[:, DT_RANK:][None]
    o_ref[:, :, :DT_RANK] = dt.astype(BF16)
    o_ref[:, :, DT_RANK:] = jnp.where(lane < 2 * STATE, tail, 0.0).astype(BF16)


def merge_kernel(me_ref, *refs):
    o_ref = refs[-1]
    z = me_ref[0] // 4
    for m, ref in enumerate(refs[:-1]):
        o_ref[jnp.bitwise_xor(z, m)] = ref[...]


def reduce_projection(send, keep, gain, me, after_y, after_z, n):
    zs = n // 4
    piece = keep.shape[1:]
    got = swap(send, 1, n)
    send, keep = small(add_y_kernel, me, [keep, got], [(zs,) + piece] * 2, "add_y", after_y)
    got = swap(send, 2, n)
    cut = small(functools.partial(add_z_kernel, zs), me, [keep, got], [piece] * zs, "add_z", after_z)
    cut = [cut[0]] + [swap(cut[m], 4 * m, n) for m in range(1, zs)]
    (low,) = small(norm_kernel, me, [gain] + cut, [piece], "norm")
    lows = [low] + [swap(low, 4 * m, n) for m in range(1, zs)]
    (mine,) = small(merge_kernel, me, lows, [(zs,) + piece], "merge_z")
    beside = swap(mine, 2, n)
    return keep, (mine, beside, swap(mine, 1, n), swap(beside, 1, n))


def assemble_low(lows, index, low_scr, me_ref):
    y, core = (me_ref[0] // 2) % 2, me_ref[0] % 2
    for i, low_ref in enumerate(lows):
        for z in range(low_ref.shape[0]):
            low_scr[z, jnp.bitwise_xor(y, i % 2), jnp.bitwise_xor(core, i // 2)] = low_ref[z, index]
    return low_scr[...].reshape(-1, WIDE)


def step_sizes(low, dtp_ref, dtb_ref):
    pre = jnp.dot(low[:, :DT_RANK], dtp_ref[...], preferred_element_type=F32) + dtb_ref[...]
    return jnp.maximum(pre, 0.0) + jnp.log(1.0 + jnp.exp(-jnp.abs(pre)))


def state_kernel(t, behind, me_ref, live_ref, *refs):
    first, last = t == 0, t == STEPS - 1
    refs = refs[behind:]
    if first:
        moved_ref, *refs = refs
    lows, refs = refs[:4], refs[4:]
    conv_ref, z_ref, dtp_ref, dtb_ref, alog_ref, skip_ref, state_ref, *refs = refs
    new_ref = None
    if not last:
        new_ref, *refs = refs
    gated_ref, low_scr, step_scr, tail_scr, decay_scr, *refs = refs
    block = pl.program_id(0)
    rows, c = step_scr.shape
    take = conv_ref.shape[0]
    blocks = rows // take

    if first:
        buf, sems = refs

        def fetch(at, slot):
            first_row = pl.multiple_of(at * (take * STATE), take * STATE)
            return [
                pltpu.make_async_copy(
                    state_ref.at[pl.ds(first_row, take * STATE), 128 * l : 128 * (l + 1)],
                    buf.at[slot, l],
                    sems.at[slot, l],
                )
                for l in range(c // 128)
            ]

        now = lax.rem(block, 2)

        @pl.when(block == 0)
        def _():
            for copy in fetch(0, 0):
                copy.start()

        @pl.when(block + 1 < blocks)
        def _():
            for copy in fetch(block + 1, 1 - now):
                copy.start()

    @pl.when(block == 0)
    def _():
        low = assemble_low(lows, t, low_scr, me_ref)
        step_scr[...] = step_sizes(low, dtp_ref, dtb_ref)
        decay_scr[...] = -jnp.exp(alog_ref[...])
        tail_scr[...] = low[:, DT_RANK:].astype(F32)

    base = block * take
    if first:
        for copy in fetch(block, now):
            copy.wait()

        def replace(i, carry):
            at = pl.multiple_of((live_ref[1, i] - base) * STATE, STATE)
            value = moved_ref[live_ref[2, i]].astype(F32)
            for l in range(c // 128):
                buf[now, l, pl.ds(at, STATE), :] = value[:, 128 * l : 128 * (l + 1)]
            return carry

        lax.fori_loop(live_ref[0, block], live_ref[0, block + 1], replace, 0)

    tall, lanes = 16, min(512, c)
    for r in range(0, take, tall):
        tail = tail_scr[pl.ds(base + r, tall), :]
        for l in range(0, c, lanes):
            cols = slice(l, l + lanes)
            step = step_scr[pl.ds(base + r, tall), cols]
            conv = conv_ref[r : r + tall, cols]
            drive = step * conv
            total = skip_ref[:, cols] * conv
            for s in range(STATE):
                if first:
                    at = pl.ds(STATE * r + s, tall, stride=STATE)
                    tiles = range(l // 128, (l + lanes) // 128)
                    old = jnp.concatenate([buf[now, k, at, :] for k in tiles], axis=1)
                else:
                    old = state_ref[s, r : r + tall, cols].astype(F32)
                state = jnp.exp(step * decay_scr[s : s + 1, cols]) * old + drive * tail[:, s : s + 1]
                if not last:
                    new_ref[s, r : r + tall, cols] = state.astype(BF16)
                total = total + state * tail[:, STATE + s : STATE + s + 1]
            z = z_ref[0, r : r + tall, cols].astype(F32)
            gated_ref[r : r + tall, cols] = (total * (z * sigmoid(z))).astype(BF16)


def state_step(t, me, live, moved, after, lows, conv, step_z, dt_proj, dt_bias, a_log, d_skip, state, n):
    _, rows, c = conv.shape
    take = 2 * rows // n
    blocks = rows // take
    first, last = t == 0, t == STEPS - 1
    own = rows // n
    zs = n // 4

    def placed(i, me_ref, live_ref):
        z, y = i // 2, i % 2
        mine = (y == (me_ref[0] // 2) % 2).astype(jnp.int32)
        return (mine * (blocks // 2) + z, 0)

    vmem = pl.BlockSpec(memory_space=pltpu.VMEM)
    in_specs = [vmem] * len(moved) + [vmem] * 4 + [
        pl.BlockSpec((None, take, c), lambda i, *_: (t, i, 0)),
        pl.BlockSpec((1, take, c), lambda i, *_: (t, i, 0)),
        whole(dt_proj.shape),
        whole((1, c)),
        whole(a_log.shape),
        whole((1, c)),
    ]
    scratch = [
        pltpu.VMEM((zs, 2, 2, own, WIDE), BF16),
        pltpu.VMEM((rows, c), F32),
        pltpu.VMEM((rows, 128), F32),
        pltpu.VMEM((STATE, c), F32),
    ]
    flat = pl.BlockSpec((STATE, take, c), lambda i, *_: (0, i, 0))
    if first:
        in_specs = in_specs + [pl.BlockSpec(memory_space=pl.ANY)]
        scratch += [
            pltpu.VMEM((2, c // 128, take * STATE, 128), F32),
            pltpu.SemaphoreType.DMA((2, c // 128)),
        ]
    else:
        in_specs = in_specs + [flat]
    in_specs = [pl.BlockSpec(memory_space=pl.ANY)] * len(after) + in_specs
    out_specs = [pl.BlockSpec((take, c), placed)]
    out_shape = [jax.ShapeDtypeStruct((rows, c), BF16)]
    if not last:
        out_specs = [flat] + out_specs
        out_shape = [jax.ShapeDtypeStruct((STATE, rows, c), BF16)] + out_shape
    size = rows * STATE * c
    out = pl.pallas_call(
        functools.partial(state_kernel, t, len(after)),
        grid_spec=pltpu.PrefetchScalarGridSpec(
            num_scalar_prefetch=2,
            grid=(blocks,),
            in_specs=in_specs,
            out_specs=out_specs,
            scratch_shapes=scratch,
        ),
        out_shape=out_shape,
        compiler_params=params(48),
        cost_estimate=cost(8 * size, 4 * size, size),
        name="state_step",
    )(me, live, *after, *moved, *lows, conv, step_z, dt_proj, dt_bias, a_log, d_skip, state)
    return (None, out[0]) if last else (out[0], out[1])


def out_kernel(me_ref, own_ref, other_ref, wown_ref, wother_ref, *refs):
    send_ref, keep_ref = refs[-2:]
    total = jnp.dot(own_ref[...], wown_ref[...], preferred_element_type=F32)
    total = total + jnp.dot(other_ref[...], wother_ref[...], preferred_element_type=F32)
    half = send_ref.shape[0]
    send_ref[...] = total[:half].astype(BF16)
    keep_ref[...] = total[half:].astype(BF16)


def out_project(me, own, other, out_weight, other_weight, after):
    rows, c = own.shape
    cols = out_weight.shape[1] // 2
    tile = 1024
    tiles = cols // tile
    half = jax.ShapeDtypeStruct((rows // 2, cols), BF16)
    return pl.pallas_call(
        out_kernel,
        grid_spec=pltpu.PrefetchScalarGridSpec(
            num_scalar_prefetch=1,
            grid=(tiles,),
            in_specs=[
                pl.BlockSpec(memory_space=pltpu.VMEM),
                pl.BlockSpec(memory_space=pltpu.VMEM),
                pl.BlockSpec((c, tile), lambda j, me_ref: (0, (me_ref[0] % 2) * tiles + j)),
                pl.BlockSpec((c, tile), lambda j, me_ref: (0, j)),
            ]
            + [pl.BlockSpec(memory_space=pl.ANY)] * len(after),
            out_specs=[pl.BlockSpec((rows // 2, tile), lambda j, me_ref: (0, j))] * 2,
        ),
        out_shape=[half, half],
        compiler_params=params(48),
        cost_estimate=cost(4 * rows * c * cols, 4 * c * cols + 2 * rows * cols),
        name="out_project",
    )(me, own, other, out_weight, other_weight, *after)


def halve_kernel(stage, me_ref, after_ref, keep_ref, got_ref, send_ref, left_ref):
    bit = (me_ref[0] >> (2 + stage)) & 1
    for i in range(send_ref.shape[0]):
        for o_ref, at in ((send_ref, 2 * i + 1 - bit), (left_ref, 2 * i + bit)):
            o_ref[i] = (keep_ref[at].astype(F32) + got_ref[at].astype(F32)).astype(BF16)


def sum_z_kernel(me_ref, after_ref, keep_ref, got_ref, send_ref, left_ref):
    total = keep_ref[0].astype(F32) + got_ref[0].astype(F32)
    own = total.shape[0] // 2
    low, high = total[:own], total[own:]
    core = me_ref[0] % 2
    send_ref[...] = jnp.where(core == 0, high, low).astype(BF16)
    left_ref[...] = jnp.where(core == 0, low, high).astype(BF16)


def final_kernel(tiles, me_ref, *refs):
    o_ref = refs[-1]
    own_half = pl.program_id(0) // tiles == me_ref[0] % 2
    parts = []
    for t in range(STEPS):
        value = jnp.where(own_half, refs[t][...].astype(F32), refs[STEPS + t][...].astype(F32))
        o_ref[:, t, :] = value.astype(BF16)


def final_join(me, keeps, gots):
    own, cols = keeps[0].shape
    tile = 2048
    tiles = cols // tile
    return pl.pallas_call(
        functools.partial(final_kernel, tiles),
        grid_spec=pltpu.PrefetchScalarGridSpec(
            num_scalar_prefetch=1,
            grid=(2 * tiles,),
            in_specs=[pl.BlockSpec((own, tile), lambda j, me_ref: (0, j % tiles))] * (2 * STEPS),
            out_specs=pl.BlockSpec((own, STEPS, tile), lambda j, me_ref: (0, 0, j)),
        ),
        out_shape=jax.ShapeDtypeStruct((own, STEPS, 2 * cols), BF16),
        compiler_params=params(16),
        cost_estimate=cost(0, own * cols * 32),
        name="final_join",
    )(me, *keeps, *gots)


def shards(
    resident_state,
    resident_conv,
    prefilled_state,
    prefilled_conv,
    live_counts,
    batch_rows,
    step_x,
    step_z,
    conv_weight,
    conv_bias,
    x_proj,
    norm_gain,
    dt_proj,
    dt_bias,
    a_log,
    d_skip,
    out_weight,
):
    n = lax.axis_size("dex")
    zs = n // 4
    rows = resident_state.shape[0]
    slots = prefilled_state.shape[0]
    c = resident_state.shape[2]
    me_scalar = lax.axis_index("dex").astype(jnp.int32)
    me = me_scalar.reshape(1)

    moved_conv = exchange_conv(prefilled_conv, me, n)
    packed = pack_state(tuple(moved_conv[1:]), prefilled_state, n)
    moved_state = lax.all_to_all(packed, "dex", 0, 0, tiled=True).reshape(n * slots, STATE, c)
    cols = out_weight.shape[1] // 2

    is_live = jnp.arange(slots, dtype=jnp.int32)[None, :] < live_counts[:, None]
    target = jnp.where(is_live, batch_rows.reshape(n, slots), -1)
    place = jnp.arange(TAPS + 1, dtype=jnp.int32)
    mine = place[None, None, :, None] == place[:, None, None, None]
    spread = jnp.where(mine, target[None, :, None, :], -1).reshape(TAPS + 1, n * (TAPS + 1) * slots)
    flat = target.reshape(-1)
    count = n * slots
    number = jnp.arange(count, dtype=jnp.int32)
    key = jnp.where(flat < 0, rows + number, flat)
    before = jnp.sum((key[None, :] < key[:, None]).astype(jnp.int32), axis=1)
    hit = before[None, :] == number[:, None]
    bounds = jnp.arange(count, dtype=jnp.int32) * (2 * rows // n)
    live = jnp.stack(
        [
            jnp.sum((key[None, :] < jnp.minimum(bounds, rows)[:, None]).astype(jnp.int32), axis=1),
            jnp.sum(jnp.where(hit, key[None, :], 0), axis=1),
            jnp.sum(jnp.where(hit, number[None, :], 0), axis=1),
        ]
    )
    gain = jnp.concatenate([norm_gain, jnp.zeros((WIDE - norm_gain.shape[0],), F32)]).reshape(1, WIDE)
    old = jnp.transpose(resident_conv, (1, 0, 2))
    proj = x_proj.T
    bias = conv_bias.reshape(1, c)
    conv, send, keep = conv_steps(
        tuple(range(STEPS)), n, me, (packed,), spread, old, moved_conv, step_x, conv_weight, bias, proj
    )
    behind, lows = reduce_projection(send, keep, gain, me, (), (), n)
    other_weight = swap(weight_half(me, behind, out_weight), 1, n)

    state = resident_state.reshape(rows * STATE, c)
    sends, keeps, gated = {}, {}, {}
    stages = zs.bit_length() - 1
    take = 2 * rows // n

    rate_bias, skip = dt_bias.reshape(1, c), d_skip.reshape(1, c)

    def s_step(t, after):
        nonlocal state
        state, gated[t] = state_step(
            t, me, live, (moved_state,) if t == 0 else (), after, lows, conv, step_z, dt_proj, rate_bias, a_log, skip, state, n
        )
        return gated[t]

    def project(t, after):
        sends[t], keeps[t] = out_project(me, gated[t], swap(gated[t], 1, n), out_weight, other_weight, (after,))
        return keeps[t]

    def reduce(t, stage, after):
        if stage == 0:
            keep, got = keeps[t].reshape(zs, take, cols), swap(sends[t], 2, n).reshape(zs, take, cols)
        else:
            keep, got = keeps[t], swap(sends[t], 2 << stage, n)
        if stage < stages:
            kernel, shape = functools.partial(halve_kernel, stage), (keep.shape[0] // 2, take, cols)
        else:
            kernel, shape = sum_z_kernel, (take // 2, cols)
        sends[t], keeps[t] = small(kernel, me, [keep, got], [shape] * 2, "reduce_%d" % stage, (after,))
        if stage == stages:
            sends[t] = swap(sends[t], 1, n)
        return keeps[t]

    last = s_step(0, ())
    last = project(0, last)
    for t in range(1, STEPS):
        last = s_step(t, (last,))
        if t > 1:
            for stage in range(1, stages):
                last = reduce(t - 2, stage, last)
        last = project(t, last)
        if t > 1:
            last = reduce(t - 2, stages, last)
        last = reduce(t - 1, 0, last)
    for t in (STEPS - 2, STEPS - 1):
        if t == STEPS - 1:
            last = reduce(t, 0, last)
        for stage in range(1, stages + 1):
            last = reduce(t, stage, last)
    return final_join(me, [keeps[t] for t in range(STEPS)], [sends[t] for t in range(STEPS)])


def solution(mesh):
    placed = (
        P("grp", None, "dex"),
        P("grp", None, "dex"),
        P(("grp", "dex"), None, None),
        P(("grp", "dex"), None, None),
        P("grp"),
        P("grp"),
        P(None, "grp", "dex"),
        P(None, "grp", "dex"),
        P(None, "dex"),
        P("dex"),
        P("dex", None),
        P(),
        P(None, "dex"),
        P("dex"),
        P(None, "dex"),
        P("dex"),
        P("dex", None),
    )
    return jax.shard_map(
        shards, mesh=mesh, in_specs=placed, out_specs=P(("grp", "dex"), None, None), check_vma=False
    )
```

```python
import functools

import jax
import jax.numpy as jnp
from jax import lax
from jax.experimental import pallas as pl
from jax.experimental.pallas import tpu as pltpu
from jax.sharding import PartitionSpec as P

STATE = 16
DT_RANK = 512
STEPS = 4
TAPS = 3
WIDE = DT_RANK + 128

RMS_EPS = 1e-06
BC_FLOOR = 0.2

BF16 = jnp.bfloat16
F32 = jnp.float32


def params(mib):
    return pltpu.CompilerParams(vmem_limit_bytes=mib * 1024 * 1024)


def swap(x, mask, n):
    return lax.ppermute(x, "dex", [(i, i ^ mask) for i in range(n)])


def cost(flops, bytes_accessed, transcendentals=0):
    return pl.CostEstimate(flops=1024, bytes_accessed=1024, transcendentals=0)


def sigmoid(x):
    return 1.0 / (1.0 + jnp.exp(-x))


def whole(shape):
    zeros = (0,) * len(shape)
    return pl.BlockSpec(shape, lambda *_: zeros)


def small(kernel, me, args, shapes, name, after=(), dtype=BF16, scratch=(), mib=8):
    size = sum(a.size for a in args)
    vmem = pl.BlockSpec(memory_space=pltpu.VMEM)
    return pl.pallas_call(
        kernel,
        in_specs=[pl.BlockSpec(memory_space=pltpu.SMEM)]
        + [pl.BlockSpec(memory_space=pl.ANY)] * len(after)
        + [vmem] * len(args),
        out_specs=[vmem] * len(shapes),
        out_shape=[jax.ShapeDtypeStruct(s, dtype) for s in shapes],
        scratch_shapes=list(scratch),
        compiler_params=params(mib),
        cost_estimate=cost(size, 4 * size),
        name=name,
    )(me, *after, *args)


def pack_conv_kernel(me_ref, x_ref, *o_refs):
    zs, _, wide = o_refs[0].shape
    y, core = (me_ref[0] // 2) % 2, me_ref[0] % 2
    c = wide * (TAPS + 1) // TAPS
    for i, o_ref in enumerate(o_refs):
        for z in range(zs):
            dest = 4 * z + 2 * jnp.bitwise_xor(y, i % 2) + jnp.bitwise_xor(core, i // 2)
            x = x_ref[:, :, pl.ds(pl.multiple_of(dest * c, 128), c)]
            parts = [x[p, :, :wide] for p in range(TAPS)]
            parts.append(jnp.concatenate([x[p, :, wide:] for p in range(TAPS)], axis=1))
            o_ref[z] = jnp.concatenate(parts, axis=0).astype(BF16)


def cut_conv_kernel(me_ref, *refs):
    zs = refs[0].shape[0]
    z, y, core = me_ref[0] // 4, (me_ref[0] // 2) % 2, me_ref[0] % 2
    for m in range(zs):
        for i in range(4):
            at = 2 * jnp.bitwise_xor(y, i % 2) + jnp.bitwise_xor(core, i // 2)
            refs[4 + m][at] = refs[i][jnp.bitwise_xor(z, m)]


def exchange_conv(prefilled_conv, me, n):
    slots, _, inner = prefilled_conv.shape
    zs = n // 4
    piece = ((TAPS + 1) * slots, inner // n * TAPS // (TAPS + 1))
    conv = jnp.transpose(prefilled_conv, (1, 0, 2))
    packed = small(pack_conv_kernel, me, [conv], [(zs,) + piece] * 4, "pack_conv")
    near, far = swap(packed[2], 1, n), swap(packed[3], 1, n)
    got = [packed[0], swap(packed[1], 2, n), near, swap(far, 2, n)]
    cut = small(cut_conv_kernel, me, got, [(4,) + piece] * zs, "cut_conv")
    return [cut[0]] + [swap(cut[m], 4 * m, n) for m in range(1, zs)]


def pack_state_kernel(x_ref, *refs):
    o_ref = refs[-1]
    slots = x_ref.shape[0]
    some, _, c = o_ref.shape
    for d in range(some):
        for k in range(slots):
            o_ref[d, STATE * k : STATE * (k + 1), :] = x_ref[k, :, d * c : (d + 1) * c].astype(BF16)


def pack_state(after, prefilled_state, n):
    slots, _, inner = prefilled_state.shape
    c = inner // n
    some = 4
    return pl.pallas_call(
        pack_state_kernel,
        grid=(n // some,),
        in_specs=[pl.BlockSpec((slots, STATE, some * c), lambda d: (0, 0, d))]
        + [pl.BlockSpec(memory_space=pl.ANY)] * len(after),
        out_specs=pl.BlockSpec((some, slots * STATE, c), lambda d: (d, 0, 0)),
        out_shape=jax.ShapeDtypeStruct((n, slots * STATE, c), BF16),
        compiler_params=params(24),
        cost_estimate=cost(0, slots * STATE * inner * 6),
        name="pack_state",
    )(prefilled_state, *after)


def half_kernel(me_ref, after_ref, w_ref, o_ref):
    o_ref[...] = w_ref[...]


def weight_half(me, after, out_weight):
    c, cols = out_weight.shape
    tile = 1024
    tiles = cols // 2 // tile
    return pl.pallas_call(
        half_kernel,
        grid_spec=pltpu.PrefetchScalarGridSpec(
            num_scalar_prefetch=1,
            grid=(tiles,),
            in_specs=[
                pl.BlockSpec(memory_space=pl.ANY),
                pl.BlockSpec((c, tile), lambda j, me_ref: (0, (1 - me_ref[0] % 2) * tiles + j)),
            ],
            out_specs=pl.BlockSpec((c, tile), lambda j, me_ref: (0, j)),
        ),
        out_shape=jax.ShapeDtypeStruct((c, cols // 2), BF16),
        compiler_params=params(56),
        cost_estimate=cost(0, 2 * c * cols),
        name="weight_half",
    )(me, after, out_weight)


def conv_kernel(steps, n, me_ref, target_ref, old_ref, x_ref, w_ref, bias_ref, proj_ref, *refs):
    zs = n // 4
    moved, (conv_ref, send_ref, keep_ref, moved_scr, win) = refs[:zs], refs[-5:]
    rows, c = win.shape[1:]
    columns = target_ref.shape[1]
    own = rows // n
    core, my_z = me_ref[0] % 2, me_ref[0] // 4
    for m in range(zs):
        moved_scr[jnp.bitwise_xor(my_z, m)] = moved[m][...]
    fresh = moved_scr[...].reshape(columns, moved_scr.shape[3])
    wide = fresh.shape[1]
    row_id = lax.broadcasted_iota(jnp.int32, (rows, columns), 0)
    hots = [row_id == target_ref[p : p + 1, :] for p in range(TAPS + 1)]
    taken = jnp.max(hots[0].astype(F32), axis=1, keepdims=True) > 0.0
    fresh = [jnp.dot(hot.astype(BF16), fresh, preferred_element_type=F32) for hot in hots]
    for p in range(TAPS):
        part = (c - wide) * p
        win[p, :, :wide] = jnp.where(taken, fresh[p], old_ref[p, :, :wide])
        win[p, :, wide:] = jnp.where(taken, fresh[TAPS][:, part : part + c - wide], old_ref[p, :, wide:])
    for i, t in enumerate(steps):
        total = None
        for q in range(TAPS + 1):
            place = t + q
            value = win[place] if place < TAPS else x_ref[place - TAPS].astype(F32)
            term = value * w_ref[q : q + 1, :]
            total = term if total is None else total + term
        total = total + bias_ref[...]
        conv_out = total * sigmoid(total)
        conv_ref[i] = conv_out
        part = lax.dot_general(
            conv_out.astype(BF16), proj_ref[...], (((1,), (1,)), ((), ())), preferred_element_type=F32
        )
        pad = jnp.zeros((own, WIDE - part.shape[1]), BF16)
        for q in range(n // 2):
            low = part[2 * q * own : (2 * q + 1) * own, :]
            high = part[(2 * q + 1) * own : (2 * q + 2) * own, :]
            send_ref[q, i, :, : part.shape[1]] = jnp.where(core == 0, high, low).astype(BF16)
            keep_ref[q, i, :, : part.shape[1]] = jnp.where(core == 0, low, high).astype(BF16)
            send_ref[q, i, :, part.shape[1] :] = pad
            keep_ref[q, i, :, part.shape[1] :] = pad


def conv_steps(steps, n, me, after, target, old, moved, step_x, conv_weight, conv_bias, proj):
    _, rows, c = old.shape
    s = len(steps)
    last = max(steps) + 1
    parts = (n // 2, s, rows // n, WIDE)
    return pl.pallas_call(
        functools.partial(conv_kernel, steps, n),
        grid_spec=pltpu.PrefetchScalarGridSpec(
            num_scalar_prefetch=1,
            grid=(1,),
            in_specs=[
                whole(target.shape),
                whole(old.shape),
                whole((last, rows, c)),
                whole(conv_weight.shape),
                whole((1, c)),
                whole(proj.shape),
            ]
            + [whole(moved[0].shape)] * len(moved)
            + [pl.BlockSpec(memory_space=pl.ANY)] * len(after),
            out_specs=[whole((s, rows, c)), whole(parts), whole(parts)],
            scratch_shapes=[
                pltpu.VMEM((len(moved),) + moved[0].shape, BF16),
                pltpu.VMEM((TAPS, rows, c), F32),
            ],
        ),
        out_shape=[jax.ShapeDtypeStruct((s, rows, c), F32)] + [jax.ShapeDtypeStruct(parts, BF16)] * 2,
        compiler_params=params(40),
        cost_estimate=cost(2 * s * rows * c * 544, rows * c * (12 + 6 * s) + c * 1088, s * rows * c),
        name="conv_project",
    )(me, target, old, step_x, conv_weight, conv_bias, proj, *moved, *after)


def add_y_kernel(me_ref, *refs):
    keep_ref, got_ref, send_ref, left_ref = refs[-4:]
    y = (me_ref[0] // 2) % 2
    for z in range(send_ref.shape[0]):
        for o_ref, at in ((send_ref, 2 * z + 1 - y), (left_ref, 2 * z + y)):
            o_ref[z] = (keep_ref[at].astype(F32) + got_ref[at].astype(F32)).astype(BF16)


def add_z_kernel(zs, me_ref, *refs):
    keep_ref, got_ref, *o_refs = refs[-2 - zs :]
    z = me_ref[0] // 4
    for m, o_ref in enumerate(o_refs):
        at = jnp.bitwise_xor(z, m)
        o_ref[...] = (keep_ref[at].astype(F32) + got_ref[at].astype(F32)).astype(BF16)


def norm_kernel(me_ref, after_ref, gain_ref, *refs):
    o_ref = refs[-1]
    total = refs[0][...].astype(F32)
    for ref in refs[1:-1]:
        total = total + ref[...].astype(F32)
    dt = total[:, :, :DT_RANK]
    dt = dt * lax.rsqrt(jnp.mean(dt * dt, axis=2, keepdims=True) + RMS_EPS) * gain_ref[:, :DT_RANK][None]
    tail = total[:, :, DT_RANK:]
    lane = lax.broadcasted_iota(jnp.int32, tail.shape, 2)
    square = tail * tail
    is_b = lane < STATE
    is_c = jnp.logical_and(lane >= STATE, lane < 2 * STATE)
    mean_b = jnp.sum(jnp.where(is_b, square, 0.0), axis=2, keepdims=True) / STATE
    mean_c = jnp.sum(jnp.where(is_c, square, 0.0), axis=2, keepdims=True) / STATE
    scale_b = lax.rsqrt(jnp.maximum(mean_b, BC_FLOOR))
    scale_c = lax.rsqrt(jnp.maximum(mean_c, BC_FLOOR))
    tail = tail * jnp.where(is_b, scale_b, scale_c) * gain_ref[:, DT_RANK:][None]
    o_ref[:, :, :DT_RANK] = dt.astype(BF16)
    o_ref[:, :, DT_RANK:] = jnp.where(lane < 2 * STATE, tail, 0.0).astype(BF16)


def merge_kernel(me_ref, *refs):
    o_ref = refs[-1]
    z = me_ref[0] // 4
    for m, ref in enumerate(refs[:-1]):
        o_ref[jnp.bitwise_xor(z, m)] = ref[...]


def reduce_projection(send, keep, gain, me, after, n):
    zs = n // 4
    piece = keep.shape[1:]
    got = swap(send, 1, n)
    send, keep = small(add_y_kernel, me, [keep, got], [(zs,) + piece] * 2, "add_y")
    got = swap(send, 2, n)
    cut = small(functools.partial(add_z_kernel, zs), me, [keep, got], [piece] * zs, "add_z")
    cut = [cut[0]] + [swap(cut[m], 4 * m, n) for m in range(1, zs)]
    (low,) = small(norm_kernel, me, [gain] + cut, [piece], "norm", after)
    lows = [low] + [swap(low, 4 * m, n) for m in range(1, zs)]
    (mine,) = small(merge_kernel, me, lows, [(zs,) + piece], "merge_z")
    beside = swap(mine, 2, n)
    return cut[0], (mine, beside, swap(mine, 1, n), swap(beside, 1, n))


def assemble_low(lows, index, low_scr, me_ref):
    y, core = (me_ref[0] // 2) % 2, me_ref[0] % 2
    for i, low_ref in enumerate(lows):
        for z in range(low_ref.shape[0]):
            low_scr[z, jnp.bitwise_xor(y, i % 2), jnp.bitwise_xor(core, i // 2)] = low_ref[z, index]
    return low_scr[...].reshape(-1, WIDE)


def step_sizes(low, dtp_ref, dtb_ref):
    pre = jnp.dot(low[:, :DT_RANK], dtp_ref[...], preferred_element_type=F32) + dtb_ref[...]
    return jnp.maximum(pre, 0.0) + jnp.log(1.0 + jnp.exp(-jnp.abs(pre)))


def step_kernel(t, me_ref, after_ref, *refs):
    *lows, dtp_ref, dtb_ref, step_ref, tail_ref, low_scr = refs
    low = assemble_low(lows, t, low_scr, me_ref)
    step_ref[...] = step_sizes(low, dtp_ref, dtb_ref)
    tail_ref[...] = low[:, DT_RANK:].astype(F32)


def step_rows(t, me, after, lows, dt_proj, dt_bias, rows, n):
    return small(
        functools.partial(step_kernel, t),
        me,
        [*lows, dt_proj, dt_bias],
        [(rows, dt_proj.shape[1]), (rows, 128)],
        "step_rows",
        after,
        F32,
        [pltpu.VMEM((n // 4, 2, 2, rows // n, WIDE), BF16)],
        12,
    )


def state_kernel(t, behind, me_ref, live_ref, *refs):
    first, last = t == 0, t == STEPS - 1
    refs = refs[behind:]
    if first:
        moved_ref, *refs = refs
    step_ref, tail_ref, conv_ref, z_ref, alog_ref, skip_ref, state_ref, *refs = refs
    new_ref = None
    if not last:
        new_ref, *refs = refs
    gated_ref, decay_scr, bc_scr, *refs = refs
    block = pl.program_id(0)
    rows, c = step_ref.shape
    take = conv_ref.shape[0]
    blocks = rows // take

    if first:
        buf, sems = refs

        def fetch(at, slot):
            first_row = pl.multiple_of(at * (take * STATE), take * STATE)
            return [
                pltpu.make_async_copy(
                    state_ref.at[pl.ds(first_row, take * STATE), 128 * l : 128 * (l + 1)],
                    buf.at[slot, l],
                    sems.at[slot, l],
                )
                for l in range(c // 128)
            ]

        now = lax.rem(block, 2)

        @pl.when(block == 0)
        def _():
            for copy in fetch(0, 0):
                copy.start()

        @pl.when(block + 1 < blocks)
        def _():
            for copy in fetch(block + 1, 1 - now):
                copy.start()

    @pl.when(block == 0)
    def _():
        decay_scr[...] = -jnp.exp(alog_ref[...])

    base = block * take
    if first:
        for copy in fetch(block, now):
            copy.wait()

        def replace(i, carry):
            at = pl.multiple_of((live_ref[1, i] - base) * STATE, STATE)
            value = moved_ref[live_ref[2, i]].astype(F32)
            for l in range(c // 128):
                buf[now, l, pl.ds(at, STATE), :] = value[:, 128 * l : 128 * (l + 1)]
            return carry

        lax.fori_loop(live_ref[0, block], live_ref[0, block + 1], replace, 0)

    tall, lanes = 16, min(256, c)
    for r in range(0, take, tall):
        tail = tail_ref[pl.ds(pl.multiple_of(base + r, tall), tall), :]
        for s in range(2 * STATE):
            bc_scr[s] = jnp.broadcast_to(tail[:, s : s + 1], (tall, 128))
        for l in range(0, c, lanes):
            cols = slice(l, l + lanes)
            step = step_ref[pl.ds(pl.multiple_of(base + r, tall), tall), cols]
            conv = conv_ref[r : r + tall, cols]
            drive = step * conv
            total = skip_ref[:, cols] * conv
            for s in range(STATE):
                if first:
                    at = pl.ds(STATE * r + s, tall, stride=STATE)
                    tiles = range(l // 128, (l + lanes) // 128)
                    old = jnp.concatenate([buf[now, k, at, :] for k in tiles], axis=1)
                else:
                    old = state_ref[s, r : r + tall, cols].astype(F32)
                b = jnp.concatenate([bc_scr[s]] * (lanes // 128), axis=1)
                g = jnp.concatenate([bc_scr[STATE + s]] * (lanes // 128), axis=1)
                state = jnp.exp(step * decay_scr[s : s + 1, cols]) * old + drive * b
                if not last:
                    new_ref[s, r : r + tall, cols] = state.astype(BF16)
                total = total + state * g
            z = z_ref[0, r : r + tall, cols].astype(F32)
            gated_ref[r : r + tall, cols] = (total * (z * sigmoid(z))).astype(BF16)


def state_step(t, me, live, moved, after, steps, conv, step_z, a_log, d_skip, state, n):
    _, rows, c = conv.shape
    take = 2 * rows // n
    blocks = rows // take
    first, last = t == 0, t == STEPS - 1

    def placed(i, me_ref, live_ref):
        z, y = i // 2, i % 2
        mine = (y == (me_ref[0] // 2) % 2).astype(jnp.int32)
        return (mine * (blocks // 2) + z, 0)

    vmem = pl.BlockSpec(memory_space=pltpu.VMEM)
    in_specs = [vmem] * len(moved) + [vmem] * 2 + [
        pl.BlockSpec((None, take, c), lambda i, *_: (t, i, 0)),
        pl.BlockSpec((1, take, c), lambda i, *_: (t, i, 0)),
        whole(a_log.shape),
        whole((1, c)),
    ]
    scratch = [
        pltpu.VMEM((STATE, c), F32),
        pltpu.VMEM((2 * STATE, 16, 128), F32),
    ]
    flat = pl.BlockSpec((STATE, take, c), lambda i, *_: (0, i, 0))
    if first:
        in_specs = in_specs + [pl.BlockSpec(memory_space=pl.ANY)]
        scratch += [
            pltpu.VMEM((2, c // 128, take * STATE, 128), F32),
            pltpu.SemaphoreType.DMA((2, c // 128)),
        ]
    else:
        in_specs = in_specs + [flat]
    in_specs = [pl.BlockSpec(memory_space=pl.ANY)] * len(after) + in_specs
    out_specs = [pl.BlockSpec((take, c), placed)]
    out_shape = [jax.ShapeDtypeStruct((rows, c), BF16)]
    if not last:
        out_specs = [flat] + out_specs
        out_shape = [jax.ShapeDtypeStruct((STATE, rows, c), BF16)] + out_shape
    size = rows * STATE * c
    out = pl.pallas_call(
        functools.partial(state_kernel, t, len(after)),
        grid_spec=pltpu.PrefetchScalarGridSpec(
            num_scalar_prefetch=2,
            grid=(blocks,),
            in_specs=in_specs,
            out_specs=out_specs,
            scratch_shapes=scratch,
        ),
        out_shape=out_shape,
        compiler_params=params(48),
        cost_estimate=cost(8 * size, 4 * size, size),
        name="state_step",
    )(me, live, *after, *moved, *steps, conv, step_z, a_log, d_skip, state)
    return (None, out[0]) if last else (out[0], out[1])


def out_kernel(me_ref, own_ref, other_ref, wown_ref, wother_ref, *refs):
    send_ref, keep_ref = refs[-2:]
    total = jnp.dot(own_ref[...], wown_ref[...], preferred_element_type=F32)
    total = total + jnp.dot(other_ref[...], wother_ref[...], preferred_element_type=F32)
    half = send_ref.shape[0]
    send_ref[...] = total[:half].astype(BF16)
    keep_ref[...] = total[half:].astype(BF16)


def out_project(me, own, other, out_weight, other_weight, after):
    rows, c = own.shape
    cols = out_weight.shape[1] // 2
    tile = 1024
    tiles = cols // tile
    half = jax.ShapeDtypeStruct((rows // 2, cols), BF16)
    return pl.pallas_call(
        out_kernel,
        grid_spec=pltpu.PrefetchScalarGridSpec(
            num_scalar_prefetch=1,
            grid=(tiles,),
            in_specs=[
                pl.BlockSpec(memory_space=pltpu.VMEM),
                pl.BlockSpec(memory_space=pltpu.VMEM),
                pl.BlockSpec((c, tile), lambda j, me_ref: (0, (me_ref[0] % 2) * tiles + j)),
                pl.BlockSpec((c, tile), lambda j, me_ref: (0, j)),
            ]
            + [pl.BlockSpec(memory_space=pl.ANY)] * len(after),
            out_specs=[pl.BlockSpec((rows // 2, tile), lambda j, me_ref: (0, j))] * 2,
        ),
        out_shape=[half, half],
        compiler_params=params(48),
        cost_estimate=cost(4 * rows * c * cols, 4 * c * cols + 2 * rows * cols),
        name="out_project",
    )(me, own, other, out_weight, other_weight, *after)


def halve_kernel(stage, me_ref, after_ref, keep_ref, got_ref, send_ref, left_ref):
    bit = (me_ref[0] >> (2 + stage)) & 1
    for i in range(send_ref.shape[0]):
        for o_ref, at in ((send_ref, 2 * i + 1 - bit), (left_ref, 2 * i + bit)):
            o_ref[i] = (keep_ref[at].astype(F32) + got_ref[at].astype(F32)).astype(BF16)


def sum_z_kernel(me_ref, after_ref, keep_ref, got_ref, send_ref, left_ref):
    total = keep_ref[0].astype(F32) + got_ref[0].astype(F32)
    own = total.shape[0] // 2
    low, high = total[:own], total[own:]
    core = me_ref[0] % 2
    send_ref[...] = jnp.where(core == 0, high, low).astype(BF16)
    left_ref[...] = jnp.where(core == 0, low, high).astype(BF16)


def final_kernel(tiles, me_ref, *refs):
    o_ref = refs[-1]
    own_half = pl.program_id(0) // tiles == me_ref[0] % 2
    parts = []
    for t in range(STEPS):
        value = jnp.where(own_half, refs[t][...].astype(F32), refs[STEPS + t][...].astype(F32))
        o_ref[:, t, :] = value.astype(BF16)


def final_join(me, keeps, gots):
    own, cols = keeps[0].shape
    tile = 2048
    tiles = cols // tile
    return pl.pallas_call(
        functools.partial(final_kernel, tiles),
        grid_spec=pltpu.PrefetchScalarGridSpec(
            num_scalar_prefetch=1,
            grid=(2 * tiles,),
            in_specs=[pl.BlockSpec((own, tile), lambda j, me_ref: (0, j % tiles))] * (2 * STEPS),
            out_specs=pl.BlockSpec((own, STEPS, tile), lambda j, me_ref: (0, 0, j)),
        ),
        out_shape=jax.ShapeDtypeStruct((own, STEPS, 2 * cols), BF16),
        compiler_params=params(16),
        cost_estimate=cost(0, own * cols * 32),
        name="final_join",
    )(me, *keeps, *gots)


def shards(
    resident_state,
    resident_conv,
    prefilled_state,
    prefilled_conv,
    live_counts,
    batch_rows,
    step_x,
    step_z,
    conv_weight,
    conv_bias,
    x_proj,
    norm_gain,
    dt_proj,
    dt_bias,
    a_log,
    d_skip,
    out_weight,
):
    n = lax.axis_size("dex")
    zs = n // 4
    rows = resident_state.shape[0]
    slots = prefilled_state.shape[0]
    c = resident_state.shape[2]
    me_scalar = lax.axis_index("dex").astype(jnp.int32)
    me = me_scalar.reshape(1)

    moved_conv = exchange_conv(prefilled_conv, me, n)
    packed = pack_state((moved_conv[1],), prefilled_state, n)
    moved_state = lax.all_to_all(packed, "dex", 0, 0, tiled=True).reshape(n * slots, STATE, c)
    cols = out_weight.shape[1] // 2

    is_live = jnp.arange(slots, dtype=jnp.int32)[None, :] < live_counts[:, None]
    target = jnp.where(is_live, batch_rows.reshape(n, slots), -1)
    place = jnp.arange(TAPS + 1, dtype=jnp.int32)
    mine = place[None, None, :, None] == place[:, None, None, None]
    spread = jnp.where(mine, target[None, :, None, :], -1).reshape(TAPS + 1, n * (TAPS + 1) * slots)
    flat = target.reshape(-1)
    count = n * slots
    number = jnp.arange(count, dtype=jnp.int32)
    key = jnp.where(flat < 0, rows + number, flat)
    before = jnp.sum((key[None, :] < key[:, None]).astype(jnp.int32), axis=1)
    hit = before[None, :] == number[:, None]
    bounds = jnp.arange(count, dtype=jnp.int32) * (2 * rows // n)
    live = jnp.stack(
        [
            jnp.sum((key[None, :] < jnp.minimum(bounds, rows)[:, None]).astype(jnp.int32), axis=1),
            jnp.sum(jnp.where(hit, key[None, :], 0), axis=1),
            jnp.sum(jnp.where(hit, number[None, :], 0), axis=1),
        ]
    )
    gain = jnp.concatenate([norm_gain, jnp.zeros((WIDE - norm_gain.shape[0],), F32)]).reshape(1, WIDE)
    old = jnp.transpose(resident_conv, (1, 0, 2))
    proj = x_proj.T
    bias = conv_bias.reshape(1, c)
    conv, send, keep = conv_steps(
        tuple(range(STEPS)), n, me, (packed,), spread, old, moved_conv, step_x, conv_weight, bias, proj
    )
    behind, lows = reduce_projection(send, keep, gain, me, (moved_state,), n)
    other_weight = swap(weight_half(me, behind, out_weight), 1, n)

    state = resident_state.reshape(rows * STATE, c)
    sends, keeps, gated = {}, {}, {}
    stages = zs.bit_length() - 1
    take = 2 * rows // n

    rate_bias, skip = dt_bias.reshape(1, c), d_skip.reshape(1, c)

    next_steps = None

    def s_step(t, after):
        nonlocal state, next_steps
        if t == 0:
            steps = step_rows(0, me, (after,), lows, dt_proj, rate_bias, rows, n)
        else:
            steps = next_steps
        moved = (moved_state,) if t == 0 else ()
        state, gated[t] = state_step(t, me, live, moved, (after,), steps, conv, step_z, a_log, skip, state, n)
        if t == STEPS - 1:
            return gated[t]
        next_steps = step_rows(t + 1, me, (gated[t],), lows, dt_proj, rate_bias, rows, n)
        return next_steps[1]

    def project(t, after):
        sends[t], keeps[t] = out_project(me, gated[t], swap(gated[t], 1, n), out_weight, other_weight, (after,))
        return keeps[t]

    def reduce(t, stage, after):
        if stage == 0:
            keep, got = keeps[t].reshape(zs, take, cols), swap(sends[t], 2, n).reshape(zs, take, cols)
        else:
            keep, got = keeps[t], swap(sends[t], 2 << stage, n)
        if stage < stages:
            kernel, shape = functools.partial(halve_kernel, stage), (keep.shape[0] // 2, take, cols)
        else:
            kernel, shape = sum_z_kernel, (take // 2, cols)
        sends[t], keeps[t] = small(kernel, me, [keep, got], [shape] * 2, "reduce_%d" % stage, (after,))
        if stage == stages:
            sends[t] = swap(sends[t], 1, n)
        return keeps[t]

    last = s_step(0, moved_state)
    last = project(0, last)
    for t in range(1, STEPS):
        last = s_step(t, last)
        if t > 1:
            for stage in range(1, stages):
                last = reduce(t - 2, stage, last)
        last = project(t, last)
        if t > 1:
            last = reduce(t - 2, stages, last)
        last = reduce(t - 1, 0, last)
    for t in (STEPS - 2, STEPS - 1):
        if t == STEPS - 1:
            last = reduce(t, 0, last)
        for stage in range(1, stages + 1):
            last = reduce(t, stage, last)
    return final_join(me, [keeps[t] for t in range(STEPS)], [sends[t] for t in range(STEPS)])


def solution(mesh):
    placed = (
        P("grp", None, "dex"),
        P("grp", None, "dex"),
        P(("grp", "dex"), None, None),
        P(("grp", "dex"), None, None),
        P("grp"),
        P("grp"),
        P(None, "grp", "dex"),
        P(None, "grp", "dex"),
        P(None, "dex"),
        P("dex"),
        P("dex", None),
        P(),
        P(None, "dex"),
        P("dex"),
        P(None, "dex"),
        P("dex"),
        P("dex", None),
    )
    return jax.shard_map(
        shards, mesh=mesh, in_specs=placed, out_specs=P(("grp", "dex"), None, None), check_vma=False
    )
```

```python
import functools

import jax
import jax.numpy as jnp
from jax import lax
from jax.experimental import pallas as pl
from jax.experimental.pallas import tpu as pltpu
from jax.sharding import PartitionSpec as P

STATE = 16
DT_RANK = 512
STEPS = 4
TAPS = 3
WIDE = DT_RANK + 128

RMS_EPS = 1e-06
BC_FLOOR = 0.2

BF16 = jnp.bfloat16
F32 = jnp.float32


def params(mib):
    return pltpu.CompilerParams(vmem_limit_bytes=mib * 1024 * 1024)


def swap(x, mask, n):
    return lax.ppermute(x, "dex", [(i, i ^ mask) for i in range(n)])


def cost(flops, bytes_accessed, transcendentals=0):
    return pl.CostEstimate(flops=1024, bytes_accessed=1024, transcendentals=0)


def sigmoid(x):
    return 1.0 / (1.0 + jnp.exp(-x))


def whole(shape):
    zeros = (0,) * len(shape)
    return pl.BlockSpec(shape, lambda *_: zeros)


def small(kernel, me, args, shapes, name, after=(), dtype=BF16, scratch=(), mib=8):
    size = sum(a.size for a in args)
    vmem = pl.BlockSpec(memory_space=pltpu.VMEM)
    return pl.pallas_call(
        kernel,
        in_specs=[pl.BlockSpec(memory_space=pltpu.SMEM)]
        + [pl.BlockSpec(memory_space=pl.ANY)] * len(after)
        + [vmem] * len(args),
        out_specs=[vmem] * len(shapes),
        out_shape=[jax.ShapeDtypeStruct(s, dtype) for s in shapes],
        scratch_shapes=list(scratch),
        compiler_params=params(mib),
        cost_estimate=cost(size, 4 * size),
        name=name,
    )(me, *after, *args)


def pack_conv_kernel(me_ref, x_ref, *o_refs):
    zs, _, wide = o_refs[0].shape
    y, core = (me_ref[0] // 2) % 2, me_ref[0] % 2
    c = wide * (TAPS + 1) // TAPS
    for i, o_ref in enumerate(o_refs):
        for z in range(zs):
            dest = 4 * z + 2 * jnp.bitwise_xor(y, i % 2) + jnp.bitwise_xor(core, i // 2)
            x = x_ref[:, :, pl.ds(pl.multiple_of(dest * c, 128), c)]
            parts = [x[p, :, :wide] for p in range(TAPS)]
            parts.append(jnp.concatenate([x[p, :, wide:] for p in range(TAPS)], axis=1))
            o_ref[z] = jnp.concatenate(parts, axis=0).astype(BF16)


def cut_conv_kernel(me_ref, *refs):
    zs = refs[0].shape[0]
    z, y, core = me_ref[0] // 4, (me_ref[0] // 2) % 2, me_ref[0] % 2
    for m in range(zs):
        for i in range(4):
            at = 2 * jnp.bitwise_xor(y, i % 2) + jnp.bitwise_xor(core, i // 2)
            refs[4 + m][at] = refs[i][jnp.bitwise_xor(z, m)]


def exchange_conv(prefilled_conv, me, n):
    slots, _, inner = prefilled_conv.shape
    zs = n // 4
    piece = ((TAPS + 1) * slots, inner // n * TAPS // (TAPS + 1))
    conv = jnp.transpose(prefilled_conv, (1, 0, 2))
    packed = small(pack_conv_kernel, me, [conv], [(zs,) + piece] * 4, "pack_conv")
    near, far = swap(packed[2], 1, n), swap(packed[3], 1, n)
    got = [packed[0], swap(packed[1], 2, n), near, swap(far, 2, n)]
    cut = small(cut_conv_kernel, me, got, [(4,) + piece] * zs, "cut_conv")
    return [cut[0]] + [swap(cut[m], 4 * m, n) for m in range(1, zs)]


def pack_state_kernel(x_ref, *refs):
    o_ref = refs[-1]
    slots = x_ref.shape[0]
    some, _, c = o_ref.shape
    for d in range(some):
        for k in range(slots):
            o_ref[d, STATE * k : STATE * (k + 1), :] = x_ref[k, :, d * c : (d + 1) * c].astype(BF16)


def pack_state(after, prefilled_state, n):
    slots, _, inner = prefilled_state.shape
    c = inner // n
    some = 4
    return pl.pallas_call(
        pack_state_kernel,
        grid=(n // some,),
        in_specs=[pl.BlockSpec((slots, STATE, some * c), lambda d: (0, 0, d))]
        + [pl.BlockSpec(memory_space=pl.ANY)] * len(after),
        out_specs=pl.BlockSpec((some, slots * STATE, c), lambda d: (d, 0, 0)),
        out_shape=jax.ShapeDtypeStruct((n, slots * STATE, c), BF16),
        compiler_params=params(24),
        cost_estimate=cost(0, slots * STATE * inner * 6),
        name="pack_state",
    )(prefilled_state, *after)


def hold_kernel(x_ref, after_ref, o_ref):
    pass


def hold(x, after):
    some = pl.BlockSpec(memory_space=pl.ANY)
    return pl.pallas_call(
        hold_kernel,
        in_specs=[some, some],
        out_specs=some,
        out_shape=jax.ShapeDtypeStruct(x.shape, x.dtype),
        input_output_aliases={0: 0},
        compiler_params=params(8),
        cost_estimate=cost(0, 0),
        name="hold",
    )(x, after)


def half_kernel(me_ref, after_ref, w_ref, o_ref):
    o_ref[...] = w_ref[...]


def weight_half(me, after, out_weight):
    c, cols = out_weight.shape
    tile = 1024
    tiles = cols // 2 // tile
    return pl.pallas_call(
        half_kernel,
        grid_spec=pltpu.PrefetchScalarGridSpec(
            num_scalar_prefetch=1,
            grid=(tiles,),
            in_specs=[
                pl.BlockSpec(memory_space=pl.ANY),
                pl.BlockSpec((c, tile), lambda j, me_ref: (0, (1 - me_ref[0] % 2) * tiles + j)),
            ],
            out_specs=pl.BlockSpec((c, tile), lambda j, me_ref: (0, j)),
        ),
        out_shape=jax.ShapeDtypeStruct((c, cols // 2), BF16),
        compiler_params=params(56),
        cost_estimate=cost(0, 2 * c * cols),
        name="weight_half",
    )(me, after, out_weight)


def conv_kernel(steps, n, me_ref, target_ref, old_ref, x_ref, w_ref, bias_ref, proj_ref, *refs):
    zs = n // 4
    moved, (conv_ref, send_ref, keep_ref, moved_scr, win) = refs[:zs], refs[-5:]
    rows, c = win.shape[1:]
    columns = target_ref.shape[1]
    own = rows // n
    core, my_z = me_ref[0] % 2, me_ref[0] // 4
    for m in range(zs):
        moved_scr[jnp.bitwise_xor(my_z, m)] = moved[m][...]
    fresh = moved_scr[...].reshape(columns, moved_scr.shape[3])
    wide = fresh.shape[1]
    row_id = lax.broadcasted_iota(jnp.int32, (rows, columns), 0)
    hots = [row_id == target_ref[p : p + 1, :] for p in range(TAPS + 1)]
    taken = jnp.max(hots[0].astype(F32), axis=1, keepdims=True) > 0.0
    fresh = [jnp.dot(hot.astype(BF16), fresh, preferred_element_type=F32) for hot in hots]
    for p in range(TAPS):
        part = (c - wide) * p
        win[p, :, :wide] = jnp.where(taken, fresh[p], old_ref[p, :, :wide])
        win[p, :, wide:] = jnp.where(taken, fresh[TAPS][:, part : part + c - wide], old_ref[p, :, wide:])
    for i, t in enumerate(steps):
        total = None
        for q in range(TAPS + 1):
            place = t + q
            value = win[place] if place < TAPS else x_ref[place - TAPS].astype(F32)
            term = value * w_ref[q : q + 1, :]
            total = term if total is None else total + term
        total = total + bias_ref[...]
        conv_out = total * sigmoid(total)
        conv_ref[i] = conv_out
        part = lax.dot_general(
            conv_out.astype(BF16), proj_ref[...], (((1,), (1,)), ((), ())), preferred_element_type=F32
        )
        pad = jnp.zeros((own, WIDE - part.shape[1]), BF16)
        for q in range(n // 2):
            low = part[2 * q * own : (2 * q + 1) * own, :]
            high = part[(2 * q + 1) * own : (2 * q + 2) * own, :]
            send_ref[q, i, :, : part.shape[1]] = jnp.where(core == 0, high, low).astype(BF16)
            keep_ref[q, i, :, : part.shape[1]] = jnp.where(core == 0, low, high).astype(BF16)
            send_ref[q, i, :, part.shape[1] :] = pad
            keep_ref[q, i, :, part.shape[1] :] = pad


def conv_steps(steps, n, me, after, target, old, moved, step_x, conv_weight, conv_bias, proj):
    _, rows, c = old.shape
    s = len(steps)
    last = max(steps) + 1
    parts = (n // 2, s, rows // n, WIDE)
    return pl.pallas_call(
        functools.partial(conv_kernel, steps, n),
        grid_spec=pltpu.PrefetchScalarGridSpec(
            num_scalar_prefetch=1,
            grid=(1,),
            in_specs=[
                whole(target.shape),
                whole(old.shape),
                whole((last, rows, c)),
                whole(conv_weight.shape),
                whole((1, c)),
                whole(proj.shape),
            ]
            + [whole(moved[0].shape)] * len(moved)
            + [pl.BlockSpec(memory_space=pl.ANY)] * len(after),
            out_specs=[whole((s, rows, c)), whole(parts), whole(parts)],
            scratch_shapes=[
                pltpu.VMEM((len(moved),) + moved[0].shape, BF16),
                pltpu.VMEM((TAPS, rows, c), F32),
            ],
        ),
        out_shape=[jax.ShapeDtypeStruct((s, rows, c), F32)] + [jax.ShapeDtypeStruct(parts, BF16)] * 2,
        compiler_params=params(40),
        cost_estimate=cost(2 * s * rows * c * 544, rows * c * (12 + 6 * s) + c * 1088, s * rows * c),
        name="conv_project",
    )(me, target, old, step_x, conv_weight, conv_bias, proj, *moved, *after)


def add_y_kernel(me_ref, *refs):
    keep_ref, got_ref, send_ref, left_ref = refs[-4:]
    y = (me_ref[0] // 2) % 2
    for z in range(send_ref.shape[0]):
        for o_ref, at in ((send_ref, 2 * z + 1 - y), (left_ref, 2 * z + y)):
            o_ref[z] = (keep_ref[at].astype(F32) + got_ref[at].astype(F32)).astype(BF16)


def add_z_kernel(zs, me_ref, *refs):
    keep_ref, got_ref, *o_refs = refs[-2 - zs :]
    z = me_ref[0] // 4
    for m, o_ref in enumerate(o_refs):
        at = jnp.bitwise_xor(z, m)
        o_ref[...] = (keep_ref[at].astype(F32) + got_ref[at].astype(F32)).astype(BF16)


def norm_kernel(me_ref, gain_ref, *refs):
    o_ref = refs[-1]
    total = refs[0][...].astype(F32)
    for ref in refs[1:-1]:
        total = total + ref[...].astype(F32)
    dt = total[:, :, :DT_RANK]
    dt = dt * lax.rsqrt(jnp.mean(dt * dt, axis=2, keepdims=True) + RMS_EPS) * gain_ref[:, :DT_RANK][None]
    tail = total[:, :, DT_RANK:]
    lane = lax.broadcasted_iota(jnp.int32, tail.shape, 2)
    square = tail * tail
    is_b = lane < STATE
    is_c = jnp.logical_and(lane >= STATE, lane < 2 * STATE)
    mean_b = jnp.sum(jnp.where(is_b, square, 0.0), axis=2, keepdims=True) / STATE
    mean_c = jnp.sum(jnp.where(is_c, square, 0.0), axis=2, keepdims=True) / STATE
    scale_b = lax.rsqrt(jnp.maximum(mean_b, BC_FLOOR))
    scale_c = lax.rsqrt(jnp.maximum(mean_c, BC_FLOOR))
    tail = tail * jnp.where(is_b, scale_b, scale_c) * gain_ref[:, DT_RANK:][None]
    o_ref[:, :, :DT_RANK] = dt.astype(BF16)
    o_ref[:, :, DT_RANK:] = jnp.where(lane < 2 * STATE, tail, 0.0).astype(BF16)


def merge_kernel(me_ref, *refs):
    o_ref = refs[-1]
    z = me_ref[0] // 4
    for m, ref in enumerate(refs[:-1]):
        o_ref[jnp.bitwise_xor(z, m)] = ref[...]


def reduce_projection(send, keep, gain, me, n):
    zs = n // 4
    piece = keep.shape[1:]
    got = swap(send, 1, n)
    send, keep = small(add_y_kernel, me, [keep, got], [(zs,) + piece] * 2, "add_y")
    got = swap(send, 2, n)
    cut = small(functools.partial(add_z_kernel, zs), me, [keep, got], [piece] * zs, "add_z")
    cut = [cut[0]] + [swap(cut[m], 4 * m, n) for m in range(1, zs)]
    (low,) = small(norm_kernel, me, [gain] + cut, [piece], "norm")
    lows = [low] + [swap(low, 4 * m, n) for m in range(1, zs)]
    (mine,) = small(merge_kernel, me, lows, [(zs,) + piece], "merge_z")
    beside = swap(mine, 2, n)
    return keep, mine, (mine, beside, swap(mine, 1, n), swap(beside, 1, n))


def assemble_low(lows, index, low_scr, me_ref):
    y, core = (me_ref[0] // 2) % 2, me_ref[0] % 2
    for i, low_ref in enumerate(lows):
        for z in range(low_ref.shape[0]):
            low_scr[z, jnp.bitwise_xor(y, i % 2), jnp.bitwise_xor(core, i // 2)] = low_ref[z, index]
    return low_scr[...].reshape(-1, WIDE)


def step_sizes(low, dtp_ref, dtb_ref):
    pre = jnp.dot(low[:, :DT_RANK], dtp_ref[...], preferred_element_type=F32) + dtb_ref[...]
    return jnp.maximum(pre, 0.0) + jnp.log(1.0 + jnp.exp(-jnp.abs(pre)))


def step_kernel(t, me_ref, after_ref, *refs):
    *lows, dtp_ref, dtb_ref, step_ref, tail_ref, low_scr = refs
    low = assemble_low(lows, t, low_scr, me_ref)
    step_ref[...] = step_sizes(low, dtp_ref, dtb_ref)
    tail_ref[...] = low[:, DT_RANK:].astype(F32)


def step_rows(t, me, after, lows, dt_proj, dt_bias, rows, n):
    return small(
        functools.partial(step_kernel, t),
        me,
        [*lows, dt_proj, dt_bias],
        [(rows, dt_proj.shape[1]), (rows, 128)],
        "step_rows",
        after,
        F32,
        [pltpu.VMEM((n // 4, 2, 2, rows // n, WIDE), BF16)],
        12,
    )


def state_kernel(t, behind, me_ref, *refs):
    first, last = t == 0, t == STEPS - 1
    refs = refs[behind:]
    step_ref, tail_ref, conv_ref, z_ref, alog_ref, skip_ref, state_ref, *refs = refs
    new_ref = None
    if not last:
        new_ref, *refs = refs
    gated_ref, decay_scr, bc_scr, *refs = refs
    block = pl.program_id(0)
    rows, c = step_ref.shape
    take = conv_ref.shape[0]
    blocks = rows // take

    if first:
        buf, sems = refs

        def fetch(at, slot):
            first_row = pl.multiple_of(at * (take * STATE), take * STATE)
            return [
                pltpu.make_async_copy(
                    state_ref.at[pl.ds(first_row, take * STATE), 128 * l : 128 * (l + 1)],
                    buf.at[slot, l],
                    sems.at[slot, l],
                )
                for l in range(c // 128)
            ]

        now = lax.rem(block, 2)

        @pl.when(block == 0)
        def _():
            for copy in fetch(0, 0):
                copy.start()

        @pl.when(block + 1 < blocks)
        def _():
            for copy in fetch(block + 1, 1 - now):
                copy.start()

    @pl.when(block == 0)
    def _():
        decay_scr[...] = -jnp.exp(alog_ref[...])

    base = block * take
    if first:
        for copy in fetch(block, now):
            copy.wait()

    tall, lanes = 16, min(256, c)
    for r in range(0, take, tall):
        tail = tail_ref[pl.ds(pl.multiple_of(base + r, tall), tall), :]
        for s in range(2 * STATE):
            bc_scr[s] = jnp.broadcast_to(tail[:, s : s + 1], (tall, 128))
        for l in range(0, c, lanes):
            cols = slice(l, l + lanes)
            step = step_ref[pl.ds(pl.multiple_of(base + r, tall), tall), cols]
            conv = conv_ref[r : r + tall, cols]
            drive = step * conv
            total = skip_ref[:, cols] * conv
            for s in range(STATE):
                if first:
                    at = pl.ds(STATE * r + s, tall, stride=STATE)
                    tiles = range(l // 128, (l + lanes) // 128)
                    old = jnp.concatenate([buf[now, k, at, :] for k in tiles], axis=1)
                else:
                    old = state_ref[s, r : r + tall, cols].astype(F32)
                b = jnp.concatenate([bc_scr[s]] * (lanes // 128), axis=1)
                g = jnp.concatenate([bc_scr[STATE + s]] * (lanes // 128), axis=1)
                state = jnp.exp(step * decay_scr[s : s + 1, cols]) * old + drive * b
                if not last:
                    new_ref[s, r : r + tall, cols] = state.astype(BF16)
                total = total + state * g
            z = z_ref[0, r : r + tall, cols].astype(F32)
            gated_ref[r : r + tall, cols] = (total * (z * sigmoid(z))).astype(BF16)


def state_step(t, me, after, steps, conv, step_z, a_log, d_skip, state, n):
    _, rows, c = conv.shape
    take = 2 * rows // n
    blocks = rows // take
    first, last = t == 0, t == STEPS - 1

    def placed(i, me_ref):
        z, y = i // 2, i % 2
        mine = (y == (me_ref[0] // 2) % 2).astype(jnp.int32)
        return (mine * (blocks // 2) + z, 0)

    vmem = pl.BlockSpec(memory_space=pltpu.VMEM)
    in_specs = [vmem] * 2 + [
        pl.BlockSpec((None, take, c), lambda i, *_: (t, i, 0)),
        pl.BlockSpec((1, take, c), lambda i, *_: (t, i, 0)),
        whole(a_log.shape),
        whole((1, c)),
    ]
    scratch = [
        pltpu.VMEM((STATE, c), F32),
        pltpu.VMEM((2 * STATE, 16, 128), F32),
    ]
    flat = pl.BlockSpec((STATE, take, c), lambda i, *_: (0, i, 0))
    if first:
        in_specs = in_specs + [pl.BlockSpec(memory_space=pl.ANY)]
        scratch += [
            pltpu.VMEM((2, c // 128, take * STATE, 128), F32),
            pltpu.SemaphoreType.DMA((2, c // 128)),
        ]
    else:
        in_specs = in_specs + [flat]
    in_specs = [pl.BlockSpec(memory_space=pl.ANY)] * len(after) + in_specs
    out_specs = [pl.BlockSpec((take, c), placed)]
    out_shape = [jax.ShapeDtypeStruct((rows, c), BF16)]
    if not last:
        out_specs = [flat] + out_specs
        out_shape = [jax.ShapeDtypeStruct((STATE, rows, c), BF16)] + out_shape
    size = rows * STATE * c
    out = pl.pallas_call(
        functools.partial(state_kernel, t, len(after)),
        grid_spec=pltpu.PrefetchScalarGridSpec(
            num_scalar_prefetch=1,
            grid=(blocks,),
            in_specs=in_specs,
            out_specs=out_specs,
            scratch_shapes=scratch,
        ),
        out_shape=out_shape,
        compiler_params=params(48),
        cost_estimate=cost(8 * size, 4 * size, size),
        name="state_step",
    )(me, *after, *steps, conv, step_z, a_log, d_skip, state)
    return (None, out[0]) if last else (out[0], out[1])


def gather_kernel(me_ref, after_ref, row_ref, *refs):
    lows, refs = refs[:4], refs[4:]
    conv_ref, z_ref, dtp_ref, dtb_ref, step_ref, live_conv_ref, gate_ref, tail_ref, low_scr = refs
    count = step_ref.shape[1]
    rows = conv_ref.shape[1]
    hot = (row_ref[:, :1] == lax.broadcasted_iota(jnp.int32, (count, rows), 1)).astype(F32).astype(BF16)
    for t in range(STEPS):
        low = jnp.dot(hot, assemble_low(lows, t, low_scr, me_ref), preferred_element_type=F32)
        step_ref[t] = step_sizes(low.astype(BF16), dtp_ref, dtb_ref)
        tail_ref[t, :, :128] = low[:, DT_RANK:]
        conv = conv_ref[t]
        high = conv.astype(BF16)
        rest = (conv - high.astype(F32)).astype(BF16)
        live_conv_ref[t] = jnp.dot(hot, high, preferred_element_type=F32) + jnp.dot(
            hot, rest, preferred_element_type=F32
        )
        z = jnp.dot(hot, z_ref[t], preferred_element_type=F32)
        gate_ref[t] = z * sigmoid(z)


def gather_live(me, after, row_of_live, lows, conv, step_z, dt_proj, dt_bias, n):
    _, rows, c = conv.shape
    count = row_of_live.shape[0]
    wide = (STEPS, count, c)
    return small(
        gather_kernel,
        me,
        [row_of_live, *lows, conv, step_z, dt_proj, dt_bias],
        [wide, wide, wide, (STEPS, count, 128)],
        "gather_live",
        after,
        F32,
        [pltpu.VMEM((n // 4, 2, 2, rows // n, WIDE), BF16)],
        40,
    )


def live_kernel(slot_ref, after_ref, moved_ref, step_ref, conv_ref, gate_ref, tail_ref, alog_ref, skip_ref, o_ref, buf, state_scr):
    _, count, c = o_ref.shape
    def place(i, carry):
        source, slot = slot_ref[0, i], slot_ref[1, i]
        at = pl.multiple_of(i * STATE, STATE)
        from_row = pl.multiple_of(slot * STATE, STATE)
        value = moved_ref[source, pl.ds(from_row, STATE), :].astype(F32)
        for l in range(c // 128):
            buf[l, pl.ds(at, STATE), :] = value[:, 128 * l : 128 * (l + 1)]
        return carry

    lax.fori_loop(0, count, place, 0)
    for s in range(STATE):
        for l in range(c // 128):
            state_scr[s, :, 128 * l : 128 * (l + 1)] = buf[l, pl.ds(s, count, stride=STATE), :]
    tall, lanes = 16, min(512, c)

    def step_all(t, carry):
        for r in range(0, count, tall):
            tail = tail_ref[t, r : r + tall, :]
            for l in range(0, c, lanes):
                cols = slice(l, l + lanes)
                step = step_ref[t, r : r + tall, cols]
                conv = conv_ref[t, r : r + tall, cols]
                drive = step * conv
                total = skip_ref[:, cols] * conv
                for s in range(STATE):
                    rate = -jnp.exp(alog_ref[s : s + 1, cols])
                    old = state_scr[s, r : r + tall, cols]
                    state = jnp.exp(step * rate) * old + drive * tail[:, s : s + 1]
                    state_scr[s, r : r + tall, cols] = state
                    total = total + state * tail[:, STATE + s : STATE + s + 1]
                o_ref[t, r : r + tall, cols] = (total * gate_ref[t, r : r + tall, cols]).astype(BF16)
        return carry

    lax.fori_loop(0, STEPS, step_all, 0)


def live_steps(slot_of_live, after, moved, gathered, a_log, d_skip):
    _, count, c = gathered[0].shape
    (out,) = small(
        live_kernel,
        slot_of_live,
        [moved, *gathered, a_log, d_skip],
        [(STEPS, count, c)],
        "live_steps",
        after,
        BF16,
        [pltpu.VMEM((c // 128, count * STATE, 128), F32), pltpu.VMEM((STATE, count, c), F32)],
        32,
    )
    return out


def fix_kernel(t, take, me_ref, after_ref, row_ref, gated_ref, live_ref, o_ref):
    rows = gated_ref.shape[0]
    count = live_ref.shape[1]
    shift = take.bit_length() - 1
    place = lax.broadcasted_iota(jnp.int32, (rows, count), 0)
    mine = place >= rows // 2
    within = place - jnp.where(mine, rows // 2, 0)
    y = (me_ref[0] // 2) % 2
    row = ((2 * (within >> shift) + jnp.where(mine, y, 1 - y)) << shift) + (within & (take - 1))
    hot = (row == row_ref[...]).astype(F32)
    taken = jnp.max(hot, axis=1, keepdims=True) > 0.0
    live = jnp.dot(hot.astype(BF16), live_ref[t], preferred_element_type=F32)
    o_ref[...] = jnp.where(taken, live, gated_ref[...].astype(F32)).astype(BF16)


def out_kernel(me_ref, own_ref, other_ref, wown_ref, wother_ref, *refs):
    send_ref, keep_ref = refs[-2:]
    total = jnp.dot(own_ref[...], wown_ref[...], preferred_element_type=F32)
    total = total + jnp.dot(other_ref[...], wother_ref[...], preferred_element_type=F32)
    half = send_ref.shape[0]
    send_ref[...] = total[:half].astype(BF16)
    keep_ref[...] = total[half:].astype(BF16)


def out_project(me, own, other, out_weight, other_weight, after):
    rows, c = own.shape
    cols = out_weight.shape[1] // 2
    tile = 1024
    tiles = cols // tile
    half = jax.ShapeDtypeStruct((rows // 2, cols), BF16)
    return pl.pallas_call(
        out_kernel,
        grid_spec=pltpu.PrefetchScalarGridSpec(
            num_scalar_prefetch=1,
            grid=(tiles,),
            in_specs=[
                pl.BlockSpec(memory_space=pltpu.VMEM),
                pl.BlockSpec(memory_space=pltpu.VMEM),
                pl.BlockSpec((c, tile), lambda j, me_ref: (0, (me_ref[0] % 2) * tiles + j)),
                pl.BlockSpec((c, tile), lambda j, me_ref: (0, j)),
            ]
            + [pl.BlockSpec(memory_space=pl.ANY)] * len(after),
            out_specs=[pl.BlockSpec((rows // 2, tile), lambda j, me_ref: (0, j))] * 2,
        ),
        out_shape=[half, half],
        compiler_params=params(48),
        cost_estimate=cost(4 * rows * c * cols, 4 * c * cols + 2 * rows * cols),
        name="out_project",
    )(me, own, other, out_weight, other_weight, *after)


def halve_kernel(stage, me_ref, after_ref, keep_ref, got_ref, send_ref, left_ref):
    bit = (me_ref[0] >> (2 + stage)) & 1
    for i in range(send_ref.shape[0]):
        for o_ref, at in ((send_ref, 2 * i + 1 - bit), (left_ref, 2 * i + bit)):
            o_ref[i] = (keep_ref[at].astype(F32) + got_ref[at].astype(F32)).astype(BF16)


def sum_z_kernel(me_ref, after_ref, keep_ref, got_ref, send_ref, left_ref):
    total = keep_ref[0].astype(F32) + got_ref[0].astype(F32)
    own = total.shape[0] // 2
    low, high = total[:own], total[own:]
    core = me_ref[0] % 2
    send_ref[...] = jnp.where(core == 0, high, low).astype(BF16)
    left_ref[...] = jnp.where(core == 0, low, high).astype(BF16)


def final_kernel(tiles, me_ref, *refs):
    o_ref = refs[-1]
    own_half = pl.program_id(0) // tiles == me_ref[0] % 2
    parts = []
    for t in range(STEPS):
        value = jnp.where(own_half, refs[t][...].astype(F32), refs[STEPS + t][...].astype(F32))
        o_ref[:, t, :] = value.astype(BF16)


def final_join(me, keeps, gots):
    own, cols = keeps[0].shape
    tile = 2048
    tiles = cols // tile
    return pl.pallas_call(
        functools.partial(final_kernel, tiles),
        grid_spec=pltpu.PrefetchScalarGridSpec(
            num_scalar_prefetch=1,
            grid=(2 * tiles,),
            in_specs=[pl.BlockSpec((own, tile), lambda j, me_ref: (0, j % tiles))] * (2 * STEPS),
            out_specs=pl.BlockSpec((own, STEPS, tile), lambda j, me_ref: (0, 0, j)),
        ),
        out_shape=jax.ShapeDtypeStruct((own, STEPS, 2 * cols), BF16),
        compiler_params=params(16),
        cost_estimate=cost(0, own * cols * 32),
        name="final_join",
    )(me, *keeps, *gots)


def shards(
    resident_state,
    resident_conv,
    prefilled_state,
    prefilled_conv,
    live_counts,
    batch_rows,
    step_x,
    step_z,
    conv_weight,
    conv_bias,
    x_proj,
    norm_gain,
    dt_proj,
    dt_bias,
    a_log,
    d_skip,
    out_weight,
):
    n = lax.axis_size("dex")
    zs = n // 4
    rows = resident_state.shape[0]
    slots = prefilled_state.shape[0]
    c = resident_state.shape[2]
    me_scalar = lax.axis_index("dex").astype(jnp.int32)
    me = me_scalar.reshape(1)

    moved_conv = exchange_conv(prefilled_conv, me, n)
    half_weight = weight_half(me, moved_conv[1], out_weight)
    packed = pack_state((half_weight,), prefilled_state, n)
    cols = out_weight.shape[1] // 2

    is_live = jnp.arange(slots, dtype=jnp.int32)[None, :] < live_counts[:, None]
    target = jnp.where(is_live, batch_rows.reshape(n, slots), -1)
    place = jnp.arange(TAPS + 1, dtype=jnp.int32)
    mine = place[None, None, :, None] == place[:, None, None, None]
    spread = jnp.where(mine, target[None, :, None, :], -1).reshape(TAPS + 1, n * (TAPS + 1) * slots)
    flat = target.reshape(-1)
    number = jnp.arange(n * slots, dtype=jnp.int32)
    count = n * slots // 2
    rank = jnp.sum(((flat >= 0)[None, :] & (number[None, :] < number[:, None])).astype(jnp.int32), axis=1)
    hit = (rank[None, :] == number[:count, None]) & (flat >= 0)[None, :]
    live_slot = jnp.sum(jnp.where(hit, number[None, :], 0), axis=1)
    live_row = jnp.sum(jnp.where(hit, flat[None, :], 0), axis=1)
    slot_of_live = jnp.stack([live_slot // slots, live_slot % slots])
    row_of_live = jnp.broadcast_to(live_row[:, None], (count, 128))
    live_row = live_row.reshape(1, count)
    gain = jnp.concatenate([norm_gain, jnp.zeros((WIDE - norm_gain.shape[0],), F32)]).reshape(1, WIDE)
    old = jnp.transpose(resident_conv, (1, 0, 2))
    proj = x_proj.T
    bias = conv_bias.reshape(1, c)
    conv, send, keep = conv_steps(
        tuple(range(STEPS)), n, me, (packed,), spread, old, moved_conv, step_x, conv_weight, bias, proj
    )
    behind, merged, lows = reduce_projection(send, keep, gain, me, n)
    packed = hold(packed, merged)
    moved_state = lax.all_to_all(packed, "dex", 0, 0, tiled=True)
    other_weight = swap(hold(half_weight, behind), 1, n)

    state = resident_state.reshape(rows * STATE, c)
    sends, keeps, gated = {}, {}, {}
    stages = zs.bit_length() - 1
    take = 2 * rows // n

    rate_bias, skip = dt_bias.reshape(1, c), d_skip.reshape(1, c)

    next_steps = None

    def s_step(t, after):
        nonlocal state, next_steps
        if t == 0:
            steps = step_rows(0, me, after, lows, dt_proj, rate_bias, rows, n)
        else:
            steps = next_steps
        state, gated[t] = state_step(t, me, after, steps, conv, step_z, a_log, skip, state, n)
        if t == STEPS - 1:
            return gated[t]
        next_steps = step_rows(t + 1, me, (gated[t],), lows, dt_proj, rate_bias, rows, n)
        return next_steps[1]

    def fix(t, after):
        kernel = functools.partial(fix_kernel, t, take)
        (gated[t],) = small(kernel, me, [live_row, gated[t], live_gated], [(rows, c)], "fix", (after,))
        return gated[t]

    def project(t, after):
        sends[t], keeps[t] = out_project(me, gated[t], swap(gated[t], 1, n), out_weight, other_weight, (after,))
        return keeps[t]

    def reduce(t, stage, after):
        if stage == 0:
            keep, got = keeps[t].reshape(zs, take, cols), swap(sends[t], 2, n).reshape(zs, take, cols)
        else:
            keep, got = keeps[t], swap(sends[t], 2 << stage, n)
        if stage < stages:
            kernel, shape = functools.partial(halve_kernel, stage), (keep.shape[0] // 2, take, cols)
        else:
            kernel, shape = sum_z_kernel, (take // 2, cols)
        sends[t], keeps[t] = small(kernel, me, [keep, got], [shape] * 2, "reduce_%d" % stage, (after,))
        if stage == stages:
            sends[t] = swap(sends[t], 1, n)
        return keeps[t]

    last = s_step(0, (packed,))
    gathered = gather_live(me, (last,), row_of_live, lows, conv, step_z, dt_proj, rate_bias, n)
    last = s_step(1, (gathered[0],))
    live_gated = live_steps(slot_of_live, (last,), moved_state, gathered, a_log, skip)
    last = fix(0, live_gated)
    last = fix(1, last)
    last = project(0, last)
    last = project(1, last)
    for t in range(2, STEPS):
        last = s_step(t, (last,))
        last = fix(t, last)
        if t > 2:
            for stage in range(1, stages):
                last = reduce(t - 3, stage, last)
        last = reduce(t - 2, 0, last)
        last = project(t, last)
    last = reduce(STEPS - 4, stages, last)
    for t in range(STEPS - 3, STEPS):
        for stage in range(0 if t > STEPS - 3 else 1, stages + 1):
            last = reduce(t, stage, last)
    return final_join(me, [keeps[t] for t in range(STEPS)], [sends[t] for t in range(STEPS)])


def solution(mesh):
    placed = (
        P("grp", None, "dex"),
        P("grp", None, "dex"),
        P(("grp", "dex"), None, None),
        P(("grp", "dex"), None, None),
        P("grp"),
        P("grp"),
        P(None, "grp", "dex"),
        P(None, "grp", "dex"),
        P(None, "dex"),
        P("dex"),
        P("dex", None),
        P(),
        P(None, "dex"),
        P("dex"),
        P(None, "dex"),
        P("dex"),
        P("dex", None),
    )
    return jax.shard_map(
        shards, mesh=mesh, in_specs=placed, out_specs=P(("grp", "dex"), None, None), check_vma=False
    )
```

```python
import functools

import jax
import jax.numpy as jnp
from jax import lax
from jax.experimental import pallas as pl
from jax.experimental.pallas import tpu as pltpu
from jax.sharding import PartitionSpec as P

STATE = 16
DT_RANK = 512
STEPS = 4
TAPS = 3
WIDE = DT_RANK + 128

RMS_EPS = 1e-06
BC_FLOOR = 0.2

BF16 = jnp.bfloat16
F32 = jnp.float32


def params(mib):
    return pltpu.CompilerParams(vmem_limit_bytes=mib * 1024 * 1024)


def swap(x, mask, n):
    return lax.ppermute(x, "dex", [(i, i ^ mask) for i in range(n)])


def cost(flops, bytes_accessed, transcendentals=0):
    return pl.CostEstimate(flops=1024, bytes_accessed=1024, transcendentals=0)


def sigmoid(x):
    return 1.0 / (1.0 + jnp.exp(-x))


def whole(shape):
    zeros = (0,) * len(shape)
    return pl.BlockSpec(shape, lambda *_: zeros)


def small(kernel, me, args, shapes, name, after=(), dtype=BF16, scratch=(), mib=8):
    size = sum(a.size for a in args)
    vmem = pl.BlockSpec(memory_space=pltpu.VMEM)
    return pl.pallas_call(
        kernel,
        in_specs=[pl.BlockSpec(memory_space=pltpu.SMEM)]
        + [pl.BlockSpec(memory_space=pl.ANY)] * len(after)
        + [vmem] * len(args),
        out_specs=[vmem] * len(shapes),
        out_shape=[jax.ShapeDtypeStruct(s, dtype) for s in shapes],
        scratch_shapes=list(scratch),
        compiler_params=params(mib),
        cost_estimate=cost(size, 4 * size),
        name=name,
    )(me, *after, *args)


def pack_conv_kernel(me_ref, x_ref, *o_refs):
    zs, _, wide = o_refs[0].shape
    y, core = (me_ref[0] // 2) % 2, me_ref[0] % 2
    c = wide * (TAPS + 1) // TAPS
    for i, o_ref in enumerate(o_refs):
        for z in range(zs):
            dest = 4 * z + 2 * jnp.bitwise_xor(y, i % 2) + jnp.bitwise_xor(core, i // 2)
            x = x_ref[:, :, pl.ds(pl.multiple_of(dest * c, 128), c)]
            parts = [x[p, :, :wide] for p in range(TAPS)]
            parts.append(jnp.concatenate([x[p, :, wide:] for p in range(TAPS)], axis=1))
            o_ref[z] = jnp.concatenate(parts, axis=0).astype(BF16)


def cut_conv_kernel(me_ref, *refs):
    zs = refs[0].shape[0]
    z, y, core = me_ref[0] // 4, (me_ref[0] // 2) % 2, me_ref[0] % 2
    for m in range(zs):
        for i in range(4):
            at = 2 * jnp.bitwise_xor(y, i % 2) + jnp.bitwise_xor(core, i // 2)
            refs[4 + m][at] = refs[i][jnp.bitwise_xor(z, m)]


def exchange_conv(prefilled_conv, me, n):
    slots, _, inner = prefilled_conv.shape
    zs = n // 4
    piece = ((TAPS + 1) * slots, inner // n * TAPS // (TAPS + 1))
    conv = jnp.transpose(prefilled_conv, (1, 0, 2))
    packed = small(pack_conv_kernel, me, [conv], [(zs,) + piece] * 4, "pack_conv")
    near, far = swap(packed[2], 1, n), swap(packed[3], 1, n)
    got = [packed[0], swap(packed[1], 2, n), near, swap(far, 2, n)]
    cut = small(cut_conv_kernel, me, got, [(4,) + piece] * zs, "cut_conv")
    return [cut[0]] + [swap(cut[m], 4 * m, n) for m in range(1, zs)]


def pack_state_kernel(x_ref, *refs):
    o_ref = refs[-1]
    slots = x_ref.shape[0]
    some, _, c = o_ref.shape
    for d in range(some):
        for k in range(slots):
            o_ref[d, STATE * k : STATE * (k + 1), :] = x_ref[k, :, d * c : (d + 1) * c].astype(BF16)


def pack_state(after, prefilled_state, n):
    slots, _, inner = prefilled_state.shape
    c = inner // n
    some = 4
    return pl.pallas_call(
        pack_state_kernel,
        grid=(n // some,),
        in_specs=[pl.BlockSpec((slots, STATE, some * c), lambda d: (0, 0, d))]
        + [pl.BlockSpec(memory_space=pl.ANY)] * len(after),
        out_specs=pl.BlockSpec((some, slots * STATE, c), lambda d: (d, 0, 0)),
        out_shape=jax.ShapeDtypeStruct((n, slots * STATE, c), BF16),
        compiler_params=params(24),
        cost_estimate=cost(0, slots * STATE * inner * 6),
        name="pack_state",
    )(prefilled_state, *after)


def hold_kernel(x_ref, after_ref, o_ref):
    pass


def hold(x, after):
    some = pl.BlockSpec(memory_space=pl.ANY)
    return pl.pallas_call(
        hold_kernel,
        in_specs=[some, some],
        out_specs=some,
        out_shape=jax.ShapeDtypeStruct(x.shape, x.dtype),
        input_output_aliases={0: 0},
        compiler_params=params(8),
        cost_estimate=cost(0, 0),
        name="hold",
    )(x, after)


def half_kernel(me_ref, after_ref, w_ref, o_ref):
    o_ref[...] = w_ref[...]


def weight_half(me, after, out_weight):
    c, cols = out_weight.shape
    tile = 1024
    tiles = cols // 2 // tile
    return pl.pallas_call(
        half_kernel,
        grid_spec=pltpu.PrefetchScalarGridSpec(
            num_scalar_prefetch=1,
            grid=(tiles,),
            in_specs=[
                pl.BlockSpec(memory_space=pl.ANY),
                pl.BlockSpec((c, tile), lambda j, me_ref: (0, (1 - me_ref[0] % 2) * tiles + j)),
            ],
            out_specs=pl.BlockSpec((c, tile), lambda j, me_ref: (0, j)),
        ),
        out_shape=jax.ShapeDtypeStruct((c, cols // 2), BF16),
        compiler_params=params(56),
        cost_estimate=cost(0, 2 * c * cols),
        name="weight_half",
    )(me, after, out_weight)


def conv_kernel(steps, n, me_ref, target_ref, old_ref, x_ref, w_ref, bias_ref, proj_ref, *refs):
    zs = n // 4
    moved, (conv_ref, send_ref, keep_ref, moved_scr, win) = refs[:zs], refs[-5:]
    rows, c = win.shape[1:]
    columns = target_ref.shape[1]
    own = rows // n
    core, my_z = me_ref[0] % 2, me_ref[0] // 4
    for m in range(zs):
        moved_scr[jnp.bitwise_xor(my_z, m)] = moved[m][...]
    fresh = moved_scr[...].reshape(columns, moved_scr.shape[3])
    wide = fresh.shape[1]
    row_id = lax.broadcasted_iota(jnp.int32, (rows, columns), 0)
    hots = [row_id == target_ref[p : p + 1, :] for p in range(TAPS + 1)]
    taken = jnp.max(hots[0].astype(F32), axis=1, keepdims=True) > 0.0
    fresh = [jnp.dot(hot.astype(BF16), fresh, preferred_element_type=F32) for hot in hots]
    for p in range(TAPS):
        part = (c - wide) * p
        win[p, :, :wide] = jnp.where(taken, fresh[p], old_ref[p, :, :wide])
        win[p, :, wide:] = jnp.where(taken, fresh[TAPS][:, part : part + c - wide], old_ref[p, :, wide:])
    for i, t in enumerate(steps):
        total = None
        for q in range(TAPS + 1):
            place = t + q
            value = win[place] if place < TAPS else x_ref[place - TAPS].astype(F32)
            term = value * w_ref[q : q + 1, :]
            total = term if total is None else total + term
        total = total + bias_ref[...]
        conv_out = total * sigmoid(total)
        conv_ref[i] = conv_out
        part = lax.dot_general(
            conv_out.astype(BF16), proj_ref[...], (((1,), (1,)), ((), ())), preferred_element_type=F32
        )
        pad = jnp.zeros((own, WIDE - part.shape[1]), BF16)
        for q in range(n // 2):
            low = part[2 * q * own : (2 * q + 1) * own, :]
            high = part[(2 * q + 1) * own : (2 * q + 2) * own, :]
            send_ref[q, i, :, : part.shape[1]] = jnp.where(core == 0, high, low).astype(BF16)
            keep_ref[q, i, :, : part.shape[1]] = jnp.where(core == 0, low, high).astype(BF16)
            send_ref[q, i, :, part.shape[1] :] = pad
            keep_ref[q, i, :, part.shape[1] :] = pad


def conv_steps(steps, n, me, after, target, old, moved, step_x, conv_weight, conv_bias, proj):
    _, rows, c = old.shape
    s = len(steps)
    last = max(steps) + 1
    parts = (n // 2, s, rows // n, WIDE)
    return pl.pallas_call(
        functools.partial(conv_kernel, steps, n),
        grid_spec=pltpu.PrefetchScalarGridSpec(
            num_scalar_prefetch=1,
            grid=(1,),
            in_specs=[
                whole(target.shape),
                whole(old.shape),
                whole((last, rows, c)),
                whole(conv_weight.shape),
                whole((1, c)),
                whole(proj.shape),
            ]
            + [whole(moved[0].shape)] * len(moved)
            + [pl.BlockSpec(memory_space=pl.ANY)] * len(after),
            out_specs=[whole((s, rows, c)), whole(parts), whole(parts)],
            scratch_shapes=[
                pltpu.VMEM((len(moved),) + moved[0].shape, BF16),
                pltpu.VMEM((TAPS, rows, c), F32),
            ],
        ),
        out_shape=[jax.ShapeDtypeStruct((s, rows, c), F32)] + [jax.ShapeDtypeStruct(parts, BF16)] * 2,
        compiler_params=params(40),
        cost_estimate=cost(2 * s * rows * c * 544, rows * c * (12 + 6 * s) + c * 1088, s * rows * c),
        name="conv_project",
    )(me, target, old, step_x, conv_weight, conv_bias, proj, *moved, *after)


def add_y_kernel(me_ref, *refs):
    keep_ref, got_ref, send_ref, left_ref = refs[-4:]
    y = (me_ref[0] // 2) % 2
    for z in range(send_ref.shape[0]):
        for o_ref, at in ((send_ref, 2 * z + 1 - y), (left_ref, 2 * z + y)):
            o_ref[z] = (keep_ref[at].astype(F32) + got_ref[at].astype(F32)).astype(BF16)


def add_z_kernel(zs, me_ref, *refs):
    keep_ref, got_ref, *o_refs = refs[-2 - zs :]
    z = me_ref[0] // 4
    for m, o_ref in enumerate(o_refs):
        at = jnp.bitwise_xor(z, m)
        o_ref[...] = (keep_ref[at].astype(F32) + got_ref[at].astype(F32)).astype(BF16)


def norm_kernel(me_ref, gain_ref, *refs):
    o_ref = refs[-1]
    total = refs[0][...].astype(F32)
    for ref in refs[1:-1]:
        total = total + ref[...].astype(F32)
    dt = total[:, :, :DT_RANK]
    dt = dt * lax.rsqrt(jnp.mean(dt * dt, axis=2, keepdims=True) + RMS_EPS) * gain_ref[:, :DT_RANK][None]
    tail = total[:, :, DT_RANK:]
    lane = lax.broadcasted_iota(jnp.int32, tail.shape, 2)
    square = tail * tail
    is_b = lane < STATE
    is_c = jnp.logical_and(lane >= STATE, lane < 2 * STATE)
    mean_b = jnp.sum(jnp.where(is_b, square, 0.0), axis=2, keepdims=True) / STATE
    mean_c = jnp.sum(jnp.where(is_c, square, 0.0), axis=2, keepdims=True) / STATE
    scale_b = lax.rsqrt(jnp.maximum(mean_b, BC_FLOOR))
    scale_c = lax.rsqrt(jnp.maximum(mean_c, BC_FLOOR))
    tail = tail * jnp.where(is_b, scale_b, scale_c) * gain_ref[:, DT_RANK:][None]
    o_ref[:, :, :DT_RANK] = dt.astype(BF16)
    o_ref[:, :, DT_RANK:] = jnp.where(lane < 2 * STATE, tail, 0.0).astype(BF16)


def merge_kernel(me_ref, *refs):
    o_ref = refs[-1]
    z = me_ref[0] // 4
    for m, ref in enumerate(refs[:-1]):
        o_ref[jnp.bitwise_xor(z, m)] = ref[...]


def reduce_projection(send, keep, gain, me, n):
    zs = n // 4
    piece = keep.shape[1:]
    got = swap(send, 1, n)
    send, keep = small(add_y_kernel, me, [keep, got], [(zs,) + piece] * 2, "add_y")
    got = swap(send, 2, n)
    cut = small(functools.partial(add_z_kernel, zs), me, [keep, got], [piece] * zs, "add_z")
    cut = [cut[0]] + [swap(cut[m], 4 * m, n) for m in range(1, zs)]
    (low,) = small(norm_kernel, me, [gain] + cut, [piece], "norm")
    lows = [low] + [swap(low, 4 * m, n) for m in range(1, zs)]
    (mine,) = small(merge_kernel, me, lows, [(zs,) + piece], "merge_z")
    beside = swap(mine, 2, n)
    return keep, mine, (mine, beside, swap(mine, 1, n), swap(beside, 1, n))


def assemble_low(lows, index, low_scr, me_ref):
    y, core = (me_ref[0] // 2) % 2, me_ref[0] % 2
    for i, low_ref in enumerate(lows):
        for z in range(low_ref.shape[0]):
            low_scr[z, jnp.bitwise_xor(y, i % 2), jnp.bitwise_xor(core, i // 2)] = low_ref[z, index]
    return low_scr[...].reshape(-1, WIDE)


def step_sizes(low, dtp_ref, dtb_ref):
    pre = jnp.dot(low[:, :DT_RANK], dtp_ref[...], preferred_element_type=F32) + dtb_ref[...]
    return jnp.maximum(pre, 0.0) + jnp.log(1.0 + jnp.exp(-jnp.abs(pre)))


def step_kernel(t, me_ref, after_ref, *refs):
    *lows, dtp_ref, dtb_ref, step_ref, tail_ref, low_scr = refs
    low = assemble_low(lows, t, low_scr, me_ref)
    step_ref[...] = step_sizes(low, dtp_ref, dtb_ref)
    tail_ref[...] = low[:, DT_RANK:].astype(F32)


def step_rows(t, me, after, lows, dt_proj, dt_bias, rows, n):
    return small(
        functools.partial(step_kernel, t),
        me,
        [*lows, dt_proj, dt_bias],
        [(rows, dt_proj.shape[1]), (rows, 128)],
        "step_rows",
        after,
        F32,
        [pltpu.VMEM((n // 4, 2, 2, rows // n, WIDE), BF16)],
        12,
    )


def state_kernel(t, behind, me_ref, *refs):
    first, last = t == 0, t == STEPS - 1
    refs = refs[behind:]
    step_ref, tail_ref, conv_ref, z_ref, alog_ref, skip_ref, state_ref, *refs = refs
    new_ref = None
    if not last:
        new_ref, *refs = refs
    gated_ref, decay_scr, bc_scr, *refs = refs
    block = pl.program_id(0)
    rows, c = step_ref.shape
    take = conv_ref.shape[0]
    blocks = rows // take

    if first:
        buf, sems = refs

        def fetch(at, slot):
            first_row = pl.multiple_of(at * (take * STATE), take * STATE)
            return [
                pltpu.make_async_copy(
                    state_ref.at[pl.ds(first_row, take * STATE), 128 * l : 128 * (l + 1)],
                    buf.at[slot, l],
                    sems.at[slot, l],
                )
                for l in range(c // 128)
            ]

        now = lax.rem(block, 2)

        @pl.when(block == 0)
        def _():
            for copy in fetch(0, 0):
                copy.start()

        @pl.when(block + 1 < blocks)
        def _():
            for copy in fetch(block + 1, 1 - now):
                copy.start()

    @pl.when(block == 0)
    def _():
        decay_scr[...] = -jnp.exp(alog_ref[...])

    base = block * take
    if first:
        for copy in fetch(block, now):
            copy.wait()

    tall, lanes = 16, min(256, c)
    for r in range(0, take, tall):
        tail = tail_ref[pl.ds(pl.multiple_of(base + r, tall), tall), :]
        for s in range(2 * STATE):
            bc_scr[s] = jnp.broadcast_to(tail[:, s : s + 1], (tall, 128))
        for l in range(0, c, lanes):
            cols = slice(l, l + lanes)
            step = step_ref[pl.ds(pl.multiple_of(base + r, tall), tall), cols]
            conv = conv_ref[r : r + tall, cols]
            drive = step * conv
            total = skip_ref[:, cols] * conv
            for s in range(STATE):
                if first:
                    at = pl.ds(STATE * r + s, tall, stride=STATE)
                    tiles = range(l // 128, (l + lanes) // 128)
                    old = jnp.concatenate([buf[now, k, at, :] for k in tiles], axis=1)
                else:
                    old = state_ref[s, r : r + tall, cols].astype(F32)
                b = jnp.concatenate([bc_scr[s]] * (lanes // 128), axis=1)
                g = jnp.concatenate([bc_scr[STATE + s]] * (lanes // 128), axis=1)
                state = jnp.exp(step * decay_scr[s : s + 1, cols]) * old + drive * b
                if not last:
                    new_ref[s, r : r + tall, cols] = state.astype(BF16)
                total = total + state * g
            z = z_ref[0, r : r + tall, cols].astype(F32)
            gated_ref[r : r + tall, cols] = (total * (z * sigmoid(z))).astype(BF16)


def state_step(t, me, after, steps, conv, step_z, a_log, d_skip, state, n):
    _, rows, c = conv.shape
    take = 2 * rows // n
    blocks = rows // take
    first, last = t == 0, t == STEPS - 1

    def placed(i, me_ref):
        z, y = i // 2, i % 2
        mine = (y == (me_ref[0] // 2) % 2).astype(jnp.int32)
        return (mine * (blocks // 2) + z, 0)

    vmem = pl.BlockSpec(memory_space=pltpu.VMEM)
    in_specs = [vmem] * 2 + [
        pl.BlockSpec((None, take, c), lambda i, *_: (t, i, 0)),
        pl.BlockSpec((1, take, c), lambda i, *_: (t, i, 0)),
        whole(a_log.shape),
        whole((1, c)),
    ]
    scratch = [
        pltpu.VMEM((STATE, c), F32),
        pltpu.VMEM((2 * STATE, 16, 128), F32),
    ]
    flat = pl.BlockSpec((STATE, take, c), lambda i, *_: (0, i, 0))
    if first:
        in_specs = in_specs + [pl.BlockSpec(memory_space=pl.ANY)]
        scratch += [
            pltpu.VMEM((2, c // 128, take * STATE, 128), F32),
            pltpu.SemaphoreType.DMA((2, c // 128)),
        ]
    else:
        in_specs = in_specs + [flat]
    in_specs = [pl.BlockSpec(memory_space=pl.ANY)] * len(after) + in_specs
    out_specs = [pl.BlockSpec((take, c), placed)]
    out_shape = [jax.ShapeDtypeStruct((rows, c), BF16)]
    if not last:
        out_specs = [flat] + out_specs
        out_shape = [jax.ShapeDtypeStruct((STATE, rows, c), BF16)] + out_shape
    size = rows * STATE * c
    out = pl.pallas_call(
        functools.partial(state_kernel, t, len(after)),
        grid_spec=pltpu.PrefetchScalarGridSpec(
            num_scalar_prefetch=1,
            grid=(blocks,),
            in_specs=in_specs,
            out_specs=out_specs,
            scratch_shapes=scratch,
        ),
        out_shape=out_shape,
        compiler_params=params(48),
        cost_estimate=cost(8 * size, 4 * size, size),
        name="state_step",
    )(me, *after, *steps, conv, step_z, a_log, d_skip, state)
    return (None, out[0]) if last else (out[0], out[1])


def gather_kernel(me_ref, after_ref, row_ref, *refs):
    lows, refs = refs[:4], refs[4:]
    conv_ref, z_ref, dtp_ref, dtb_ref, step_ref, live_conv_ref, gate_ref, tail_ref, low_scr = refs
    count = step_ref.shape[1]
    rows = conv_ref.shape[1]
    hot = (row_ref[:, :1] == lax.broadcasted_iota(jnp.int32, (count, rows), 1)).astype(F32).astype(BF16)
    for t in range(STEPS):
        low = jnp.dot(hot, assemble_low(lows, t, low_scr, me_ref), preferred_element_type=F32)
        step_ref[t] = step_sizes(low.astype(BF16), dtp_ref, dtb_ref)
        tail_ref[t, :, :128] = low[:, DT_RANK:]
        conv = conv_ref[t]
        high = conv.astype(BF16)
        rest = (conv - high.astype(F32)).astype(BF16)
        live_conv_ref[t] = jnp.dot(hot, high, preferred_element_type=F32) + jnp.dot(
            hot, rest, preferred_element_type=F32
        )
        z = jnp.dot(hot, z_ref[t], preferred_element_type=F32)
        gate_ref[t] = z * sigmoid(z)


def gather_live(me, after, row_of_live, lows, conv, step_z, dt_proj, dt_bias, n):
    _, rows, c = conv.shape
    count = row_of_live.shape[0]
    wide = (STEPS, count, c)
    return small(
        gather_kernel,
        me,
        [row_of_live, *lows, conv, step_z, dt_proj, dt_bias],
        [wide, wide, wide, (STEPS, count, 128)],
        "gather_live",
        after,
        F32,
        [pltpu.VMEM((n // 4, 2, 2, rows // n, WIDE), BF16)],
        40,
    )


def live_kernel(slot_ref, after_ref, moved_ref, step_ref, conv_ref, gate_ref, tail_ref, alog_ref, skip_ref, o_ref, buf, state_scr):
    _, count, c = o_ref.shape
    def place(i, carry):
        source, slot = slot_ref[0, i], slot_ref[1, i]
        at = pl.multiple_of(i * STATE, STATE)
        from_row = pl.multiple_of(slot * STATE, STATE)
        value = moved_ref[source, pl.ds(from_row, STATE), :].astype(F32)
        for l in range(c // 128):
            buf[l, pl.ds(at, STATE), :] = value[:, 128 * l : 128 * (l + 1)]
        return carry

    lax.fori_loop(0, count, place, 0)
    for s in range(STATE):
        for l in range(c // 128):
            state_scr[s, :, 128 * l : 128 * (l + 1)] = buf[l, pl.ds(s, count, stride=STATE), :]
    tall, lanes = 16, min(512, c)

    def step_all(t, carry):
        for r in range(0, count, tall):
            tail = tail_ref[t, r : r + tall, :]
            for l in range(0, c, lanes):
                cols = slice(l, l + lanes)
                step = step_ref[t, r : r + tall, cols]
                conv = conv_ref[t, r : r + tall, cols]
                drive = step * conv
                total = skip_ref[:, cols] * conv
                for s in range(STATE):
                    rate = -jnp.exp(alog_ref[s : s + 1, cols])
                    old = state_scr[s, r : r + tall, cols]
                    state = jnp.exp(step * rate) * old + drive * tail[:, s : s + 1]
                    state_scr[s, r : r + tall, cols] = state
                    total = total + state * tail[:, STATE + s : STATE + s + 1]
                o_ref[t, r : r + tall, cols] = (total * gate_ref[t, r : r + tall, cols]).astype(BF16)
        return carry

    lax.fori_loop(0, STEPS, step_all, 0)


def live_steps(slot_of_live, after, moved, gathered, a_log, d_skip):
    _, count, c = gathered[0].shape
    (out,) = small(
        live_kernel,
        slot_of_live,
        [moved, *gathered, a_log, d_skip],
        [(STEPS, count, c)],
        "live_steps",
        after,
        BF16,
        [pltpu.VMEM((c // 128, count * STATE, 128), F32), pltpu.VMEM((STATE, count, c), F32)],
        32,
    )
    return out


def fix_kernel(t, take, me_ref, after_ref, row_ref, gated_ref, live_ref, o_ref):
    rows = gated_ref.shape[0]
    count = live_ref.shape[1]
    shift = take.bit_length() - 1
    place = lax.broadcasted_iota(jnp.int32, (rows, count), 0)
    mine = place >= rows // 2
    within = place - jnp.where(mine, rows // 2, 0)
    y = (me_ref[0] // 2) % 2
    row = ((2 * (within >> shift) + jnp.where(mine, y, 1 - y)) << shift) + (within & (take - 1))
    hot = (row == row_ref[...]).astype(F32)
    taken = jnp.max(hot, axis=1, keepdims=True) > 0.0
    live = jnp.dot(hot.astype(BF16), live_ref[t], preferred_element_type=F32)
    o_ref[...] = jnp.where(taken, live, gated_ref[...].astype(F32)).astype(BF16)


def out_kernel(me_ref, own_ref, other_ref, wown_ref, wother_ref, *refs):
    send_ref, keep_ref = refs[-2:]
    total = jnp.dot(own_ref[...], wown_ref[...], preferred_element_type=F32)
    total = total + jnp.dot(other_ref[...], wother_ref[...], preferred_element_type=F32)
    half = send_ref.shape[0]
    send_ref[...] = total[:half].astype(BF16)
    keep_ref[...] = total[half:].astype(BF16)


def out_project(me, own, other, out_weight, other_weight, after):
    rows, c = own.shape
    cols = out_weight.shape[1] // 2
    tile = 1024
    tiles = cols // tile
    half = jax.ShapeDtypeStruct((rows // 2, cols), BF16)
    return pl.pallas_call(
        out_kernel,
        grid_spec=pltpu.PrefetchScalarGridSpec(
            num_scalar_prefetch=1,
            grid=(tiles,),
            in_specs=[
                pl.BlockSpec(memory_space=pltpu.VMEM),
                pl.BlockSpec(memory_space=pltpu.VMEM),
                pl.BlockSpec((c, tile), lambda j, me_ref: (0, (me_ref[0] % 2) * tiles + j)),
                pl.BlockSpec((c, tile), lambda j, me_ref: (0, j)),
            ]
            + [pl.BlockSpec(memory_space=pl.ANY)] * len(after),
            out_specs=[pl.BlockSpec((rows // 2, tile), lambda j, me_ref: (0, j))] * 2,
        ),
        out_shape=[half, half],
        compiler_params=params(48),
        cost_estimate=cost(4 * rows * c * cols, 4 * c * cols + 2 * rows * cols),
        name="out_project",
    )(me, own, other, out_weight, other_weight, *after)


def halve_kernel(stage, me_ref, after_ref, keep_ref, got_ref, send_ref, left_ref):
    bit = (me_ref[0] >> (2 + stage)) & 1
    for i in range(send_ref.shape[0]):
        for o_ref, at in ((send_ref, 2 * i + 1 - bit), (left_ref, 2 * i + bit)):
            o_ref[i] = (keep_ref[at].astype(F32) + got_ref[at].astype(F32)).astype(BF16)


def sum_z_kernel(me_ref, after_ref, keep_ref, got_ref, send_ref, left_ref):
    total = keep_ref[0].astype(F32) + got_ref[0].astype(F32)
    own = total.shape[0] // 2
    low, high = total[:own], total[own:]
    core = me_ref[0] % 2
    send_ref[...] = jnp.where(core == 0, high, low).astype(BF16)
    left_ref[...] = jnp.where(core == 0, low, high).astype(BF16)


def final_kernel(tiles, me_ref, *refs):
    o_ref = refs[-1]
    own_half = pl.program_id(0) // tiles == me_ref[0] % 2
    parts = []
    for t in range(STEPS):
        value = jnp.where(own_half, refs[t][...].astype(F32), refs[STEPS + t][...].astype(F32))
        o_ref[:, t, :] = value.astype(BF16)


def final_join(me, keeps, gots):
    own, cols = keeps[0].shape
    tile = 2048
    tiles = cols // tile
    return pl.pallas_call(
        functools.partial(final_kernel, tiles),
        grid_spec=pltpu.PrefetchScalarGridSpec(
            num_scalar_prefetch=1,
            grid=(2 * tiles,),
            in_specs=[pl.BlockSpec((own, tile), lambda j, me_ref: (0, j % tiles))] * (2 * STEPS),
            out_specs=pl.BlockSpec((own, STEPS, tile), lambda j, me_ref: (0, 0, j)),
        ),
        out_shape=jax.ShapeDtypeStruct((own, STEPS, 2 * cols), BF16),
        compiler_params=params(16),
        cost_estimate=cost(0, own * cols * 32),
        name="final_join",
    )(me, *keeps, *gots)


def shards(
    resident_state,
    resident_conv,
    prefilled_state,
    prefilled_conv,
    live_counts,
    batch_rows,
    step_x,
    step_z,
    conv_weight,
    conv_bias,
    x_proj,
    norm_gain,
    dt_proj,
    dt_bias,
    a_log,
    d_skip,
    out_weight,
):
    n = lax.axis_size("dex")
    zs = n // 4
    rows = resident_state.shape[0]
    slots = prefilled_state.shape[0]
    c = resident_state.shape[2]
    me_scalar = lax.axis_index("dex").astype(jnp.int32)
    me = me_scalar.reshape(1)

    moved_conv = exchange_conv(prefilled_conv, me, n)
    half_weight = weight_half(me, moved_conv[1], out_weight)
    packed = pack_state((half_weight,), prefilled_state, n)
    cols = out_weight.shape[1] // 2

    is_live = jnp.arange(slots, dtype=jnp.int32)[None, :] < live_counts[:, None]
    target = jnp.where(is_live, batch_rows.reshape(n, slots), -1)
    place = jnp.arange(TAPS + 1, dtype=jnp.int32)
    mine = place[None, None, :, None] == place[:, None, None, None]
    spread = jnp.where(mine, target[None, :, None, :], -1).reshape(TAPS + 1, n * (TAPS + 1) * slots)
    flat = target.reshape(-1)
    number = jnp.arange(n * slots, dtype=jnp.int32)
    count = n * slots // 2
    rank = jnp.sum(((flat >= 0)[None, :] & (number[None, :] < number[:, None])).astype(jnp.int32), axis=1)
    hit = (rank[None, :] == number[:count, None]) & (flat >= 0)[None, :]
    live_slot = jnp.sum(jnp.where(hit, number[None, :], 0), axis=1)
    live_row = jnp.sum(jnp.where(hit, flat[None, :], 0), axis=1)
    slot_of_live = jnp.stack([live_slot // slots, live_slot % slots])
    row_of_live = jnp.broadcast_to(live_row[:, None], (count, 128))
    live_row = live_row.reshape(1, count)
    gain = jnp.concatenate([norm_gain, jnp.zeros((WIDE - norm_gain.shape[0],), F32)]).reshape(1, WIDE)
    old = jnp.transpose(resident_conv, (1, 0, 2))
    proj = x_proj.T
    bias = conv_bias.reshape(1, c)
    conv, send, keep = conv_steps(
        tuple(range(STEPS)), n, me, (packed,), spread, old, moved_conv, step_x, conv_weight, bias, proj
    )
    behind, merged, lows = reduce_projection(send, keep, gain, me, n)
    packed = hold(packed, merged)
    moved_state = lax.all_to_all(packed, "dex", 0, 0, tiled=True)
    other_weight = swap(hold(half_weight, behind), 1, n)

    state = resident_state.reshape(rows * STATE, c)
    sends, keeps, gated = {}, {}, {}
    stages = zs.bit_length() - 1
    take = 2 * rows // n

    rate_bias, skip = dt_bias.reshape(1, c), d_skip.reshape(1, c)

    next_steps = None

    def s_step(t, after):
        nonlocal state, next_steps
        if t == 0:
            steps = step_rows(0, me, after, lows, dt_proj, rate_bias, rows, n)
        else:
            steps = next_steps
        state, gated[t] = state_step(t, me, after, steps, conv, step_z, a_log, skip, state, n)
        if t == STEPS - 1:
            return gated[t]
        next_steps = step_rows(t + 1, me, (gated[t],), lows, dt_proj, rate_bias, rows, n)
        return next_steps[1]

    def fix(t, after):
        kernel = functools.partial(fix_kernel, t, take)
        (gated[t],) = small(kernel, me, [live_row, gated[t], live_gated], [(rows, c)], "fix", (after,))
        return gated[t]

    def project(t, after):
        sends[t], keeps[t] = out_project(me, gated[t], swap(gated[t], 1, n), out_weight, other_weight, (after,))
        return keeps[t]

    def reduce(t, stage, after):
        if stage == 0:
            keep, got = keeps[t].reshape(zs, take, cols), swap(sends[t], 2, n).reshape(zs, take, cols)
        else:
            keep, got = keeps[t], swap(sends[t], 2 << stage, n)
        if stage < stages:
            kernel, shape = functools.partial(halve_kernel, stage), (keep.shape[0] // 2, take, cols)
        else:
            kernel, shape = sum_z_kernel, (take // 2, cols)
        sends[t], keeps[t] = small(kernel, me, [keep, got], [shape] * 2, "reduce_%d" % stage, (after,))
        if stage == stages:
            sends[t] = swap(sends[t], 1, n)
        return keeps[t]

    last = s_step(0, (packed,))
    gathered = gather_live(me, (last,), row_of_live, lows, conv, step_z, dt_proj, rate_bias, n)
    live_gated = live_steps(slot_of_live, (last,), moved_state, gathered, a_log, skip)
    last = fix(0, live_gated)
    last = project(0, last)
    for t in range(1, STEPS):
        last = s_step(t, (last,))
        last = fix(t, last)
        if t > 1:
            for stage in range(1, stages):
                last = reduce(t - 2, stage, last)
        last = project(t, last)
        if 1 < t < STEPS - 1:
            last = reduce(t - 2, stages, last)
        last = reduce(t - 1, 0, last)
    last = reduce(STEPS - 3, stages, last)
    for stage in range(1, stages):
        last = reduce(STEPS - 2, stage, last)
    last = reduce(STEPS - 1, 0, last)
    last = reduce(STEPS - 2, stages, last)
    for stage in range(1, stages + 1):
        last = reduce(STEPS - 1, stage, last)
    return final_join(me, [keeps[t] for t in range(STEPS)], [sends[t] for t in range(STEPS)])


def solution(mesh):
    placed = (
        P("grp", None, "dex"),
        P("grp", None, "dex"),
        P(("grp", "dex"), None, None),
        P(("grp", "dex"), None, None),
        P("grp"),
        P("grp"),
        P(None, "grp", "dex"),
        P(None, "grp", "dex"),
        P(None, "dex"),
        P("dex"),
        P("dex", None),
        P(),
        P(None, "dex"),
        P("dex"),
        P(None, "dex"),
        P("dex"),
        P("dex", None),
    )
    return jax.shard_map(
        shards, mesh=mesh, in_specs=placed, out_specs=P(("grp", "dex"), None, None), check_vma=False
    )
```

```python
import functools

import jax
import jax.numpy as jnp
from jax import lax
from jax.experimental import pallas as pl
from jax.experimental.pallas import tpu as pltpu
from jax.sharding import PartitionSpec as P

STATE = 16
DT_RANK = 512
STEPS = 4
TAPS = 3
WIDE = DT_RANK + 128

RMS_EPS = 1e-06
BC_FLOOR = 0.2

BF16 = jnp.bfloat16
F32 = jnp.float32


def params(mib):
    return pltpu.CompilerParams(vmem_limit_bytes=mib * 1024 * 1024)


def swap(x, mask, n):
    return lax.ppermute(x, "dex", [(i, i ^ mask) for i in range(n)])


def cost(flops, bytes_accessed, transcendentals=0):
    return pl.CostEstimate(flops=1024, bytes_accessed=1024, transcendentals=0)


def sigmoid(x):
    return 1.0 / (1.0 + jnp.exp(-x))


def whole(shape):
    zeros = (0,) * len(shape)
    return pl.BlockSpec(shape, lambda *_: zeros)


def small(kernel, me, args, shapes, name, after=(), dtype=BF16, scratch=(), mib=8):
    size = sum(a.size for a in args)
    vmem = pl.BlockSpec(memory_space=pltpu.VMEM)
    return pl.pallas_call(
        kernel,
        in_specs=[pl.BlockSpec(memory_space=pltpu.SMEM)]
        + [pl.BlockSpec(memory_space=pl.ANY)] * len(after)
        + [vmem] * len(args),
        out_specs=[vmem] * len(shapes),
        out_shape=[jax.ShapeDtypeStruct(s, dtype) for s in shapes],
        scratch_shapes=list(scratch),
        compiler_params=params(mib),
        cost_estimate=cost(size, 4 * size),
        name=name,
    )(me, *after, *args)


def pack_conv_kernel(me_ref, x_ref, *o_refs):
    zs, _, wide = o_refs[0].shape
    y, core = (me_ref[0] // 2) % 2, me_ref[0] % 2
    c = wide * (TAPS + 1) // TAPS
    for i, o_ref in enumerate(o_refs):
        for z in range(zs):
            dest = 4 * z + 2 * jnp.bitwise_xor(y, i % 2) + jnp.bitwise_xor(core, i // 2)
            x = x_ref[:, :, pl.ds(pl.multiple_of(dest * c, 128), c)]
            parts = [x[p, :, :wide] for p in range(TAPS)]
            parts.append(jnp.concatenate([x[p, :, wide:] for p in range(TAPS)], axis=1))
            o_ref[z] = jnp.concatenate(parts, axis=0).astype(BF16)


def cut_conv_kernel(me_ref, *refs):
    zs = refs[0].shape[0]
    z, y, core = me_ref[0] // 4, (me_ref[0] // 2) % 2, me_ref[0] % 2
    for m in range(zs):
        for i in range(4):
            at = 2 * jnp.bitwise_xor(y, i % 2) + jnp.bitwise_xor(core, i // 2)
            refs[4 + m][at] = refs[i][jnp.bitwise_xor(z, m)]


def exchange_conv(prefilled_conv, me, n):
    slots, _, inner = prefilled_conv.shape
    zs = n // 4
    piece = ((TAPS + 1) * slots, inner // n * TAPS // (TAPS + 1))
    conv = jnp.transpose(prefilled_conv, (1, 0, 2))
    packed = small(pack_conv_kernel, me, [conv], [(zs,) + piece] * 4, "pack_conv")
    near, far = swap(packed[2], 1, n), swap(packed[3], 1, n)
    got = [packed[0], swap(packed[1], 2, n), near, swap(far, 2, n)]
    cut = small(cut_conv_kernel, me, got, [(4,) + piece] * zs, "cut_conv")
    return [cut[0]] + [swap(cut[m], 4 * m, n) for m in range(1, zs)]


def pack_state_kernel(x_ref, *refs):
    o_ref = refs[-1]
    slots = x_ref.shape[0]
    some, _, c = o_ref.shape
    for d in range(some):
        for k in range(slots):
            o_ref[d, STATE * k : STATE * (k + 1), :] = x_ref[k, :, d * c : (d + 1) * c].astype(BF16)


def pack_state(after, prefilled_state, n):
    slots, _, inner = prefilled_state.shape
    c = inner // n
    some = 4
    return pl.pallas_call(
        pack_state_kernel,
        grid=(n // some,),
        in_specs=[pl.BlockSpec((slots, STATE, some * c), lambda d: (0, 0, d))]
        + [pl.BlockSpec(memory_space=pl.ANY)] * len(after),
        out_specs=pl.BlockSpec((some, slots * STATE, c), lambda d: (d, 0, 0)),
        out_shape=jax.ShapeDtypeStruct((n, slots * STATE, c), BF16),
        compiler_params=params(24),
        cost_estimate=cost(0, slots * STATE * inner * 6),
        name="pack_state",
    )(prefilled_state, *after)


def hold_kernel(x_ref, after_ref, o_ref):
    pass


def hold(x, after):
    some = pl.BlockSpec(memory_space=pl.ANY)
    return pl.pallas_call(
        hold_kernel,
        in_specs=[some, some],
        out_specs=some,
        out_shape=jax.ShapeDtypeStruct(x.shape, x.dtype),
        input_output_aliases={0: 0},
        compiler_params=params(8),
        cost_estimate=cost(0, 0),
        name="hold",
    )(x, after)


def half_kernel(me_ref, after_ref, w_ref, o_ref):
    o_ref[...] = w_ref[...]


def weight_half(me, after, out_weight):
    c, cols = out_weight.shape
    tile = 1024
    tiles = cols // 2 // tile
    return pl.pallas_call(
        half_kernel,
        grid_spec=pltpu.PrefetchScalarGridSpec(
            num_scalar_prefetch=1,
            grid=(tiles,),
            in_specs=[
                pl.BlockSpec(memory_space=pl.ANY),
                pl.BlockSpec((c, tile), lambda j, me_ref: (0, (1 - me_ref[0] % 2) * tiles + j)),
            ],
            out_specs=pl.BlockSpec((c, tile), lambda j, me_ref: (0, j)),
        ),
        out_shape=jax.ShapeDtypeStruct((c, cols // 2), BF16),
        compiler_params=params(56),
        cost_estimate=cost(0, 2 * c * cols),
        name="weight_half",
    )(me, after, out_weight)


def conv_kernel(steps, n, me_ref, target_ref, old_ref, x_ref, w_ref, bias_ref, proj_ref, *refs):
    zs = n // 4
    moved, (conv_ref, send_ref, keep_ref, moved_scr, win) = refs[:zs], refs[-5:]
    rows, c = win.shape[1:]
    columns = target_ref.shape[1]
    own = rows // n
    core, my_z = me_ref[0] % 2, me_ref[0] // 4
    for m in range(zs):
        moved_scr[jnp.bitwise_xor(my_z, m)] = moved[m][...]
    fresh = moved_scr[...].reshape(columns, moved_scr.shape[3])
    wide = fresh.shape[1]
    row_id = lax.broadcasted_iota(jnp.int32, (rows, columns), 0)
    hots = [row_id == target_ref[p : p + 1, :] for p in range(TAPS + 1)]
    taken = jnp.max(hots[0].astype(F32), axis=1, keepdims=True) > 0.0
    fresh = [jnp.dot(hot.astype(BF16), fresh, preferred_element_type=F32) for hot in hots]
    for p in range(TAPS):
        part = (c - wide) * p
        win[p, :, :wide] = jnp.where(taken, fresh[p], old_ref[p, :, :wide])
        win[p, :, wide:] = jnp.where(taken, fresh[TAPS][:, part : part + c - wide], old_ref[p, :, wide:])
    for i, t in enumerate(steps):
        total = None
        for q in range(TAPS + 1):
            place = t + q
            value = win[place] if place < TAPS else x_ref[place - TAPS].astype(F32)
            term = value * w_ref[q : q + 1, :]
            total = term if total is None else total + term
        total = total + bias_ref[...]
        conv_out = total * sigmoid(total)
        conv_ref[i] = conv_out
        part = lax.dot_general(
            conv_out.astype(BF16), proj_ref[...], (((1,), (1,)), ((), ())), preferred_element_type=F32
        )
        pad = jnp.zeros((own, WIDE - part.shape[1]), BF16)
        for q in range(n // 2):
            low = part[2 * q * own : (2 * q + 1) * own, :]
            high = part[(2 * q + 1) * own : (2 * q + 2) * own, :]
            send_ref[q, i, :, : part.shape[1]] = jnp.where(core == 0, high, low).astype(BF16)
            keep_ref[q, i, :, : part.shape[1]] = jnp.where(core == 0, low, high).astype(BF16)
            send_ref[q, i, :, part.shape[1] :] = pad
            keep_ref[q, i, :, part.shape[1] :] = pad


def conv_steps(steps, n, me, after, target, old, moved, step_x, conv_weight, conv_bias, proj):
    _, rows, c = old.shape
    s = len(steps)
    last = max(steps) + 1
    parts = (n // 2, s, rows // n, WIDE)
    return pl.pallas_call(
        functools.partial(conv_kernel, steps, n),
        grid_spec=pltpu.PrefetchScalarGridSpec(
            num_scalar_prefetch=1,
            grid=(1,),
            in_specs=[
                whole(target.shape),
                whole(old.shape),
                whole((last, rows, c)),
                whole(conv_weight.shape),
                whole((1, c)),
                whole(proj.shape),
            ]
            + [whole(moved[0].shape)] * len(moved)
            + [pl.BlockSpec(memory_space=pl.ANY)] * len(after),
            out_specs=[whole((s, rows, c)), whole(parts), whole(parts)],
            scratch_shapes=[
                pltpu.VMEM((len(moved),) + moved[0].shape, BF16),
                pltpu.VMEM((TAPS, rows, c), F32),
            ],
        ),
        out_shape=[jax.ShapeDtypeStruct((s, rows, c), F32)] + [jax.ShapeDtypeStruct(parts, BF16)] * 2,
        compiler_params=params(40),
        cost_estimate=cost(2 * s * rows * c * 544, rows * c * (12 + 6 * s) + c * 1088, s * rows * c),
        name="conv_project",
    )(me, target, old, step_x, conv_weight, conv_bias, proj, *moved, *after)


def add_y_kernel(me_ref, *refs):
    keep_ref, got_ref, send_ref, left_ref = refs[-4:]
    y = (me_ref[0] // 2) % 2
    for z in range(send_ref.shape[0]):
        for o_ref, at in ((send_ref, 2 * z + 1 - y), (left_ref, 2 * z + y)):
            o_ref[z] = (keep_ref[at].astype(F32) + got_ref[at].astype(F32)).astype(BF16)


def add_z_kernel(zs, me_ref, *refs):
    keep_ref, got_ref, *o_refs = refs[-2 - zs :]
    z = me_ref[0] // 4
    for m, o_ref in enumerate(o_refs):
        at = jnp.bitwise_xor(z, m)
        o_ref[...] = (keep_ref[at].astype(F32) + got_ref[at].astype(F32)).astype(BF16)


def norm_kernel(me_ref, gain_ref, *refs):
    o_ref = refs[-1]
    total = refs[0][...].astype(F32)
    for ref in refs[1:-1]:
        total = total + ref[...].astype(F32)
    dt = total[:, :, :DT_RANK]
    dt = dt * lax.rsqrt(jnp.mean(dt * dt, axis=2, keepdims=True) + RMS_EPS) * gain_ref[:, :DT_RANK][None]
    tail = total[:, :, DT_RANK:]
    lane = lax.broadcasted_iota(jnp.int32, tail.shape, 2)
    square = tail * tail
    is_b = lane < STATE
    is_c = jnp.logical_and(lane >= STATE, lane < 2 * STATE)
    mean_b = jnp.sum(jnp.where(is_b, square, 0.0), axis=2, keepdims=True) / STATE
    mean_c = jnp.sum(jnp.where(is_c, square, 0.0), axis=2, keepdims=True) / STATE
    scale_b = lax.rsqrt(jnp.maximum(mean_b, BC_FLOOR))
    scale_c = lax.rsqrt(jnp.maximum(mean_c, BC_FLOOR))
    tail = tail * jnp.where(is_b, scale_b, scale_c) * gain_ref[:, DT_RANK:][None]
    o_ref[:, :, :DT_RANK] = dt.astype(BF16)
    o_ref[:, :, DT_RANK:] = jnp.where(lane < 2 * STATE, tail, 0.0).astype(BF16)


def merge_kernel(me_ref, *refs):
    o_ref = refs[-1]
    z = me_ref[0] // 4
    for m, ref in enumerate(refs[:-1]):
        o_ref[jnp.bitwise_xor(z, m)] = ref[...]


def reduce_projection(send, keep, gain, me, n):
    zs = n // 4
    piece = keep.shape[1:]
    got = swap(send, 1, n)
    send, keep = small(add_y_kernel, me, [keep, got], [(zs,) + piece] * 2, "add_y")
    got = swap(send, 2, n)
    cut = small(functools.partial(add_z_kernel, zs), me, [keep, got], [piece] * zs, "add_z")
    cut = [cut[0]] + [swap(cut[m], 4 * m, n) for m in range(1, zs)]
    (low,) = small(norm_kernel, me, [gain] + cut, [piece], "norm")
    lows = [low] + [swap(low, 4 * m, n) for m in range(1, zs)]
    (mine,) = small(merge_kernel, me, lows, [(zs,) + piece], "merge_z")
    beside = swap(mine, 2, n)
    return keep, mine, (mine, beside, swap(mine, 1, n), swap(beside, 1, n))


def assemble_low(lows, index, low_scr, me_ref):
    y, core = (me_ref[0] // 2) % 2, me_ref[0] % 2
    for i, low_ref in enumerate(lows):
        for z in range(low_ref.shape[0]):
            low_scr[z, jnp.bitwise_xor(y, i % 2), jnp.bitwise_xor(core, i // 2)] = low_ref[z, index]
    return low_scr[...].reshape(-1, WIDE)


def step_sizes(low, dtp_ref, dtb_ref):
    pre = jnp.dot(low[:, :DT_RANK], dtp_ref[...], preferred_element_type=F32) + dtb_ref[...]
    return jnp.maximum(pre, 0.0) + jnp.log(1.0 + jnp.exp(-jnp.abs(pre)))


def step_kernel(t, me_ref, after_ref, *refs):
    *lows, dtp_ref, dtb_ref, step_ref, tail_ref, low_scr = refs
    low = assemble_low(lows, t, low_scr, me_ref)
    step_ref[...] = step_sizes(low, dtp_ref, dtb_ref)
    tail_ref[...] = low[:, DT_RANK:].astype(F32)


def step_rows(t, me, after, lows, dt_proj, dt_bias, rows, n):
    return small(
        functools.partial(step_kernel, t),
        me,
        [*lows, dt_proj, dt_bias],
        [(rows, dt_proj.shape[1]), (rows, 128)],
        "step_rows",
        after,
        F32,
        [pltpu.VMEM((n // 4, 2, 2, rows // n, WIDE), BF16)],
        12,
    )


def state_kernel(t, behind, me_ref, *refs):
    first, last = t == 0, t == STEPS - 1
    refs = refs[behind:]
    step_ref, tail_ref, conv_ref, z_ref, alog_ref, skip_ref, state_ref, *refs = refs
    new_ref = None
    if not last:
        new_ref, *refs = refs
    gated_ref, decay_scr, bc_scr, *refs = refs
    block = pl.program_id(0)
    rows, c = step_ref.shape
    take = conv_ref.shape[0]
    blocks = rows // take

    if first:
        buf, sems = refs

        def fetch(at, slot):
            first_row = pl.multiple_of(at * (take * STATE), take * STATE)
            return [
                pltpu.make_async_copy(
                    state_ref.at[pl.ds(first_row, take * STATE), 128 * l : 128 * (l + 1)],
                    buf.at[slot, l],
                    sems.at[slot, l],
                )
                for l in range(c // 128)
            ]

        now = lax.rem(block, 2)

        @pl.when(block == 0)
        def _():
            for copy in fetch(0, 0):
                copy.start()

        @pl.when(block + 1 < blocks)
        def _():
            for copy in fetch(block + 1, 1 - now):
                copy.start()

    @pl.when(block == 0)
    def _():
        decay_scr[...] = -jnp.exp(alog_ref[...])

    base = block * take
    if first:
        for copy in fetch(block, now):
            copy.wait()

    tall, lanes = 16, min(256, c)
    for r in range(0, take, tall):
        tail = tail_ref[pl.ds(pl.multiple_of(base + r, tall), tall), :]
        for s in range(2 * STATE):
            bc_scr[s] = jnp.broadcast_to(tail[:, s : s + 1], (tall, 128))
        for l in range(0, c, lanes):
            cols = slice(l, l + lanes)
            step = step_ref[pl.ds(pl.multiple_of(base + r, tall), tall), cols]
            conv = conv_ref[r : r + tall, cols]
            drive = step * conv
            total = skip_ref[:, cols] * conv
            for s in range(STATE):
                if first:
                    at = pl.ds(STATE * r + s, tall, stride=STATE)
                    tiles = range(l // 128, (l + lanes) // 128)
                    old = jnp.concatenate([buf[now, k, at, :] for k in tiles], axis=1)
                else:
                    old = state_ref[s, r : r + tall, cols].astype(F32)
                b = jnp.concatenate([bc_scr[s]] * (lanes // 128), axis=1)
                g = jnp.concatenate([bc_scr[STATE + s]] * (lanes // 128), axis=1)
                state = jnp.exp(step * decay_scr[s : s + 1, cols]) * old + drive * b
                if not last:
                    new_ref[s, r : r + tall, cols] = state.astype(BF16)
                total = total + state * g
            z = z_ref[0, r : r + tall, cols].astype(F32)
            gated_ref[r : r + tall, cols] = (total * (z * sigmoid(z))).astype(BF16)


def state_step(t, me, after, steps, conv, step_z, a_log, d_skip, state, n):
    _, rows, c = conv.shape
    take = 2 * rows // n
    blocks = rows // take
    first, last = t == 0, t == STEPS - 1

    def placed(i, me_ref):
        z, y = i // 2, i % 2
        mine = (y == (me_ref[0] // 2) % 2).astype(jnp.int32)
        return (mine * (blocks // 2) + z, 0)

    vmem = pl.BlockSpec(memory_space=pltpu.VMEM)
    in_specs = [vmem] * 2 + [
        pl.BlockSpec((None, take, c), lambda i, *_: (t, i, 0)),
        pl.BlockSpec((1, take, c), lambda i, *_: (t, i, 0)),
        whole(a_log.shape),
        whole((1, c)),
    ]
    scratch = [
        pltpu.VMEM((STATE, c), F32),
        pltpu.VMEM((2 * STATE, 16, 128), F32),
    ]
    flat = pl.BlockSpec((STATE, take, c), lambda i, *_: (0, i, 0))
    if first:
        in_specs = in_specs + [pl.BlockSpec(memory_space=pl.ANY)]
        scratch += [
            pltpu.VMEM((2, c // 128, take * STATE, 128), F32),
            pltpu.SemaphoreType.DMA((2, c // 128)),
        ]
    else:
        in_specs = in_specs + [flat]
    in_specs = [pl.BlockSpec(memory_space=pl.ANY)] * len(after) + in_specs
    out_specs = [pl.BlockSpec((take, c), placed)]
    out_shape = [jax.ShapeDtypeStruct((rows, c), BF16)]
    if not last:
        out_specs = [flat] + out_specs
        out_shape = [jax.ShapeDtypeStruct((STATE, rows, c), BF16)] + out_shape
    size = rows * STATE * c
    out = pl.pallas_call(
        functools.partial(state_kernel, t, len(after)),
        grid_spec=pltpu.PrefetchScalarGridSpec(
            num_scalar_prefetch=1,
            grid=(blocks,),
            in_specs=in_specs,
            out_specs=out_specs,
            scratch_shapes=scratch,
        ),
        out_shape=out_shape,
        compiler_params=params(48),
        cost_estimate=cost(8 * size, 4 * size, size),
        name="state_step",
    )(me, *after, *steps, conv, step_z, a_log, d_skip, state)
    return (None, out[0]) if last else (out[0], out[1])


def gather_kernel(me_ref, after_ref, row_ref, *refs):
    lows, refs = refs[:4], refs[4:]
    conv_ref, z_ref, dtp_ref, dtb_ref, step_ref, live_conv_ref, gate_ref, tail_ref, low_scr = refs
    count = step_ref.shape[1]
    rows = conv_ref.shape[1]
    hot = (row_ref[:, :1] == lax.broadcasted_iota(jnp.int32, (count, rows), 1)).astype(F32).astype(BF16)
    for t in range(STEPS):
        low = jnp.dot(hot, assemble_low(lows, t, low_scr, me_ref), preferred_element_type=F32)
        step_ref[t] = step_sizes(low.astype(BF16), dtp_ref, dtb_ref)
        tail_ref[t, :, :128] = low[:, DT_RANK:]
        conv = conv_ref[t]
        high = conv.astype(BF16)
        rest = (conv - high.astype(F32)).astype(BF16)
        live_conv_ref[t] = jnp.dot(hot, high, preferred_element_type=F32) + jnp.dot(
            hot, rest, preferred_element_type=F32
        )
        z = jnp.dot(hot, z_ref[t], preferred_element_type=F32)
        gate_ref[t] = z * sigmoid(z)


def gather_live(me, after, row_of_live, lows, conv, step_z, dt_proj, dt_bias, n):
    _, rows, c = conv.shape
    count = row_of_live.shape[0]
    wide = (STEPS, count, c)
    return small(
        gather_kernel,
        me,
        [row_of_live, *lows, conv, step_z, dt_proj, dt_bias],
        [wide, wide, wide, (STEPS, count, 128)],
        "gather_live",
        after,
        F32,
        [pltpu.VMEM((n // 4, 2, 2, rows // n, WIDE), BF16)],
        40,
    )


def live_kernel(slot_ref, after_ref, moved_ref, step_ref, conv_ref, gate_ref, tail_ref, alog_ref, skip_ref, o_ref, buf, state_scr):
    _, count, c = o_ref.shape
    def place(i, carry):
        source, slot = slot_ref[0, i], slot_ref[1, i]
        at = pl.multiple_of(i * STATE, STATE)
        from_row = pl.multiple_of(slot * STATE, STATE)
        value = moved_ref[source, pl.ds(from_row, STATE), :].astype(F32)
        for l in range(c // 128):
            buf[l, pl.ds(at, STATE), :] = value[:, 128 * l : 128 * (l + 1)]
        return carry

    lax.fori_loop(0, count, place, 0)
    for s in range(STATE):
        for l in range(c // 128):
            state_scr[s, :, 128 * l : 128 * (l + 1)] = buf[l, pl.ds(s, count, stride=STATE), :]
    tall, lanes = 16, min(512, c)

    def step_all(t, carry):
        for r in range(0, count, tall):
            tail = tail_ref[t, r : r + tall, :]
            for l in range(0, c, lanes):
                cols = slice(l, l + lanes)
                step = step_ref[t, r : r + tall, cols]
                conv = conv_ref[t, r : r + tall, cols]
                drive = step * conv
                total = skip_ref[:, cols] * conv
                for s in range(STATE):
                    rate = -jnp.exp(alog_ref[s : s + 1, cols])
                    old = state_scr[s, r : r + tall, cols]
                    state = jnp.exp(step * rate) * old + drive * tail[:, s : s + 1]
                    state_scr[s, r : r + tall, cols] = state
                    total = total + state * tail[:, STATE + s : STATE + s + 1]
                o_ref[t, r : r + tall, cols] = (total * gate_ref[t, r : r + tall, cols]).astype(BF16)
        return carry

    lax.fori_loop(0, STEPS, step_all, 0)


def live_steps(slot_of_live, after, moved, gathered, a_log, d_skip):
    _, count, c = gathered[0].shape
    (out,) = small(
        live_kernel,
        slot_of_live,
        [moved, *gathered, a_log, d_skip],
        [(STEPS, count, c)],
        "live_steps",
        after,
        BF16,
        [pltpu.VMEM((c // 128, count * STATE, 128), F32), pltpu.VMEM((STATE, count, c), F32)],
        40,
    )
    return out


def fix_kernel(t, take, me_ref, after_ref, row_ref, gated_ref, live_ref, o_ref):
    rows = gated_ref.shape[0]
    count = live_ref.shape[1]
    shift = take.bit_length() - 1
    place = lax.broadcasted_iota(jnp.int32, (rows, count), 0)
    mine = place >= rows // 2
    within = place - jnp.where(mine, rows // 2, 0)
    y = (me_ref[0] // 2) % 2
    row = ((2 * (within >> shift) + jnp.where(mine, y, 1 - y)) << shift) + (within & (take - 1))
    hot = (row == row_ref[...]).astype(F32)
    taken = jnp.max(hot, axis=1, keepdims=True) > 0.0
    live = jnp.dot(hot.astype(BF16), live_ref[t], preferred_element_type=F32)
    o_ref[...] = jnp.where(taken, live, gated_ref[...].astype(F32)).astype(BF16)


def out_kernel(me_ref, own_ref, other_ref, wown_ref, wother_ref, *refs):
    send_ref, keep_ref = refs[-2:]
    total = jnp.dot(own_ref[...], wown_ref[...], preferred_element_type=F32)
    total = total + jnp.dot(other_ref[...], wother_ref[...], preferred_element_type=F32)
    half = send_ref.shape[0]
    send_ref[...] = total[:half].astype(BF16)
    keep_ref[...] = total[half:].astype(BF16)


def out_project(me, own, other, out_weight, other_weight, after, part, parts):
    rows, c = own.shape
    tile = 1024
    every = out_weight.shape[1] // 2 // tile
    tiles = every // parts
    cols = tiles * tile
    first = part * tiles
    half = jax.ShapeDtypeStruct((rows // 2, cols), BF16)
    return pl.pallas_call(
        out_kernel,
        grid_spec=pltpu.PrefetchScalarGridSpec(
            num_scalar_prefetch=1,
            grid=(tiles,),
            in_specs=[
                pl.BlockSpec(memory_space=pltpu.VMEM),
                pl.BlockSpec(memory_space=pltpu.VMEM),
                pl.BlockSpec((c, tile), lambda j, me_ref: (0, (me_ref[0] % 2) * every + first + j)),
                pl.BlockSpec((c, tile), lambda j, me_ref: (0, first + j)),
            ]
            + [pl.BlockSpec(memory_space=pl.ANY)] * len(after),
            out_specs=[pl.BlockSpec((rows // 2, tile), lambda j, me_ref: (0, j))] * 2,
        ),
        out_shape=[half, half],
        compiler_params=params(48),
        cost_estimate=cost(4 * rows * c * cols, 4 * c * cols + 2 * rows * cols),
        name="out_project",
    )(me, own, other, out_weight, other_weight, *after)


def halve_kernel(stage, me_ref, after_ref, keep_ref, got_ref, send_ref, left_ref):
    bit = (me_ref[0] >> (2 + stage)) & 1
    for i in range(send_ref.shape[0]):
        for o_ref, at in ((send_ref, 2 * i + 1 - bit), (left_ref, 2 * i + bit)):
            o_ref[i] = (keep_ref[at].astype(F32) + got_ref[at].astype(F32)).astype(BF16)


def sum_z_kernel(me_ref, after_ref, keep_ref, got_ref, send_ref, left_ref):
    total = keep_ref[0].astype(F32) + got_ref[0].astype(F32)
    own = total.shape[0] // 2
    low, high = total[:own], total[own:]
    core = me_ref[0] % 2
    send_ref[...] = jnp.where(core == 0, high, low).astype(BF16)
    left_ref[...] = jnp.where(core == 0, low, high).astype(BF16)


def final_kernel(tiles, counts, me_ref, *refs):
    o_ref = refs[-1]
    own_half = pl.program_id(0) // tiles == me_ref[0] % 2
    tile = pl.program_id(0) % tiles
    at = 0
    for t, count in enumerate(counts):
        value = None
        for part in range(count):
            mine, theirs = refs[at][...].astype(F32), refs[at + 1][...].astype(F32)
            here = jnp.where(own_half, mine, theirs)
            value = here if value is None else jnp.where(tile == part, here, value)
            at += 2
        o_ref[:, t, :] = value.astype(BF16)


def final_join(me, pieces):
    own = pieces[0][0][0].shape[0]
    cols = sum(keep.shape[1] for keep, _ in pieces[0])
    tiles = max(len(parts) for parts in pieces)
    tile = cols // tiles
    args, specs = [], []
    for parts in pieces:
        for keep, got in parts:
            many = keep.shape[1] // tile
            spec = pl.BlockSpec((own, tile), lambda j, me_ref, many=many: (0, (j % tiles) % many))
            args += [keep, got]
            specs += [spec, spec]
    return pl.pallas_call(
        functools.partial(final_kernel, tiles, [len(parts) for parts in pieces]),
        grid_spec=pltpu.PrefetchScalarGridSpec(
            num_scalar_prefetch=1,
            grid=(2 * tiles,),
            in_specs=specs,
            out_specs=pl.BlockSpec((own, STEPS, tile), lambda j, me_ref: (0, 0, j)),
        ),
        out_shape=jax.ShapeDtypeStruct((own, STEPS, 2 * cols), BF16),
        compiler_params=params(16),
        cost_estimate=cost(0, own * cols * 32),
        name="final_join",
    )(me, *args)


def shards(
    resident_state,
    resident_conv,
    prefilled_state,
    prefilled_conv,
    live_counts,
    batch_rows,
    step_x,
    step_z,
    conv_weight,
    conv_bias,
    x_proj,
    norm_gain,
    dt_proj,
    dt_bias,
    a_log,
    d_skip,
    out_weight,
):
    n = lax.axis_size("dex")
    zs = n // 4
    rows = resident_state.shape[0]
    slots = prefilled_state.shape[0]
    c = resident_state.shape[2]
    me_scalar = lax.axis_index("dex").astype(jnp.int32)
    me = me_scalar.reshape(1)

    moved_conv = exchange_conv(prefilled_conv, me, n)
    half_weight = weight_half(me, moved_conv[1], out_weight)
    packed = pack_state((half_weight,), prefilled_state, n)
    cols = out_weight.shape[1] // 2

    is_live = jnp.arange(slots, dtype=jnp.int32)[None, :] < live_counts[:, None]
    target = jnp.where(is_live, batch_rows.reshape(n, slots), -1)
    place = jnp.arange(TAPS + 1, dtype=jnp.int32)
    mine = place[None, None, :, None] == place[:, None, None, None]
    spread = jnp.where(mine, target[None, :, None, :], -1).reshape(TAPS + 1, n * (TAPS + 1) * slots)
    flat = target.reshape(-1)
    number = jnp.arange(n * slots, dtype=jnp.int32)
    count = n * slots // 2
    rank = jnp.sum(((flat >= 0)[None, :] & (number[None, :] < number[:, None])).astype(jnp.int32), axis=1)
    hit = (rank[None, :] == number[:count, None]) & (flat >= 0)[None, :]
    live_slot = jnp.sum(jnp.where(hit, number[None, :], 0), axis=1)
    live_row = jnp.sum(jnp.where(hit, flat[None, :], 0), axis=1)
    slot_of_live = jnp.stack([live_slot // slots, live_slot % slots])
    row_of_live = jnp.broadcast_to(live_row[:, None], (count, 128))
    live_row = live_row.reshape(1, count)
    gain = jnp.concatenate([norm_gain, jnp.zeros((WIDE - norm_gain.shape[0],), F32)]).reshape(1, WIDE)
    old = jnp.transpose(resident_conv, (1, 0, 2))
    proj = x_proj.T
    bias = conv_bias.reshape(1, c)
    conv, send, keep = conv_steps(
        tuple(range(STEPS)), n, me, (packed,), spread, old, moved_conv, step_x, conv_weight, bias, proj
    )
    behind, merged, lows = reduce_projection(send, keep, gain, me, n)
    packed = hold(packed, merged)
    moved_state = lax.all_to_all(packed, "dex", 0, 0, tiled=True)
    other_weight = swap(hold(half_weight, behind), 1, n)

    state = resident_state.reshape(rows * STATE, c)
    sends, keeps, gated = {}, {}, {}
    stages = zs.bit_length() - 1
    take = 2 * rows // n

    rate_bias, skip = dt_bias.reshape(1, c), d_skip.reshape(1, c)

    next_steps = None

    def s_step(t, after):
        nonlocal state, next_steps
        if t == 0:
            steps = step_rows(0, me, after, lows, dt_proj, rate_bias, rows, n)
        else:
            steps = next_steps
        state, gated[t] = state_step(t, me, after, steps, conv, step_z, a_log, skip, state, n)
        if t == STEPS - 1:
            return gated[t]
        next_steps = step_rows(t + 1, me, (gated[t],), lows, dt_proj, rate_bias, rows, n)
        return next_steps[1]

    def fix(t, after):
        kernel = functools.partial(fix_kernel, t, take)
        (gated[t],) = small(kernel, me, [live_row, gated[t], live_gated], [(rows, c)], "fix", (after,))
        return gated[t]

    def project(t, after, parts=1):
        other = swap(gated[t], 1, n)
        for part in range(parts):
            sends[t, part], keeps[t, part] = out_project(
                me, gated[t], other, out_weight, other_weight, (after,), part, parts
            )
            after = keeps[t, part]
        return after

    def reduce(t, stage, after, part=0):
        at = t, part
        width = keeps[at].shape[-1]
        if stage == 0:
            keep = keeps[at].reshape(zs, take, width)
            got = swap(sends[at], 2, n).reshape(zs, take, width)
        else:
            keep, got = keeps[at], swap(sends[at], 2 << stage, n)
        if stage < stages:
            kernel, shape = functools.partial(halve_kernel, stage), (keep.shape[0] // 2, take, width)
        else:
            kernel, shape = sum_z_kernel, (take // 2, width)
        sends[at], keeps[at] = small(kernel, me, [keep, got], [shape] * 2, "reduce_%d" % stage, (after,))
        if stage == stages:
            sends[at] = swap(sends[at], 1, n)
        return keeps[at]

    last = s_step(0, (packed,))
    gathered = gather_live(me, (last,), row_of_live, lows, conv, step_z, dt_proj, rate_bias, n)
    live_gated = live_steps(slot_of_live, (last,), moved_state, gathered, a_log, skip)
    last = fix(0, live_gated)
    last = project(0, last)
    for t in range(1, STEPS - 1):
        last = s_step(t, (last,))
        last = fix(t, last)
        last = project(t, last)
        if t > 1:
            for stage in range(1, stages):
                last = reduce(t - 2, stage, last)
        last = reduce(t - 1, 0, last)
    t = STEPS - 1
    last = s_step(t, (last,))
    last = fix(t, last)
    last = project(t, last, 2)
    for stage in range(1, stages):
        last = reduce(t - 2, stage, last)
    last = reduce(t - 3, stages, last)
    last = reduce(t - 1, 0, last)
    for stage in range(1, stages):
        last = reduce(t - 1, stage, last)
    last = reduce(t - 2, stages, last)
    last = reduce(t, 0, last, 0)
    for stage in range(1, stages):
        last = reduce(t, stage, last, 0)
    last = reduce(t - 1, stages, last)
    last = reduce(t, 0, last, 1)
    for stage in range(1, stages):
        last = reduce(t, stage, last, 1)
    last = reduce(t, stages, last, 0)
    last = reduce(t, stages, last, 1)
    pieces = [[(keeps[t, part], sends[t, part]) for part in range(1 if t < STEPS - 1 else 2)] for t in range(STEPS)]
    return final_join(me, pieces)


def solution(mesh):
    placed = (
        P("grp", None, "dex"),
        P("grp", None, "dex"),
        P(("grp", "dex"), None, None),
        P(("grp", "dex"), None, None),
        P("grp"),
        P("grp"),
        P(None, "grp", "dex"),
        P(None, "grp", "dex"),
        P(None, "dex"),
        P("dex"),
        P("dex", None),
        P(),
        P(None, "dex"),
        P("dex"),
        P(None, "dex"),
        P("dex"),
        P("dex", None),
    )
    return jax.shard_map(
        shards, mesh=mesh, in_specs=placed, out_specs=P(("grp", "dex"), None, None), check_vma=False
    )
```

```python
import functools

import jax
import jax.numpy as jnp
from jax import lax
from jax.experimental import pallas as pl
from jax.experimental.pallas import tpu as pltpu
from jax.sharding import PartitionSpec as P

STATE = 16
DT_RANK = 512
STEPS = 4
TAPS = 3
WIDE = DT_RANK + 128

RMS_EPS = 1e-06
BC_FLOOR = 0.2

BF16 = jnp.bfloat16
F32 = jnp.float32


def params(mib):
    return pltpu.CompilerParams(vmem_limit_bytes=mib * 1024 * 1024)


def swap(x, mask, n):
    return lax.ppermute(x, "dex", [(i, i ^ mask) for i in range(n)])


def cost(flops, bytes_accessed, transcendentals=0):
    return pl.CostEstimate(flops=1024, bytes_accessed=1024, transcendentals=0)


def sigmoid(x):
    return 1.0 / (1.0 + jnp.exp(-x))


def whole(shape):
    zeros = (0,) * len(shape)
    return pl.BlockSpec(shape, lambda *_: zeros)


def small(kernel, me, args, shapes, name, after=(), dtype=BF16, scratch=(), mib=8):
    size = sum(a.size for a in args)
    vmem = pl.BlockSpec(memory_space=pltpu.VMEM)
    return pl.pallas_call(
        kernel,
        in_specs=[pl.BlockSpec(memory_space=pltpu.SMEM)]
        + [pl.BlockSpec(memory_space=pl.ANY)] * len(after)
        + [vmem] * len(args),
        out_specs=[vmem] * len(shapes),
        out_shape=[jax.ShapeDtypeStruct(s, dtype) for s in shapes],
        scratch_shapes=list(scratch),
        compiler_params=params(mib),
        cost_estimate=cost(size, 4 * size),
        name=name,
    )(me, *after, *args)


def pack_conv_kernel(me_ref, x_ref, *o_refs):
    zs, _, wide = o_refs[0].shape
    y, core = (me_ref[0] // 2) % 2, me_ref[0] % 2
    c = wide * (TAPS + 1) // TAPS
    for i, o_ref in enumerate(o_refs):
        for z in range(zs):
            dest = 4 * z + 2 * jnp.bitwise_xor(y, i % 2) + jnp.bitwise_xor(core, i // 2)
            x = x_ref[:, :, pl.ds(pl.multiple_of(dest * c, 128), c)]
            parts = [x[p, :, :wide] for p in range(TAPS)]
            parts.append(jnp.concatenate([x[p, :, wide:] for p in range(TAPS)], axis=1))
            o_ref[z] = jnp.concatenate(parts, axis=0).astype(BF16)


def cut_conv_kernel(me_ref, *refs):
    zs = refs[0].shape[0]
    z, y, core = me_ref[0] // 4, (me_ref[0] // 2) % 2, me_ref[0] % 2
    for m in range(zs):
        for i in range(4):
            at = 2 * jnp.bitwise_xor(y, i % 2) + jnp.bitwise_xor(core, i // 2)
            refs[4 + m][at] = refs[i][jnp.bitwise_xor(z, m)]


def exchange_conv(prefilled_conv, me, n):
    slots, _, inner = prefilled_conv.shape
    zs = n // 4
    piece = ((TAPS + 1) * slots, inner // n * TAPS // (TAPS + 1))
    conv = jnp.transpose(prefilled_conv, (1, 0, 2))
    packed = small(pack_conv_kernel, me, [conv], [(zs,) + piece] * 4, "pack_conv")
    near, far = swap(packed[2], 1, n), swap(packed[3], 1, n)
    got = [packed[0], swap(packed[1], 2, n), near, swap(far, 2, n)]
    cut = small(cut_conv_kernel, me, got, [(4,) + piece] * zs, "cut_conv")
    return [cut[0]] + [swap(cut[m], 4 * m, n) for m in range(1, zs)]


def pack_state_kernel(x_ref, *refs):
    o_ref = refs[-1]
    slots = x_ref.shape[0]
    some, _, c = o_ref.shape
    for d in range(some):
        for k in range(slots):
            o_ref[d, STATE * k : STATE * (k + 1), :] = x_ref[k, :, d * c : (d + 1) * c].astype(BF16)


def pack_state(after, prefilled_state, n):
    slots, _, inner = prefilled_state.shape
    c = inner // n
    some = 4
    return pl.pallas_call(
        pack_state_kernel,
        grid=(n // some,),
        in_specs=[pl.BlockSpec((slots, STATE, some * c), lambda d: (0, 0, d))]
        + [pl.BlockSpec(memory_space=pl.ANY)] * len(after),
        out_specs=pl.BlockSpec((some, slots * STATE, c), lambda d: (d, 0, 0)),
        out_shape=jax.ShapeDtypeStruct((n, slots * STATE, c), BF16),
        compiler_params=params(24),
        cost_estimate=cost(0, slots * STATE * inner * 6),
        name="pack_state",
    )(prefilled_state, *after)


def hold_kernel(x_ref, after_ref, o_ref):
    pass


def hold(x, after):
    some = pl.BlockSpec(memory_space=pl.ANY)
    return pl.pallas_call(
        hold_kernel,
        in_specs=[some, some],
        out_specs=some,
        out_shape=jax.ShapeDtypeStruct(x.shape, x.dtype),
        input_output_aliases={0: 0},
        compiler_params=params(8),
        cost_estimate=cost(0, 0),
        name="hold",
    )(x, after)


def half_kernel(me_ref, after_ref, w_ref, o_ref):
    o_ref[...] = w_ref[...]


def weight_half(me, after, out_weight):
    c, cols = out_weight.shape
    tile = 1024
    tiles = cols // 2 // tile
    return pl.pallas_call(
        half_kernel,
        grid_spec=pltpu.PrefetchScalarGridSpec(
            num_scalar_prefetch=1,
            grid=(tiles,),
            in_specs=[
                pl.BlockSpec(memory_space=pl.ANY),
                pl.BlockSpec((c, tile), lambda j, me_ref: (0, (1 - me_ref[0] % 2) * tiles + j)),
            ],
            out_specs=pl.BlockSpec((c, tile), lambda j, me_ref: (0, j)),
        ),
        out_shape=jax.ShapeDtypeStruct((c, cols // 2), BF16),
        compiler_params=params(56),
        cost_estimate=cost(0, 2 * c * cols),
        name="weight_half",
    )(me, after, out_weight)


def conv_kernel(steps, n, me_ref, target_ref, old_ref, x_ref, w_ref, bias_ref, proj_ref, *refs):
    zs = n // 4
    moved, (conv_ref, send_ref, keep_ref, moved_scr, win) = refs[:zs], refs[-5:]
    rows, c = win.shape[1:]
    columns = target_ref.shape[1]
    own = rows // n
    core, my_z = me_ref[0] % 2, me_ref[0] // 4
    for m in range(zs):
        moved_scr[jnp.bitwise_xor(my_z, m)] = moved[m][...]
    fresh = moved_scr[...].reshape(columns, moved_scr.shape[3])
    wide = fresh.shape[1]
    row_id = lax.broadcasted_iota(jnp.int32, (rows, columns), 0)
    hots = [row_id == target_ref[p : p + 1, :] for p in range(TAPS + 1)]
    taken = jnp.max(hots[0].astype(F32), axis=1, keepdims=True) > 0.0
    fresh = [jnp.dot(hot.astype(BF16), fresh, preferred_element_type=F32) for hot in hots]
    for p in range(TAPS):
        part = (c - wide) * p
        win[p, :, :wide] = jnp.where(taken, fresh[p], old_ref[p, :, :wide])
        win[p, :, wide:] = jnp.where(taken, fresh[TAPS][:, part : part + c - wide], old_ref[p, :, wide:])
    for i, t in enumerate(steps):
        total = None
        for q in range(TAPS + 1):
            place = t + q
            value = win[place] if place < TAPS else x_ref[place - TAPS].astype(F32)
            term = value * w_ref[q : q + 1, :]
            total = term if total is None else total + term
        total = total + bias_ref[...]
        conv_out = total * sigmoid(total)
        conv_ref[i] = conv_out
        part = lax.dot_general(
            conv_out.astype(BF16), proj_ref[...], (((1,), (1,)), ((), ())), preferred_element_type=F32
        )
        pad = jnp.zeros((own, WIDE - part.shape[1]), BF16)
        for q in range(n // 2):
            low = part[2 * q * own : (2 * q + 1) * own, :]
            high = part[(2 * q + 1) * own : (2 * q + 2) * own, :]
            send_ref[q, i, :, : part.shape[1]] = jnp.where(core == 0, high, low).astype(BF16)
            keep_ref[q, i, :, : part.shape[1]] = jnp.where(core == 0, low, high).astype(BF16)
            send_ref[q, i, :, part.shape[1] :] = pad
            keep_ref[q, i, :, part.shape[1] :] = pad


def conv_steps(steps, n, me, after, target, old, moved, step_x, conv_weight, conv_bias, proj):
    _, rows, c = old.shape
    s = len(steps)
    last = max(steps) + 1
    parts = (n // 2, s, rows // n, WIDE)
    return pl.pallas_call(
        functools.partial(conv_kernel, steps, n),
        grid_spec=pltpu.PrefetchScalarGridSpec(
            num_scalar_prefetch=1,
            grid=(1,),
            in_specs=[
                whole(target.shape),
                whole(old.shape),
                whole((last, rows, c)),
                whole(conv_weight.shape),
                whole((1, c)),
                whole(proj.shape),
            ]
            + [whole(moved[0].shape)] * len(moved)
            + [pl.BlockSpec(memory_space=pl.ANY)] * len(after),
            out_specs=[whole((s, rows, c)), whole(parts), whole(parts)],
            scratch_shapes=[
                pltpu.VMEM((len(moved),) + moved[0].shape, BF16),
                pltpu.VMEM((TAPS, rows, c), F32),
            ],
        ),
        out_shape=[jax.ShapeDtypeStruct((s, rows, c), F32)] + [jax.ShapeDtypeStruct(parts, BF16)] * 2,
        compiler_params=params(40),
        cost_estimate=cost(2 * s * rows * c * 544, rows * c * (12 + 6 * s) + c * 1088, s * rows * c),
        name="conv_project",
    )(me, target, old, step_x, conv_weight, conv_bias, proj, *moved, *after)


def add_y_kernel(me_ref, *refs):
    keep_ref, got_ref, send_ref, left_ref = refs[-4:]
    y = (me_ref[0] // 2) % 2
    for z in range(send_ref.shape[0]):
        for o_ref, at in ((send_ref, 2 * z + 1 - y), (left_ref, 2 * z + y)):
            o_ref[z] = (keep_ref[at].astype(F32) + got_ref[at].astype(F32)).astype(BF16)


def add_z_kernel(zs, me_ref, *refs):
    keep_ref, got_ref, *o_refs = refs[-2 - zs :]
    z = me_ref[0] // 4
    for m, o_ref in enumerate(o_refs):
        at = jnp.bitwise_xor(z, m)
        o_ref[...] = (keep_ref[at].astype(F32) + got_ref[at].astype(F32)).astype(BF16)


def norm_kernel(me_ref, gain_ref, *refs):
    o_ref = refs[-1]
    total = refs[0][...].astype(F32)
    for ref in refs[1:-1]:
        total = total + ref[...].astype(F32)
    dt = total[:, :, :DT_RANK]
    dt = dt * lax.rsqrt(jnp.mean(dt * dt, axis=2, keepdims=True) + RMS_EPS) * gain_ref[:, :DT_RANK][None]
    tail = total[:, :, DT_RANK:]
    lane = lax.broadcasted_iota(jnp.int32, tail.shape, 2)
    square = tail * tail
    is_b = lane < STATE
    is_c = jnp.logical_and(lane >= STATE, lane < 2 * STATE)
    mean_b = jnp.sum(jnp.where(is_b, square, 0.0), axis=2, keepdims=True) / STATE
    mean_c = jnp.sum(jnp.where(is_c, square, 0.0), axis=2, keepdims=True) / STATE
    scale_b = lax.rsqrt(jnp.maximum(mean_b, BC_FLOOR))
    scale_c = lax.rsqrt(jnp.maximum(mean_c, BC_FLOOR))
    tail = tail * jnp.where(is_b, scale_b, scale_c) * gain_ref[:, DT_RANK:][None]
    o_ref[:, :, :DT_RANK] = dt.astype(BF16)
    o_ref[:, :, DT_RANK:] = jnp.where(lane < 2 * STATE, tail, 0.0).astype(BF16)


def merge_kernel(me_ref, *refs):
    o_ref = refs[-1]
    z = me_ref[0] // 4
    for m, ref in enumerate(refs[:-1]):
        o_ref[jnp.bitwise_xor(z, m)] = ref[...]


def reduce_projection(send, keep, gain, me, n):
    zs = n // 4
    piece = keep.shape[1:]
    got = swap(send, 1, n)
    send, keep = small(add_y_kernel, me, [keep, got], [(zs,) + piece] * 2, "add_y")
    got = swap(send, 2, n)
    cut = small(functools.partial(add_z_kernel, zs), me, [keep, got], [piece] * zs, "add_z")
    cut = [cut[0]] + [swap(cut[m], 4 * m, n) for m in range(1, zs)]
    (low,) = small(norm_kernel, me, [gain] + cut, [piece], "norm")
    lows = [low] + [swap(low, 4 * m, n) for m in range(1, zs)]
    (mine,) = small(merge_kernel, me, lows, [(zs,) + piece], "merge_z")
    beside = swap(mine, 2, n)
    return keep, mine, (mine, beside, swap(mine, 1, n), swap(beside, 1, n))


def assemble_low(lows, index, low_scr, me_ref):
    y, core = (me_ref[0] // 2) % 2, me_ref[0] % 2
    for i, low_ref in enumerate(lows):
        for z in range(low_ref.shape[0]):
            low_scr[z, jnp.bitwise_xor(y, i % 2), jnp.bitwise_xor(core, i // 2)] = low_ref[z, index]
    return low_scr[...].reshape(-1, WIDE)


def step_sizes(low, dtp_ref, dtb_ref):
    pre = jnp.dot(low[:, :DT_RANK], dtp_ref[...], preferred_element_type=F32) + dtb_ref[...]
    return jnp.maximum(pre, 0.0) + jnp.log(1.0 + jnp.exp(-jnp.abs(pre)))


def step_kernel(t, me_ref, after_ref, *refs):
    *lows, dtp_ref, dtb_ref, step_ref, tail_ref, low_scr = refs
    low = assemble_low(lows, t, low_scr, me_ref)
    step_ref[...] = step_sizes(low, dtp_ref, dtb_ref)
    tail_ref[...] = low[:, DT_RANK:].astype(F32)


def step_rows(t, me, after, lows, dt_proj, dt_bias, rows, n):
    return small(
        functools.partial(step_kernel, t),
        me,
        [*lows, dt_proj, dt_bias],
        [(rows, dt_proj.shape[1]), (rows, 128)],
        "step_rows",
        after,
        F32,
        [pltpu.VMEM((n // 4, 2, 2, rows // n, WIDE), BF16)],
        12,
    )


def state_kernel(t, behind, me_ref, *refs):
    first, last = t == 0, t == STEPS - 1
    refs = refs[behind:]
    step_ref, tail_ref, conv_ref, z_ref, alog_ref, skip_ref, state_ref, *refs = refs
    new_ref = None
    if not last:
        new_ref, *refs = refs
    gated_ref, decay_scr, bc_scr, *refs = refs
    block = pl.program_id(0)
    rows, c = step_ref.shape
    take = conv_ref.shape[0]
    blocks = rows // take

    if first:
        buf, sems = refs

        def fetch(at, slot):
            first_row = pl.multiple_of(at * (take * STATE), take * STATE)
            return [
                pltpu.make_async_copy(
                    state_ref.at[pl.ds(first_row, take * STATE), 128 * l : 128 * (l + 1)],
                    buf.at[slot, l],
                    sems.at[slot, l],
                )
                for l in range(c // 128)
            ]

        now = lax.rem(block, 2)

        @pl.when(block == 0)
        def _():
            for copy in fetch(0, 0):
                copy.start()

        @pl.when(block + 1 < blocks)
        def _():
            for copy in fetch(block + 1, 1 - now):
                copy.start()

    @pl.when(block == 0)
    def _():
        decay_scr[...] = -jnp.exp(alog_ref[...])

    base = block * take
    if first:
        for copy in fetch(block, now):
            copy.wait()

    tall, lanes = 16, min(256, c)
    for r in range(0, take, tall):
        tail = tail_ref[pl.ds(pl.multiple_of(base + r, tall), tall), :]
        for s in range(2 * STATE):
            bc_scr[s] = jnp.broadcast_to(tail[:, s : s + 1], (tall, 128))
        for l in range(0, c, lanes):
            cols = slice(l, l + lanes)
            step = step_ref[pl.ds(pl.multiple_of(base + r, tall), tall), cols]
            conv = conv_ref[r : r + tall, cols]
            drive = step * conv
            total = skip_ref[:, cols] * conv
            for s in range(STATE):
                if first:
                    at = pl.ds(STATE * r + s, tall, stride=STATE)
                    tiles = range(l // 128, (l + lanes) // 128)
                    old = jnp.concatenate([buf[now, k, at, :] for k in tiles], axis=1)
                else:
                    old = state_ref[s, r : r + tall, cols].astype(F32)
                b = jnp.concatenate([bc_scr[s]] * (lanes // 128), axis=1)
                g = jnp.concatenate([bc_scr[STATE + s]] * (lanes // 128), axis=1)
                state = jnp.exp(step * decay_scr[s : s + 1, cols]) * old + drive * b
                if not last:
                    new_ref[s, r : r + tall, cols] = state.astype(BF16)
                total = total + state * g
            z = z_ref[0, r : r + tall, cols].astype(F32)
            gated_ref[r : r + tall, cols] = (total * (z * sigmoid(z))).astype(BF16)


def state_step(t, me, after, steps, conv, step_z, a_log, d_skip, state, n):
    _, rows, c = conv.shape
    take = 2 * rows // n
    blocks = rows // take
    first, last = t == 0, t == STEPS - 1

    def placed(i, me_ref):
        z, y = i // 2, i % 2
        mine = (y == (me_ref[0] // 2) % 2).astype(jnp.int32)
        return (mine * (blocks // 2) + z, 0)

    vmem = pl.BlockSpec(memory_space=pltpu.VMEM)
    in_specs = [vmem] * 2 + [
        pl.BlockSpec((None, take, c), lambda i, *_: (t, i, 0)),
        pl.BlockSpec((1, take, c), lambda i, *_: (t, i, 0)),
        whole(a_log.shape),
        whole((1, c)),
    ]
    scratch = [
        pltpu.VMEM((STATE, c), F32),
        pltpu.VMEM((2 * STATE, 16, 128), F32),
    ]
    flat = pl.BlockSpec((STATE, take, c), lambda i, *_: (0, i, 0))
    if first:
        in_specs = in_specs + [pl.BlockSpec(memory_space=pl.ANY)]
        scratch += [
            pltpu.VMEM((2, c // 128, take * STATE, 128), F32),
            pltpu.SemaphoreType.DMA((2, c // 128)),
        ]
    else:
        in_specs = in_specs + [flat]
    in_specs = [pl.BlockSpec(memory_space=pl.ANY)] * len(after) + in_specs
    out_specs = [pl.BlockSpec((take, c), placed)]
    out_shape = [jax.ShapeDtypeStruct((rows, c), BF16)]
    if not last:
        out_specs = [flat] + out_specs
        out_shape = [jax.ShapeDtypeStruct((STATE, rows, c), BF16)] + out_shape
    size = rows * STATE * c
    out = pl.pallas_call(
        functools.partial(state_kernel, t, len(after)),
        grid_spec=pltpu.PrefetchScalarGridSpec(
            num_scalar_prefetch=1,
            grid=(blocks,),
            in_specs=in_specs,
            out_specs=out_specs,
            scratch_shapes=scratch,
        ),
        out_shape=out_shape,
        compiler_params=params(48),
        cost_estimate=cost(8 * size, 4 * size, size),
        name="state_step",
    )(me, *after, *steps, conv, step_z, a_log, d_skip, state)
    return (None, out[0]) if last else (out[0], out[1])


def gather_kernel(me_ref, after_ref, row_ref, *refs):
    lows, refs = refs[:4], refs[4:]
    conv_ref, z_ref, dtp_ref, dtb_ref, o_ref, low_scr = refs
    count = o_ref.shape[1]
    _, rows, c = conv_ref.shape
    hot = (row_ref[:, :1] == lax.broadcasted_iota(jnp.int32, (count, rows), 1)).astype(F32).astype(BF16)
    for t in range(STEPS):
        low = jnp.dot(hot, assemble_low(lows, t, low_scr, me_ref), preferred_element_type=F32)
        o_ref[t, :, :c] = step_sizes(low.astype(BF16), dtp_ref, dtb_ref)
        o_ref[t, :, 3 * c :] = low[:, DT_RANK:]
        conv = conv_ref[t]
        high = conv.astype(BF16)
        rest = (conv - high.astype(F32)).astype(BF16)
        o_ref[t, :, c : 2 * c] = jnp.dot(hot, high, preferred_element_type=F32) + jnp.dot(
            hot, rest, preferred_element_type=F32
        )
        z = jnp.dot(hot, z_ref[t], preferred_element_type=F32)
        o_ref[t, :, 2 * c : 3 * c] = z * sigmoid(z)


def gather_live(me, after, row_of_live, lows, conv, step_z, dt_proj, dt_bias, n):
    _, rows, c = conv.shape
    count = row_of_live.shape[0]
    (out,) = small(
        gather_kernel,
        me,
        [row_of_live, *lows, conv, step_z, dt_proj, dt_bias],
        [(STEPS, count, 3 * c + 128)],
        "gather_live",
        after,
        F32,
        [pltpu.VMEM((n // 4, 2, 2, rows // n, WIDE), BF16)],
        40,
    )
    return out


def live_kernel(slot_ref, after_ref, moved_ref, live_ref, alog_ref, skip_ref, o_ref, buf, state_scr):
    _, count, c = o_ref.shape
    def place(i, carry):
        source, slot = slot_ref[0, i], slot_ref[1, i]
        at = pl.multiple_of(i * STATE, STATE)
        from_row = pl.multiple_of(slot * STATE, STATE)
        value = moved_ref[source, pl.ds(from_row, STATE), :].astype(F32)
        for l in range(c // 128):
            buf[l, pl.ds(at, STATE), :] = value[:, 128 * l : 128 * (l + 1)]
        return carry

    lax.fori_loop(0, count, place, 0)
    for s in range(STATE):
        for l in range(c // 128):
            state_scr[s, :, 128 * l : 128 * (l + 1)] = buf[l, pl.ds(s, count, stride=STATE), :]
    tall, lanes = 16, min(512, c)

    def step_all(t, carry):
        for r in range(0, count, tall):
            tail = live_ref[t, r : r + tall, 3 * c :]
            for l in range(0, c, lanes):
                cols = slice(l, l + lanes)
                step = live_ref[t, r : r + tall, cols]
                conv = live_ref[t, r : r + tall, c + l : c + l + lanes]
                gate = live_ref[t, r : r + tall, 2 * c + l : 2 * c + l + lanes]
                drive = step * conv
                total = skip_ref[:, cols] * conv
                for s in range(STATE):
                    rate = -jnp.exp(alog_ref[s : s + 1, cols])
                    old = state_scr[s, r : r + tall, cols]
                    state = jnp.exp(step * rate) * old + drive * tail[:, s : s + 1]
                    state_scr[s, r : r + tall, cols] = state
                    total = total + state * tail[:, STATE + s : STATE + s + 1]
                o_ref[t, r : r + tall, cols] = (total * gate).astype(BF16)
        return carry

    lax.fori_loop(0, STEPS, step_all, 0)


def live_steps(slot_of_live, after, moved, gathered, a_log, d_skip):
    count, c = gathered.shape[1], a_log.shape[1]
    (out,) = small(
        live_kernel,
        slot_of_live,
        [moved, gathered, a_log, d_skip],
        [(STEPS, count, c)],
        "live_steps",
        after,
        BF16,
        [pltpu.VMEM((c // 128, count * STATE, 128), F32), pltpu.VMEM((STATE, count, c), F32)],
        40,
    )
    return out


def fix_kernel(t, take, me_ref, after_ref, row_ref, gated_ref, live_ref, o_ref):
    rows = gated_ref.shape[0]
    count = live_ref.shape[1]
    shift = take.bit_length() - 1
    place = lax.broadcasted_iota(jnp.int32, (rows, count), 0)
    mine = place >= rows // 2
    within = place - jnp.where(mine, rows // 2, 0)
    y = (me_ref[0] // 2) % 2
    row = ((2 * (within >> shift) + jnp.where(mine, y, 1 - y)) << shift) + (within & (take - 1))
    hot = (row == row_ref[...]).astype(F32)
    taken = jnp.max(hot, axis=1, keepdims=True) > 0.0
    live = jnp.dot(hot.astype(BF16), live_ref[t], preferred_element_type=F32)
    o_ref[...] = jnp.where(taken, live, gated_ref[...].astype(F32)).astype(BF16)


def out_kernel(me_ref, own_ref, other_ref, wown_ref, wother_ref, *refs):
    send_ref, keep_ref = refs[-2:]
    total = jnp.dot(own_ref[...], wown_ref[...], preferred_element_type=F32)
    total = total + jnp.dot(other_ref[...], wother_ref[...], preferred_element_type=F32)
    half = send_ref.shape[0]
    send_ref[...] = total[:half].astype(BF16)
    keep_ref[...] = total[half:].astype(BF16)


def out_project(me, own, other, out_weight, other_weight, after, part, parts):
    rows, c = own.shape
    tile = 1024
    every = out_weight.shape[1] // 2 // tile
    tiles = every // parts
    cols = tiles * tile
    first = part * tiles
    half = jax.ShapeDtypeStruct((rows // 2, cols), BF16)
    return pl.pallas_call(
        out_kernel,
        grid_spec=pltpu.PrefetchScalarGridSpec(
            num_scalar_prefetch=1,
            grid=(tiles,),
            in_specs=[
                pl.BlockSpec(memory_space=pltpu.VMEM),
                pl.BlockSpec(memory_space=pltpu.VMEM),
                pl.BlockSpec((c, tile), lambda j, me_ref: (0, (me_ref[0] % 2) * every + first + j)),
                pl.BlockSpec((c, tile), lambda j, me_ref: (0, first + j)),
            ]
            + [pl.BlockSpec(memory_space=pl.ANY)] * len(after),
            out_specs=[pl.BlockSpec((rows // 2, tile), lambda j, me_ref: (0, j))] * 2,
        ),
        out_shape=[half, half],
        compiler_params=params(48),
        cost_estimate=cost(4 * rows * c * cols, 4 * c * cols + 2 * rows * cols),
        name="out_project",
    )(me, own, other, out_weight, other_weight, *after)


def halve_kernel(stage, me_ref, after_ref, keep_ref, got_ref, send_ref, left_ref):
    bit = (me_ref[0] >> (2 + stage)) & 1
    for i in range(send_ref.shape[0]):
        for o_ref, at in ((send_ref, 2 * i + 1 - bit), (left_ref, 2 * i + bit)):
            o_ref[i] = (keep_ref[at].astype(F32) + got_ref[at].astype(F32)).astype(BF16)


def sum_z_kernel(me_ref, after_ref, keep_ref, got_ref, send_ref, left_ref):
    total = keep_ref[0].astype(F32) + got_ref[0].astype(F32)
    own = total.shape[0] // 2
    low, high = total[:own], total[own:]
    core = me_ref[0] % 2
    send_ref[...] = jnp.where(core == 0, high, low).astype(BF16)
    left_ref[...] = jnp.where(core == 0, low, high).astype(BF16)


def final_kernel(tiles, counts, me_ref, *refs):
    o_ref = refs[-1]
    own_half = pl.program_id(0) // tiles == me_ref[0] % 2
    tile = pl.program_id(0) % tiles
    at = 0
    for t, count in enumerate(counts):
        value = None
        for part in range(count):
            mine, theirs = refs[at][...].astype(F32), refs[at + 1][...].astype(F32)
            here = jnp.where(own_half, mine, theirs)
            value = here if value is None else jnp.where(tile == part, here, value)
            at += 2
        o_ref[:, t, :] = value.astype(BF16)


def final_join(me, pieces):
    own = pieces[0][0][0].shape[0]
    cols = sum(keep.shape[1] for keep, _ in pieces[0])
    tiles = max(len(parts) for parts in pieces)
    tile = cols // tiles
    args, specs = [], []
    for parts in pieces:
        for keep, got in parts:
            many = keep.shape[1] // tile
            spec = pl.BlockSpec((own, tile), lambda j, me_ref, many=many: (0, (j % tiles) % many))
            args += [keep, got]
            specs += [spec, spec]
    return pl.pallas_call(
        functools.partial(final_kernel, tiles, [len(parts) for parts in pieces]),
        grid_spec=pltpu.PrefetchScalarGridSpec(
            num_scalar_prefetch=1,
            grid=(2 * tiles,),
            in_specs=specs,
            out_specs=pl.BlockSpec((own, STEPS, tile), lambda j, me_ref: (0, 0, j)),
        ),
        out_shape=jax.ShapeDtypeStruct((own, STEPS, 2 * cols), BF16),
        compiler_params=params(16),
        cost_estimate=cost(0, own * cols * 32),
        name="final_join",
    )(me, *args)


def shards(
    resident_state,
    resident_conv,
    prefilled_state,
    prefilled_conv,
    live_counts,
    batch_rows,
    step_x,
    step_z,
    conv_weight,
    conv_bias,
    x_proj,
    norm_gain,
    dt_proj,
    dt_bias,
    a_log,
    d_skip,
    out_weight,
):
    n = lax.axis_size("dex")
    zs = n // 4
    rows = resident_state.shape[0]
    slots = prefilled_state.shape[0]
    c = resident_state.shape[2]
    me_scalar = lax.axis_index("dex").astype(jnp.int32)
    me = me_scalar.reshape(1)

    moved_conv = exchange_conv(prefilled_conv, me, n)
    half_weight = weight_half(me, moved_conv[1], out_weight)
    packed = pack_state((half_weight,), prefilled_state, n)
    cols = out_weight.shape[1] // 2

    is_live = jnp.arange(slots, dtype=jnp.int32)[None, :] < live_counts[:, None]
    target = jnp.where(is_live, batch_rows.reshape(n, slots), -1)
    place = jnp.arange(TAPS + 1, dtype=jnp.int32)
    mine = place[None, None, :, None] == place[:, None, None, None]
    spread = jnp.where(mine, target[None, :, None, :], -1).reshape(TAPS + 1, n * (TAPS + 1) * slots)
    flat = target.reshape(-1)
    number = jnp.arange(n * slots, dtype=jnp.int32)
    count = n * slots // 2
    rank = jnp.sum(((flat >= 0)[None, :] & (number[None, :] < number[:, None])).astype(jnp.int32), axis=1)
    hit = (rank[None, :] == number[:count, None]) & (flat >= 0)[None, :]
    live_slot = jnp.sum(jnp.where(hit, number[None, :], 0), axis=1)
    live_row = jnp.sum(jnp.where(hit, flat[None, :], 0), axis=1)
    slot_of_live = jnp.stack([live_slot // slots, live_slot % slots])
    row_of_live = jnp.broadcast_to(live_row[:, None], (count, 128))
    live_row = live_row.reshape(1, count)
    gain = jnp.concatenate([norm_gain, jnp.zeros((WIDE - norm_gain.shape[0],), F32)]).reshape(1, WIDE)
    old = jnp.transpose(resident_conv, (1, 0, 2))
    proj = x_proj.T
    bias = conv_bias.reshape(1, c)
    conv, send, keep = conv_steps(
        tuple(range(STEPS)), n, me, (packed,), spread, old, moved_conv, step_x, conv_weight, bias, proj
    )
    behind, merged, lows = reduce_projection(send, keep, gain, me, n)
    packed = hold(packed, merged)
    moved_state = lax.all_to_all(packed, "dex", 0, 0, tiled=True)
    other_weight = swap(hold(half_weight, behind), 1, n)

    state = resident_state.reshape(rows * STATE, c)
    sends, keeps, gated = {}, {}, {}
    stages = zs.bit_length() - 1
    take = 2 * rows // n

    rate_bias, skip = dt_bias.reshape(1, c), d_skip.reshape(1, c)

    next_steps = None

    def s_step(t, after):
        nonlocal state
        if t == 0:
            steps = step_rows(0, me, after, lows, dt_proj, rate_bias, rows, n)
        else:
            steps = next_steps
        state, gated[t] = state_step(t, me, after, steps, conv, step_z, a_log, skip, state, n)
        return gated[t]

    def fix(t, after):
        kernel = functools.partial(fix_kernel, t, take)
        (gated[t],) = small(kernel, me, [live_row, gated[t], live_gated], [(rows, c)], "fix", (after,))
        if t == STEPS - 1:
            return gated[t]
        nonlocal next_steps
        next_steps = step_rows(t + 1, me, (gated[t],), lows, dt_proj, rate_bias, rows, n)
        return next_steps[1]

    def project(t, after, parts=1):
        other = swap(gated[t], 1, n)
        for part in range(parts):
            sends[t, part], keeps[t, part] = out_project(
                me, gated[t], other, out_weight, other_weight, (after,), part, parts
            )
            after = keeps[t, part]
        return after

    def reduce(t, stage, after, part=0):
        at = t, part
        width = keeps[at].shape[-1]
        if stage == 0:
            keep = keeps[at].reshape(zs, take, width)
            got = swap(sends[at], 2, n).reshape(zs, take, width)
        else:
            keep, got = keeps[at], swap(sends[at], 2 << stage, n)
        if stage < stages:
            kernel, shape = functools.partial(halve_kernel, stage), (keep.shape[0] // 2, take, width)
        else:
            kernel, shape = sum_z_kernel, (take // 2, width)
        sends[at], keeps[at] = small(kernel, me, [keep, got], [shape] * 2, "reduce_%d" % stage, (after,))
        if stage == stages:
            sends[at] = swap(sends[at], 1, n)
        return keeps[at]

    last = s_step(0, (packed,))
    gathered = gather_live(me, (last,), row_of_live, lows, conv, step_z, dt_proj, rate_bias, n)
    live_gated = live_steps(slot_of_live, (last,), moved_state, gathered, a_log, skip)
    last = fix(0, live_gated)
    last = project(0, last)
    for t in range(1, STEPS):
        last = s_step(t, (last,))
        last = fix(t, last)
        if t > 1:
            for stage in range(1, stages):
                last = reduce(t - 2, stage, last)
        last = project(t, last, 1 if t < STEPS - 1 else 2)
        if t < STEPS - 1:
            last = reduce(t - 1, 0, last)
    last = reduce(t - 3, stages, last)
    last = reduce(t - 1, 0, last)
    last = reduce(t, 0, last, 0)
    for stage in range(1, stages):
        last = reduce(t - 1, stage, last)
    last = reduce(t - 2, stages, last)
    for stage in range(1, stages):
        last = reduce(t, stage, last, 0)
    last = reduce(t, 0, last, 1)
    last = reduce(t - 1, stages, last)
    for stage in range(1, stages):
        last = reduce(t, stage, last, 1)
    last = reduce(t, stages, last, 0)
    last = reduce(t, stages, last, 1)
    pieces = [[(keeps[t, part], sends[t, part]) for part in range(1 if t < STEPS - 1 else 2)] for t in range(STEPS)]
    return final_join(me, pieces)


def solution(mesh):
    placed = (
        P("grp", None, "dex"),
        P("grp", None, "dex"),
        P(("grp", "dex"), None, None),
        P(("grp", "dex"), None, None),
        P("grp"),
        P("grp"),
        P(None, "grp", "dex"),
        P(None, "grp", "dex"),
        P(None, "dex"),
        P("dex"),
        P("dex", None),
        P(),
        P(None, "dex"),
        P("dex"),
        P(None, "dex"),
        P("dex"),
        P("dex", None),
    )
    return jax.shard_map(
        shards, mesh=mesh, in_specs=placed, out_specs=P(("grp", "dex"), None, None), check_vma=False
    )
```

```python
import functools

import jax
import jax.numpy as jnp
from jax import lax
from jax.experimental import pallas as pl
from jax.experimental.pallas import tpu as pltpu
from jax.sharding import PartitionSpec as P

STATE = 16
DT_RANK = 512
STEPS = 4
TAPS = 3
WIDE = DT_RANK + 128

RMS_EPS = 1e-06
BC_FLOOR = 0.2

BF16 = jnp.bfloat16
F32 = jnp.float32


def params(mib):
    return pltpu.CompilerParams(vmem_limit_bytes=mib * 1024 * 1024)


def swap(x, mask, n):
    return lax.ppermute(x, "dex", [(i, i ^ mask) for i in range(n)])


def cost(flops, bytes_accessed, transcendentals=0):
    return pl.CostEstimate(flops=1024, bytes_accessed=1024, transcendentals=0)


def sigmoid(x):
    return 1.0 / (1.0 + jnp.exp(-x))


def whole(shape):
    zeros = (0,) * len(shape)
    return pl.BlockSpec(shape, lambda *_: zeros)


def small(kernel, me, args, shapes, name, after=(), dtype=BF16, scratch=(), mib=8):
    size = sum(a.size for a in args)
    vmem = pl.BlockSpec(memory_space=pltpu.VMEM)
    return pl.pallas_call(
        kernel,
        in_specs=[pl.BlockSpec(memory_space=pltpu.SMEM)]
        + [pl.BlockSpec(memory_space=pl.ANY)] * len(after)
        + [vmem] * len(args),
        out_specs=[vmem] * len(shapes),
        out_shape=[jax.ShapeDtypeStruct(s, dtype) for s in shapes],
        scratch_shapes=list(scratch),
        compiler_params=params(mib),
        cost_estimate=cost(size, 4 * size),
        name=name,
    )(me, *after, *args)


def pack_conv_kernel(me_ref, x_ref, *o_refs):
    zs, _, wide = o_refs[0].shape
    y, core = (me_ref[0] // 2) % 2, me_ref[0] % 2
    c = wide * (TAPS + 1) // TAPS
    for i, o_ref in enumerate(o_refs):
        for z in range(zs):
            dest = 4 * z + 2 * jnp.bitwise_xor(y, i % 2) + jnp.bitwise_xor(core, i // 2)
            x = x_ref[:, :, pl.ds(pl.multiple_of(dest * c, 128), c)]
            parts = [x[p, :, :wide] for p in range(TAPS)]
            parts.append(jnp.concatenate([x[p, :, wide:] for p in range(TAPS)], axis=1))
            o_ref[z] = jnp.concatenate(parts, axis=0).astype(BF16)


def cut_conv_kernel(me_ref, *refs):
    zs = refs[0].shape[0]
    z, y, core = me_ref[0] // 4, (me_ref[0] // 2) % 2, me_ref[0] % 2
    for m in range(zs):
        for i in range(4):
            at = 2 * jnp.bitwise_xor(y, i % 2) + jnp.bitwise_xor(core, i // 2)
            refs[4 + m][at] = refs[i][jnp.bitwise_xor(z, m)]


def exchange_conv(prefilled_conv, me, n):
    slots, _, inner = prefilled_conv.shape
    zs = n // 4
    piece = ((TAPS + 1) * slots, inner // n * TAPS // (TAPS + 1))
    conv = jnp.transpose(prefilled_conv, (1, 0, 2))
    packed = small(pack_conv_kernel, me, [conv], [(zs,) + piece] * 4, "pack_conv")
    near, far = swap(packed[2], 1, n), swap(packed[3], 1, n)
    got = [packed[0], swap(packed[1], 2, n), near, swap(far, 2, n)]
    cut = small(cut_conv_kernel, me, got, [(4,) + piece] * zs, "cut_conv")
    return [cut[0]] + [swap(cut[m], 4 * m, n) for m in range(1, zs)]


def pack_state_kernel(x_ref, *refs):
    o_ref = refs[-1]
    slots = x_ref.shape[0]
    some, _, c = o_ref.shape
    for d in range(some):
        for k in range(slots):
            o_ref[d, STATE * k : STATE * (k + 1), :] = x_ref[k, :, d * c : (d + 1) * c].astype(BF16)


def pack_state(after, prefilled_state, n):
    slots, _, inner = prefilled_state.shape
    c = inner // n
    some = 4
    return pl.pallas_call(
        pack_state_kernel,
        grid=(n // some,),
        in_specs=[pl.BlockSpec((slots, STATE, some * c), lambda d: (0, 0, d))]
        + [pl.BlockSpec(memory_space=pl.ANY)] * len(after),
        out_specs=pl.BlockSpec((some, slots * STATE, c), lambda d: (d, 0, 0)),
        out_shape=jax.ShapeDtypeStruct((n, slots * STATE, c), BF16),
        compiler_params=params(24),
        cost_estimate=cost(0, slots * STATE * inner * 6),
        name="pack_state",
    )(prefilled_state, *after)


def hold_kernel(x_ref, after_ref, o_ref):
    pass


def hold(x, after):
    some = pl.BlockSpec(memory_space=pl.ANY)
    return pl.pallas_call(
        hold_kernel,
        in_specs=[some, some],
        out_specs=some,
        out_shape=jax.ShapeDtypeStruct(x.shape, x.dtype),
        input_output_aliases={0: 0},
        compiler_params=params(8),
        cost_estimate=cost(0, 0),
        name="hold",
    )(x, after)


def half_kernel(me_ref, after_ref, w_ref, o_ref):
    o_ref[...] = w_ref[...]


def weight_half(me, after, out_weight):
    c, cols = out_weight.shape
    tile = 1024
    tiles = cols // 2 // tile
    return pl.pallas_call(
        half_kernel,
        grid_spec=pltpu.PrefetchScalarGridSpec(
            num_scalar_prefetch=1,
            grid=(tiles,),
            in_specs=[
                pl.BlockSpec(memory_space=pl.ANY),
                pl.BlockSpec((c, tile), lambda j, me_ref: (0, (1 - me_ref[0] % 2) * tiles + j)),
            ],
            out_specs=pl.BlockSpec((c, tile), lambda j, me_ref: (0, j)),
        ),
        out_shape=jax.ShapeDtypeStruct((c, cols // 2), BF16),
        compiler_params=params(56),
        cost_estimate=cost(0, 2 * c * cols),
        name="weight_half",
    )(me, after, out_weight)


def conv_kernel(steps, n, me_ref, target_ref, old_ref, x_ref, w_ref, bias_ref, proj_ref, *refs):
    zs = n // 4
    moved, (conv_ref, send_ref, keep_ref, moved_scr, win) = refs[:zs], refs[-5:]
    rows, c = win.shape[1:]
    columns = target_ref.shape[1]
    own = rows // n
    core, my_z = me_ref[0] % 2, me_ref[0] // 4
    for m in range(zs):
        moved_scr[jnp.bitwise_xor(my_z, m)] = moved[m][...]
    fresh = moved_scr[...].reshape(columns, moved_scr.shape[3])
    wide = fresh.shape[1]
    row_id = lax.broadcasted_iota(jnp.int32, (rows, columns), 0)
    hots = [row_id == target_ref[p : p + 1, :] for p in range(TAPS + 1)]
    taken = jnp.max(hots[0].astype(F32), axis=1, keepdims=True) > 0.0
    fresh = [jnp.dot(hot.astype(BF16), fresh, preferred_element_type=F32) for hot in hots]
    for p in range(TAPS):
        part = (c - wide) * p
        win[p, :, :wide] = jnp.where(taken, fresh[p], old_ref[p, :, :wide])
        win[p, :, wide:] = jnp.where(taken, fresh[TAPS][:, part : part + c - wide], old_ref[p, :, wide:])
    for i, t in enumerate(steps):
        total = None
        for q in range(TAPS + 1):
            place = t + q
            value = win[place] if place < TAPS else x_ref[place - TAPS].astype(F32)
            term = value * w_ref[q : q + 1, :]
            total = term if total is None else total + term
        total = total + bias_ref[...]
        conv_out = total * sigmoid(total)
        conv_ref[i] = conv_out
        part = lax.dot_general(
            conv_out.astype(BF16), proj_ref[...], (((1,), (1,)), ((), ())), preferred_element_type=F32
        )
        pad = jnp.zeros((own, WIDE - part.shape[1]), BF16)
        for q in range(n // 2):
            low = part[2 * q * own : (2 * q + 1) * own, :]
            high = part[(2 * q + 1) * own : (2 * q + 2) * own, :]
            send_ref[q, i, :, : part.shape[1]] = jnp.where(core == 0, high, low).astype(BF16)
            keep_ref[q, i, :, : part.shape[1]] = jnp.where(core == 0, low, high).astype(BF16)
            send_ref[q, i, :, part.shape[1] :] = pad
            keep_ref[q, i, :, part.shape[1] :] = pad


def conv_steps(steps, n, me, after, target, old, moved, step_x, conv_weight, conv_bias, proj):
    _, rows, c = old.shape
    s = len(steps)
    last = max(steps) + 1
    parts = (n // 2, s, rows // n, WIDE)
    return pl.pallas_call(
        functools.partial(conv_kernel, steps, n),
        grid_spec=pltpu.PrefetchScalarGridSpec(
            num_scalar_prefetch=1,
            grid=(1,),
            in_specs=[
                whole(target.shape),
                whole(old.shape),
                whole((last, rows, c)),
                whole(conv_weight.shape),
                whole((1, c)),
                whole(proj.shape),
            ]
            + [whole(moved[0].shape)] * len(moved)
            + [pl.BlockSpec(memory_space=pl.ANY)] * len(after),
            out_specs=[whole((s, rows, c)), whole(parts), whole(parts)],
            scratch_shapes=[
                pltpu.VMEM((len(moved),) + moved[0].shape, BF16),
                pltpu.VMEM((TAPS, rows, c), F32),
            ],
        ),
        out_shape=[jax.ShapeDtypeStruct((s, rows, c), F32)] + [jax.ShapeDtypeStruct(parts, BF16)] * 2,
        compiler_params=params(40),
        cost_estimate=cost(2 * s * rows * c * 544, rows * c * (12 + 6 * s) + c * 1088, s * rows * c),
        name="conv_project",
    )(me, target, old, step_x, conv_weight, conv_bias, proj, *moved, *after)


def add_y_kernel(me_ref, *refs):
    keep_ref, got_ref, send_ref, left_ref = refs[-4:]
    y = (me_ref[0] // 2) % 2
    for z in range(send_ref.shape[0]):
        for o_ref, at in ((send_ref, 2 * z + 1 - y), (left_ref, 2 * z + y)):
            o_ref[z] = (keep_ref[at].astype(F32) + got_ref[at].astype(F32)).astype(BF16)


def add_z_kernel(zs, me_ref, *refs):
    keep_ref, got_ref, *o_refs = refs[-2 - zs :]
    z = me_ref[0] // 4
    for m, o_ref in enumerate(o_refs):
        at = jnp.bitwise_xor(z, m)
        o_ref[...] = (keep_ref[at].astype(F32) + got_ref[at].astype(F32)).astype(BF16)


def norm_kernel(me_ref, gain_ref, *refs):
    o_ref = refs[-1]
    total = refs[0][...].astype(F32)
    for ref in refs[1:-1]:
        total = total + ref[...].astype(F32)
    dt = total[:, :, :DT_RANK]
    dt = dt * lax.rsqrt(jnp.mean(dt * dt, axis=2, keepdims=True) + RMS_EPS) * gain_ref[:, :DT_RANK][None]
    tail = total[:, :, DT_RANK:]
    lane = lax.broadcasted_iota(jnp.int32, tail.shape, 2)
    square = tail * tail
    is_b = lane < STATE
    is_c = jnp.logical_and(lane >= STATE, lane < 2 * STATE)
    mean_b = jnp.sum(jnp.where(is_b, square, 0.0), axis=2, keepdims=True) / STATE
    mean_c = jnp.sum(jnp.where(is_c, square, 0.0), axis=2, keepdims=True) / STATE
    scale_b = lax.rsqrt(jnp.maximum(mean_b, BC_FLOOR))
    scale_c = lax.rsqrt(jnp.maximum(mean_c, BC_FLOOR))
    tail = tail * jnp.where(is_b, scale_b, scale_c) * gain_ref[:, DT_RANK:][None]
    o_ref[:, :, :DT_RANK] = dt.astype(BF16)
    o_ref[:, :, DT_RANK:] = jnp.where(lane < 2 * STATE, tail, 0.0).astype(BF16)


def merge_kernel(me_ref, *refs):
    o_ref = refs[-1]
    z = me_ref[0] // 4
    for m, ref in enumerate(refs[:-1]):
        o_ref[jnp.bitwise_xor(z, m)] = ref[...]


def reduce_projection(send, keep, gain, me, n):
    zs = n // 4
    piece = keep.shape[1:]
    got = swap(send, 1, n)
    send, keep = small(add_y_kernel, me, [keep, got], [(zs,) + piece] * 2, "add_y")
    got = swap(send, 2, n)
    cut = small(functools.partial(add_z_kernel, zs), me, [keep, got], [piece] * zs, "add_z")
    cut = [cut[0]] + [swap(cut[m], 4 * m, n) for m in range(1, zs)]
    (low,) = small(norm_kernel, me, [gain] + cut, [piece], "norm")
    lows = [low] + [swap(low, 4 * m, n) for m in range(1, zs)]
    (mine,) = small(merge_kernel, me, lows, [(zs,) + piece], "merge_z")
    beside = swap(mine, 2, n)
    return keep, low, mine, (mine, beside, swap(mine, 1, n), swap(beside, 1, n))


def assemble_low(lows, index, low_scr, me_ref):
    y, core = (me_ref[0] // 2) % 2, me_ref[0] % 2
    for i, low_ref in enumerate(lows):
        for z in range(low_ref.shape[0]):
            low_scr[z, jnp.bitwise_xor(y, i % 2), jnp.bitwise_xor(core, i // 2)] = low_ref[z, index]
    return low_scr[...].reshape(-1, WIDE)


def step_sizes(low, dtp_ref, dtb_ref):
    pre = jnp.dot(low[:, :DT_RANK], dtp_ref[...], preferred_element_type=F32) + dtb_ref[...]
    return jnp.maximum(pre, 0.0) + jnp.log(1.0 + jnp.exp(-jnp.abs(pre)))


def step_kernel(t, me_ref, after_ref, *refs):
    *lows, dtp_ref, dtb_ref, step_ref, tail_ref, low_scr = refs
    low = assemble_low(lows, t, low_scr, me_ref)
    step_ref[...] = step_sizes(low, dtp_ref, dtb_ref)
    tail_ref[...] = low[:, DT_RANK:].astype(F32)


def step_rows(t, me, after, lows, dt_proj, dt_bias, rows, n):
    return small(
        functools.partial(step_kernel, t),
        me,
        [*lows, dt_proj, dt_bias],
        [(rows, dt_proj.shape[1]), (rows, 128)],
        "step_rows",
        after,
        F32,
        [pltpu.VMEM((n // 4, 2, 2, rows // n, WIDE), BF16)],
        12,
    )


def state_kernel(t, behind, me_ref, *refs):
    first, last = t == 0, t == STEPS - 1
    refs = refs[behind:]
    step_ref, tail_ref, conv_ref, z_ref, alog_ref, skip_ref, state_ref, *refs = refs
    new_ref = None
    if not last:
        new_ref, *refs = refs
    gated_ref, decay_scr, bc_scr, *refs = refs
    block = pl.program_id(0)
    rows, c = step_ref.shape
    take = conv_ref.shape[0]
    blocks = rows // take

    if first:
        buf, sems = refs

        def fetch(at, slot):
            first_row = pl.multiple_of(at * (take * STATE), take * STATE)
            return [
                pltpu.make_async_copy(
                    state_ref.at[pl.ds(first_row, take * STATE), 128 * l : 128 * (l + 1)],
                    buf.at[slot, l],
                    sems.at[slot, l],
                )
                for l in range(c // 128)
            ]

        now = lax.rem(block, 2)

        @pl.when(block == 0)
        def _():
            for copy in fetch(0, 0):
                copy.start()

        @pl.when(block + 1 < blocks)
        def _():
            for copy in fetch(block + 1, 1 - now):
                copy.start()

    @pl.when(block == 0)
    def _():
        decay_scr[...] = -jnp.exp(alog_ref[...])

    base = block * take
    if first:
        for copy in fetch(block, now):
            copy.wait()

    tall, lanes = 16, min(256, c)
    for r in range(0, take, tall):
        tail = tail_ref[pl.ds(pl.multiple_of(base + r, tall), tall), :]
        for s in range(2 * STATE):
            bc_scr[s] = jnp.broadcast_to(tail[:, s : s + 1], (tall, 128))
        for l in range(0, c, lanes):
            cols = slice(l, l + lanes)
            step = step_ref[pl.ds(pl.multiple_of(base + r, tall), tall), cols]
            conv = conv_ref[r : r + tall, cols]
            drive = step * conv
            total = skip_ref[:, cols] * conv
            for s in range(STATE):
                if first:
                    at = pl.ds(STATE * r + s, tall, stride=STATE)
                    tiles = range(l // 128, (l + lanes) // 128)
                    old = jnp.concatenate([buf[now, k, at, :] for k in tiles], axis=1)
                else:
                    old = state_ref[s, r : r + tall, cols].astype(F32)
                b = jnp.concatenate([bc_scr[s]] * (lanes // 128), axis=1)
                g = jnp.concatenate([bc_scr[STATE + s]] * (lanes // 128), axis=1)
                state = jnp.exp(step * decay_scr[s : s + 1, cols]) * old + drive * b
                if not last:
                    new_ref[s, r : r + tall, cols] = state.astype(BF16)
                total = total + state * g
            z = z_ref[0, r : r + tall, cols].astype(F32)
            gated_ref[r : r + tall, cols] = (total * (z * sigmoid(z))).astype(BF16)


def state_step(t, me, after, steps, conv, step_z, a_log, d_skip, state, n):
    _, rows, c = conv.shape
    take = 2 * rows // n
    blocks = rows // take
    first, last = t == 0, t == STEPS - 1

    def placed(i, me_ref):
        z, y = i // 2, i % 2
        mine = (y == (me_ref[0] // 2) % 2).astype(jnp.int32)
        return (mine * (blocks // 2) + z, 0)

    vmem = pl.BlockSpec(memory_space=pltpu.VMEM)
    in_specs = [vmem] * 2 + [
        pl.BlockSpec((None, take, c), lambda i, *_: (t, i, 0)),
        pl.BlockSpec((1, take, c), lambda i, *_: (t, i, 0)),
        whole(a_log.shape),
        whole((1, c)),
    ]
    scratch = [
        pltpu.VMEM((STATE, c), F32),
        pltpu.VMEM((2 * STATE, 16, 128), F32),
    ]
    flat = pl.BlockSpec((STATE, take, c), lambda i, *_: (0, i, 0))
    if first:
        in_specs = in_specs + [pl.BlockSpec(memory_space=pl.ANY)]
        scratch += [
            pltpu.VMEM((2, c // 128, take * STATE, 128), F32),
            pltpu.SemaphoreType.DMA((2, c // 128)),
        ]
    else:
        in_specs = in_specs + [flat]
    in_specs = [pl.BlockSpec(memory_space=pl.ANY)] * len(after) + in_specs
    out_specs = [pl.BlockSpec((take, c), placed)]
    out_shape = [jax.ShapeDtypeStruct((rows, c), BF16)]
    if not last:
        out_specs = [flat] + out_specs
        out_shape = [jax.ShapeDtypeStruct((STATE, rows, c), BF16)] + out_shape
    size = rows * STATE * c
    out = pl.pallas_call(
        functools.partial(state_kernel, t, len(after)),
        grid_spec=pltpu.PrefetchScalarGridSpec(
            num_scalar_prefetch=1,
            grid=(blocks,),
            in_specs=in_specs,
            out_specs=out_specs,
            scratch_shapes=scratch,
        ),
        out_shape=out_shape,
        compiler_params=params(48),
        cost_estimate=cost(8 * size, 4 * size, size),
        name="state_step",
    )(me, *after, *steps, conv, step_z, a_log, d_skip, state)
    return (None, out[0]) if last else (out[0], out[1])


def gather_kernel(me_ref, after_ref, row_ref, *refs):
    lows, refs = refs[:4], refs[4:]
    conv_ref, z_ref, dtp_ref, dtb_ref, o_ref, low_scr = refs
    count = o_ref.shape[1]
    _, rows, c = conv_ref.shape
    hot = (row_ref[:, :1] == lax.broadcasted_iota(jnp.int32, (count, rows), 1)).astype(F32).astype(BF16)
    for t in range(STEPS):
        low = jnp.dot(hot, assemble_low(lows, t, low_scr, me_ref), preferred_element_type=F32)
        o_ref[t, :, :c] = step_sizes(low.astype(BF16), dtp_ref, dtb_ref)
        o_ref[t, :, 3 * c :] = low[:, DT_RANK:]
        conv = conv_ref[t]
        high = conv.astype(BF16)
        rest = (conv - high.astype(F32)).astype(BF16)
        o_ref[t, :, c : 2 * c] = jnp.dot(hot, high, preferred_element_type=F32) + jnp.dot(
            hot, rest, preferred_element_type=F32
        )
        z = jnp.dot(hot, z_ref[t], preferred_element_type=F32)
        o_ref[t, :, 2 * c : 3 * c] = z * sigmoid(z)


def gather_live(me, after, row_of_live, lows, conv, step_z, dt_proj, dt_bias, n):
    _, rows, c = conv.shape
    count = row_of_live.shape[0]
    (out,) = small(
        gather_kernel,
        me,
        [row_of_live, *lows, conv, step_z, dt_proj, dt_bias],
        [(STEPS, count, 3 * c + 128)],
        "gather_live",
        after,
        F32,
        [pltpu.VMEM((n // 4, 2, 2, rows // n, WIDE), BF16)],
        40,
    )
    return out


def live_kernel(slot_ref, after_ref, moved_ref, live_ref, alog_ref, skip_ref, o_ref, buf, state_scr):
    _, count, c = o_ref.shape
    def place(i, carry):
        source, slot = slot_ref[0, i], slot_ref[1, i]
        at = pl.multiple_of(i * STATE, STATE)
        from_row = pl.multiple_of(slot * STATE, STATE)
        value = moved_ref[source, pl.ds(from_row, STATE), :].astype(F32)
        for l in range(c // 128):
            buf[l, pl.ds(at, STATE), :] = value[:, 128 * l : 128 * (l + 1)]
        return carry

    lax.fori_loop(0, count, place, 0)
    for s in range(STATE):
        for l in range(c // 128):
            state_scr[s, :, 128 * l : 128 * (l + 1)] = buf[l, pl.ds(s, count, stride=STATE), :]
    tall, lanes = 16, min(512, c)

    def step_all(t, carry):
        for r in range(0, count, tall):
            tail = live_ref[t, r : r + tall, 3 * c :]
            for l in range(0, c, lanes):
                cols = slice(l, l + lanes)
                step = live_ref[t, r : r + tall, cols]
                conv = live_ref[t, r : r + tall, c + l : c + l + lanes]
                gate = live_ref[t, r : r + tall, 2 * c + l : 2 * c + l + lanes]
                drive = step * conv
                total = skip_ref[:, cols] * conv
                for s in range(STATE):
                    rate = -jnp.exp(alog_ref[s : s + 1, cols])
                    old = state_scr[s, r : r + tall, cols]
                    state = jnp.exp(step * rate) * old + drive * tail[:, s : s + 1]
                    state_scr[s, r : r + tall, cols] = state
                    total = total + state * tail[:, STATE + s : STATE + s + 1]
                o_ref[t, r : r + tall, cols] = (total * gate).astype(BF16)
        return carry

    lax.fori_loop(0, STEPS, step_all, 0)


def live_steps(slot_of_live, after, moved, gathered, a_log, d_skip):
    count, c = gathered.shape[1], a_log.shape[1]
    (out,) = small(
        live_kernel,
        slot_of_live,
        [moved, gathered, a_log, d_skip],
        [(STEPS, count, c)],
        "live_steps",
        after,
        BF16,
        [pltpu.VMEM((c // 128, count * STATE, 128), F32), pltpu.VMEM((STATE, count, c), F32)],
        40,
    )
    return out


def fix_kernel(t, take, me_ref, after_ref, row_ref, gated_ref, live_ref, o_ref):
    rows = gated_ref.shape[0]
    count = live_ref.shape[1]
    shift = take.bit_length() - 1
    place = lax.broadcasted_iota(jnp.int32, (rows, count), 0)
    mine = place >= rows // 2
    within = place - jnp.where(mine, rows // 2, 0)
    y = (me_ref[0] // 2) % 2
    row = ((2 * (within >> shift) + jnp.where(mine, y, 1 - y)) << shift) + (within & (take - 1))
    hot = (row == row_ref[...]).astype(F32)
    taken = jnp.max(hot, axis=1, keepdims=True) > 0.0
    live = jnp.dot(hot.astype(BF16), live_ref[t], preferred_element_type=F32)
    o_ref[...] = jnp.where(taken, live, gated_ref[...].astype(F32)).astype(BF16)


def out_kernel(me_ref, own_ref, other_ref, wown_ref, wother_ref, *refs):
    send_ref, keep_ref = refs[-2:]
    total = jnp.dot(own_ref[...], wown_ref[...], preferred_element_type=F32)
    total = total + jnp.dot(other_ref[...], wother_ref[...], preferred_element_type=F32)
    half = send_ref.shape[0]
    send_ref[...] = total[:half].astype(BF16)
    keep_ref[...] = total[half:].astype(BF16)


def out_project(me, own, other, out_weight, other_weight, after, part, parts):
    rows, c = own.shape
    tile = 1024
    every = out_weight.shape[1] // 2 // tile
    tiles = every // parts
    cols = tiles * tile
    first = part * tiles
    half = jax.ShapeDtypeStruct((rows // 2, cols), BF16)
    return pl.pallas_call(
        out_kernel,
        grid_spec=pltpu.PrefetchScalarGridSpec(
            num_scalar_prefetch=1,
            grid=(tiles,),
            in_specs=[
                pl.BlockSpec(memory_space=pltpu.VMEM),
                pl.BlockSpec(memory_space=pltpu.VMEM),
                pl.BlockSpec((c, tile), lambda j, me_ref: (0, (me_ref[0] % 2) * every + first + j)),
                pl.BlockSpec((c, tile), lambda j, me_ref: (0, first + j)),
            ]
            + [pl.BlockSpec(memory_space=pl.ANY)] * len(after),
            out_specs=[pl.BlockSpec((rows // 2, tile), lambda j, me_ref: (0, j))] * 2,
        ),
        out_shape=[half, half],
        compiler_params=params(48),
        cost_estimate=cost(4 * rows * c * cols, 4 * c * cols + 2 * rows * cols),
        name="out_project",
    )(me, own, other, out_weight, other_weight, *after)


def halve_kernel(stage, me_ref, after_ref, keep_ref, got_ref, send_ref, left_ref):
    bit = (me_ref[0] >> (2 + stage)) & 1
    for i in range(send_ref.shape[0]):
        for o_ref, at in ((send_ref, 2 * i + 1 - bit), (left_ref, 2 * i + bit)):
            o_ref[i] = (keep_ref[at].astype(F32) + got_ref[at].astype(F32)).astype(BF16)


def sum_z_kernel(me_ref, after_ref, keep_ref, got_ref, send_ref, left_ref):
    total = keep_ref[0].astype(F32) + got_ref[0].astype(F32)
    own = total.shape[0] // 2
    low, high = total[:own], total[own:]
    core = me_ref[0] % 2
    send_ref[...] = jnp.where(core == 0, high, low).astype(BF16)
    left_ref[...] = jnp.where(core == 0, low, high).astype(BF16)


def final_kernel(tiles, counts, me_ref, *refs):
    o_ref = refs[-1]
    own_half = pl.program_id(0) // tiles == me_ref[0] % 2
    tile = pl.program_id(0) % tiles
    at = 0
    for t, count in enumerate(counts):
        value = None
        for part in range(count):
            mine, theirs = refs[at][...].astype(F32), refs[at + 1][...].astype(F32)
            here = jnp.where(own_half, mine, theirs)
            value = here if value is None else jnp.where(tile == part, here, value)
            at += 2
        o_ref[:, t, :] = value.astype(BF16)


def final_join(me, pieces):
    own = pieces[0][0][0].shape[0]
    cols = sum(keep.shape[1] for keep, _ in pieces[0])
    tiles = max(len(parts) for parts in pieces)
    tile = cols // tiles
    args, specs = [], []
    for parts in pieces:
        for keep, got in parts:
            many = keep.shape[1] // tile
            spec = pl.BlockSpec((own, tile), lambda j, me_ref, many=many: (0, (j % tiles) % many))
            args += [keep, got]
            specs += [spec, spec]
    return pl.pallas_call(
        functools.partial(final_kernel, tiles, [len(parts) for parts in pieces]),
        grid_spec=pltpu.PrefetchScalarGridSpec(
            num_scalar_prefetch=1,
            grid=(2 * tiles,),
            in_specs=specs,
            out_specs=pl.BlockSpec((own, STEPS, tile), lambda j, me_ref: (0, 0, j)),
        ),
        out_shape=jax.ShapeDtypeStruct((own, STEPS, 2 * cols), BF16),
        compiler_params=params(16),
        cost_estimate=cost(0, own * cols * 32),
        name="final_join",
    )(me, *args)


def shards(
    resident_state,
    resident_conv,
    prefilled_state,
    prefilled_conv,
    live_counts,
    batch_rows,
    step_x,
    step_z,
    conv_weight,
    conv_bias,
    x_proj,
    norm_gain,
    dt_proj,
    dt_bias,
    a_log,
    d_skip,
    out_weight,
):
    n = lax.axis_size("dex")
    zs = n // 4
    rows = resident_state.shape[0]
    slots = prefilled_state.shape[0]
    c = resident_state.shape[2]
    me_scalar = lax.axis_index("dex").astype(jnp.int32)
    me = me_scalar.reshape(1)

    moved_conv = exchange_conv(prefilled_conv, me, n)
    packed = pack_state((moved_conv[1],), prefilled_state, n)
    cols = out_weight.shape[1] // 2

    is_live = jnp.arange(slots, dtype=jnp.int32)[None, :] < live_counts[:, None]
    target = jnp.where(is_live, batch_rows.reshape(n, slots), -1)
    place = jnp.arange(TAPS + 1, dtype=jnp.int32)
    mine = place[None, None, :, None] == place[:, None, None, None]
    spread = jnp.where(mine, target[None, :, None, :], -1).reshape(TAPS + 1, n * (TAPS + 1) * slots)
    flat = target.reshape(-1)
    number = jnp.arange(n * slots, dtype=jnp.int32)
    count = n * slots // 2
    rank = jnp.sum(((flat >= 0)[None, :] & (number[None, :] < number[:, None])).astype(jnp.int32), axis=1)
    hit = (rank[None, :] == number[:count, None]) & (flat >= 0)[None, :]
    live_slot = jnp.sum(jnp.where(hit, number[None, :], 0), axis=1)
    live_row = jnp.sum(jnp.where(hit, flat[None, :], 0), axis=1)
    slot_of_live = jnp.stack([live_slot // slots, live_slot % slots])
    row_of_live = jnp.broadcast_to(live_row[:, None], (count, 128))
    live_row = live_row.reshape(1, count)
    gain = jnp.concatenate([norm_gain, jnp.zeros((WIDE - norm_gain.shape[0],), F32)]).reshape(1, WIDE)
    old = jnp.transpose(resident_conv, (1, 0, 2))
    proj = x_proj.T
    bias = conv_bias.reshape(1, c)
    conv, send, keep = conv_steps(
        tuple(range(STEPS)), n, me, (packed,), spread, old, moved_conv, step_x, conv_weight, bias, proj
    )
    behind, low, merged, lows = reduce_projection(send, keep, gain, me, n)
    half_weight = weight_half(me, behind, out_weight)
    packed = hold(packed, merged)
    moved_state = lax.all_to_all(packed, "dex", 0, 0, tiled=True)
    other_weight = swap(hold(half_weight, low), 1, n)

    state = resident_state.reshape(rows * STATE, c)
    sends, keeps, gated = {}, {}, {}
    stages = zs.bit_length() - 1
    take = 2 * rows // n

    rate_bias, skip = dt_bias.reshape(1, c), d_skip.reshape(1, c)

    next_steps = None

    def s_step(t, after):
        nonlocal state
        if t == 0:
            steps = step_rows(0, me, after, lows, dt_proj, rate_bias, rows, n)
        else:
            steps = next_steps
        state, gated[t] = state_step(t, me, after, steps, conv, step_z, a_log, skip, state, n)
        return gated[t]

    def fix(t, after):
        kernel = functools.partial(fix_kernel, t, take)
        (gated[t],) = small(kernel, me, [live_row, gated[t], live_gated], [(rows, c)], "fix", (after,))
        if t == STEPS - 1:
            return gated[t]
        nonlocal next_steps
        next_steps = step_rows(t + 1, me, (gated[t],), lows, dt_proj, rate_bias, rows, n)
        return next_steps[1]

    def project(t, after, parts=1):
        other = swap(gated[t], 1, n)
        for part in range(parts):
            sends[t, part], keeps[t, part] = out_project(
                me, gated[t], other, out_weight, other_weight, (after,), part, parts
            )
            after = keeps[t, part]
        return after

    def reduce(t, stage, after, part=0):
        at = t, part
        width = keeps[at].shape[-1]
        if stage == 0:
            keep = keeps[at].reshape(zs, take, width)
            got = swap(sends[at], 2, n).reshape(zs, take, width)
        else:
            keep, got = keeps[at], swap(sends[at], 2 << stage, n)
        if stage < stages:
            kernel, shape = functools.partial(halve_kernel, stage), (keep.shape[0] // 2, take, width)
        else:
            kernel, shape = sum_z_kernel, (take // 2, width)
        sends[at], keeps[at] = small(kernel, me, [keep, got], [shape] * 2, "reduce_%d" % stage, (after,))
        if stage == stages:
            sends[at] = swap(sends[at], 1, n)
        return keeps[at]

    last = s_step(0, (packed,))
    gathered = gather_live(me, (last,), row_of_live, lows, conv, step_z, dt_proj, rate_bias, n)
    live_gated = live_steps(slot_of_live, (last,), moved_state, gathered, a_log, skip)
    last = fix(0, live_gated)
    last = project(0, last)
    for t in range(1, STEPS):
        last = s_step(t, (last,))
        last = fix(t, last)
        if t > 1:
            for stage in range(1, stages):
                last = reduce(t - 2, stage, last)
        last = project(t, last, 1 if t < STEPS - 1 else 2)
        if t < STEPS - 1:
            last = reduce(t - 1, 0, last)
    last = reduce(t - 3, stages, last)
    last = reduce(t - 1, 0, last)
    last = reduce(t, 0, last, 0)
    for stage in range(1, stages):
        last = reduce(t - 1, stage, last)
    last = reduce(t, 0, last, 1)
    last = reduce(t - 2, stages, last)
    for part in range(2):
        for stage in range(1, stages):
            last = reduce(t, stage, last, part)
    last = reduce(t - 1, stages, last)
    last = reduce(t, stages, last, 0)
    last = reduce(t, stages, last, 1)
    pieces = [[(keeps[t, part], sends[t, part]) for part in range(1 if t < STEPS - 1 else 2)] for t in range(STEPS)]
    return final_join(me, pieces)


def solution(mesh):
    placed = (
        P("grp", None, "dex"),
        P("grp", None, "dex"),
        P(("grp", "dex"), None, None),
        P(("grp", "dex"), None, None),
        P("grp"),
        P("grp"),
        P(None, "grp", "dex"),
        P(None, "grp", "dex"),
        P(None, "dex"),
        P("dex"),
        P("dex", None),
        P(),
        P(None, "dex"),
        P("dex"),
        P(None, "dex"),
        P("dex"),
        P("dex", None),
    )
    return jax.shard_map(
        shards, mesh=mesh, in_specs=placed, out_specs=P(("grp", "dex"), None, None), check_vma=False
    )
```

```python
import functools

import jax
import jax.numpy as jnp
from jax import lax
from jax.experimental import pallas as pl
from jax.experimental.pallas import tpu as pltpu
from jax.sharding import PartitionSpec as P

STATE = 16
DT_RANK = 512
STEPS = 4
TAPS = 3
WIDE = DT_RANK + 128

RMS_EPS = 1e-06
BC_FLOOR = 0.2

BF16 = jnp.bfloat16
F32 = jnp.float32


def params(mib):
    return pltpu.CompilerParams(vmem_limit_bytes=mib * 1024 * 1024)


def swap(x, mask, n):
    return lax.ppermute(x, "dex", [(i, i ^ mask) for i in range(n)])


def cost(flops, bytes_accessed, transcendentals=0):
    return pl.CostEstimate(flops=1024, bytes_accessed=1024, transcendentals=0)


def sigmoid(x):
    return 1.0 / (1.0 + jnp.exp(-x))


def whole(shape):
    zeros = (0,) * len(shape)
    return pl.BlockSpec(shape, lambda *_: zeros)


def small(kernel, me, args, shapes, name, after=(), dtype=BF16, scratch=(), mib=8):
    size = sum(a.size for a in args)
    vmem = pl.BlockSpec(memory_space=pltpu.VMEM)
    return pl.pallas_call(
        kernel,
        in_specs=[pl.BlockSpec(memory_space=pltpu.SMEM)]
        + [pl.BlockSpec(memory_space=pl.ANY)] * len(after)
        + [vmem] * len(args),
        out_specs=[vmem] * len(shapes),
        out_shape=[jax.ShapeDtypeStruct(s, dtype) for s in shapes],
        scratch_shapes=list(scratch),
        compiler_params=params(mib),
        cost_estimate=cost(size, 4 * size),
        name=name,
    )(me, *after, *args)


def pack_conv_kernel(me_ref, x_ref, *o_refs):
    zs, _, wide = o_refs[0].shape
    y, core = (me_ref[0] // 2) % 2, me_ref[0] % 2
    c = wide * (TAPS + 1) // TAPS
    for i, o_ref in enumerate(o_refs):
        for z in range(zs):
            dest = 4 * z + 2 * jnp.bitwise_xor(y, i % 2) + jnp.bitwise_xor(core, i // 2)
            x = x_ref[:, :, pl.ds(pl.multiple_of(dest * c, 128), c)]
            parts = [x[p, :, :wide] for p in range(TAPS)]
            parts.append(jnp.concatenate([x[p, :, wide:] for p in range(TAPS)], axis=1))
            o_ref[z] = jnp.concatenate(parts, axis=0).astype(BF16)


def cut_conv_kernel(me_ref, *refs):
    zs = refs[0].shape[0]
    z, y, core = me_ref[0] // 4, (me_ref[0] // 2) % 2, me_ref[0] % 2
    for m in range(zs):
        for i in range(4):
            at = 2 * jnp.bitwise_xor(y, i % 2) + jnp.bitwise_xor(core, i // 2)
            refs[4 + m][at] = refs[i][jnp.bitwise_xor(z, m)]


def exchange_conv(prefilled_conv, me, n):
    slots, _, inner = prefilled_conv.shape
    zs = n // 4
    piece = ((TAPS + 1) * slots, inner // n * TAPS // (TAPS + 1))
    conv = jnp.transpose(prefilled_conv, (1, 0, 2))
    packed = small(pack_conv_kernel, me, [conv], [(zs,) + piece] * 4, "pack_conv")
    near, far = swap(packed[2], 1, n), swap(packed[3], 1, n)
    got = [packed[0], swap(packed[1], 2, n), near, swap(far, 2, n)]
    cut = small(cut_conv_kernel, me, got, [(4,) + piece] * zs, "cut_conv")
    return [cut[0]] + [swap(cut[m], 4 * m, n) for m in range(1, zs)]


def pack_state_kernel(x_ref, *refs):
    o_ref = refs[-1]
    slots = x_ref.shape[0]
    some, _, c = o_ref.shape
    for d in range(some):
        for k in range(slots):
            o_ref[d, STATE * k : STATE * (k + 1), :] = x_ref[k, :, d * c : (d + 1) * c].astype(BF16)


def pack_state(after, prefilled_state, n):
    slots, _, inner = prefilled_state.shape
    c = inner // n
    some = 4
    return pl.pallas_call(
        pack_state_kernel,
        grid=(n // some,),
        in_specs=[pl.BlockSpec((slots, STATE, some * c), lambda d: (0, 0, d))]
        + [pl.BlockSpec(memory_space=pl.ANY)] * len(after),
        out_specs=pl.BlockSpec((some, slots * STATE, c), lambda d: (d, 0, 0)),
        out_shape=jax.ShapeDtypeStruct((n, slots * STATE, c), BF16),
        compiler_params=params(24),
        cost_estimate=cost(0, slots * STATE * inner * 6),
        name="pack_state",
    )(prefilled_state, *after)


def hold_kernel(x_ref, after_ref, o_ref):
    pass


def hold(x, after):
    some = pl.BlockSpec(memory_space=pl.ANY)
    return pl.pallas_call(
        hold_kernel,
        in_specs=[some, some],
        out_specs=some,
        out_shape=jax.ShapeDtypeStruct(x.shape, x.dtype),
        input_output_aliases={0: 0},
        compiler_params=params(8),
        cost_estimate=cost(0, 0),
        name="hold",
    )(x, after)


def half_kernel(me_ref, after_ref, w_ref, o_ref):
    o_ref[...] = w_ref[...]


def weight_half(me, after, out_weight):
    c, cols = out_weight.shape
    tile = 1024
    tiles = cols // 2 // tile
    return pl.pallas_call(
        half_kernel,
        grid_spec=pltpu.PrefetchScalarGridSpec(
            num_scalar_prefetch=1,
            grid=(tiles,),
            in_specs=[
                pl.BlockSpec(memory_space=pl.ANY),
                pl.BlockSpec((c, tile), lambda j, me_ref: (0, (1 - me_ref[0] % 2) * tiles + j)),
            ],
            out_specs=pl.BlockSpec((c, tile), lambda j, me_ref: (0, j)),
        ),
        out_shape=jax.ShapeDtypeStruct((c, cols // 2), BF16),
        compiler_params=params(56),
        cost_estimate=cost(0, 2 * c * cols),
        name="weight_half",
    )(me, after, out_weight)


def conv_kernel(steps, n, me_ref, target_ref, old_ref, x_ref, w_ref, bias_ref, proj_ref, *refs):
    zs = n // 4
    moved, (conv_ref, send_ref, keep_ref, moved_scr, win) = refs[:zs], refs[-5:]
    rows, c = win.shape[1:]
    columns = target_ref.shape[1]
    own = rows // n
    core, my_z = me_ref[0] % 2, me_ref[0] // 4
    for m in range(zs):
        moved_scr[jnp.bitwise_xor(my_z, m)] = moved[m][...]
    fresh = moved_scr[...].reshape(columns, moved_scr.shape[3])
    wide = fresh.shape[1]
    row_id = lax.broadcasted_iota(jnp.int32, (rows, columns), 0)
    hots = [row_id == target_ref[p : p + 1, :] for p in range(TAPS + 1)]
    taken = jnp.max(hots[0].astype(F32), axis=1, keepdims=True) > 0.0
    fresh = [jnp.dot(hot.astype(BF16), fresh, preferred_element_type=F32) for hot in hots]
    for p in range(TAPS):
        part = (c - wide) * p
        win[p, :, :wide] = jnp.where(taken, fresh[p], old_ref[p, :, :wide])
        win[p, :, wide:] = jnp.where(taken, fresh[TAPS][:, part : part + c - wide], old_ref[p, :, wide:])
    for i, t in enumerate(steps):
        total = None
        for q in range(TAPS + 1):
            place = t + q
            value = win[place] if place < TAPS else x_ref[place - TAPS].astype(F32)
            term = value * w_ref[q : q + 1, :]
            total = term if total is None else total + term
        total = total + bias_ref[...]
        conv_out = total * sigmoid(total)
        conv_ref[i] = conv_out
        part = lax.dot_general(
            conv_out.astype(BF16), proj_ref[...], (((1,), (1,)), ((), ())), preferred_element_type=F32
        )
        pad = jnp.zeros((own, WIDE - part.shape[1]), BF16)
        for q in range(n // 2):
            low = part[2 * q * own : (2 * q + 1) * own, :]
            high = part[(2 * q + 1) * own : (2 * q + 2) * own, :]
            send_ref[q, i, :, : part.shape[1]] = jnp.where(core == 0, high, low).astype(BF16)
            keep_ref[q, i, :, : part.shape[1]] = jnp.where(core == 0, low, high).astype(BF16)
            send_ref[q, i, :, part.shape[1] :] = pad
            keep_ref[q, i, :, part.shape[1] :] = pad


def conv_steps(steps, n, me, after, target, old, moved, step_x, conv_weight, conv_bias, proj):
    _, rows, c = old.shape
    s = len(steps)
    last = max(steps) + 1
    parts = (n // 2, s, rows // n, WIDE)
    return pl.pallas_call(
        functools.partial(conv_kernel, steps, n),
        grid_spec=pltpu.PrefetchScalarGridSpec(
            num_scalar_prefetch=1,
            grid=(1,),
            in_specs=[
                whole(target.shape),
                whole(old.shape),
                whole((last, rows, c)),
                whole(conv_weight.shape),
                whole((1, c)),
                whole(proj.shape),
            ]
            + [whole(moved[0].shape)] * len(moved)
            + [pl.BlockSpec(memory_space=pl.ANY)] * len(after),
            out_specs=[whole((s, rows, c)), whole(parts), whole(parts)],
            scratch_shapes=[
                pltpu.VMEM((len(moved),) + moved[0].shape, BF16),
                pltpu.VMEM((TAPS, rows, c), F32),
            ],
        ),
        out_shape=[jax.ShapeDtypeStruct((s, rows, c), F32)] + [jax.ShapeDtypeStruct(parts, BF16)] * 2,
        compiler_params=params(40),
        cost_estimate=cost(2 * s * rows * c * 544, rows * c * (12 + 6 * s) + c * 1088, s * rows * c),
        name="conv_project",
    )(me, target, old, step_x, conv_weight, conv_bias, proj, *moved, *after)


def add_y_kernel(me_ref, *refs):
    keep_ref, got_ref, send_ref, left_ref = refs[-4:]
    y = (me_ref[0] // 2) % 2
    for z in range(send_ref.shape[0]):
        for o_ref, at in ((send_ref, 2 * z + 1 - y), (left_ref, 2 * z + y)):
            o_ref[z] = (keep_ref[at].astype(F32) + got_ref[at].astype(F32)).astype(BF16)


def add_z_kernel(zs, me_ref, *refs):
    keep_ref, got_ref, *o_refs = refs[-2 - zs :]
    z = me_ref[0] // 4
    for m, o_ref in enumerate(o_refs):
        at = jnp.bitwise_xor(z, m)
        o_ref[...] = (keep_ref[at].astype(F32) + got_ref[at].astype(F32)).astype(BF16)


def norm_kernel(me_ref, gain_ref, *refs):
    o_ref = refs[-1]
    total = refs[0][...].astype(F32)
    for ref in refs[1:-1]:
        total = total + ref[...].astype(F32)
    dt = total[:, :, :DT_RANK]
    dt = dt * lax.rsqrt(jnp.mean(dt * dt, axis=2, keepdims=True) + RMS_EPS) * gain_ref[:, :DT_RANK][None]
    tail = total[:, :, DT_RANK:]
    lane = lax.broadcasted_iota(jnp.int32, tail.shape, 2)
    square = tail * tail
    is_b = lane < STATE
    is_c = jnp.logical_and(lane >= STATE, lane < 2 * STATE)
    mean_b = jnp.sum(jnp.where(is_b, square, 0.0), axis=2, keepdims=True) / STATE
    mean_c = jnp.sum(jnp.where(is_c, square, 0.0), axis=2, keepdims=True) / STATE
    scale_b = lax.rsqrt(jnp.maximum(mean_b, BC_FLOOR))
    scale_c = lax.rsqrt(jnp.maximum(mean_c, BC_FLOOR))
    tail = tail * jnp.where(is_b, scale_b, scale_c) * gain_ref[:, DT_RANK:][None]
    o_ref[:, :, :DT_RANK] = dt.astype(BF16)
    o_ref[:, :, DT_RANK:] = jnp.where(lane < 2 * STATE, tail, 0.0).astype(BF16)


def merge_kernel(me_ref, *refs):
    o_ref = refs[-1]
    z = me_ref[0] // 4
    for m, ref in enumerate(refs[:-1]):
        o_ref[jnp.bitwise_xor(z, m)] = ref[...]


def reduce_projection(send, keep, gain, me, n):
    zs = n // 4
    piece = keep.shape[1:]
    got = swap(send, 1, n)
    send, keep = small(add_y_kernel, me, [keep, got], [(zs,) + piece] * 2, "add_y")
    got = swap(send, 2, n)
    cut = small(functools.partial(add_z_kernel, zs), me, [keep, got], [piece] * zs, "add_z")
    cut = [cut[0]] + [swap(cut[m], 4 * m, n) for m in range(1, zs)]
    (low,) = small(norm_kernel, me, [gain] + cut, [piece], "norm")
    lows = [low] + [swap(low, 4 * m, n) for m in range(1, zs)]
    (mine,) = small(merge_kernel, me, lows, [(zs,) + piece], "merge_z")
    beside = swap(mine, 2, n)
    return keep, low, mine, (mine, beside, swap(mine, 1, n), swap(beside, 1, n))


def assemble_low(lows, index, low_scr, me_ref):
    y, core = (me_ref[0] // 2) % 2, me_ref[0] % 2
    for i, low_ref in enumerate(lows):
        for z in range(low_ref.shape[0]):
            low_scr[z, jnp.bitwise_xor(y, i % 2), jnp.bitwise_xor(core, i // 2)] = low_ref[z, index]
    return low_scr[...].reshape(-1, WIDE)


def step_sizes(low, dtp_ref, dtb_ref):
    pre = jnp.dot(low[:, :DT_RANK], dtp_ref[...], preferred_element_type=F32) + dtb_ref[...]
    return jnp.maximum(pre, 0.0) + jnp.log(1.0 + jnp.exp(-jnp.abs(pre)))


def step_kernel(t, me_ref, after_ref, *refs):
    *lows, dtp_ref, dtb_ref, step_ref, tail_ref, low_scr = refs
    low = assemble_low(lows, t, low_scr, me_ref)
    step_ref[...] = step_sizes(low, dtp_ref, dtb_ref)
    tail_ref[...] = low[:, DT_RANK:].astype(F32)


def step_rows(t, me, after, lows, dt_proj, dt_bias, rows, n):
    return small(
        functools.partial(step_kernel, t),
        me,
        [*lows, dt_proj, dt_bias],
        [(rows, dt_proj.shape[1]), (rows, 128)],
        "step_rows",
        after,
        F32,
        [pltpu.VMEM((n // 4, 2, 2, rows // n, WIDE), BF16)],
        12,
    )


def state_kernel(t, behind, me_ref, *refs):
    first, last = t == 0, t == STEPS - 1
    refs = refs[behind:]
    step_ref, tail_ref, conv_ref, z_ref, alog_ref, skip_ref, state_ref, *refs = refs
    new_ref = None
    if not last:
        new_ref, *refs = refs
    gated_ref, decay_scr, bc_scr, *refs = refs
    block = pl.program_id(0)
    rows, c = step_ref.shape
    take = conv_ref.shape[0]
    blocks = rows // take

    if first:
        buf, sems = refs

        def fetch(at, slot):
            first_row = pl.multiple_of(at * (take * STATE), take * STATE)
            return [
                pltpu.make_async_copy(
                    state_ref.at[pl.ds(first_row, take * STATE), 128 * l : 128 * (l + 1)],
                    buf.at[slot, l],
                    sems.at[slot, l],
                )
                for l in range(c // 128)
            ]

        now = lax.rem(block, 2)

        @pl.when(block == 0)
        def _():
            for copy in fetch(0, 0):
                copy.start()

        @pl.when(block + 1 < blocks)
        def _():
            for copy in fetch(block + 1, 1 - now):
                copy.start()

    @pl.when(block == 0)
    def _():
        decay_scr[...] = -jnp.exp(alog_ref[...])

    base = block * take
    if first:
        for copy in fetch(block, now):
            copy.wait()

    tall, lanes = 16, min(256, c)
    for r in range(0, take, tall):
        tail = tail_ref[pl.ds(pl.multiple_of(base + r, tall), tall), :]
        for s in range(2 * STATE):
            bc_scr[s] = jnp.broadcast_to(tail[:, s : s + 1], (tall, 128))
        for l in range(0, c, lanes):
            cols = slice(l, l + lanes)
            step = step_ref[pl.ds(pl.multiple_of(base + r, tall), tall), cols]
            conv = conv_ref[r : r + tall, cols]
            drive = step * conv
            total = skip_ref[:, cols] * conv
            for s in range(STATE):
                if first:
                    at = pl.ds(STATE * r + s, tall, stride=STATE)
                    tiles = range(l // 128, (l + lanes) // 128)
                    old = jnp.concatenate([buf[now, k, at, :] for k in tiles], axis=1)
                else:
                    old = state_ref[s, r : r + tall, cols].astype(F32)
                b = jnp.concatenate([bc_scr[s]] * (lanes // 128), axis=1)
                g = jnp.concatenate([bc_scr[STATE + s]] * (lanes // 128), axis=1)
                state = jnp.exp(step * decay_scr[s : s + 1, cols]) * old + drive * b
                if not last:
                    new_ref[s, r : r + tall, cols] = state.astype(BF16)
                total = total + state * g
            z = z_ref[0, r : r + tall, cols].astype(F32)
            gated_ref[r : r + tall, cols] = (total * (z * sigmoid(z))).astype(BF16)


def state_step(t, me, after, steps, conv, step_z, a_log, d_skip, state, n):
    _, rows, c = conv.shape
    take = 2 * rows // n
    blocks = rows // take
    first, last = t == 0, t == STEPS - 1

    def placed(i, me_ref):
        z, y = i // 2, i % 2
        mine = (y == (me_ref[0] // 2) % 2).astype(jnp.int32)
        return (mine * (blocks // 2) + z, 0)

    vmem = pl.BlockSpec(memory_space=pltpu.VMEM)
    in_specs = [vmem] * 2 + [
        pl.BlockSpec((None, take, c), lambda i, *_: (t, i, 0)),
        pl.BlockSpec((1, take, c), lambda i, *_: (t, i, 0)),
        whole(a_log.shape),
        whole((1, c)),
    ]
    scratch = [
        pltpu.VMEM((STATE, c), F32),
        pltpu.VMEM((2 * STATE, 16, 128), F32),
    ]
    flat = pl.BlockSpec((STATE, take, c), lambda i, *_: (0, i, 0))
    if first:
        in_specs = in_specs + [pl.BlockSpec(memory_space=pl.ANY)]
        scratch += [
            pltpu.VMEM((2, c // 128, take * STATE, 128), F32),
            pltpu.SemaphoreType.DMA((2, c // 128)),
        ]
    else:
        in_specs = in_specs + [flat]
    in_specs = [pl.BlockSpec(memory_space=pl.ANY)] * len(after) + in_specs
    out_specs = [pl.BlockSpec((take, c), placed)]
    out_shape = [jax.ShapeDtypeStruct((rows, c), BF16)]
    if not last:
        out_specs = [flat] + out_specs
        out_shape = [jax.ShapeDtypeStruct((STATE, rows, c), BF16)] + out_shape
    size = rows * STATE * c
    out = pl.pallas_call(
        functools.partial(state_kernel, t, len(after)),
        grid_spec=pltpu.PrefetchScalarGridSpec(
            num_scalar_prefetch=1,
            grid=(blocks,),
            in_specs=in_specs,
            out_specs=out_specs,
            scratch_shapes=scratch,
        ),
        out_shape=out_shape,
        compiler_params=params(48),
        cost_estimate=cost(8 * size, 4 * size, size),
        name="state_step",
    )(me, *after, *steps, conv, step_z, a_log, d_skip, state)
    return (None, out[0]) if last else (out[0], out[1])


def gather_kernel(me_ref, after_ref, row_ref, *refs):
    lows, refs = refs[:4], refs[4:]
    conv_ref, z_ref, dtp_ref, dtb_ref, o_ref, low_scr = refs
    count = o_ref.shape[1]
    _, rows, c = conv_ref.shape
    hot = (row_ref[:, :1] == lax.broadcasted_iota(jnp.int32, (count, rows), 1)).astype(F32).astype(BF16)
    for t in range(STEPS):
        low = jnp.dot(hot, assemble_low(lows, t, low_scr, me_ref), preferred_element_type=F32)
        o_ref[t, :, :c] = step_sizes(low.astype(BF16), dtp_ref, dtb_ref)
        o_ref[t, :, 3 * c :] = low[:, DT_RANK:]
        conv = conv_ref[t]
        high = conv.astype(BF16)
        rest = (conv - high.astype(F32)).astype(BF16)
        o_ref[t, :, c : 2 * c] = jnp.dot(hot, high, preferred_element_type=F32) + jnp.dot(
            hot, rest, preferred_element_type=F32
        )
        z = jnp.dot(hot, z_ref[t], preferred_element_type=F32)
        o_ref[t, :, 2 * c : 3 * c] = z * sigmoid(z)


def gather_live(me, after, row_of_live, lows, conv, step_z, dt_proj, dt_bias, n):
    _, rows, c = conv.shape
    count = row_of_live.shape[0]
    (out,) = small(
        gather_kernel,
        me,
        [row_of_live, *lows, conv, step_z, dt_proj, dt_bias],
        [(STEPS, count, 3 * c + 128)],
        "gather_live",
        after,
        F32,
        [pltpu.VMEM((n // 4, 2, 2, rows // n, WIDE), BF16)],
        40,
    )
    return out


def live_kernel(slot_ref, after_ref, moved_ref, live_ref, alog_ref, skip_ref, o_ref, buf, state_scr):
    _, count, c = o_ref.shape
    def place(i, carry):
        source, slot = slot_ref[0, i], slot_ref[1, i]
        at = pl.multiple_of(i * STATE, STATE)
        from_row = pl.multiple_of(slot * STATE, STATE)
        value = moved_ref[source, pl.ds(from_row, STATE), :].astype(F32)
        for l in range(c // 128):
            buf[l, pl.ds(at, STATE), :] = value[:, 128 * l : 128 * (l + 1)]
        return carry

    lax.fori_loop(0, count, place, 0)
    for s in range(STATE):
        for l in range(c // 128):
            state_scr[s, :, 128 * l : 128 * (l + 1)] = buf[l, pl.ds(s, count, stride=STATE), :]
    tall, lanes = 16, min(512, c)

    def step_all(t, carry):
        for r in range(0, count, tall):
            tail = live_ref[t, r : r + tall, 3 * c :]
            for l in range(0, c, lanes):
                cols = slice(l, l + lanes)
                step = live_ref[t, r : r + tall, cols]
                conv = live_ref[t, r : r + tall, c + l : c + l + lanes]
                gate = live_ref[t, r : r + tall, 2 * c + l : 2 * c + l + lanes]
                drive = step * conv
                total = skip_ref[:, cols] * conv
                for s in range(STATE):
                    rate = -jnp.exp(alog_ref[s : s + 1, cols])
                    old = state_scr[s, r : r + tall, cols]
                    state = jnp.exp(step * rate) * old + drive * tail[:, s : s + 1]
                    state_scr[s, r : r + tall, cols] = state
                    total = total + state * tail[:, STATE + s : STATE + s + 1]
                o_ref[t, r : r + tall, cols] = (total * gate).astype(BF16)
        return carry

    lax.fori_loop(0, STEPS, step_all, 0)


def live_steps(slot_of_live, after, moved, gathered, a_log, d_skip):
    count, c = gathered.shape[1], a_log.shape[1]
    (out,) = small(
        live_kernel,
        slot_of_live,
        [moved, gathered, a_log, d_skip],
        [(STEPS, count, c)],
        "live_steps",
        after,
        BF16,
        [pltpu.VMEM((c // 128, count * STATE, 128), F32), pltpu.VMEM((STATE, count, c), F32)],
        40,
    )
    return out


def fix_kernel(t, take, me_ref, after_ref, row_ref, gated_ref, live_ref, o_ref):
    rows = gated_ref.shape[0]
    count = live_ref.shape[1]
    shift = take.bit_length() - 1
    place = lax.broadcasted_iota(jnp.int32, (rows, count), 0)
    mine = place >= rows // 2
    within = place - jnp.where(mine, rows // 2, 0)
    y = (me_ref[0] // 2) % 2
    row = ((2 * (within >> shift) + jnp.where(mine, y, 1 - y)) << shift) + (within & (take - 1))
    hot = (row == row_ref[...]).astype(F32)
    taken = jnp.max(hot, axis=1, keepdims=True) > 0.0
    live = jnp.dot(hot.astype(BF16), live_ref[t], preferred_element_type=F32)
    o_ref[...] = jnp.where(taken, live, gated_ref[...].astype(F32)).astype(BF16)


def out_kernel(me_ref, own_ref, other_ref, wown_ref, wother_ref, *refs):
    send_ref, keep_ref = refs[-2:]
    total = jnp.dot(own_ref[...], wown_ref[...], preferred_element_type=F32)
    total = total + jnp.dot(other_ref[...], wother_ref[...], preferred_element_type=F32)
    half = send_ref.shape[0]
    send_ref[...] = total[:half].astype(BF16)
    keep_ref[...] = total[half:].astype(BF16)


def out_project(me, own, other, out_weight, other_weight, after, part, parts):
    rows, c = own.shape
    tile = 1024
    every = out_weight.shape[1] // 2 // tile
    tiles = every // parts
    cols = tiles * tile
    first = part * tiles
    half = jax.ShapeDtypeStruct((rows // 2, cols), BF16)
    return pl.pallas_call(
        out_kernel,
        grid_spec=pltpu.PrefetchScalarGridSpec(
            num_scalar_prefetch=1,
            grid=(tiles,),
            in_specs=[
                pl.BlockSpec(memory_space=pltpu.VMEM),
                pl.BlockSpec(memory_space=pltpu.VMEM),
                pl.BlockSpec((c, tile), lambda j, me_ref: (0, (me_ref[0] % 2) * every + first + j)),
                pl.BlockSpec((c, tile), lambda j, me_ref: (0, first + j)),
            ]
            + [pl.BlockSpec(memory_space=pl.ANY)] * len(after),
            out_specs=[pl.BlockSpec((rows // 2, tile), lambda j, me_ref: (0, j))] * 2,
        ),
        out_shape=[half, half],
        compiler_params=params(48),
        cost_estimate=cost(4 * rows * c * cols, 4 * c * cols + 2 * rows * cols),
        name="out_project",
    )(me, own, other, out_weight, other_weight, *after)


def halve_kernel(stage, me_ref, after_ref, keep_ref, got_ref, send_ref, left_ref):
    bit = (me_ref[0] >> (2 + stage)) & 1
    for i in range(send_ref.shape[0]):
        for o_ref, at in ((send_ref, 2 * i + 1 - bit), (left_ref, 2 * i + bit)):
            o_ref[i] = (keep_ref[at].astype(F32) + got_ref[at].astype(F32)).astype(BF16)


def sum_z_kernel(me_ref, after_ref, keep_ref, got_ref, send_ref, left_ref):
    total = keep_ref[0].astype(F32) + got_ref[0].astype(F32)
    own = total.shape[0] // 2
    low, high = total[:own], total[own:]
    core = me_ref[0] % 2
    send_ref[...] = jnp.where(core == 0, high, low).astype(BF16)
    left_ref[...] = jnp.where(core == 0, low, high).astype(BF16)


def final_kernel(tiles, counts, me_ref, *refs):
    o_ref = refs[-1]
    own_half = pl.program_id(0) // tiles == me_ref[0] % 2
    tile = pl.program_id(0) % tiles
    at = 0
    for t, count in enumerate(counts):
        value = None
        for part in range(count):
            mine, theirs = refs[at][...].astype(F32), refs[at + 1][...].astype(F32)
            here = jnp.where(own_half, mine, theirs)
            value = here if value is None else jnp.where(tile == part, here, value)
            at += 2
        o_ref[:, t, :] = value.astype(BF16)


def final_join(me, pieces):
    own = pieces[0][0][0].shape[0]
    cols = sum(keep.shape[1] for keep, _ in pieces[0])
    tiles = max(len(parts) for parts in pieces)
    tile = cols // tiles
    args, specs = [], []
    for parts in pieces:
        for keep, got in parts:
            many = keep.shape[1] // tile
            spec = pl.BlockSpec((own, tile), lambda j, me_ref, many=many: (0, (j % tiles) % many))
            args += [keep, got]
            specs += [spec, spec]
    return pl.pallas_call(
        functools.partial(final_kernel, tiles, [len(parts) for parts in pieces]),
        grid_spec=pltpu.PrefetchScalarGridSpec(
            num_scalar_prefetch=1,
            grid=(2 * tiles,),
            in_specs=specs,
            out_specs=pl.BlockSpec((own, STEPS, tile), lambda j, me_ref: (0, 0, j)),
        ),
        out_shape=jax.ShapeDtypeStruct((own, STEPS, 2 * cols), BF16),
        compiler_params=params(16),
        cost_estimate=cost(0, own * cols * 32),
        name="final_join",
    )(me, *args)


def shards(
    resident_state,
    resident_conv,
    prefilled_state,
    prefilled_conv,
    live_counts,
    batch_rows,
    step_x,
    step_z,
    conv_weight,
    conv_bias,
    x_proj,
    norm_gain,
    dt_proj,
    dt_bias,
    a_log,
    d_skip,
    out_weight,
):
    n = lax.axis_size("dex")
    zs = n // 4
    rows = resident_state.shape[0]
    slots = prefilled_state.shape[0]
    c = resident_state.shape[2]
    me_scalar = lax.axis_index("dex").astype(jnp.int32)
    me = me_scalar.reshape(1)

    moved_conv = exchange_conv(prefilled_conv, me, n)
    packed = pack_state((moved_conv[1],), prefilled_state, n)
    cols = out_weight.shape[1] // 2

    is_live = jnp.arange(slots, dtype=jnp.int32)[None, :] < live_counts[:, None]
    target = jnp.where(is_live, batch_rows.reshape(n, slots), -1)
    place = jnp.arange(TAPS + 1, dtype=jnp.int32)
    mine = place[None, None, :, None] == place[:, None, None, None]
    spread = jnp.where(mine, target[None, :, None, :], -1).reshape(TAPS + 1, n * (TAPS + 1) * slots)
    flat = target.reshape(-1)
    number = jnp.arange(n * slots, dtype=jnp.int32)
    count = n * slots // 2
    rank = jnp.sum(((flat >= 0)[None, :] & (number[None, :] < number[:, None])).astype(jnp.int32), axis=1)
    hit = (rank[None, :] == number[:count, None]) & (flat >= 0)[None, :]
    live_slot = jnp.sum(jnp.where(hit, number[None, :], 0), axis=1)
    live_row = jnp.sum(jnp.where(hit, flat[None, :], 0), axis=1)
    slot_of_live = jnp.stack([live_slot // slots, live_slot % slots])
    row_of_live = jnp.broadcast_to(live_row[:, None], (count, 128))
    live_row = live_row.reshape(1, count)
    gain = jnp.concatenate([norm_gain, jnp.zeros((WIDE - norm_gain.shape[0],), F32)]).reshape(1, WIDE)
    old = jnp.transpose(resident_conv, (1, 0, 2))
    proj = x_proj.T
    bias = conv_bias.reshape(1, c)
    conv, send, keep = conv_steps(
        tuple(range(STEPS)), n, me, (packed,), spread, old, moved_conv, step_x, conv_weight, bias, proj
    )
    behind, low, merged, lows = reduce_projection(send, keep, gain, me, n)
    half_weight = weight_half(me, behind, out_weight)
    packed = hold(packed, merged)
    moved_state = lax.all_to_all(packed, "dex", 0, 0, tiled=True)
    other_weight = swap(hold(half_weight, low), 1, n)

    state = resident_state.reshape(rows * STATE, c)
    sends, keeps, gated = {}, {}, {}
    stages = zs.bit_length() - 1
    take = 2 * rows // n

    rate_bias, skip = dt_bias.reshape(1, c), d_skip.reshape(1, c)

    next_steps = None

    def s_step(t, after):
        nonlocal state
        if t == 0:
            steps = step_rows(0, me, after, lows, dt_proj, rate_bias, rows, n)
        else:
            steps = next_steps
        state, gated[t] = state_step(t, me, after, steps, conv, step_z, a_log, skip, state, n)
        return gated[t]

    def fix(t, after):
        kernel = functools.partial(fix_kernel, t, take)
        (gated[t],) = small(kernel, me, [live_row, gated[t], live_gated], [(rows, c)], "fix", (after,))
        if t == STEPS - 1:
            return gated[t]
        nonlocal next_steps
        next_steps = step_rows(t + 1, me, (gated[t],), lows, dt_proj, rate_bias, rows, n)
        return next_steps[1]

    def project(t, after, parts=1):
        other = swap(gated[t], 1, n)
        for part in range(parts):
            sends[t, part], keeps[t, part] = out_project(
                me, gated[t], other, out_weight, other_weight, (after,), part, parts
            )
            after = keeps[t, part]
        return after

    def reduce(t, stage, after, part=0):
        at = t, part
        width = keeps[at].shape[-1]
        if stage == 0:
            keep = keeps[at].reshape(zs, take, width)
            got = swap(sends[at], 2, n).reshape(zs, take, width)
        else:
            keep, got = keeps[at], swap(sends[at], 2 << stage, n)
        if stage < stages:
            kernel, shape = functools.partial(halve_kernel, stage), (keep.shape[0] // 2, take, width)
        else:
            kernel, shape = sum_z_kernel, (take // 2, width)
        sends[at], keeps[at] = small(kernel, me, [keep, got], [shape] * 2, "reduce_%d" % stage, (after,))
        if stage == stages:
            sends[at] = swap(sends[at], 1, n)
        return keeps[at]

    last = s_step(0, (packed,))
    gathered = gather_live(me, (last,), row_of_live, lows, conv, step_z, dt_proj, rate_bias, n)
    live_gated = live_steps(slot_of_live, (last,), moved_state, gathered, a_log, skip)
    last = fix(0, live_gated)
    last = project(0, last)
    for t in range(1, STEPS):
        last = s_step(t, (last,))
        last = fix(t, last)
        if t > 1:
            for stage in range(1, stages):
                last = reduce(t - 2, stage, last)
        last = project(t, last, 1 if t < STEPS - 1 else 2)
        if t < STEPS - 1:
            last = reduce(t - 1, 0, last)
    last = reduce(t - 3, stages, last)
    last = reduce(t - 2, stages, last)
    last = reduce(t - 1, 0, last)
    last = reduce(t, 0, last, 0)
    for stage in range(1, stages):
        last = reduce(t - 1, stage, last)
    last = reduce(t, 0, last, 1)
    for part in range(2):
        for stage in range(1, stages):
            last = reduce(t, stage, last, part)
    last = reduce(t - 1, stages, last)
    last = reduce(t, stages, last, 0)
    last = reduce(t, stages, last, 1)
    pieces = [[(keeps[t, part], sends[t, part]) for part in range(1 if t < STEPS - 1 else 2)] for t in range(STEPS)]
    return final_join(me, pieces)


def solution(mesh):
    placed = (
        P("grp", None, "dex"),
        P("grp", None, "dex"),
        P(("grp", "dex"), None, None),
        P(("grp", "dex"), None, None),
        P("grp"),
        P("grp"),
        P(None, "grp", "dex"),
        P(None, "grp", "dex"),
        P(None, "dex"),
        P("dex"),
        P("dex", None),
        P(),
        P(None, "dex"),
        P("dex"),
        P(None, "dex"),
        P("dex"),
        P("dex", None),
    )
    return jax.shard_map(
        shards, mesh=mesh, in_specs=placed, out_specs=P(("grp", "dex"), None, None), check_vma=False
    )
```

```python
import functools

import jax
import jax.numpy as jnp
from jax import lax
from jax.experimental import pallas as pl
from jax.experimental.pallas import tpu as pltpu
from jax.sharding import PartitionSpec as P

STATE = 16
DT_RANK = 512
STEPS = 4
TAPS = 3
WIDE = DT_RANK + 128

RMS_EPS = 1e-06
BC_FLOOR = 0.2

BF16 = jnp.bfloat16
F32 = jnp.float32


def params(mib):
    return pltpu.CompilerParams(vmem_limit_bytes=mib * 1024 * 1024)


def swap(x, mask, n):
    return lax.ppermute(x, "dex", [(i, i ^ mask) for i in range(n)])


def cost(flops, bytes_accessed, transcendentals=0):
    return pl.CostEstimate(flops=1024, bytes_accessed=1024, transcendentals=0)


def sigmoid(x):
    return 1.0 / (1.0 + jnp.exp(-x))


def whole(shape):
    zeros = (0,) * len(shape)
    return pl.BlockSpec(shape, lambda *_: zeros)


def small(kernel, me, args, shapes, name, after=(), dtype=BF16, scratch=(), mib=8):
    size = sum(a.size for a in args)
    vmem = pl.BlockSpec(memory_space=pltpu.VMEM)
    return pl.pallas_call(
        kernel,
        in_specs=[pl.BlockSpec(memory_space=pltpu.SMEM)]
        + [pl.BlockSpec(memory_space=pl.ANY)] * len(after)
        + [vmem] * len(args),
        out_specs=[vmem] * len(shapes),
        out_shape=[jax.ShapeDtypeStruct(s, dtype) for s in shapes],
        scratch_shapes=list(scratch),
        compiler_params=params(mib),
        cost_estimate=cost(size, 4 * size),
        name=name,
    )(me, *after, *args)


def pack_conv_kernel(me_ref, x_ref, *o_refs):
    zs, _, wide = o_refs[0].shape
    y, core = (me_ref[0] // 2) % 2, me_ref[0] % 2
    c = wide * (TAPS + 1) // TAPS
    for i, o_ref in enumerate(o_refs):
        for z in range(zs):
            dest = 4 * z + 2 * jnp.bitwise_xor(y, i % 2) + jnp.bitwise_xor(core, i // 2)
            x = x_ref[:, :, pl.ds(pl.multiple_of(dest * c, 128), c)]
            parts = [x[p, :, :wide] for p in range(TAPS)]
            parts.append(jnp.concatenate([x[p, :, wide:] for p in range(TAPS)], axis=1))
            o_ref[z] = jnp.concatenate(parts, axis=0).astype(BF16)


def cut_conv_kernel(me_ref, *refs):
    zs = refs[0].shape[0]
    z, y, core = me_ref[0] // 4, (me_ref[0] // 2) % 2, me_ref[0] % 2
    for m in range(zs):
        for i in range(4):
            at = 2 * jnp.bitwise_xor(y, i % 2) + jnp.bitwise_xor(core, i // 2)
            refs[4 + m][at] = refs[i][jnp.bitwise_xor(z, m)]


def exchange_conv(prefilled_conv, me, n):
    slots, _, inner = prefilled_conv.shape
    zs = n // 4
    piece = ((TAPS + 1) * slots, inner // n * TAPS // (TAPS + 1))
    conv = jnp.transpose(prefilled_conv, (1, 0, 2))
    packed = small(pack_conv_kernel, me, [conv], [(zs,) + piece] * 4, "pack_conv")
    near, far = swap(packed[2], 1, n), swap(packed[3], 1, n)
    got = [packed[0], swap(packed[1], 2, n), near, swap(far, 2, n)]
    cut = small(cut_conv_kernel, me, got, [(4,) + piece] * zs, "cut_conv")
    return [cut[0]] + [swap(cut[m], 4 * m, n) for m in range(1, zs)]


def pack_state_kernel(x_ref, *refs):
    o_ref = refs[-1]
    slots = x_ref.shape[0]
    some, _, c = o_ref.shape
    for d in range(some):
        for k in range(slots):
            o_ref[d, STATE * k : STATE * (k + 1), :] = x_ref[k, :, d * c : (d + 1) * c].astype(BF16)


def pack_state(after, prefilled_state, n):
    slots, _, inner = prefilled_state.shape
    c = inner // n
    some = 4
    return pl.pallas_call(
        pack_state_kernel,
        grid=(n // some,),
        in_specs=[pl.BlockSpec((slots, STATE, some * c), lambda d: (0, 0, d))]
        + [pl.BlockSpec(memory_space=pl.ANY)] * len(after),
        out_specs=pl.BlockSpec((some, slots * STATE, c), lambda d: (d, 0, 0)),
        out_shape=jax.ShapeDtypeStruct((n, slots * STATE, c), BF16),
        compiler_params=params(24),
        cost_estimate=cost(0, slots * STATE * inner * 6),
        name="pack_state",
    )(prefilled_state, *after)


def hold_kernel(x_ref, after_ref, o_ref):
    pass


def hold(x, after):
    some = pl.BlockSpec(memory_space=pl.ANY)
    return pl.pallas_call(
        hold_kernel,
        in_specs=[some, some],
        out_specs=some,
        out_shape=jax.ShapeDtypeStruct(x.shape, x.dtype),
        input_output_aliases={0: 0},
        compiler_params=params(8),
        cost_estimate=cost(0, 0),
        name="hold",
    )(x, after)


def half_kernel(me_ref, after_ref, w_ref, o_ref):
    o_ref[...] = w_ref[...]


def weight_half(me, after, out_weight):
    c, cols = out_weight.shape
    tile = 1024
    tiles = cols // 2 // tile
    return pl.pallas_call(
        half_kernel,
        grid_spec=pltpu.PrefetchScalarGridSpec(
            num_scalar_prefetch=1,
            grid=(tiles,),
            in_specs=[
                pl.BlockSpec(memory_space=pl.ANY),
                pl.BlockSpec((c, tile), lambda j, me_ref: (0, (1 - me_ref[0] % 2) * tiles + j)),
            ],
            out_specs=pl.BlockSpec((c, tile), lambda j, me_ref: (0, j)),
        ),
        out_shape=jax.ShapeDtypeStruct((c, cols // 2), BF16),
        compiler_params=params(56),
        cost_estimate=cost(0, 2 * c * cols),
        name="weight_half",
    )(me, after, out_weight)


def conv_kernel(steps, n, me_ref, target_ref, old_ref, x_ref, w_ref, bias_ref, proj_ref, *refs):
    zs = n // 4
    moved, (conv_ref, send_ref, keep_ref, moved_scr, win) = refs[:zs], refs[-5:]
    rows, c = win.shape[1:]
    columns = target_ref.shape[1]
    own = rows // n
    core, my_z = me_ref[0] % 2, me_ref[0] // 4
    for m in range(zs):
        moved_scr[jnp.bitwise_xor(my_z, m)] = moved[m][...]
    fresh = moved_scr[...].reshape(columns, moved_scr.shape[3])
    wide = fresh.shape[1]
    row_id = lax.broadcasted_iota(jnp.int32, (rows, columns), 0)
    hots = [row_id == target_ref[p : p + 1, :] for p in range(TAPS + 1)]
    taken = jnp.max(hots[0].astype(F32), axis=1, keepdims=True) > 0.0
    fresh = [jnp.dot(hot.astype(BF16), fresh, preferred_element_type=F32) for hot in hots]
    for p in range(TAPS):
        part = (c - wide) * p
        win[p, :, :wide] = jnp.where(taken, fresh[p], old_ref[p, :, :wide])
        win[p, :, wide:] = jnp.where(taken, fresh[TAPS][:, part : part + c - wide], old_ref[p, :, wide:])
    for i, t in enumerate(steps):
        total = None
        for q in range(TAPS + 1):
            place = t + q
            value = win[place] if place < TAPS else x_ref[place - TAPS].astype(F32)
            term = value * w_ref[q : q + 1, :]
            total = term if total is None else total + term
        total = total + bias_ref[...]
        conv_out = total * sigmoid(total)
        conv_ref[i] = conv_out
        part = lax.dot_general(
            conv_out.astype(BF16), proj_ref[...], (((1,), (1,)), ((), ())), preferred_element_type=F32
        )
        pad = jnp.zeros((own, WIDE - part.shape[1]), BF16)
        for q in range(n // 2):
            low = part[2 * q * own : (2 * q + 1) * own, :]
            high = part[(2 * q + 1) * own : (2 * q + 2) * own, :]
            send_ref[q, i, :, : part.shape[1]] = jnp.where(core == 0, high, low).astype(BF16)
            keep_ref[q, i, :, : part.shape[1]] = jnp.where(core == 0, low, high).astype(BF16)
            send_ref[q, i, :, part.shape[1] :] = pad
            keep_ref[q, i, :, part.shape[1] :] = pad


def conv_steps(steps, n, me, after, target, old, moved, step_x, conv_weight, conv_bias, proj):
    _, rows, c = old.shape
    s = len(steps)
    last = max(steps) + 1
    parts = (n // 2, s, rows // n, WIDE)
    return pl.pallas_call(
        functools.partial(conv_kernel, steps, n),
        grid_spec=pltpu.PrefetchScalarGridSpec(
            num_scalar_prefetch=1,
            grid=(1,),
            in_specs=[
                whole(target.shape),
                whole(old.shape),
                whole((last, rows, c)),
                whole(conv_weight.shape),
                whole((1, c)),
                whole(proj.shape),
            ]
            + [whole(moved[0].shape)] * len(moved)
            + [pl.BlockSpec(memory_space=pl.ANY)] * len(after),
            out_specs=[whole((s, rows, c)), whole(parts), whole(parts)],
            scratch_shapes=[
                pltpu.VMEM((len(moved),) + moved[0].shape, BF16),
                pltpu.VMEM((TAPS, rows, c), F32),
            ],
        ),
        out_shape=[jax.ShapeDtypeStruct((s, rows, c), F32)] + [jax.ShapeDtypeStruct(parts, BF16)] * 2,
        compiler_params=params(40),
        cost_estimate=cost(2 * s * rows * c * 544, rows * c * (12 + 6 * s) + c * 1088, s * rows * c),
        name="conv_project",
    )(me, target, old, step_x, conv_weight, conv_bias, proj, *moved, *after)


def add_y_kernel(me_ref, *refs):
    keep_ref, got_ref, send_ref, left_ref = refs[-4:]
    y = (me_ref[0] // 2) % 2
    for z in range(send_ref.shape[0]):
        for o_ref, at in ((send_ref, 2 * z + 1 - y), (left_ref, 2 * z + y)):
            o_ref[z] = (keep_ref[at].astype(F32) + got_ref[at].astype(F32)).astype(BF16)


def add_z_kernel(zs, me_ref, *refs):
    keep_ref, got_ref, *o_refs = refs[-2 - zs :]
    z = me_ref[0] // 4
    for m, o_ref in enumerate(o_refs):
        at = jnp.bitwise_xor(z, m)
        o_ref[...] = (keep_ref[at].astype(F32) + got_ref[at].astype(F32)).astype(BF16)


def norm_kernel(me_ref, gain_ref, *refs):
    o_ref = refs[-1]
    total = refs[0][...].astype(F32)
    for ref in refs[1:-1]:
        total = total + ref[...].astype(F32)
    dt = total[:, :, :DT_RANK]
    dt = dt * lax.rsqrt(jnp.mean(dt * dt, axis=2, keepdims=True) + RMS_EPS) * gain_ref[:, :DT_RANK][None]
    tail = total[:, :, DT_RANK:]
    lane = lax.broadcasted_iota(jnp.int32, tail.shape, 2)
    square = tail * tail
    is_b = lane < STATE
    is_c = jnp.logical_and(lane >= STATE, lane < 2 * STATE)
    mean_b = jnp.sum(jnp.where(is_b, square, 0.0), axis=2, keepdims=True) / STATE
    mean_c = jnp.sum(jnp.where(is_c, square, 0.0), axis=2, keepdims=True) / STATE
    scale_b = lax.rsqrt(jnp.maximum(mean_b, BC_FLOOR))
    scale_c = lax.rsqrt(jnp.maximum(mean_c, BC_FLOOR))
    tail = tail * jnp.where(is_b, scale_b, scale_c) * gain_ref[:, DT_RANK:][None]
    o_ref[:, :, :DT_RANK] = dt.astype(BF16)
    o_ref[:, :, DT_RANK:] = jnp.where(lane < 2 * STATE, tail, 0.0).astype(BF16)


def merge_kernel(me_ref, *refs):
    o_ref = refs[-1]
    z = me_ref[0] // 4
    for m, ref in enumerate(refs[:-1]):
        o_ref[jnp.bitwise_xor(z, m)] = ref[...]


def reduce_projection(send, keep, gain, me, n):
    zs = n // 4
    piece = keep.shape[1:]
    got = swap(send, 1, n)
    send, keep = small(add_y_kernel, me, [keep, got], [(zs,) + piece] * 2, "add_y")
    got = swap(send, 2, n)
    cut = small(functools.partial(add_z_kernel, zs), me, [keep, got], [piece] * zs, "add_z")
    cut = [cut[0]] + [swap(cut[m], 4 * m, n) for m in range(1, zs)]
    (low,) = small(norm_kernel, me, [gain] + cut, [piece], "norm")
    lows = [low] + [swap(low, 4 * m, n) for m in range(1, zs)]
    (mine,) = small(merge_kernel, me, lows, [(zs,) + piece], "merge_z")
    beside = swap(mine, 2, n)
    return keep, low, mine, (mine, beside, swap(mine, 1, n), swap(beside, 1, n))


def assemble_low(lows, index, low_scr, me_ref):
    y, core = (me_ref[0] // 2) % 2, me_ref[0] % 2
    for i, low_ref in enumerate(lows):
        for z in range(low_ref.shape[0]):
            low_scr[z, jnp.bitwise_xor(y, i % 2), jnp.bitwise_xor(core, i // 2)] = low_ref[z, index]
    return low_scr[...].reshape(-1, WIDE)


def step_sizes(low, dtp_ref, dtb_ref):
    pre = jnp.dot(low[:, :DT_RANK], dtp_ref[...], preferred_element_type=F32) + dtb_ref[...]
    return jnp.maximum(pre, 0.0) + jnp.log(1.0 + jnp.exp(-jnp.abs(pre)))


def step_kernel(t, me_ref, after_ref, *refs):
    *lows, dtp_ref, dtb_ref, step_ref, tail_ref, low_scr = refs
    low = assemble_low(lows, t, low_scr, me_ref)
    step_ref[...] = step_sizes(low, dtp_ref, dtb_ref)
    tail_ref[...] = low[:, DT_RANK:].astype(F32)


def step_rows(t, me, after, lows, dt_proj, dt_bias, rows, n):
    return small(
        functools.partial(step_kernel, t),
        me,
        [*lows, dt_proj, dt_bias],
        [(rows, dt_proj.shape[1]), (rows, 128)],
        "step_rows",
        after,
        F32,
        [pltpu.VMEM((n // 4, 2, 2, rows // n, WIDE), BF16)],
        12,
    )


def state_kernel(t, behind, me_ref, *refs):
    first, last = t == 0, t == STEPS - 1
    refs = refs[behind:]
    step_ref, tail_ref, conv_ref, z_ref, alog_ref, skip_ref, state_ref, *refs = refs
    new_ref = None
    if not last:
        new_ref, *refs = refs
    gated_ref, decay_scr, bc_scr, *refs = refs
    block = pl.program_id(0)
    rows, c = step_ref.shape
    take = conv_ref.shape[0]
    blocks = rows // take

    if first:
        buf, sems = refs

        def fetch(at, slot):
            first_row = pl.multiple_of(at * (take * STATE), take * STATE)
            return [
                pltpu.make_async_copy(
                    state_ref.at[pl.ds(first_row, take * STATE), 128 * l : 128 * (l + 1)],
                    buf.at[slot, l],
                    sems.at[slot, l],
                )
                for l in range(c // 128)
            ]

        now = lax.rem(block, 2)

        @pl.when(block == 0)
        def _():
            for copy in fetch(0, 0):
                copy.start()

        @pl.when(block + 1 < blocks)
        def _():
            for copy in fetch(block + 1, 1 - now):
                copy.start()

    @pl.when(block == 0)
    def _():
        decay_scr[...] = -jnp.exp(alog_ref[...])

    base = block * take
    if first:
        for copy in fetch(block, now):
            copy.wait()

    tall, lanes = 16, min(512, c)
    for r in range(0, take, tall):
        tail = tail_ref[pl.ds(pl.multiple_of(base + r, tall), tall), :]
        for s in range(2 * STATE):
            bc_scr[s] = jnp.broadcast_to(tail[:, s : s + 1], (tall, 128))
        for l in range(0, c, lanes):
            cols = slice(l, l + lanes)
            step = step_ref[pl.ds(pl.multiple_of(base + r, tall), tall), cols]
            conv = conv_ref[r : r + tall, cols]
            drive = step * conv
            total = skip_ref[:, cols] * conv
            for s in range(STATE):
                if first:
                    at = pl.ds(STATE * r + s, tall, stride=STATE)
                    tiles = range(l // 128, (l + lanes) // 128)
                    old = jnp.concatenate([buf[now, k, at, :] for k in tiles], axis=1)
                else:
                    old = state_ref[s, r : r + tall, cols].astype(F32)
                b = jnp.concatenate([bc_scr[s]] * (lanes // 128), axis=1)
                g = jnp.concatenate([bc_scr[STATE + s]] * (lanes // 128), axis=1)
                state = jnp.exp(step * decay_scr[s : s + 1, cols]) * old + drive * b
                if not last:
                    new_ref[s, r : r + tall, cols] = state.astype(BF16)
                total = total + state * g
            z = z_ref[0, r : r + tall, cols].astype(F32)
            gated_ref[r : r + tall, cols] = (total * (z * sigmoid(z))).astype(BF16)


def state_step(t, me, after, steps, conv, step_z, a_log, d_skip, state, n):
    _, rows, c = conv.shape
    take = 2 * rows // n
    blocks = rows // take
    first, last = t == 0, t == STEPS - 1

    def placed(i, me_ref):
        z, y = i // 2, i % 2
        mine = (y == (me_ref[0] // 2) % 2).astype(jnp.int32)
        return (mine * (blocks // 2) + z, 0)

    vmem = pl.BlockSpec(memory_space=pltpu.VMEM)
    in_specs = [vmem] * 2 + [
        pl.BlockSpec((None, take, c), lambda i, *_: (t, i, 0)),
        pl.BlockSpec((1, take, c), lambda i, *_: (t, i, 0)),
        whole(a_log.shape),
        whole((1, c)),
    ]
    scratch = [
        pltpu.VMEM((STATE, c), F32),
        pltpu.VMEM((2 * STATE, 16, 128), F32),
    ]
    flat = pl.BlockSpec((STATE, take, c), lambda i, *_: (0, i, 0))
    if first:
        in_specs = in_specs + [pl.BlockSpec(memory_space=pl.ANY)]
        scratch += [
            pltpu.VMEM((2, c // 128, take * STATE, 128), F32),
            pltpu.SemaphoreType.DMA((2, c // 128)),
        ]
    else:
        in_specs = in_specs + [flat]
    in_specs = [pl.BlockSpec(memory_space=pl.ANY)] * len(after) + in_specs
    out_specs = [pl.BlockSpec((take, c), placed)]
    out_shape = [jax.ShapeDtypeStruct((rows, c), BF16)]
    if not last:
        out_specs = [flat] + out_specs
        out_shape = [jax.ShapeDtypeStruct((STATE, rows, c), BF16)] + out_shape
    size = rows * STATE * c
    out = pl.pallas_call(
        functools.partial(state_kernel, t, len(after)),
        grid_spec=pltpu.PrefetchScalarGridSpec(
            num_scalar_prefetch=1,
            grid=(blocks,),
            in_specs=in_specs,
            out_specs=out_specs,
            scratch_shapes=scratch,
        ),
        out_shape=out_shape,
        compiler_params=params(48),
        cost_estimate=cost(8 * size, 4 * size, size),
        name="state_step",
    )(me, *after, *steps, conv, step_z, a_log, d_skip, state)
    return (None, out[0]) if last else (out[0], out[1])


def gather_kernel(me_ref, after_ref, row_ref, *refs):
    lows, refs = refs[:4], refs[4:]
    conv_ref, z_ref, dtp_ref, dtb_ref, o_ref, low_scr = refs
    count = o_ref.shape[1]
    _, rows, c = conv_ref.shape
    hot = (row_ref[:, :1] == lax.broadcasted_iota(jnp.int32, (count, rows), 1)).astype(F32).astype(BF16)
    for t in range(STEPS):
        low = jnp.dot(hot, assemble_low(lows, t, low_scr, me_ref), preferred_element_type=F32)
        o_ref[t, :, :c] = step_sizes(low.astype(BF16), dtp_ref, dtb_ref)
        o_ref[t, :, 3 * c :] = low[:, DT_RANK:]
        conv = conv_ref[t]
        high = conv.astype(BF16)
        rest = (conv - high.astype(F32)).astype(BF16)
        o_ref[t, :, c : 2 * c] = jnp.dot(hot, high, preferred_element_type=F32) + jnp.dot(
            hot, rest, preferred_element_type=F32
        )
        z = jnp.dot(hot, z_ref[t], preferred_element_type=F32)
        o_ref[t, :, 2 * c : 3 * c] = z * sigmoid(z)


def gather_live(me, after, row_of_live, lows, conv, step_z, dt_proj, dt_bias, n):
    _, rows, c = conv.shape
    count = row_of_live.shape[0]
    (out,) = small(
        gather_kernel,
        me,
        [row_of_live, *lows, conv, step_z, dt_proj, dt_bias],
        [(STEPS, count, 3 * c + 128)],
        "gather_live",
        after,
        F32,
        [pltpu.VMEM((n // 4, 2, 2, rows // n, WIDE), BF16)],
        40,
    )
    return out


def live_kernel(slot_ref, after_ref, moved_ref, live_ref, alog_ref, skip_ref, o_ref, buf, state_scr):
    _, count, c = o_ref.shape
    def place(i, carry):
        source, slot = slot_ref[0, i], slot_ref[1, i]
        at = pl.multiple_of(i * STATE, STATE)
        from_row = pl.multiple_of(slot * STATE, STATE)
        value = moved_ref[source, pl.ds(from_row, STATE), :].astype(F32)
        for l in range(c // 128):
            buf[l, pl.ds(at, STATE), :] = value[:, 128 * l : 128 * (l + 1)]
        return carry

    lax.fori_loop(0, count, place, 0)
    for s in range(STATE):
        for l in range(c // 128):
            state_scr[s, :, 128 * l : 128 * (l + 1)] = buf[l, pl.ds(s, count, stride=STATE), :]
    tall, lanes = 16, min(512, c)

    def step_all(t, carry):
        for r in range(0, count, tall):
            tail = live_ref[t, r : r + tall, 3 * c :]
            for l in range(0, c, lanes):
                cols = slice(l, l + lanes)
                step = live_ref[t, r : r + tall, cols]
                conv = live_ref[t, r : r + tall, c + l : c + l + lanes]
                gate = live_ref[t, r : r + tall, 2 * c + l : 2 * c + l + lanes]
                drive = step * conv
                total = skip_ref[:, cols] * conv
                for s in range(STATE):
                    rate = -jnp.exp(alog_ref[s : s + 1, cols])
                    old = state_scr[s, r : r + tall, cols]
                    state = jnp.exp(step * rate) * old + drive * tail[:, s : s + 1]
                    state_scr[s, r : r + tall, cols] = state
                    total = total + state * tail[:, STATE + s : STATE + s + 1]
                o_ref[t, r : r + tall, cols] = (total * gate).astype(BF16)
        return carry

    lax.fori_loop(0, STEPS, step_all, 0)


def live_steps(slot_of_live, after, moved, gathered, a_log, d_skip):
    count, c = gathered.shape[1], a_log.shape[1]
    (out,) = small(
        live_kernel,
        slot_of_live,
        [moved, gathered, a_log, d_skip],
        [(STEPS, count, c)],
        "live_steps",
        after,
        BF16,
        [pltpu.VMEM((c // 128, count * STATE, 128), F32), pltpu.VMEM((STATE, count, c), F32)],
        40,
    )
    return out


def fix_kernel(t, take, me_ref, after_ref, row_ref, gated_ref, live_ref, o_ref):
    rows = gated_ref.shape[0]
    count = live_ref.shape[1]
    shift = take.bit_length() - 1
    place = lax.broadcasted_iota(jnp.int32, (rows, count), 0)
    mine = place >= rows // 2
    within = place - jnp.where(mine, rows // 2, 0)
    y = (me_ref[0] // 2) % 2
    row = ((2 * (within >> shift) + jnp.where(mine, y, 1 - y)) << shift) + (within & (take - 1))
    hot = (row == row_ref[...]).astype(F32)
    taken = jnp.max(hot, axis=1, keepdims=True) > 0.0
    live = jnp.dot(hot.astype(BF16), live_ref[t], preferred_element_type=F32)
    o_ref[...] = jnp.where(taken, live, gated_ref[...].astype(F32)).astype(BF16)


def out_kernel(me_ref, own_ref, other_ref, wown_ref, wother_ref, *refs):
    send_ref, keep_ref = refs[-2:]
    total = jnp.dot(own_ref[...], wown_ref[...], preferred_element_type=F32)
    total = total + jnp.dot(other_ref[...], wother_ref[...], preferred_element_type=F32)
    half = send_ref.shape[0]
    send_ref[...] = total[:half].astype(BF16)
    keep_ref[...] = total[half:].astype(BF16)


def out_project(me, own, other, out_weight, other_weight, after, part, parts):
    rows, c = own.shape
    tile = 1024
    every = out_weight.shape[1] // 2 // tile
    tiles = every // parts
    cols = tiles * tile
    first = part * tiles
    half = jax.ShapeDtypeStruct((rows // 2, cols), BF16)
    return pl.pallas_call(
        out_kernel,
        grid_spec=pltpu.PrefetchScalarGridSpec(
            num_scalar_prefetch=1,
            grid=(tiles,),
            in_specs=[
                pl.BlockSpec(memory_space=pltpu.VMEM),
                pl.BlockSpec(memory_space=pltpu.VMEM),
                pl.BlockSpec((c, tile), lambda j, me_ref: (0, (me_ref[0] % 2) * every + first + j)),
                pl.BlockSpec((c, tile), lambda j, me_ref: (0, first + j)),
            ]
            + [pl.BlockSpec(memory_space=pl.ANY)] * len(after),
            out_specs=[pl.BlockSpec((rows // 2, tile), lambda j, me_ref: (0, j))] * 2,
        ),
        out_shape=[half, half],
        compiler_params=params(48),
        cost_estimate=cost(4 * rows * c * cols, 4 * c * cols + 2 * rows * cols),
        name="out_project",
    )(me, own, other, out_weight, other_weight, *after)


def halve_kernel(stage, me_ref, after_ref, keep_ref, got_ref, send_ref, left_ref):
    bit = (me_ref[0] >> (2 + stage)) & 1
    for i in range(send_ref.shape[0]):
        for o_ref, at in ((send_ref, 2 * i + 1 - bit), (left_ref, 2 * i + bit)):
            o_ref[i] = (keep_ref[at].astype(F32) + got_ref[at].astype(F32)).astype(BF16)


def sum_z_kernel(me_ref, after_ref, keep_ref, got_ref, send_ref, left_ref):
    total = keep_ref[0].astype(F32) + got_ref[0].astype(F32)
    own = total.shape[0] // 2
    low, high = total[:own], total[own:]
    core = me_ref[0] % 2
    send_ref[...] = jnp.where(core == 0, high, low).astype(BF16)
    left_ref[...] = jnp.where(core == 0, low, high).astype(BF16)


def final_kernel(tiles, counts, me_ref, *refs):
    o_ref = refs[-1]
    own_half = pl.program_id(0) // tiles == me_ref[0] % 2
    tile = pl.program_id(0) % tiles
    at = 0
    for t, count in enumerate(counts):
        value = None
        for part in range(count):
            mine, theirs = refs[at][...].astype(F32), refs[at + 1][...].astype(F32)
            here = jnp.where(own_half, mine, theirs)
            value = here if value is None else jnp.where(tile == part, here, value)
            at += 2
        o_ref[:, t, :] = value.astype(BF16)


def final_join(me, pieces):
    own = pieces[0][0][0].shape[0]
    cols = sum(keep.shape[1] for keep, _ in pieces[0])
    tiles = max(len(parts) for parts in pieces)
    tile = cols // tiles
    args, specs = [], []
    for parts in pieces:
        for keep, got in parts:
            many = keep.shape[1] // tile
            spec = pl.BlockSpec((own, tile), lambda j, me_ref, many=many: (0, (j % tiles) % many))
            args += [keep, got]
            specs += [spec, spec]
    return pl.pallas_call(
        functools.partial(final_kernel, tiles, [len(parts) for parts in pieces]),
        grid_spec=pltpu.PrefetchScalarGridSpec(
            num_scalar_prefetch=1,
            grid=(2 * tiles,),
            in_specs=specs,
            out_specs=pl.BlockSpec((own, STEPS, tile), lambda j, me_ref: (0, 0, j)),
        ),
        out_shape=jax.ShapeDtypeStruct((own, STEPS, 2 * cols), BF16),
        compiler_params=params(16),
        cost_estimate=cost(0, own * cols * 32),
        name="final_join",
    )(me, *args)


def shards(
    resident_state,
    resident_conv,
    prefilled_state,
    prefilled_conv,
    live_counts,
    batch_rows,
    step_x,
    step_z,
    conv_weight,
    conv_bias,
    x_proj,
    norm_gain,
    dt_proj,
    dt_bias,
    a_log,
    d_skip,
    out_weight,
):
    n = lax.axis_size("dex")
    zs = n // 4
    rows = resident_state.shape[0]
    slots = prefilled_state.shape[0]
    c = resident_state.shape[2]
    me_scalar = lax.axis_index("dex").astype(jnp.int32)
    me = me_scalar.reshape(1)

    moved_conv = exchange_conv(prefilled_conv, me, n)
    packed = pack_state((moved_conv[1],), prefilled_state, n)
    cols = out_weight.shape[1] // 2

    is_live = jnp.arange(slots, dtype=jnp.int32)[None, :] < live_counts[:, None]
    target = jnp.where(is_live, batch_rows.reshape(n, slots), -1)
    place = jnp.arange(TAPS + 1, dtype=jnp.int32)
    mine = place[None, None, :, None] == place[:, None, None, None]
    spread = jnp.where(mine, target[None, :, None, :], -1).reshape(TAPS + 1, n * (TAPS + 1) * slots)
    flat = target.reshape(-1)
    number = jnp.arange(n * slots, dtype=jnp.int32)
    count = n * slots // 2
    rank = jnp.sum(((flat >= 0)[None, :] & (number[None, :] < number[:, None])).astype(jnp.int32), axis=1)
    hit = (rank[None, :] == number[:count, None]) & (flat >= 0)[None, :]
    live_slot = jnp.sum(jnp.where(hit, number[None, :], 0), axis=1)
    live_row = jnp.sum(jnp.where(hit, flat[None, :], 0), axis=1)
    slot_of_live = jnp.stack([live_slot // slots, live_slot % slots])
    row_of_live = jnp.broadcast_to(live_row[:, None], (count, 128))
    live_row = live_row.reshape(1, count)
    gain = jnp.concatenate([norm_gain, jnp.zeros((WIDE - norm_gain.shape[0],), F32)]).reshape(1, WIDE)
    old = jnp.transpose(resident_conv, (1, 0, 2))
    proj = x_proj.T
    bias = conv_bias.reshape(1, c)
    conv, send, keep = conv_steps(
        tuple(range(STEPS)), n, me, (packed,), spread, old, moved_conv, step_x, conv_weight, bias, proj
    )
    behind, low, merged, lows = reduce_projection(send, keep, gain, me, n)
    half_weight = weight_half(me, behind, out_weight)
    packed = hold(packed, merged)
    moved_state = lax.all_to_all(packed, "dex", 0, 0, tiled=True)
    other_weight = swap(hold(half_weight, low), 1, n)

    state = resident_state.reshape(rows * STATE, c)
    sends, keeps, gated = {}, {}, {}
    stages = zs.bit_length() - 1
    take = 2 * rows // n

    rate_bias, skip = dt_bias.reshape(1, c), d_skip.reshape(1, c)

    next_steps = None

    def s_step(t, after):
        nonlocal state
        if t == 0:
            steps = step_rows(0, me, after, lows, dt_proj, rate_bias, rows, n)
        else:
            steps = next_steps
        state, gated[t] = state_step(t, me, after, steps, conv, step_z, a_log, skip, state, n)
        return gated[t]

    def fix(t, after):
        kernel = functools.partial(fix_kernel, t, take)
        (gated[t],) = small(kernel, me, [live_row, gated[t], live_gated], [(rows, c)], "fix", (after,))
        if t == STEPS - 1:
            return gated[t]
        nonlocal next_steps
        next_steps = step_rows(t + 1, me, (gated[t],), lows, dt_proj, rate_bias, rows, n)
        return next_steps[1]

    def project(t, after, parts=1):
        other = swap(gated[t], 1, n)
        for part in range(parts):
            sends[t, part], keeps[t, part] = out_project(
                me, gated[t], other, out_weight, other_weight, (after,), part, parts
            )
            after = keeps[t, part]
        return after

    def reduce(t, stage, after, part=0):
        at = t, part
        width = keeps[at].shape[-1]
        if stage == 0:
            keep = keeps[at].reshape(zs, take, width)
            got = swap(sends[at], 2, n).reshape(zs, take, width)
        else:
            keep, got = keeps[at], swap(sends[at], 2 << stage, n)
        if stage < stages:
            kernel, shape = functools.partial(halve_kernel, stage), (keep.shape[0] // 2, take, width)
        else:
            kernel, shape = sum_z_kernel, (take // 2, width)
        sends[at], keeps[at] = small(kernel, me, [keep, got], [shape] * 2, "reduce_%d" % stage, (after,))
        if stage == stages:
            sends[at] = swap(sends[at], 1, n)
        return keeps[at]

    last = s_step(0, (packed,))
    gathered = gather_live(me, (last,), row_of_live, lows, conv, step_z, dt_proj, rate_bias, n)
    live_gated = live_steps(slot_of_live, (last,), moved_state, gathered, a_log, skip)
    last = fix(0, live_gated)
    last = project(0, last)
    for t in range(1, STEPS):
        last = s_step(t, (last,))
        last = fix(t, last)
        if t > 1:
            for stage in range(1, stages):
                last = reduce(t - 2, stage, last)
        last = project(t, last, 1 if t < STEPS - 1 else 2)
        if t < STEPS - 1:
            last = reduce(t - 1, 0, last)
    last = reduce(t - 3, stages, last)
    last = reduce(t - 1, 0, last)
    last = reduce(t, 0, last, 0)
    for stage in range(1, stages):
        last = reduce(t - 1, stage, last)
    last = reduce(t, 0, last, 1)
    last = reduce(t - 2, stages, last)
    for part in range(2):
        for stage in range(1, stages):
            last = reduce(t, stage, last, part)
    last = reduce(t - 1, stages, last)
    last = reduce(t, stages, last, 0)
    last = reduce(t, stages, last, 1)
    pieces = [[(keeps[t, part], sends[t, part]) for part in range(1 if t < STEPS - 1 else 2)] for t in range(STEPS)]
    return final_join(me, pieces)


def solution(mesh):
    placed = (
        P("grp", None, "dex"),
        P("grp", None, "dex"),
        P(("grp", "dex"), None, None),
        P(("grp", "dex"), None, None),
        P("grp"),
        P("grp"),
        P(None, "grp", "dex"),
        P(None, "grp", "dex"),
        P(None, "dex"),
        P("dex"),
        P("dex", None),
        P(),
        P(None, "dex"),
        P("dex"),
        P(None, "dex"),
        P("dex"),
        P("dex", None),
    )
    return jax.shard_map(
        shards, mesh=mesh, in_specs=placed, out_specs=P(("grp", "dex"), None, None), check_vma=False
    )
```
